32 devices in a mesh: section: 4 (over x, core), sub: 2 (over y), rng: 4 (over z).
Axes of the slice: x: 2, y: 2, z: 4, core: 2. Of those that a mesh axis runs over, the one named last changes fastest.
Arguments:
- echoes: bfloat16 [2, 2, 24, 16384], P(None, 'sub', 'section', 'rng'), may hold values from -6 to 6
- chirp: bfloat16 [2, 2048], replicated, may hold values from -0.25 to 0.25
- steer: bfloat16 [2, 2, 128, 24], P(None, 'sub'), may hold values from -2 to 2
- pulse_order: int32 [2, 24], P('sub'), may hold values from 0 to 23, each once within a row
- band_coef: bfloat16 [5, 2, 2, 2, 128, 16], P(None, 'sub'), may hold values from -2.5 to 2.5
- band_start: int32 [5, 2, 2, 128], P(None, 'sub'), may hold values from 0 to 112
- band_width: int32 [5, 2, 2, 128], P(None, 'sub'), may hold values from 1 to 16
Outputs:
- image: bfloat16 [2, 256, 4, 4096], P(None, 'sub', 'rng', 'section')
The draws below stay inside these ranges and needn't reach their ends.
Inputs may be any that keep to these rules, and one draw needn't show every extreme that they name: `pulse_order`: each row is a permutation of the 24 aperture positions.
All inputs are finite; a program needn't handle non-finite values.
Results may differ from the reference program's by a relative error of at most 0.0085.
Values may be sent and summed in bfloat16 or wider, within the bound.
No kernel may reach another device: no remote copies, remote signals or barrier semaphores. Data moves between devices by JAX's collectives and lax.ppermute only.
A program may use at most 64 MiB of HBM per device.

```python
import jax
import jax.numpy as jnp
from jax import lax

RS = 16384
K = 2048
BL = 128
BW = 16
LEVELS = 5
SUBS = 2
PSUB = 24
BEAMS = 256
RC = 4096
N_SUB = 2
N_RNG = 4


def with_ends(entries, own_key, low, top_value):
    extent = entries.shape
    place = [jax.random.randint(jax.random.fold_in(own_key, axis), (), 0, extent[axis]) for axis in range(len(extent))]
    entries = entries.at[tuple(place)].set(low)
    longest = extent.index(max(extent))
    place[longest] = (place[longest] + 1) % extent[longest]
    return entries.at[tuple(place)].set(top_value)


def steps_of(own_key, extent, split, smallest, high):
    loudness, own = 1.0, jax.random.fold_in(own_key, 6)
    for dim, blocks in split:
        heights = jnp.exp(jax.random.uniform(jax.random.fold_in(own, dim), (blocks,), jnp.float32, smallest / len(split), high / len(split)))
        loudness = loudness * jnp.repeat(heights, extent[dim] // blocks).reshape([-1 if axis == dim else 1 for axis in range(len(extent))])
    return loudness


def centred(own_key, extent, scale, limit, pieces=(), held_as=jnp.bfloat16):
    entries = scale * jax.random.normal(own_key, extent, jnp.float32)
    if pieces:
        entries = entries * steps_of(own_key, extent, pieces, -0.22, 0.18)
    return jnp.clip(entries, -limit, limit).astype(held_as)


def setup_inputs(seed: int = 0) -> dict:
    seeds = jax.random.split(jax.random.key(seed), 8)
    echoes = centred(seeds[0], (2, SUBS, PSUB, RS), 1.0, 6.0, ((1, 2), (2, 4), (3, 4)))
    chirp = centred(seeds[1], (2, K), (1.0 / (2 * K) ** 0.5), 0.25)
    steer = centred(seeds[2], (2, SUBS, BL, PSUB), (1.0 / (2 * PSUB) ** 0.5), 2.0, ((1, 2),))
    pulse_order = jax.vmap(lambda own: jax.random.permutation(own, PSUB))(jax.random.split(seeds[3], SUBS)).reshape((SUBS, PSUB)).astype(jnp.int32)
    band_coef = centred(seeds[4], (LEVELS, SUBS, 2, 2, BL, BW), (1.0 / (2 * BW + 2) ** 0.5), 2.5, ((1, 2),))
    band_start = with_ends(jax.random.randint(seeds[5], (LEVELS, SUBS, 2, BL), 0, BL - BW + 1), jax.random.fold_in(seeds[5], 1), 0, BL - BW).astype(jnp.int32)
    band_width = with_ends(jax.random.randint(seeds[6], (LEVELS, SUBS, 2, BL), 1, BW + 1), jax.random.fold_in(seeds[6], 1), 1, BW).astype(jnp.int32)
    return {"echoes": echoes, "chirp": chirp, "steer": steer, "pulse_order": pulse_order, "band_coef": band_coef, "band_start": band_start, "band_width": band_width}


def compress_and_form(inputs):
    signal, weights_all, order_row, kernel_parts = inputs
    length = 1 << (RS + K - 1).bit_length()
    wave = lax.complex(signal[0].astype(jnp.float32), signal[1].astype(jnp.float32))
    kernel = lax.complex(kernel_parts[0].astype(jnp.float32), kernel_parts[1].astype(jnp.float32))
    spectrum = jnp.fft.fft(wave, n=length, axis=1) * jnp.conj(jnp.fft.fft(kernel, n=length))[None, :]
    result = jnp.fft.ifft(spectrum, axis=1)[:, :RS]
    compressed = jnp.stack([jnp.real(result), jnp.imag(result)]).astype(jnp.bfloat16)
    weights = jnp.take(weights_all, order_row, axis=2)
    real_part = jnp.dot(weights[0], compressed[0], preferred_element_type=jnp.float32) - jnp.dot(weights[1], compressed[1], preferred_element_type=jnp.float32)
    imag_part = jnp.dot(weights[0], compressed[1], preferred_element_type=jnp.float32) + jnp.dot(weights[1], compressed[0], preferred_element_type=jnp.float32)
    return jnp.stack([real_part, imag_part]).astype(jnp.bfloat16)


def reference(echoes, chirp, steer, pulse_order, band_coef, band_start, band_width):
    kernels = jnp.broadcast_to(chirp[None], (N_SUB, 2, K))
    images = lax.map(compress_and_form, (jnp.transpose(echoes, (1, 0, 2, 3)), jnp.transpose(steer, (1, 0, 2, 3)), pulse_order, kernels))
    nbits = N_SUB.bit_length() - 1
    for level in range(LEVELS):
        flip = 1 << (level % nbits)

        def merge_one(inputs):
            position, coef_sub, start_sub, width_sub = inputs
            own = images[position].astype(jnp.float32)
            other = images[jnp.bitwise_xor(position, flip)].astype(jnp.float32)
            total_real = jnp.zeros((BL, RS), jnp.float32)
            total_imag = jnp.zeros((BL, RS), jnp.float32)
            for side in range(2):
                source = own if side == 0 else other
                for tap in range(BW):
                    picked_rows = (start_sub[side] + tap).astype(jnp.int32)
                    gathered = source[:, picked_rows, :]
                    active = (tap < width_sub[side]).astype(jnp.float32)
                    weight_real = (coef_sub[side, 0, :, tap].astype(jnp.float32) * active)[:, None]
                    weight_imag = (coef_sub[side, 1, :, tap].astype(jnp.float32) * active)[:, None]
                    total_real = total_real + weight_real * gathered[0] - weight_imag * gathered[1]
                    total_imag = total_imag + weight_real * gathered[1] + weight_imag * gathered[0]
            return jnp.stack([total_real, total_imag]).astype(jnp.bfloat16)

        images = lax.map(merge_one, (jnp.arange(N_SUB, dtype=jnp.int32), band_coef[level], band_start[level], band_width[level]))
    image = jnp.transpose(images, (1, 0, 2, 3)).reshape(2, BEAMS, N_RNG, RC)
    return image
```

```python
import functools

import jax
import jax.numpy as jnp
from jax import lax
from jax.experimental import pallas as pl
from jax.experimental.pallas import tpu as pltpu
from jax.sharding import PartitionSpec as P

LANE = 128
SUBL = 8
F32 = jnp.float32
BF16 = jnp.bfloat16


def ceil_to(value, unit):
    return -(-value // unit) * unit


def pack_kernel(coef_ref, start_ref, width_ref, steer_ref, order_ref, pack_ref, starts, *, sections, group):
    levels, _, sides, parts, taps, beams = coef_ref.shape
    tap = lax.broadcasted_iota(jnp.int32, (taps, beams), 0)
    row = 0
    for level in range(levels):
        for side in range(sides):
            used = tap < width_ref[level, 0, side : side + 1, :]
            for part in range(parts):
                entries = coef_ref[level, 0, side, part].astype(F32)
                pack_ref[row : row + taps] = jnp.where(used, entries, 0.0).astype(BF16)
                row += taps
    pulses = order_ref.shape[1]
    each = pulses // sections
    position = lax.broadcasted_iota(jnp.int32, (pulses, pulses), 0)
    hit = (position == order_ref[0:1, :]).astype(F32)
    slot = lax.broadcasted_iota(jnp.int32, (sections * group, pulses), 0)
    pulse = lax.broadcasted_iota(jnp.int32, (sections * group, pulses), 1)
    place = jnp.zeros((sections * group, pulses), F32)
    for s in range(sections):
        inside = (pulse >= s * each) & (pulse < (s + 1) * each)
        place = jnp.where(inside & (slot - s * group == pulse - s * each), 1.0, place)
    pick = lax.dot_general(
        place.astype(BF16), hit.astype(BF16), (((1,), (1,)), ((), ())), preferred_element_type=F32
    )
    for part in range(parts):
        chosen = jnp.dot(pick.astype(BF16), steer_ref[part, 0], preferred_element_type=F32)
        pack_ref[row : row + sections * group] = chosen.astype(BF16)
        row += sections * group
    starts[...] = jnp.zeros_like(starts)
    for level in range(levels):
        starts[sides * level : sides * level + sides] = start_ref[level, 0].astype(F32)
    pack_ref[row : row + starts.shape[0]] = starts[...].astype(BF16)


def pack_rows(levels, sides, parts, taps, sections, group):
    return levels * sides * parts * taps + parts * sections * group + ceil_to(levels * sides, 16)


def pack_parameters(coef, start, width, steer, order, sections, group):
    levels, _, sides, parts, taps, beams = coef.shape
    return pl.pallas_call(
        functools.partial(pack_kernel, sections=sections, group=group),
        out_shape=jax.ShapeDtypeStruct((pack_rows(levels, sides, parts, taps, sections, group), beams), BF16),
        scratch_shapes=[pltpu.VMEM((ceil_to(levels * sides, 16), beams), F32)],
        name="pack_parameters",
    )(coef, start, width, steer, order)


def split_two(value):
    high = value.astype(BF16)
    return high, (value - high.astype(F32)).astype(BF16)


def operator_kernel(index_ref, own_ref, partner_ref, out_ref, weights, *, dims, sections, group):
    levels, sides, parts, taps, beams = dims
    width = sections * group
    refs = (own_ref, partner_ref)
    weight_row = levels * sides * parts * taps
    start_row = weight_row + parts * width

    def band(ref, level, side):
        first = ((level * sides + side) * parts) * taps
        tables = [ref[first + p * taps : first + (p + 1) * taps].astype(F32) for p in range(parts)]
        start = ref[start_row : start_row + ceil_to(levels * sides, 16)].astype(F32)
        start = start[level * sides + side : level * sides + side + 1].astype(jnp.int32)
        found = [[], []]
        for c in range(0, beams, SUBL):
            column = lax.broadcasted_iota(jnp.int32, (SUBL, beams), 0) + c
            offset = column - start
            spot = offset & (SUBL - 1)
            for p in range(parts):
                value = jnp.zeros((SUBL, beams), F32)
                for t in range(0, taps, SUBL):
                    got = jnp.take_along_axis(
                        tables[p][t : t + SUBL], spot, axis=0, mode="promise_in_bounds"
                    )
                    value = jnp.where((offset >= t) & (offset < t + SUBL), got, value)
                found[p].append(value)
        return [jnp.concatenate(f, axis=0) for f in found]

    def complex_operand(real, imag):
        top = jnp.concatenate([real, imag], axis=1)
        low = jnp.concatenate([-imag, real], axis=1)
        return jnp.concatenate([top, low], axis=0).astype(BF16)

    section = index_ref[0]
    images = []
    for a in range(2):
        for p in range(parts):
            weights[...] = refs[a][weight_row + p * width : weight_row + (p + 1) * width].astype(F32)
            rows = []
            for j in range(sections):
                at = pl.multiple_of((section ^ j) * group, group)
                rows.append(weights[pl.ds(at, group)])
            images.append(jnp.concatenate(rows, axis=0))
    zero = jnp.zeros((width, 2 * beams), F32)
    own = jnp.concatenate([jnp.concatenate(images[0:2], axis=1), zero], axis=0)
    partner = jnp.concatenate([zero, jnp.concatenate(images[2:4], axis=1)], axis=0)
    for level in range(levels):
        own_high, own_low = split_two(own)
        partner_high, partner_low = split_two(partner)
        own_rows = jnp.concatenate([own_high, own_low], axis=0)
        partner_rows = jnp.concatenate([partner_high, partner_low], axis=0)

        def merged(ref, mine, other):
            product = jnp.dot(
                mine, complex_operand(*band(ref, level, 0)), preferred_element_type=F32
            ) + jnp.dot(other, complex_operand(*band(ref, level, 1)), preferred_element_type=F32)
            return product[: 2 * width] + product[2 * width :]

        following = merged(own_ref, own_rows, partner_rows)
        if level < levels - 1:
            partner = merged(partner_ref, partner_rows, own_rows)
        own = following
    blocks = []
    for j in range(2 * sections):
        real = own[j * group : (j + 1) * group, :beams]
        imag = own[j * group : (j + 1) * group, beams:]
        blocks.append(jnp.concatenate([real, imag], axis=1))
        blocks.append(jnp.concatenate([-imag, real], axis=1))
    whole = jnp.concatenate(blocks, axis=0).T
    high, low = split_two(whole)
    out_ref[...] = jnp.concatenate([high, low], axis=1)


def fold_operator(section, own, partner, dims, sections, group):
    beams = dims[-1]
    width = sections * group
    return pl.pallas_call(
        functools.partial(operator_kernel, dims=dims, sections=sections, group=group),
        out_shape=jax.ShapeDtypeStruct((2 * beams, 8 * width), BF16),
        in_specs=[
            pl.BlockSpec(memory_space=pltpu.SMEM),
            pl.BlockSpec(memory_space=pltpu.VMEM),
            pl.BlockSpec(memory_space=pltpu.VMEM),
        ],
        scratch_shapes=[pltpu.VMEM((width, beams), F32)],
        name="fold_operator",
    )(section, own, partner)


def compress_kernel(index_ref, echo_ref, halo_ref, chirp_ref, out_ref, rows, even, odd, table, *, sections, group):
    pulses, _, length = echo_ref.shape
    taps = chirp_ref.shape[1]
    blocks, extra = length // LANE, taps // LANE
    total = blocks + extra
    reverse = LANE - 1 - lax.broadcasted_iota(jnp.int32, (2, LANE), 1)
    below = lax.broadcasted_iota(jnp.int32, (LANE, LANE), 1) <= lax.broadcasted_iota(
        jnp.int32, (LANE, LANE), 0
    )
    before = [jnp.zeros((LANE, LANE), F32)] * 2
    for lag in range(extra + 1):
        if lag < extra:
            piece = chirp_ref[:, lag * LANE : (lag + 1) * LANE].astype(F32)
            piece = jnp.take_along_axis(piece, reverse, axis=1, mode="promise_in_bounds")
            turned = [
                pltpu.roll(
                    jnp.broadcast_to(piece[c : c + 1], (LANE, LANE)), 1, 1, stride=1, stride_axis=0
                )
                for c in range(2)
            ]
        else:
            turned = [jnp.zeros((LANE, LANE), F32)] * 2
        real, imag = [jnp.where(below, turned[c], before[c]) for c in range(2)]
        before = turned
        at = lag * 2 * LANE
        table[at : at + LANE, :LANE] = real.astype(BF16)
        table[at : at + LANE, LANE:] = (-imag).astype(BF16)
        table[at + LANE : at + 2 * LANE, :LANE] = imag.astype(BF16)
        table[at + LANE : at + 2 * LANE, LANE:] = real.astype(BF16)
    rows[...] = jnp.zeros_like(rows)
    for p in range(pulses):
        near = echo_ref[p].astype(F32)
        far = halo_ref[p, :, :taps].astype(F32)
        for c in range(2):
            rows[c * group + p : c * group + p + 1, :length] = near[c : c + 1]
            rows[c * group + p : c * group + p + 1, length:] = far[c : c + 1]
    held = [
        jnp.concatenate(
            [rows[:group, b * LANE : (b + 1) * LANE], rows[group:, b * LANE : (b + 1) * LANE]], axis=1
        )
        for b in range(total)
    ]
    for b in range(0, total, 2):
        even[b * group : (b + 2) * group] = jnp.concatenate(held[b : b + 2], axis=0).astype(BF16)
    for b in range(1, total - 1, 2):
        odd[(b - 1) * group : (b + 1) * group] = jnp.concatenate(held[b : b + 2], axis=0).astype(BF16)
    window = blocks * group
    pieces = []
    for lag in range(extra + 1):
        source, at = (even, lag) if lag % 2 == 0 else (odd, lag - 1)
        pieces.append(source[at * group : at * group + window])
    done = jnp.dot(jnp.concatenate(pieces, axis=1), table[...], preferred_element_type=F32)
    section = index_ref[0]
    chunk = blocks // sections
    for s in range(sections):
        real = [done[(s * chunk + b) * group : (s * chunk + b + 1) * group, :LANE] for b in range(chunk)]
        imag = [done[(s * chunk + b) * group : (s * chunk + b + 1) * group, LANE:] for b in range(chunk)]
        stacked = jnp.concatenate(
            [jnp.concatenate(real, axis=1), jnp.concatenate(imag, axis=1)], axis=0
        )
        out_ref[section ^ s] = stacked.astype(BF16)


def compress_pulses(section, echo, halo, chirp, sections, group):
    pulses, _, length = echo.shape
    taps = chirp.shape[1]
    blocks, extra = length // LANE, taps // LANE
    total = blocks + extra
    return pl.pallas_call(
        functools.partial(compress_kernel, sections=sections, group=group),
        out_shape=jax.ShapeDtypeStruct((sections, 2 * group, length // sections), BF16),
        in_specs=[pl.BlockSpec(memory_space=pltpu.SMEM)] + [pl.BlockSpec(memory_space=pltpu.VMEM)] * 3,
        scratch_shapes=[
            pltpu.VMEM((2 * group, total * LANE), F32),
            pltpu.VMEM((total * group, 2 * LANE), BF16),
            pltpu.VMEM((total * group, 2 * LANE), BF16),
            pltpu.VMEM(((extra + 1) * 2 * LANE, 2 * LANE), BF16),
        ],
        compiler_params=pltpu.CompilerParams(vmem_limit_bytes=24 * 1024 * 1024),
        name="compress_pulses",
    )(section, echo, halo, chirp)


def image_kernel(operator_ref, *refs):
    out_ref = refs[-1]
    pulses = jnp.concatenate([ref[...] for ref in refs[:-1]], axis=0)
    result = jnp.dot(
        operator_ref[...], jnp.concatenate([pulses, pulses], axis=0), preferred_element_type=F32
    )
    out_ref[...] = result.astype(BF16)


def form_image(operator, chunks):
    return pl.pallas_call(
        image_kernel,
        out_shape=jax.ShapeDtypeStruct((operator.shape[0], chunks[0].shape[1]), BF16),
        compiler_params=pltpu.CompilerParams(vmem_limit_bytes=24 * 1024 * 1024),
        name="form_image",
    )(operator, *chunks)


def swap(value, axis, by):
    count = lax.axis_size(axis)
    return lax.ppermute(value, axis, [(i, i ^ by) for i in range(count)])


def swap_both(value, by_section, by_sub):
    sections, subs = lax.axis_size("section"), lax.axis_size("sub")
    pairs = [
        (s * subs + a, (s ^ by_section) * subs + (a ^ by_sub)) for s in range(sections) for a in range(subs)
    ]
    return lax.ppermute(value, ("section", "sub"), pairs)


def from_behind(value, axis, by):
    size = lax.axis_size(axis)
    pairs = [(i, i + by) for i in range(size) if 0 <= i + by < size]
    return lax.ppermute(value, axis, pairs)


def on_device(echoes, chirp, steer, pulse_order, band_coef, band_start, band_width):
    sections, subs = lax.axis_size("section"), lax.axis_size("sub")
    pulses_each = echoes.shape[2]
    group = ceil_to(pulses_each, SUBL)
    section = lax.axis_index("section").astype(jnp.int32).reshape(1)
    coef = jnp.swapaxes(band_coef, 4, 5)
    weights = jnp.swapaxes(steer, 2, 3)
    levels, _, sides, parts, taps, beams = coef.shape
    dims = (levels, sides, parts, taps, beams)

    echo = jnp.transpose(echoes[:, 0], (1, 0, 2))
    halo = from_behind(echo, "rng", -1)
    packed = pack_parameters(coef, band_start, band_width, weights, pulse_order, sections, group)
    if subs == 2:
        packed_partner = swap(packed, "sub", 1)
    compressed = compress_pulses(section, echo, halo, chirp, sections, group)
    if subs == 2:
        chunks = [compressed[0]]
        chunks += [swap(compressed[j], "section", j) for j in range(1, sections)]
        chunks += [swap_both(compressed[j], j, 1) for j in range(sections)]
        operator = fold_operator(section, packed, packed_partner, dims, sections, group)
        image = form_image(operator, chunks)
        return image.reshape(2, beams, 1, image.shape[1])
    own = [compressed[0]] + [swap(compressed[j], "section", j) for j in range(1, sections)]
    return merge_images(section, own, packed, dims, sections, group)


def merge_images(section, chunks, packed, dims, sections, group):
    levels, sides, parts, taps, beams = dims
    width = sections * group
    first = levels * sides * parts * taps
    table = packed[first : first + parts * width].reshape(parts, sections, group, beams)
    table = jnp.take(table, section[0] ^ jnp.arange(sections), axis=1)
    real, imag = table[0], table[1]
    rows = jnp.concatenate(
        [jnp.concatenate([real, -imag], axis=1), jnp.concatenate([imag, real], axis=1)], axis=2
    ).reshape(sections * 2 * group, 2 * beams)
    image = lax.dot_general(
        rows, jnp.concatenate(chunks, axis=0), (((0,), (0,)), ((), ())), preferred_element_type=F32
    ).astype(BF16)
    starts = packed[first + parts * width :].astype(jnp.int32)
    column = jnp.arange(beams, dtype=jnp.int32)
    bits = lax.axis_size("sub").bit_length() - 1
    for level in range(levels):
        partner = swap(image, "sub", 1 << (level % bits))
        operands = []
        for side in range(sides):
            at = (level * sides + side) * parts * taps
            coef = packed[at : at + parts * taps].reshape(parts, taps, beams)
            offset = column[:, None] - starts[level * sides + side][None, :]
            hits = (offset[None] == jnp.arange(taps, dtype=jnp.int32)[:, None, None]).astype(BF16)
            operands.append(jnp.einsum("ptq,tcq->pqc", coef, hits, preferred_element_type=F32).astype(BF16))
        top = jnp.concatenate([operands[0][0], -operands[0][1], operands[1][0], -operands[1][1]], axis=1)
        low = jnp.concatenate([operands[0][1], operands[0][0], operands[1][1], operands[1][0]], axis=1)
        image = jnp.dot(
            jnp.concatenate([top, low], axis=0),
            jnp.concatenate([image, partner], axis=0),
            preferred_element_type=F32,
        ).astype(BF16)
    return image.reshape(2, beams, 1, image.shape[1])


def solution(mesh):
    return jax.shard_map(
        on_device,
        mesh=mesh,
        in_specs=(
            P(None, "sub", "section", "rng"),
            P(),
            P(None, "sub", None, None),
            P("sub", None),
            P(None, "sub", None, None, None, None),
            P(None, "sub", None, None),
            P(None, "sub", None, None),
        ),
        out_specs=P(None, "sub", "rng", "section"),
        check_vma=False,
    )
```

```python
import functools

import jax
import jax.numpy as jnp
from jax import lax
from jax.experimental import pallas as pl
from jax.experimental.pallas import tpu as pltpu
from jax.sharding import PartitionSpec as P

LANE = 128
SUBL = 8
F32 = jnp.float32
BF16 = jnp.bfloat16


def ceil_to(value, unit):
    return -(-value // unit) * unit


def split_two(value):
    high = value.astype(BF16)
    return high, (value - high.astype(F32)).astype(BF16)


def operator_kernel(
    index_ref, coef_ref, start_ref, width_ref, steer_ref, order_ref, out_ref, *, sections, group
):
    _, levels, _, sides, parts, taps, beams = coef_ref.shape
    pulses = order_ref.shape[2]
    each = pulses // sections
    section, sub = index_ref[0], index_ref[1]
    members = (sub, 1 - sub)
    tap = lax.broadcasted_iota(jnp.int32, (taps, beams), 0)
    column = [lax.broadcasted_iota(jnp.int32, (SUBL, beams), 0) + c for c in range(0, beams, SUBL)]

    def band(member, level, side):
        used = tap < width_ref[member, level, 0, side : side + 1, :]
        tables = [
            jnp.where(used, coef_ref[member, level, 0, side, p].astype(F32), 0.0) for p in range(parts)
        ]
        start = start_ref[member, level, 0, side : side + 1, :]
        found = [[], []]
        for own_column in column:
            offset = own_column - start
            spot = offset & (SUBL - 1)
            for p in range(parts):
                value = jnp.zeros((SUBL, beams), F32)
                for t in range(0, taps, SUBL):
                    got = jnp.take_along_axis(
                        tables[p][t : t + SUBL], spot, axis=0, mode="promise_in_bounds"
                    )
                    value = jnp.where((offset >= t) & (offset < t + SUBL), got, value)
                found[p].append(value)
        return [jnp.concatenate(f, axis=0) for f in found]

    def complex_operand(real, imag):
        top = jnp.concatenate([real, imag], axis=1)
        low = jnp.concatenate([-imag, real], axis=1)
        return jnp.concatenate([top, low], axis=0).astype(BF16)

    height = sections * 2 * group
    slot = lax.broadcasted_iota(jnp.int32, (height, pulses), 0)
    pulse = lax.broadcasted_iota(jnp.int32, (height, pulses), 1)
    position = lax.broadcasted_iota(jnp.int32, (pulses, pulses), 0)
    images = []
    for a in range(2):
        place = jnp.zeros((height, pulses), F32)
        for j in range(sections):
            first = (section ^ j) * each
            inside = (pulse >= first) & (pulse < first + each)
            place = jnp.where(
                inside & (slot - (2 * j + a) * group == pulse - first), 1.0, place
            )
        hit = (position == order_ref[members[a]]).astype(BF16)
        pick = lax.dot_general(
            place.astype(BF16), hit, (((1,), (1,)), ((), ())), preferred_element_type=F32
        )
        steer = jnp.concatenate([steer_ref[members[a], 0, 0], steer_ref[members[a], 1, 0]], axis=1)
        images.append(jnp.dot(pick.astype(BF16), steer, preferred_element_type=F32))
    own, partner = images
    for level in range(levels):
        own_rows = jnp.concatenate(split_two(own), axis=0)
        partner_rows = jnp.concatenate(split_two(partner), axis=0)

        def merged(member, mine, other):
            product = jnp.dot(
                mine, complex_operand(*band(member, level, 0)), preferred_element_type=F32
            ) + jnp.dot(other, complex_operand(*band(member, level, 1)), preferred_element_type=F32)
            return product[:height] + product[height:]

        following = merged(members[0], own_rows, partner_rows)
        if level < levels - 1:
            partner = merged(members[1], partner_rows, own_rows)
        own = following
    blocks = []
    for j in range(2 * sections):
        real = own[j * group : (j + 1) * group, :beams]
        imag = own[j * group : (j + 1) * group, beams:]
        blocks.append(jnp.concatenate([real, imag], axis=1))
        blocks.append(jnp.concatenate([-imag, real], axis=1))
    whole = jnp.concatenate(blocks, axis=0).T
    high, low = split_two(whole)
    out_ref[...] = jnp.concatenate([high, low], axis=1)


def fold_operator(index, coef, start, width, steer, order, sections, group):
    beams = coef.shape[-1]
    return pl.pallas_call(
        functools.partial(operator_kernel, sections=sections, group=group),
        out_shape=jax.ShapeDtypeStruct((2 * beams, 8 * sections * group), BF16),
        in_specs=[pl.BlockSpec(memory_space=pltpu.SMEM)] + [pl.BlockSpec(memory_space=pltpu.VMEM)] * 5,
        compiler_params=pltpu.CompilerParams(vmem_limit_bytes=16 * 1024 * 1024),
        name="fold_operator",
    )(index, coef, start, width, steer, order)


def compress_kernel(index_ref, *refs, sections, group, members):
    echoes, halos = refs[:members], refs[members : 2 * members]
    chirp_ref, out_ref, rows, held, table = refs[2 * members :]
    pulses, _, length = echoes[0].shape
    taps = chirp_ref.shape[1]
    blocks, extra = length // LANE, taps // LANE
    total = blocks + extra
    stack = rows.shape[1]
    reverse = LANE - 1 - lax.broadcasted_iota(jnp.int32, (2, LANE), 1)
    below = lax.broadcasted_iota(jnp.int32, (LANE, LANE), 1) <= lax.broadcasted_iota(
        jnp.int32, (LANE, LANE), 0
    )
    before = [jnp.zeros((LANE, LANE), F32)] * 2
    for lag in range(extra + 1):
        if lag < extra:
            piece = chirp_ref[:, lag * LANE : (lag + 1) * LANE].astype(F32)
            piece = jnp.take_along_axis(piece, reverse, axis=1, mode="promise_in_bounds")
            turned = [
                pltpu.roll(
                    jnp.broadcast_to(piece[c : c + 1], (LANE, LANE)), 1, 1, stride=1, stride_axis=0
                )
                for c in range(2)
            ]
        else:
            turned = [jnp.zeros((LANE, LANE), F32)] * 2
        real, imag = [jnp.where(below, turned[c], before[c]) for c in range(2)]
        before = turned
        at = lag * 2 * LANE
        table[at : at + LANE, :LANE] = real.astype(BF16)
        table[at : at + LANE, LANE:] = (-imag).astype(BF16)
        table[at + LANE : at + 2 * LANE, :LANE] = imag.astype(BF16)
        table[at + LANE : at + 2 * LANE, LANE:] = real.astype(BF16)
    rows[...] = jnp.zeros_like(rows)
    for m in range(members):
        for p in range(pulses):
            near = echoes[m][p].astype(F32)
            far = halos[m][p, :, :taps].astype(F32)
            at = m * group + p
            for c in range(2):
                rows[c, at : at + 1, :length] = near[c : c + 1]
                rows[c, at : at + 1, length:] = far[c : c + 1]
    for b in range(total):
        for c in range(2):
            held[b * stack : (b + 1) * stack, c * LANE : (c + 1) * LANE] = rows[
                c, :, b * LANE : (b + 1) * LANE
            ].astype(BF16)
    window = blocks * stack
    pieces = [held[lag * stack : lag * stack + window] for lag in range(extra + 1)]
    done = jnp.dot(jnp.concatenate(pieces, axis=1), table[...], preferred_element_type=F32)
    section = index_ref[0]
    chunk = blocks // sections
    for s in range(sections):
        lines = []
        for m in range(members):
            for c in range(2):
                lines.append(
                    jnp.concatenate(
                        [
                            done[
                                (s * chunk + b) * stack + m * group : (s * chunk + b) * stack
                                + (m + 1) * group,
                                c * LANE : (c + 1) * LANE,
                            ]
                            for b in range(chunk)
                        ],
                        axis=1,
                    )
                )
        out_ref[section ^ s] = jnp.concatenate(lines, axis=0).astype(BF16)


def compress_pulses(index, echoes, halos, chirp, sections, group):
    members = len(echoes)
    _, _, length = echoes[0].shape
    taps = chirp.shape[1]
    blocks, extra = length // LANE, taps // LANE
    total = blocks + extra
    stack = ceil_to(members * group, 2 * SUBL)
    return pl.pallas_call(
        functools.partial(compress_kernel, sections=sections, group=group, members=members),
        out_shape=jax.ShapeDtypeStruct((sections, members * 2 * group, length // sections), BF16),
        in_specs=[pl.BlockSpec(memory_space=pltpu.SMEM)]
        + [pl.BlockSpec(memory_space=pltpu.VMEM)] * (2 * members + 1),
        scratch_shapes=[
            pltpu.VMEM((2, stack, total * LANE), F32),
            pltpu.VMEM((total * stack, 2 * LANE), BF16),
            pltpu.VMEM(((extra + 1) * 2 * LANE, 2 * LANE), BF16),
        ],
        compiler_params=pltpu.CompilerParams(vmem_limit_bytes=24 * 1024 * 1024),
        name="compress_pulses",
    )(index, *echoes, *halos, chirp)


def image_kernel(operator_ref, *refs):
    out_ref = refs[-1]
    pulses = jnp.concatenate([ref[...] for ref in refs[:-1]], axis=0)
    result = jnp.dot(
        operator_ref[...], jnp.concatenate([pulses, pulses], axis=0), preferred_element_type=F32
    )
    out_ref[...] = result.astype(BF16)


def form_image(operator, chunks):
    return pl.pallas_call(
        image_kernel,
        out_shape=jax.ShapeDtypeStruct((operator.shape[0], chunks[0].shape[1]), BF16),
        compiler_params=pltpu.CompilerParams(vmem_limit_bytes=16 * 1024 * 1024),
        name="form_image",
    )(operator, *chunks)


def swap(value, axis, by):
    count = lax.axis_size(axis)
    return lax.ppermute(value, axis, [(i, i ^ by) for i in range(count)])


def from_behind(value, axis, by):
    size = lax.axis_size(axis)
    pairs = [(i, i + by) for i in range(size) if 0 <= i + by < size]
    return lax.ppermute(value, axis, pairs)


def on_device(echoes, chirp, steer, pulse_order, band_coef, band_start, band_width):
    sections, subs = lax.axis_size("section"), lax.axis_size("sub")
    group = ceil_to(echoes.shape[2], SUBL)
    section = lax.axis_index("section").astype(jnp.int32)
    index = jnp.stack([section, lax.axis_index("sub").astype(jnp.int32)])
    coef = jnp.swapaxes(band_coef, 4, 5)
    weights = jnp.swapaxes(steer, 2, 3)
    beams = coef.shape[-1]

    echo = jnp.transpose(echoes[:, 0], (1, 0, 2))
    if subs != 2:
        halo = from_behind(echo, "rng", -1)
        compressed = compress_pulses(index, [echo], [halo], chirp, sections, group)
        chunks = [compressed[0]] + [swap(compressed[j], "section", j) for j in range(1, sections)]
        return merge_images(section, chunks, weights, pulse_order, coef, band_start, band_width, group)
    gathered = [
        lax.all_gather(x, "sub") for x in (coef, band_start, band_width, weights, pulse_order)
    ]
    echo_partner = swap(echo, "sub", 1)
    halo = from_behind(echo, "rng", -1)
    halo_partner = from_behind(echo_partner, "rng", -1)
    compressed = compress_pulses(
        index, [echo, echo_partner], [halo, halo_partner], chirp, sections, group
    )
    chunks = [compressed[0]] + [swap(compressed[j], "section", j) for j in range(1, sections)]
    operator = fold_operator(index, *gathered, sections, group)
    image = form_image(operator, chunks)
    return image.reshape(2, beams, 1, image.shape[1])


def merge_images(section, chunks, weights, order, coef, start, width, group):
    levels, _, sides, parts, taps, beams = coef.shape
    pulses, sections = order.shape[1], len(chunks)
    each = pulses // sections
    table = jnp.take(weights[:, 0], order[0], axis=1).reshape(parts, sections, each, beams)
    table = jnp.take(table, section ^ jnp.arange(sections), axis=1)
    table = jnp.pad(table, ((0, 0), (0, 0), (0, group - each), (0, 0)))
    real, imag = table[0], table[1]
    rows = jnp.concatenate(
        [jnp.concatenate([real, imag], axis=2), jnp.concatenate([-imag, real], axis=2)], axis=1
    ).reshape(sections * 2 * group, 2 * beams)
    image = lax.dot_general(
        rows, jnp.concatenate(chunks, axis=0), (((0,), (0,)), ((), ())), preferred_element_type=F32
    ).astype(BF16)
    column = jnp.arange(beams, dtype=jnp.int32)
    tap = jnp.arange(taps, dtype=jnp.int32)
    bits = lax.axis_size("sub").bit_length() - 1
    for level in range(levels):
        partner = swap(image, "sub", 1 << (level % bits))
        operands = []
        for side in range(sides):
            offset = column[:, None] - start[level, 0, side][None, :]
            hits = (offset[None] == tap[:, None, None]) & (
                tap[:, None, None] < width[level, 0, side][None, None, :]
            )
            operands.append(
                jnp.einsum(
                    "ptq,tcq->pqc",
                    coef[level, 0, side],
                    hits.astype(BF16),
                    preferred_element_type=F32,
                ).astype(BF16)
            )
        top = jnp.concatenate([operands[0][0], -operands[0][1], operands[1][0], -operands[1][1]], axis=1)
        low = jnp.concatenate([operands[0][1], operands[0][0], operands[1][1], operands[1][0]], axis=1)
        image = jnp.dot(
            jnp.concatenate([top, low], axis=0),
            jnp.concatenate([image, partner], axis=0),
            preferred_element_type=F32,
        ).astype(BF16)
    return image.reshape(2, beams, 1, image.shape[1])


def solution(mesh):
    return jax.shard_map(
        on_device,
        mesh=mesh,
        in_specs=(
            P(None, "sub", "section", "rng"),
            P(),
            P(None, "sub", None, None),
            P("sub", None),
            P(None, "sub", None, None, None, None),
            P(None, "sub", None, None),
            P(None, "sub", None, None),
        ),
        out_specs=P(None, "sub", "rng", "section"),
        check_vma=False,
    )
```

```python
import functools

import jax
import jax.numpy as jnp
from jax import lax
from jax.experimental import pallas as pl
from jax.experimental.pallas import tpu as pltpu
from jax.sharding import PartitionSpec as P

LANE = 128
SUBL = 8
F32 = jnp.float32
BF16 = jnp.bfloat16


def ceil_to(value, unit):
    return -(-value // unit) * unit


def pack_kernel(coef_ref, start_ref, width_ref, steer_ref, order_ref, pack_ref, starts, *, sections, group):
    levels, _, sides, parts, taps, beams = coef_ref.shape
    tap = lax.broadcasted_iota(jnp.int32, (taps, beams), 0)
    row = 0
    for level in range(levels):
        for side in range(sides):
            used = tap < width_ref[level, 0, side : side + 1, :]
            for part in range(parts):
                entries = coef_ref[level, 0, side, part].astype(F32)
                pack_ref[row : row + taps] = jnp.where(used, entries, 0.0).astype(BF16)
                row += taps
    pulses = order_ref.shape[1]
    each = pulses // sections
    position = lax.broadcasted_iota(jnp.int32, (pulses, pulses), 0)
    hit = (position == order_ref[0:1, :]).astype(F32)
    slot = lax.broadcasted_iota(jnp.int32, (sections * group, pulses), 0)
    pulse = lax.broadcasted_iota(jnp.int32, (sections * group, pulses), 1)
    place = jnp.zeros((sections * group, pulses), F32)
    for s in range(sections):
        inside = (pulse >= s * each) & (pulse < (s + 1) * each)
        place = jnp.where(inside & (slot - s * group == pulse - s * each), 1.0, place)
    pick = lax.dot_general(
        place.astype(BF16), hit.astype(BF16), (((1,), (1,)), ((), ())), preferred_element_type=F32
    )
    for part in range(parts):
        chosen = jnp.dot(pick.astype(BF16), steer_ref[part, 0], preferred_element_type=F32)
        pack_ref[row : row + sections * group] = chosen.astype(BF16)
        row += sections * group
    starts[...] = jnp.zeros_like(starts)
    for level in range(levels):
        starts[sides * level : sides * level + sides] = start_ref[level, 0].astype(F32)
    pack_ref[row : row + starts.shape[0]] = starts[...].astype(BF16)


def pack_rows(levels, sides, parts, taps, sections, group):
    return levels * sides * parts * taps + parts * sections * group + ceil_to(levels * sides, 16)


def pack_parameters(coef, start, width, steer, order, sections, group):
    levels, _, sides, parts, taps, beams = coef.shape
    return pl.pallas_call(
        functools.partial(pack_kernel, sections=sections, group=group),
        out_shape=jax.ShapeDtypeStruct((pack_rows(levels, sides, parts, taps, sections, group), beams), BF16),
        scratch_shapes=[pltpu.VMEM((ceil_to(levels * sides, 16), beams), F32)],
        compiler_params=pltpu.CompilerParams(vmem_limit_bytes=16 * 1024 * 1024),
        name="pack_parameters",
    )(coef, start, width, steer, order)


def split_two(value):
    high = value.astype(BF16)
    return high, (value - high.astype(F32)).astype(BF16)


def operator_kernel(index_ref, own_ref, partner_ref, out_ref, *, dims, sections, group):
    levels, sides, parts, taps, beams = dims
    width = sections * group
    refs = (own_ref, partner_ref)
    weight_row = levels * sides * parts * taps
    start_row = weight_row + parts * width

    def band(ref, level, side):
        first = ((level * sides + side) * parts) * taps
        tables = [ref[first + p * taps : first + (p + 1) * taps].astype(F32) for p in range(parts)]
        start = ref[start_row : start_row + ceil_to(levels * sides, 16)].astype(F32)
        start = start[level * sides + side : level * sides + side + 1].astype(jnp.int32)
        found = [[], []]
        for c in range(0, beams, SUBL):
            column = lax.broadcasted_iota(jnp.int32, (SUBL, beams), 0) + c
            offset = column - start
            spot = offset & (SUBL - 1)
            for p in range(parts):
                value = jnp.zeros((SUBL, beams), F32)
                for t in range(0, taps, SUBL):
                    got = jnp.take_along_axis(
                        tables[p][t : t + SUBL], spot, axis=0, mode="promise_in_bounds"
                    )
                    value = jnp.where((offset >= t) & (offset < t + SUBL), got, value)
                found[p].append(value)
        return [jnp.concatenate(f, axis=0) for f in found]

    def complex_operand(real, imag):
        top = jnp.concatenate([real, imag], axis=1)
        low = jnp.concatenate([-imag, real], axis=1)
        return jnp.concatenate([top, low], axis=0).astype(BF16)

    first_is_own = index_ref[0] == 0
    zero = jnp.zeros((group, 2 * beams), F32)
    images = []
    for a in range(2):
        weights = jnp.concatenate(
            [
                refs[a][weight_row + p * width : weight_row + (p + 1) * width].astype(F32)
                for p in range(parts)
            ],
            axis=1,
        )
        rows = []
        for s in range(sections):
            some = weights[s * group : (s + 1) * group]
            first = jnp.where(first_is_own, some, zero) if a == 0 else jnp.where(first_is_own, zero, some)
            rows += [first, some - first]
        images.append(jnp.concatenate(rows, axis=0))
    own, partner = images
    for level in range(levels):
        own_high, own_low = split_two(own)
        partner_high, partner_low = split_two(partner)
        own_rows = jnp.concatenate([own_high, own_low], axis=0)
        partner_rows = jnp.concatenate([partner_high, partner_low], axis=0)

        def merged(ref, mine, other):
            product = jnp.dot(
                mine, complex_operand(*band(ref, level, 0)), preferred_element_type=F32
            ) + jnp.dot(other, complex_operand(*band(ref, level, 1)), preferred_element_type=F32)
            return product[: 2 * width] + product[2 * width :]

        following = merged(own_ref, own_rows, partner_rows)
        if level < levels - 1:
            partner = merged(partner_ref, partner_rows, own_rows)
        own = following
    blocks = []
    for j in range(2 * sections):
        real = own[j * group : (j + 1) * group, :beams]
        imag = own[j * group : (j + 1) * group, beams:]
        blocks.append(jnp.concatenate([real, imag], axis=1))
        blocks.append(jnp.concatenate([-imag, real], axis=1))
    whole = jnp.concatenate(blocks, axis=0).T
    high, low = split_two(whole)
    out_ref[...] = jnp.concatenate([high, low], axis=1)


def fold_operator(index, own, partner, dims, sections, group):
    beams = dims[-1]
    width = sections * group
    return pl.pallas_call(
        functools.partial(operator_kernel, dims=dims, sections=sections, group=group),
        out_shape=jax.ShapeDtypeStruct((2 * beams, 8 * width), BF16),
        in_specs=[
            pl.BlockSpec(memory_space=pltpu.SMEM),
            pl.BlockSpec(memory_space=pltpu.VMEM),
            pl.BlockSpec(memory_space=pltpu.VMEM),
        ],
        compiler_params=pltpu.CompilerParams(vmem_limit_bytes=16 * 1024 * 1024),
        name="fold_operator",
    )(index, own, partner)


def compress_kernel(echo_ref, halo_ref, chirp_ref, out_ref, rows, even, odd, table, *, sections, group):
    pulses, _, length = echo_ref.shape
    taps = chirp_ref.shape[1]
    blocks, extra = length // LANE, taps // LANE
    total = blocks + extra
    reverse = LANE - 1 - lax.broadcasted_iota(jnp.int32, (2, LANE), 1)
    below = lax.broadcasted_iota(jnp.int32, (LANE, LANE), 1) <= lax.broadcasted_iota(
        jnp.int32, (LANE, LANE), 0
    )
    before = [jnp.zeros((LANE, LANE), F32)] * 2
    for lag in range(extra + 1):
        if lag < extra:
            piece = chirp_ref[:, lag * LANE : (lag + 1) * LANE].astype(F32)
            piece = jnp.take_along_axis(piece, reverse, axis=1, mode="promise_in_bounds")
            turned = [
                pltpu.roll(
                    jnp.broadcast_to(piece[c : c + 1], (LANE, LANE)), 1, 1, stride=1, stride_axis=0
                )
                for c in range(2)
            ]
        else:
            turned = [jnp.zeros((LANE, LANE), F32)] * 2
        real, imag = [jnp.where(below, turned[c], before[c]) for c in range(2)]
        before = turned
        at = lag * 2 * LANE
        table[at : at + LANE, :LANE] = real.astype(BF16)
        table[at : at + LANE, LANE:] = (-imag).astype(BF16)
        table[at + LANE : at + 2 * LANE, :LANE] = imag.astype(BF16)
        table[at + LANE : at + 2 * LANE, LANE:] = real.astype(BF16)
    rows[...] = jnp.zeros_like(rows)
    for p in range(pulses):
        near = echo_ref[p].astype(F32)
        far = halo_ref[p, :, :taps].astype(F32)
        for c in range(2):
            rows[c * group + p : c * group + p + 1, :length] = near[c : c + 1]
            rows[c * group + p : c * group + p + 1, length:] = far[c : c + 1]
    held = [
        jnp.concatenate(
            [rows[:group, b * LANE : (b + 1) * LANE], rows[group:, b * LANE : (b + 1) * LANE]], axis=1
        )
        for b in range(total)
    ]
    for b in range(0, total, 2):
        even[b * group : (b + 2) * group] = jnp.concatenate(held[b : b + 2], axis=0).astype(BF16)
    for b in range(1, total - 1, 2):
        odd[(b - 1) * group : (b + 1) * group] = jnp.concatenate(held[b : b + 2], axis=0).astype(BF16)
    window = blocks * group
    pieces = []
    for lag in range(extra + 1):
        source, at = (even, lag) if lag % 2 == 0 else (odd, lag - 1)
        pieces.append(source[at * group : at * group + window])
    done = jnp.dot(jnp.concatenate(pieces, axis=1), table[...], preferred_element_type=F32)
    chunk = blocks // sections
    for s in range(sections):
        real = [done[(s * chunk + b) * group : (s * chunk + b + 1) * group, :LANE] for b in range(chunk)]
        imag = [done[(s * chunk + b) * group : (s * chunk + b + 1) * group, LANE:] for b in range(chunk)]
        stacked = jnp.concatenate(
            [jnp.concatenate(real, axis=1), jnp.concatenate(imag, axis=1)], axis=0
        )
        for a in range(out_ref.shape[1]):
            out_ref[s, a] = stacked.astype(BF16)


def compress_pulses(echo, halo, chirp, sections, copies, group):
    pulses, _, length = echo.shape
    taps = chirp.shape[1]
    blocks, extra = length // LANE, taps // LANE
    total = blocks + extra
    return pl.pallas_call(
        functools.partial(compress_kernel, sections=sections, group=group),
        out_shape=jax.ShapeDtypeStruct((sections, copies, 2 * group, length // sections), BF16),
        scratch_shapes=[
            pltpu.VMEM((2 * group, total * LANE), F32),
            pltpu.VMEM((total * group, 2 * LANE), BF16),
            pltpu.VMEM((total * group, 2 * LANE), BF16),
            pltpu.VMEM(((extra + 1) * 2 * LANE, 2 * LANE), BF16),
        ],
        compiler_params=pltpu.CompilerParams(vmem_limit_bytes=24 * 1024 * 1024),
        name="compress_pulses",
    )(echo, halo, chirp)


def image_kernel(operator_ref, pulses_ref, out_ref):
    pulses = pulses_ref[...]
    result = jnp.dot(
        operator_ref[...], jnp.concatenate([pulses, pulses], axis=0), preferred_element_type=F32
    )
    out_ref[...] = result.astype(BF16)


def form_image(operator, pulses):
    return pl.pallas_call(
        image_kernel,
        out_shape=jax.ShapeDtypeStruct((operator.shape[0], pulses.shape[1]), BF16),
        compiler_params=pltpu.CompilerParams(vmem_limit_bytes=16 * 1024 * 1024),
        name="form_image",
    )(operator, pulses)


def swap(value, axis, by):
    count = lax.axis_size(axis)
    return lax.ppermute(value, axis, [(i, i ^ by) for i in range(count)])


def from_behind(value, axis, by):
    size = lax.axis_size(axis)
    pairs = [(i, i + by) for i in range(size) if 0 <= i + by < size]
    return lax.ppermute(value, axis, pairs)


def on_device(echoes, chirp, steer, pulse_order, band_coef, band_start, band_width):
    sections, subs = lax.axis_size("section"), lax.axis_size("sub")
    pulses_each = echoes.shape[2]
    group = ceil_to(pulses_each, SUBL)
    coef = jnp.swapaxes(band_coef, 4, 5)
    weights = jnp.swapaxes(steer, 2, 3)
    levels, _, sides, parts, taps, beams = coef.shape
    dims = (levels, sides, parts, taps, beams)

    echo = jnp.transpose(echoes[:, 0], (1, 0, 2))
    halo = from_behind(echo, "rng", -1)
    packed = pack_parameters(coef, band_start, band_width, weights, pulse_order, sections, group)
    if subs != 2:
        chunks = compress_pulses(echo, halo, chirp, sections, 1, group)
        pulses = lax.all_to_all(chunks, "section", 0, 0, tiled=True)
        pulses = pulses.reshape(-1, pulses.shape[3])
        return merge_images(pulses, packed, dims, sections, group)
    index = lax.axis_index("sub").astype(jnp.int32).reshape(1)
    packed_partner = swap(packed, "sub", 1)
    chunks = compress_pulses(echo, halo, chirp, sections, subs, group)
    chunks = chunks.reshape(sections * subs, *chunks.shape[2:])
    pulses = lax.all_to_all(chunks, ("section", "sub"), 0, 0, tiled=True)
    pulses = pulses.reshape(-1, pulses.shape[2])
    operator = fold_operator(index, packed, packed_partner, dims, sections, group)
    image = form_image(operator, pulses)
    return image.reshape(2, beams, 1, image.shape[1])


def merge_images(pulses, packed, dims, sections, group):
    levels, sides, parts, taps, beams = dims
    width = sections * group
    first = levels * sides * parts * taps
    table = packed[first : first + parts * width].reshape(parts, sections, group, beams)
    real, imag = table[0], table[1]
    rows = jnp.concatenate(
        [jnp.concatenate([real, -imag], axis=1), jnp.concatenate([imag, real], axis=1)], axis=2
    ).reshape(sections * 2 * group, 2 * beams)
    image = lax.dot_general(
        rows, pulses, (((0,), (0,)), ((), ())), preferred_element_type=F32
    ).astype(BF16)
    starts = packed[first + parts * width :].astype(jnp.int32)
    column = jnp.arange(beams, dtype=jnp.int32)
    bits = lax.axis_size("sub").bit_length() - 1
    for level in range(levels):
        partner = swap(image, "sub", 1 << (level % bits))
        operands = []
        for side in range(sides):
            at = (level * sides + side) * parts * taps
            coef = packed[at : at + parts * taps].reshape(parts, taps, beams)
            offset = column[:, None] - starts[level * sides + side][None, :]
            hits = (offset[None] == jnp.arange(taps, dtype=jnp.int32)[:, None, None]).astype(BF16)
            operands.append(jnp.einsum("ptq,tcq->pqc", coef, hits, preferred_element_type=F32).astype(BF16))
        top = jnp.concatenate([operands[0][0], -operands[0][1], operands[1][0], -operands[1][1]], axis=1)
        low = jnp.concatenate([operands[0][1], operands[0][0], operands[1][1], operands[1][0]], axis=1)
        image = jnp.dot(
            jnp.concatenate([top, low], axis=0),
            jnp.concatenate([image, partner], axis=0),
            preferred_element_type=F32,
        ).astype(BF16)
    return image.reshape(2, beams, 1, image.shape[1])


def solution(mesh):
    return jax.shard_map(
        on_device,
        mesh=mesh,
        in_specs=(
            P(None, "sub", "section", "rng"),
            P(),
            P(None, "sub", None, None),
            P("sub", None),
            P(None, "sub", None, None, None, None),
            P(None, "sub", None, None),
            P(None, "sub", None, None),
        ),
        out_specs=P(None, "sub", "rng", "section"),
        check_vma=False,
    )
```

```python
import functools

import jax
import jax.numpy as jnp
from jax import lax
from jax.experimental import pallas as pl
from jax.experimental.pallas import tpu as pltpu
from jax.sharding import PartitionSpec as P

LANE = 128
SUBL = 8
F32 = jnp.float32
BF16 = jnp.bfloat16


def ceil_to(value, unit):
    return -(-value // unit) * unit


def prepare_kernel(
    echo_ref, chirp_ref, coef_ref, start_ref, width_ref, steer_ref, order_ref,
    rim_ref, echo_out, chirp_out, pack_ref, starts, *, sections, group
):
    rim_ref[...] = echo_ref[:, :, : rim_ref.shape[2]]
    echo_out[...] = echo_ref[...]
    chirp_out[...] = chirp_ref[...]
    levels, _, sides, parts, taps, beams = coef_ref.shape
    tap = lax.broadcasted_iota(jnp.int32, (taps, beams), 0)
    row = 0
    for level in range(levels):
        for side in range(sides):
            used = tap < width_ref[level, 0, side : side + 1, :]
            for part in range(parts):
                entries = coef_ref[level, 0, side, part].astype(F32)
                pack_ref[row : row + taps] = jnp.where(used, entries, 0.0).astype(BF16)
                row += taps
    pulses = order_ref.shape[1]
    each = pulses // sections
    position = lax.broadcasted_iota(jnp.int32, (pulses, pulses), 0)
    hit = (position == order_ref[0:1, :]).astype(F32)
    slot = lax.broadcasted_iota(jnp.int32, (sections * group, pulses), 0)
    pulse = lax.broadcasted_iota(jnp.int32, (sections * group, pulses), 1)
    place = jnp.zeros((sections * group, pulses), F32)
    for s in range(sections):
        inside = (pulse >= s * each) & (pulse < (s + 1) * each)
        place = jnp.where(inside & (slot - s * group == pulse - s * each), 1.0, place)
    pick = lax.dot_general(
        place.astype(BF16), hit.astype(BF16), (((1,), (1,)), ((), ())), preferred_element_type=F32
    )
    for part in range(parts):
        chosen = jnp.dot(pick.astype(BF16), steer_ref[part, 0], preferred_element_type=F32)
        pack_ref[row : row + sections * group] = chosen.astype(BF16)
        row += sections * group
    starts[...] = jnp.zeros_like(starts)
    for level in range(levels):
        starts[sides * level : sides * level + sides] = start_ref[level, 0].astype(F32)
    pack_ref[row : row + starts.shape[0]] = starts[...].astype(BF16)


def pack_rows(levels, sides, parts, taps, sections, group):
    return levels * sides * parts * taps + parts * sections * group + ceil_to(levels * sides, 16)


def prepare(echo, chirp, coef, start, width, steer, order, sections, group):
    levels, _, sides, parts, taps, beams = coef.shape
    pulses, _, length = echo.shape
    return pl.pallas_call(
        functools.partial(prepare_kernel, sections=sections, group=group),
        out_shape=(
            jax.ShapeDtypeStruct((pulses, parts, chirp.shape[1]), BF16),
            jax.ShapeDtypeStruct(echo.shape, BF16),
            jax.ShapeDtypeStruct(chirp.shape, BF16),
            jax.ShapeDtypeStruct((pack_rows(levels, sides, parts, taps, sections, group), beams), BF16),
        ),
        scratch_shapes=[pltpu.VMEM((ceil_to(levels * sides, 16), beams), F32)],
        compiler_params=pltpu.CompilerParams(vmem_limit_bytes=16 * 1024 * 1024),
        name="prepare",
    )(echo, chirp, coef, start, width, steer, order)


def split_two(value):
    high = value.astype(BF16)
    return high, (value - high.astype(F32)).astype(BF16)


def operator_kernel(index_ref, own_ref, partner_ref, out_ref, *, dims, sections, group):
    levels, sides, parts, taps, beams = dims
    width = sections * group
    refs = (own_ref, partner_ref)
    weight_row = levels * sides * parts * taps
    start_row = weight_row + parts * width

    def band(ref, level, side):
        first = ((level * sides + side) * parts) * taps
        tables = [ref[first + p * taps : first + (p + 1) * taps].astype(F32) for p in range(parts)]
        start = ref[start_row : start_row + ceil_to(levels * sides, 16)].astype(F32)
        start = start[level * sides + side : level * sides + side + 1].astype(jnp.int32)
        found = [[], []]
        for c in range(0, beams, SUBL):
            column = lax.broadcasted_iota(jnp.int32, (SUBL, beams), 0) + c
            offset = column - start
            spot = offset & (SUBL - 1)
            for p in range(parts):
                value = jnp.zeros((SUBL, beams), F32)
                for t in range(0, taps, SUBL):
                    got = jnp.take_along_axis(
                        tables[p][t : t + SUBL], spot, axis=0, mode="promise_in_bounds"
                    )
                    value = jnp.where((offset >= t) & (offset < t + SUBL), got, value)
                found[p].append(value)
        return [jnp.concatenate(f, axis=0) for f in found]

    def complex_operand(real, imag):
        top = jnp.concatenate([real, imag], axis=1)
        low = jnp.concatenate([-imag, real], axis=1)
        return jnp.concatenate([top, low], axis=0).astype(BF16)

    first_is_own = index_ref[0] == 0
    zero = jnp.zeros((group, 2 * beams), F32)
    images = []
    for a in range(2):
        weights = jnp.concatenate(
            [
                refs[a][weight_row + p * width : weight_row + (p + 1) * width].astype(F32)
                for p in range(parts)
            ],
            axis=1,
        )
        rows = []
        for s in range(sections):
            some = weights[s * group : (s + 1) * group]
            first = jnp.where(first_is_own, some, zero) if a == 0 else jnp.where(first_is_own, zero, some)
            rows += [first, some - first]
        images.append(jnp.concatenate(rows, axis=0))
    own, partner = images
    for level in range(levels):
        own_high, own_low = split_two(own)
        partner_high, partner_low = split_two(partner)
        own_rows = jnp.concatenate([own_high, own_low], axis=0)
        partner_rows = jnp.concatenate([partner_high, partner_low], axis=0)

        def merged(ref, mine, other):
            product = jnp.dot(
                mine, complex_operand(*band(ref, level, 0)), preferred_element_type=F32
            ) + jnp.dot(other, complex_operand(*band(ref, level, 1)), preferred_element_type=F32)
            return product[: 2 * width] + product[2 * width :]

        following = merged(own_ref, own_rows, partner_rows)
        if level < levels - 1:
            partner = merged(partner_ref, partner_rows, own_rows)
        own = following
    blocks = []
    for j in range(2 * sections):
        real = own[j * group : (j + 1) * group, :beams]
        imag = own[j * group : (j + 1) * group, beams:]
        blocks.append(jnp.concatenate([real, imag], axis=1))
        blocks.append(jnp.concatenate([-imag, real], axis=1))
    whole = jnp.concatenate(blocks, axis=0).T
    high, low = split_two(whole)
    out_ref[...] = jnp.concatenate([high, low], axis=1)


def fold_operator(index, own, partner, dims, sections, group):
    beams = dims[-1]
    width = sections * group
    return pl.pallas_call(
        functools.partial(operator_kernel, dims=dims, sections=sections, group=group),
        out_shape=jax.ShapeDtypeStruct((2 * beams, 8 * width), BF16),
        in_specs=[
            pl.BlockSpec(memory_space=pltpu.SMEM),
            pl.BlockSpec(memory_space=pltpu.VMEM),
            pl.BlockSpec(memory_space=pltpu.VMEM),
        ],
        compiler_params=pltpu.CompilerParams(vmem_limit_bytes=16 * 1024 * 1024),
        name="fold_operator",
    )(index, own, partner)


def correlate(rows, even, odd, table, out_ref, first, blocks, extra, group):
    total = blocks + extra
    held = [
        jnp.concatenate(
            [rows[:group, b * LANE : (b + 1) * LANE], rows[group:, b * LANE : (b + 1) * LANE]], axis=1
        )
        for b in range(total)
    ]
    for b in range(0, total, 2):
        even[b * group : (b + 2) * group] = jnp.concatenate(held[b : b + 2], axis=0).astype(BF16)
    for b in range(1, total - 1, 2):
        odd[(b - 1) * group : (b + 1) * group] = jnp.concatenate(held[b : b + 2], axis=0).astype(BF16)
    window = blocks * group
    pieces = []
    for lag in range(extra + 1):
        source, at = (even, lag) if lag % 2 == 0 else (odd, lag - 1)
        pieces.append(source[at * group : at * group + window])
    done = jnp.dot(jnp.concatenate(pieces, axis=1), table[...], preferred_element_type=F32)
    chunk = out_ref.shape[3] // LANE
    for s in range(blocks // chunk):
        real = [done[(s * chunk + b) * group : (s * chunk + b + 1) * group, :LANE] for b in range(chunk)]
        imag = [done[(s * chunk + b) * group : (s * chunk + b + 1) * group, LANE:] for b in range(chunk)]
        stacked = jnp.concatenate(
            [jnp.concatenate(real, axis=1), jnp.concatenate(imag, axis=1)], axis=0
        )
        for a in range(out_ref.shape[1]):
            out_ref[first + s, a] = stacked.astype(BF16)


def begin_kernel(echo_ref, chirp_ref, out_ref, late_ref, table, rows, even, odd, *, group):
    pulses, _, length = echo_ref.shape
    extra = chirp_ref.shape[1] // LANE
    reverse = LANE - 1 - lax.broadcasted_iota(jnp.int32, (2, LANE), 1)
    below = lax.broadcasted_iota(jnp.int32, (LANE, LANE), 1) <= lax.broadcasted_iota(
        jnp.int32, (LANE, LANE), 0
    )
    before = [jnp.zeros((LANE, LANE), F32)] * 2
    for lag in range(extra + 1):
        if lag < extra:
            piece = chirp_ref[:, lag * LANE : (lag + 1) * LANE].astype(F32)
            piece = jnp.take_along_axis(piece, reverse, axis=1, mode="promise_in_bounds")
            turned = [
                pltpu.roll(
                    jnp.broadcast_to(piece[c : c + 1], (LANE, LANE)), 1, 1, stride=1, stride_axis=0
                )
                for c in range(2)
            ]
        else:
            turned = [jnp.zeros((LANE, LANE), F32)] * 2
        real, imag = [jnp.where(below, turned[c], before[c]) for c in range(2)]
        before = turned
        at = lag * 2 * LANE
        table[at : at + LANE, :LANE] = real.astype(BF16)
        table[at : at + LANE, LANE:] = (-imag).astype(BF16)
        table[at + LANE : at + 2 * LANE, :LANE] = imag.astype(BF16)
        table[at + LANE : at + 2 * LANE, LANE:] = real.astype(BF16)
    rows[...] = jnp.zeros_like(rows)
    for p in range(pulses):
        near = echo_ref[p].astype(F32)
        for c in range(2):
            rows[c * group + p : c * group + p + 1, :] = near[c : c + 1]
    late_ref[...] = rows[:, length - late_ref.shape[1] :]
    correlate(rows, even, odd, table, out_ref, 0, length // LANE - extra, extra, group)


def finish_kernel(early_ref, late_ref, halo_ref, table, out_ref, rows, even, odd, *, group):
    pulses = halo_ref.shape[0]
    span = late_ref.shape[1]
    taps = halo_ref.shape[2]
    extra = taps // LANE
    rows[:, :span] = late_ref[...]
    rows[:, span:] = jnp.zeros((2 * group, taps), F32)
    for p in range(pulses):
        far = halo_ref[p].astype(F32)
        for c in range(2):
            rows[c * group + p : c * group + p + 1, span:] = far[c : c + 1]
    ready = early_ref.shape[0]
    for s in range(ready):
        out_ref[s] = early_ref[s]
    correlate(rows, even, odd, table, out_ref, ready, span // LANE, extra, group)


def row_scratch(blocks, group):
    return [
        pltpu.VMEM((2 * group, blocks * LANE), F32),
        pltpu.VMEM((blocks * group, 2 * LANE), BF16),
        pltpu.VMEM((blocks * group, 2 * LANE), BF16),
    ]


def begin_compression(echo, chirp, sections, copies, group):
    _, _, length = echo.shape
    taps = chirp.shape[1]
    extra = taps // LANE
    chunk = length // sections
    early = (length - taps) // chunk
    return pl.pallas_call(
        functools.partial(begin_kernel, group=group),
        out_shape=(
            jax.ShapeDtypeStruct((early, copies, 2 * group, chunk), BF16),
            jax.ShapeDtypeStruct((2 * group, length - early * chunk), F32),
            jax.ShapeDtypeStruct(((extra + 1) * 2 * LANE, 2 * LANE), BF16),
        ),
        scratch_shapes=row_scratch(length // LANE, group),
        compiler_params=pltpu.CompilerParams(vmem_limit_bytes=24 * 1024 * 1024),
        name="begin_compression",
    )(echo, chirp)


def finish_compression(early, late, halo, table, sections, group):
    _, copies, height, chunk = early.shape
    blocks = (late.shape[1] + halo.shape[2]) // LANE
    return pl.pallas_call(
        functools.partial(finish_kernel, group=group),
        out_shape=jax.ShapeDtypeStruct((sections, copies, height, chunk), BF16),
        scratch_shapes=row_scratch(blocks, group),
        compiler_params=pltpu.CompilerParams(vmem_limit_bytes=24 * 1024 * 1024),
        name="finish_compression",
    )(early, late, halo, table)


def image_kernel(operator_ref, pulses_ref, out_ref, parts, sems):
    count, _, tile = parts.shape
    operator = operator_ref[...]
    copies = []
    for i in range(count):
        pulses = pulses_ref[:, i * tile : (i + 1) * tile]
        result = jnp.dot(
            operator, jnp.concatenate([pulses, pulses], axis=0), preferred_element_type=F32
        )
        parts[i] = result.astype(BF16)
        copy = pltpu.make_async_copy(parts.at[i], out_ref.at[:, i * tile : (i + 1) * tile], sems.at[i])
        copy.start()
        copies.append(copy)
    for copy in copies:
        copy.wait()


def form_image(operator, pulses):
    height, width = operator.shape[0], pulses.shape[1]
    tile = 256 if width % 256 == 0 else width
    return pl.pallas_call(
        image_kernel,
        out_shape=jax.ShapeDtypeStruct((height, width), BF16),
        in_specs=[pl.BlockSpec(memory_space=pltpu.VMEM)] * 2,
        out_specs=pl.BlockSpec(memory_space=pl.ANY),
        scratch_shapes=[
            pltpu.VMEM((width // tile, height, tile), BF16),
            pltpu.SemaphoreType.DMA((width // tile,)),
        ],
        compiler_params=pltpu.CompilerParams(vmem_limit_bytes=16 * 1024 * 1024),
        name="form_image",
    )(operator, pulses)


def swap(value, axis, by):
    count = lax.axis_size(axis)
    return lax.ppermute(value, axis, [(i, i ^ by) for i in range(count)])


def from_behind(value, axis, by):
    size = lax.axis_size(axis)
    pairs = [(i, i + by) for i in range(size) if 0 <= i + by < size]
    return lax.ppermute(value, axis, pairs)


def on_device(echoes, chirp, steer, pulse_order, band_coef, band_start, band_width):
    sections, subs = lax.axis_size("section"), lax.axis_size("sub")
    pulses_each = echoes.shape[2]
    group = ceil_to(pulses_each, SUBL)
    coef = jnp.swapaxes(band_coef, 4, 5)
    weights = jnp.swapaxes(steer, 2, 3)
    levels, _, sides, parts, taps, beams = coef.shape
    dims = (levels, sides, parts, taps, beams)

    echo = jnp.transpose(echoes[:, 0], (1, 0, 2))
    rim, echo, chirp, packed = prepare(
        echo, chirp, coef, band_start, band_width, weights, pulse_order, sections, group
    )
    halo = from_behind(rim, "rng", -1)
    if subs != 2:
        early, late, table = begin_compression(echo, chirp, sections, 1, group)
        chunks = finish_compression(early, late, halo, table, sections, group)
        pulses = lax.all_to_all(chunks, "section", 0, 0, tiled=True)
        pulses = pulses.reshape(-1, pulses.shape[3])
        return merge_images(pulses, packed, dims, sections, group)
    index = lax.axis_index("sub").astype(jnp.int32).reshape(1)
    packed_partner = swap(packed, "sub", 1)
    early, late, table = begin_compression(echo, chirp, sections, subs, group)
    halo, packed_partner = lax.optimization_barrier((halo, packed_partner))
    chunks = finish_compression(early, late, halo, table, sections, group)
    chunks = chunks.reshape(sections * subs, *chunks.shape[2:])
    pulses = lax.all_to_all(chunks, ("section", "sub"), 0, 0, tiled=True)
    pulses = pulses.reshape(-1, pulses.shape[2])
    operator = fold_operator(index, packed, packed_partner, dims, sections, group)
    image = form_image(operator, pulses)
    return image.reshape(2, beams, 1, image.shape[1])


def merge_images(pulses, packed, dims, sections, group):
    levels, sides, parts, taps, beams = dims
    width = sections * group
    first = levels * sides * parts * taps
    table = packed[first : first + parts * width].reshape(parts, sections, group, beams)
    real, imag = table[0], table[1]
    rows = jnp.concatenate(
        [jnp.concatenate([real, -imag], axis=1), jnp.concatenate([imag, real], axis=1)], axis=2
    ).reshape(sections * 2 * group, 2 * beams)
    image = lax.dot_general(
        rows, pulses, (((0,), (0,)), ((), ())), preferred_element_type=F32
    ).astype(BF16)
    starts = packed[first + parts * width :].astype(jnp.int32)
    column = jnp.arange(beams, dtype=jnp.int32)
    bits = lax.axis_size("sub").bit_length() - 1
    for level in range(levels):
        partner = swap(image, "sub", 1 << (level % bits))
        operands = []
        for side in range(sides):
            at = (level * sides + side) * parts * taps
            coef = packed[at : at + parts * taps].reshape(parts, taps, beams)
            offset = column[:, None] - starts[level * sides + side][None, :]
            hits = (offset[None] == jnp.arange(taps, dtype=jnp.int32)[:, None, None]).astype(BF16)
            operands.append(jnp.einsum("ptq,tcq->pqc", coef, hits, preferred_element_type=F32).astype(BF16))
        top = jnp.concatenate([operands[0][0], -operands[0][1], operands[1][0], -operands[1][1]], axis=1)
        low = jnp.concatenate([operands[0][1], operands[0][0], operands[1][1], operands[1][0]], axis=1)
        image = jnp.dot(
            jnp.concatenate([top, low], axis=0),
            jnp.concatenate([image, partner], axis=0),
            preferred_element_type=F32,
        ).astype(BF16)
    return image.reshape(2, beams, 1, image.shape[1])


def solution(mesh):
    return jax.shard_map(
        on_device,
        mesh=mesh,
        in_specs=(
            P(None, "sub", "section", "rng"),
            P(),
            P(None, "sub", None, None),
            P("sub", None),
            P(None, "sub", None, None, None, None),
            P(None, "sub", None, None),
            P(None, "sub", None, None),
        ),
        out_specs=P(None, "sub", "rng", "section"),
        check_vma=False,
    )
```

```python
import functools

import jax
import jax.numpy as jnp
from jax import lax
from jax.experimental import pallas as pl
from jax.experimental.pallas import tpu as pltpu
from jax.sharding import PartitionSpec as P

LANE = 128
SUBL = 8
F32 = jnp.float32
BF16 = jnp.bfloat16


def ceil_to(value, unit):
    return -(-value // unit) * unit


def prepare_kernel(*refs, sections, group):
    sources, (echo_out, chirp_out, pack_ref), scratch = refs[:7], refs[7:10], refs[10:]
    coef_ref, start_ref, width_ref, steer_ref, order_ref, starts, sems = scratch
    targets = (coef_ref, start_ref, width_ref, steer_ref, order_ref, chirp_out, echo_out)
    loads = [
        pltpu.make_async_copy(source, target, sems.at[i])
        for i, (source, target) in enumerate(zip(sources, targets))
    ]
    for load in loads:
        load.start()
    for load in loads:
        load.wait()
    levels, _, sides, parts, taps, beams = coef_ref.shape
    tap = lax.broadcasted_iota(jnp.int32, (taps, beams), 0)
    row = 0
    for level in range(levels):
        for side in range(sides):
            used = tap < width_ref[level, 0, side : side + 1, :]
            for part in range(parts):
                entries = coef_ref[level, 0, side, part].astype(F32)
                pack_ref[row : row + taps] = jnp.where(used, entries, 0.0).astype(BF16)
                row += taps
    pulses = order_ref.shape[1]
    each = pulses // sections
    position = lax.broadcasted_iota(jnp.int32, (pulses, pulses), 0)
    hit = (position == order_ref[0:1, :]).astype(F32)
    slot = lax.broadcasted_iota(jnp.int32, (sections * group, pulses), 0)
    pulse = lax.broadcasted_iota(jnp.int32, (sections * group, pulses), 1)
    place = jnp.zeros((sections * group, pulses), F32)
    for s in range(sections):
        inside = (pulse >= s * each) & (pulse < (s + 1) * each)
        place = jnp.where(inside & (slot - s * group == pulse - s * each), 1.0, place)
    pick = lax.dot_general(
        place.astype(BF16), hit.astype(BF16), (((1,), (1,)), ((), ())), preferred_element_type=F32
    )
    for part in range(parts):
        chosen = jnp.dot(pick.astype(BF16), steer_ref[part, 0], preferred_element_type=F32)
        pack_ref[row : row + sections * group] = chosen.astype(BF16)
        row += sections * group
    starts[...] = jnp.zeros_like(starts)
    for level in range(levels):
        starts[sides * level : sides * level + sides] = start_ref[level, 0].astype(F32)
    pack_ref[row : row + starts.shape[0]] = starts[...].astype(BF16)


def pack_rows(levels, sides, parts, taps, sections, group):
    return levels * sides * parts * taps + parts * sections * group + ceil_to(levels * sides, 16)


def prepare(echo, chirp, coef, start, width, steer, order, sections, group):
    levels, _, sides, parts, taps, beams = coef.shape
    sources = (coef, start, width, steer, order, chirp, echo)
    return pl.pallas_call(
        functools.partial(prepare_kernel, sections=sections, group=group),
        out_shape=(
            jax.ShapeDtypeStruct(echo.shape, BF16),
            jax.ShapeDtypeStruct(chirp.shape, BF16),
            jax.ShapeDtypeStruct((pack_rows(levels, sides, parts, taps, sections, group), beams), BF16),
        ),
        in_specs=[pl.BlockSpec(memory_space=pl.ANY)] * len(sources),
        scratch_shapes=[pltpu.VMEM(x.shape, x.dtype) for x in sources[:5]]
        + [pltpu.VMEM((ceil_to(levels * sides, 16), beams), F32), pltpu.SemaphoreType.DMA((len(sources),))],
        name="prepare",
    )(*sources)


def split_two(value):
    high = value.astype(BF16)
    return high, (value - high.astype(F32)).astype(BF16)


def operator_kernel(index_ref, own_ref, partner_ref, out_ref, weights, *, dims, sections, group):
    levels, sides, parts, taps, beams = dims
    width = sections * group
    refs = (own_ref, partner_ref)
    weight_row = levels * sides * parts * taps
    start_row = weight_row + parts * width

    def band(ref, level, side):
        first = ((level * sides + side) * parts) * taps
        tables = [ref[first + p * taps : first + (p + 1) * taps].astype(F32) for p in range(parts)]
        start = ref[start_row : start_row + ceil_to(levels * sides, 16)].astype(F32)
        start = start[level * sides + side : level * sides + side + 1].astype(jnp.int32)
        found = [[], []]
        for c in range(0, beams, SUBL):
            column = lax.broadcasted_iota(jnp.int32, (SUBL, beams), 0) + c
            offset = column - start
            spot = offset & (SUBL - 1)
            for p in range(parts):
                value = jnp.zeros((SUBL, beams), F32)
                for t in range(0, taps, SUBL):
                    got = jnp.take_along_axis(
                        tables[p][t : t + SUBL], spot, axis=0, mode="promise_in_bounds"
                    )
                    value = jnp.where((offset >= t) & (offset < t + SUBL), got, value)
                found[p].append(value)
        return [jnp.concatenate(f, axis=0) for f in found]

    def complex_operand(real, imag):
        top = jnp.concatenate([real, imag], axis=1)
        low = jnp.concatenate([-imag, real], axis=1)
        return jnp.concatenate([top, low], axis=0).astype(BF16)

    section = index_ref[0]
    images = []
    for a in range(2):
        for p in range(parts):
            weights[...] = refs[a][weight_row + p * width : weight_row + (p + 1) * width].astype(F32)
            rows = []
            for j in range(sections):
                at = pl.multiple_of((section ^ j) * group, group)
                rows.append(weights[pl.ds(at, group)])
            images.append(jnp.concatenate(rows, axis=0))
    zero = jnp.zeros((width, 2 * beams), F32)
    own = jnp.concatenate([jnp.concatenate(images[0:2], axis=1), zero], axis=0)
    partner = jnp.concatenate([zero, jnp.concatenate(images[2:4], axis=1)], axis=0)
    for level in range(levels):
        own_high, own_low = split_two(own)
        partner_high, partner_low = split_two(partner)
        own_rows = jnp.concatenate([own_high, own_low], axis=0)
        partner_rows = jnp.concatenate([partner_high, partner_low], axis=0)

        def merged(ref, mine, other):
            product = jnp.dot(
                mine, complex_operand(*band(ref, level, 0)), preferred_element_type=F32
            ) + jnp.dot(other, complex_operand(*band(ref, level, 1)), preferred_element_type=F32)
            return product[: 2 * width] + product[2 * width :]

        following = merged(own_ref, own_rows, partner_rows)
        if level < levels - 1:
            partner = merged(partner_ref, partner_rows, own_rows)
        own = following
    blocks = []
    for j in range(2 * sections):
        real = own[j * group : (j + 1) * group, :beams]
        imag = own[j * group : (j + 1) * group, beams:]
        blocks.append(jnp.concatenate([real, imag], axis=1))
        blocks.append(jnp.concatenate([-imag, real], axis=1))
    whole = jnp.concatenate(blocks, axis=0).T
    high, low = split_two(whole)
    out_ref[...] = jnp.concatenate([high, low], axis=1)


def fold_operator(index, own, partner, dims, sections, group):
    beams = dims[-1]
    width = sections * group
    return pl.pallas_call(
        functools.partial(operator_kernel, dims=dims, sections=sections, group=group),
        out_shape=jax.ShapeDtypeStruct((2 * beams, 8 * width), BF16),
        in_specs=[
            pl.BlockSpec(memory_space=pltpu.SMEM),
            pl.BlockSpec(memory_space=pltpu.VMEM),
            pl.BlockSpec(memory_space=pltpu.VMEM),
        ],
        scratch_shapes=[pltpu.VMEM((width, beams), F32)],
        compiler_params=pltpu.CompilerParams(vmem_limit_bytes=16 * 1024 * 1024),
        name="fold_operator",
    )(index, own, partner)


def correlate(rows, even, odd, table, blocks, extra, group):
    total = blocks + extra
    held = [
        jnp.concatenate(
            [rows[:group, b * LANE : (b + 1) * LANE], rows[group:, b * LANE : (b + 1) * LANE]], axis=1
        )
        for b in range(total)
    ]
    for b in range(0, total, 2):
        even[b * group : (b + 2) * group] = jnp.concatenate(held[b : b + 2], axis=0).astype(BF16)
    for b in range(1, total - 1, 2):
        odd[(b - 1) * group : (b + 1) * group] = jnp.concatenate(held[b : b + 2], axis=0).astype(BF16)
    window = blocks * group
    pieces = []
    for lag in range(extra + 1):
        source, at = (even, lag) if lag % 2 == 0 else (odd, lag - 1)
        pieces.append(source[at * group : at * group + window])
    return jnp.dot(jnp.concatenate(pieces, axis=1), table[...], preferred_element_type=F32)


def as_chunk(done, s, chunk, group):
    return jnp.concatenate(
        [
            jnp.concatenate(
                [
                    done[(s * chunk + b) * group : (s * chunk + b + 1) * group, c * LANE : (c + 1) * LANE]
                    for b in range(chunk)
                ],
                axis=1,
            )
            for c in range(2)
        ],
        axis=0,
    ).astype(BF16)


def begin_kernel(echo_ref, chirp_ref, out_ref, late_ref, table, rows, even, odd, *, group):
    pulses, _, length = echo_ref.shape
    extra = chirp_ref.shape[1] // LANE
    reverse = LANE - 1 - lax.broadcasted_iota(jnp.int32, (2, LANE), 1)
    below = lax.broadcasted_iota(jnp.int32, (LANE, LANE), 1) <= lax.broadcasted_iota(
        jnp.int32, (LANE, LANE), 0
    )
    before = [jnp.zeros((LANE, LANE), F32)] * 2
    for lag in range(extra + 1):
        if lag < extra:
            piece = chirp_ref[:, lag * LANE : (lag + 1) * LANE].astype(F32)
            piece = jnp.take_along_axis(piece, reverse, axis=1, mode="promise_in_bounds")
            turned = [
                pltpu.roll(
                    jnp.broadcast_to(piece[c : c + 1], (LANE, LANE)), 1, 1, stride=1, stride_axis=0
                )
                for c in range(2)
            ]
        else:
            turned = [jnp.zeros((LANE, LANE), F32)] * 2
        real, imag = [jnp.where(below, turned[c], before[c]) for c in range(2)]
        before = turned
        at = lag * 2 * LANE
        table[at : at + LANE, :LANE] = real.astype(BF16)
        table[at : at + LANE, LANE:] = (-imag).astype(BF16)
        table[at + LANE : at + 2 * LANE, :LANE] = imag.astype(BF16)
        table[at + LANE : at + 2 * LANE, LANE:] = real.astype(BF16)
    rows[...] = jnp.zeros_like(rows)
    for p in range(pulses):
        near = echo_ref[p].astype(F32)
        for c in range(2):
            rows[c * group + p : c * group + p + 1, :] = near[c : c + 1]
    late_ref[...] = rows[:, length - late_ref.shape[1] :]
    done = correlate(rows, even, odd, table, length // LANE - extra, extra, group)
    for s in range(out_ref.shape[0]):
        out_ref[s] = as_chunk(done, s, out_ref.shape[2] // LANE, group)


def finish_kernel(index_ref, early_ref, late_ref, halo_ref, table, out_ref, rows, even, odd, *, group):
    section, has_next = index_ref[0], index_ref[1] != 0
    pulses = halo_ref.shape[0]
    span = late_ref.shape[1]
    extra = even.shape[0] // group - span // LANE
    taps = extra * LANE
    rows[:, :span] = late_ref[...]
    rows[:, span:] = jnp.zeros((2 * group, taps), F32)
    for p in range(pulses):
        far = halo_ref[p, :, :taps].astype(F32)
        far = jnp.where(has_next, far, 0.0)
        for c in range(2):
            rows[c * group + p : c * group + p + 1, span:] = far[c : c + 1]
    done = correlate(rows, even, odd, table, span // LANE, extra, group)
    ready = early_ref.shape[0]
    for s in range(ready):
        out_ref[section ^ s] = early_ref[s]
    for s in range(ready, out_ref.shape[0]):
        out_ref[section ^ s] = as_chunk(done, s - ready, out_ref.shape[2] // LANE, group)


def row_scratch(blocks, group):
    return [
        pltpu.VMEM((2 * group, blocks * LANE), F32),
        pltpu.VMEM((blocks * group, 2 * LANE), BF16),
        pltpu.VMEM((blocks * group, 2 * LANE), BF16),
    ]


def begin_compression(echo, chirp, sections, group):
    _, _, length = echo.shape
    taps = chirp.shape[1]
    extra = taps // LANE
    chunk = length // sections
    early = (length - taps) // chunk
    return pl.pallas_call(
        functools.partial(begin_kernel, group=group),
        out_shape=(
            jax.ShapeDtypeStruct((early, 2 * group, chunk), BF16),
            jax.ShapeDtypeStruct((2 * group, length - early * chunk), F32),
            jax.ShapeDtypeStruct(((extra + 1) * 2 * LANE, 2 * LANE), BF16),
        ),
        scratch_shapes=row_scratch(length // LANE, group),
        compiler_params=pltpu.CompilerParams(vmem_limit_bytes=24 * 1024 * 1024),
        name="begin_compression",
    )(echo, chirp)


def finish_compression(index, early, late, halo, table, sections, group):
    _, height, chunk = early.shape
    blocks = late.shape[1] // LANE + table.shape[0] // (2 * LANE) - 1
    return pl.pallas_call(
        functools.partial(finish_kernel, group=group),
        out_shape=jax.ShapeDtypeStruct((sections, height, chunk), BF16),
        in_specs=[pl.BlockSpec(memory_space=pltpu.SMEM)] + [pl.BlockSpec(memory_space=pltpu.VMEM)] * 4,
        scratch_shapes=row_scratch(blocks, group),
        compiler_params=pltpu.CompilerParams(vmem_limit_bytes=24 * 1024 * 1024),
        name="finish_compression",
    )(index, early, late, halo, table)


def image_kernel(operator_ref, *refs):
    chunks, (out_ref, parts, sems) = refs[:-3], refs[-3:]
    count, _, tile = parts.shape
    operator = operator_ref[...]
    copies = []
    for i in range(count):
        pulses = [chunk[:, i * tile : (i + 1) * tile] for chunk in chunks]
        result = jnp.dot(operator, jnp.concatenate(pulses + pulses, axis=0), preferred_element_type=F32)
        parts[i] = result.astype(BF16)
        copy = pltpu.make_async_copy(parts.at[i], out_ref.at[:, i * tile : (i + 1) * tile], sems.at[i])
        copy.start()
        copies.append(copy)
    for copy in copies:
        copy.wait()


def form_image(operator, chunks):
    height, width = operator.shape[0], chunks[0].shape[1]
    tile = 256 if width % 256 == 0 else width
    return pl.pallas_call(
        image_kernel,
        out_shape=jax.ShapeDtypeStruct((height, width), BF16),
        in_specs=[pl.BlockSpec(memory_space=pltpu.VMEM)] * (1 + len(chunks)),
        out_specs=pl.BlockSpec(memory_space=pl.ANY),
        scratch_shapes=[
            pltpu.VMEM((width // tile, height, tile), BF16),
            pltpu.SemaphoreType.DMA((width // tile,)),
        ],
        compiler_params=pltpu.CompilerParams(vmem_limit_bytes=16 * 1024 * 1024),
        name="form_image",
    )(operator, *chunks)


def swap(value, axis, by):
    count = lax.axis_size(axis)
    return lax.ppermute(value, axis, [(i, i ^ by) for i in range(count)])


def swap_both(value, by_section, by_sub):
    sections, subs = lax.axis_size("section"), lax.axis_size("sub")
    pairs = [
        (s * subs + a, (s ^ by_section) * subs + (a ^ by_sub)) for s in range(sections) for a in range(subs)
    ]
    return lax.ppermute(value, ("section", "sub"), pairs)


def from_next(value, axis):
    count = lax.axis_size(axis)
    return lax.ppermute(value, axis, [(i, (i - 1) % count) for i in range(count)])


def on_device(echoes, chirp, steer, pulse_order, band_coef, band_start, band_width):
    sections, subs = lax.axis_size("section"), lax.axis_size("sub")
    pulses_each = echoes.shape[2]
    group = ceil_to(pulses_each, SUBL)
    coef = jnp.swapaxes(band_coef, 4, 5)
    weights = jnp.swapaxes(steer, 2, 3)
    levels, _, sides, parts, taps, beams = coef.shape
    dims = (levels, sides, parts, taps, beams)

    section = lax.axis_index("section").astype(jnp.int32)
    has_next = (lax.axis_index("rng") < lax.axis_size("rng") - 1).astype(jnp.int32)
    index = jnp.stack([section, has_next])
    echo = jnp.transpose(echoes[:, 0], (1, 0, 2))
    halo = from_next(echo, "rng")
    echo, chirp, packed = prepare(
        echo, chirp, coef, band_start, band_width, weights, pulse_order, sections, group
    )
    packed_partner = swap(packed, "sub", 1) if subs == 2 else packed
    early, late, table = begin_compression(echo, chirp, sections, group)
    halo, packed_partner = lax.optimization_barrier((halo, packed_partner))
    compressed = finish_compression(index, early, late, halo, table, sections, group)
    chunks = [compressed[0]] + [swap(compressed[j], "section", j) for j in range(1, sections)]
    if subs != 2:
        return merge_images(section, chunks, packed, dims, sections, group)
    chunks += [swap_both(compressed[j], j, 1) for j in range(sections)]
    operator = fold_operator(index, packed, packed_partner, dims, sections, group)
    image = form_image(operator, chunks)
    return image.reshape(2, beams, 1, image.shape[1])


def merge_images(section, chunks, packed, dims, sections, group):
    levels, sides, parts, taps, beams = dims
    width = sections * group
    first = levels * sides * parts * taps
    table = packed[first : first + parts * width].reshape(parts, sections, group, beams)
    table = jnp.take(table, section ^ jnp.arange(sections), axis=1)
    real, imag = table[0], table[1]
    rows = jnp.concatenate(
        [jnp.concatenate([real, -imag], axis=1), jnp.concatenate([imag, real], axis=1)], axis=2
    ).reshape(sections * 2 * group, 2 * beams)
    image = lax.dot_general(
        rows, jnp.concatenate(chunks, axis=0), (((0,), (0,)), ((), ())), preferred_element_type=F32
    ).astype(BF16)
    starts = packed[first + parts * width :].astype(jnp.int32)
    column = jnp.arange(beams, dtype=jnp.int32)
    bits = lax.axis_size("sub").bit_length() - 1
    for level in range(levels):
        partner = swap(image, "sub", 1 << (level % bits))
        operands = []
        for side in range(sides):
            at = (level * sides + side) * parts * taps
            coef = packed[at : at + parts * taps].reshape(parts, taps, beams)
            offset = column[:, None] - starts[level * sides + side][None, :]
            hits = (offset[None] == jnp.arange(taps, dtype=jnp.int32)[:, None, None]).astype(BF16)
            operands.append(jnp.einsum("ptq,tcq->pqc", coef, hits, preferred_element_type=F32).astype(BF16))
        top = jnp.concatenate([operands[0][0], -operands[0][1], operands[1][0], -operands[1][1]], axis=1)
        low = jnp.concatenate([operands[0][1], operands[0][0], operands[1][1], operands[1][0]], axis=1)
        image = jnp.dot(
            jnp.concatenate([top, low], axis=0),
            jnp.concatenate([image, partner], axis=0),
            preferred_element_type=F32,
        ).astype(BF16)
    return image.reshape(2, beams, 1, image.shape[1])


def solution(mesh):
    return jax.shard_map(
        on_device,
        mesh=mesh,
        in_specs=(
            P(None, "sub", "section", "rng"),
            P(),
            P(None, "sub", None, None),
            P("sub", None),
            P(None, "sub", None, None, None, None),
            P(None, "sub", None, None),
            P(None, "sub", None, None),
        ),
        out_specs=P(None, "sub", "rng", "section"),
        check_vma=False,
    )
```

```python
import functools

import jax
import jax.numpy as jnp
from jax import lax
from jax.experimental import pallas as pl
from jax.experimental.pallas import tpu as pltpu
from jax.sharding import PartitionSpec as P

LANE = 128
SUBL = 8
F32 = jnp.float32
BF16 = jnp.bfloat16


def ceil_to(value, unit):
    return -(-value // unit) * unit


def pack_kernel(coef_ref, start_ref, width_ref, steer_ref, order_ref, pack_ref, starts, *, sections, group):
    levels, _, sides, parts, taps, beams = coef_ref.shape
    tap = lax.broadcasted_iota(jnp.int32, (taps, beams), 0)
    row = 0
    for level in range(levels):
        for side in range(sides):
            used = tap < width_ref[level, 0, side : side + 1, :]
            for part in range(parts):
                entries = coef_ref[level, 0, side, part].astype(F32)
                pack_ref[row : row + taps] = jnp.where(used, entries, 0.0).astype(BF16)
                row += taps
    pulses = order_ref.shape[1]
    each = pulses // sections
    position = lax.broadcasted_iota(jnp.int32, (pulses, pulses), 0)
    hit = (position == order_ref[0:1, :]).astype(F32)
    slot = lax.broadcasted_iota(jnp.int32, (sections * group, pulses), 0)
    pulse = lax.broadcasted_iota(jnp.int32, (sections * group, pulses), 1)
    place = jnp.zeros((sections * group, pulses), F32)
    for s in range(sections):
        inside = (pulse >= s * each) & (pulse < (s + 1) * each)
        place = jnp.where(inside & (slot - s * group == pulse - s * each), 1.0, place)
    pick = lax.dot_general(
        place.astype(BF16), hit.astype(BF16), (((1,), (1,)), ((), ())), preferred_element_type=F32
    )
    for part in range(parts):
        chosen = jnp.dot(pick.astype(BF16), steer_ref[part, 0], preferred_element_type=F32)
        pack_ref[row : row + sections * group] = chosen.astype(BF16)
        row += sections * group
    starts[...] = jnp.zeros_like(starts)
    for level in range(levels):
        starts[sides * level : sides * level + sides] = start_ref[level, 0].astype(F32)
    pack_ref[row : row + starts.shape[0]] = starts[...].astype(BF16)


def pack_rows(levels, sides, parts, taps, sections, group):
    return levels * sides * parts * taps + parts * sections * group + ceil_to(levels * sides, 16)


def pack_parameters(coef, start, width, steer, order, sections, group):
    levels, _, sides, parts, taps, beams = coef.shape
    return pl.pallas_call(
        functools.partial(pack_kernel, sections=sections, group=group),
        out_shape=jax.ShapeDtypeStruct((pack_rows(levels, sides, parts, taps, sections, group), beams), BF16),
        scratch_shapes=[pltpu.VMEM((ceil_to(levels * sides, 16), beams), F32)],
        name="pack_parameters",
    )(coef, start, width, steer, order)


def split_two(value):
    high = value.astype(BF16)
    return high, (value - high.astype(F32)).astype(BF16)


def operator_kernel(index_ref, own_ref, partner_ref, out_ref, weights, *, dims, sections, group):
    levels, sides, parts, taps, beams = dims
    width = sections * group
    refs = (own_ref, partner_ref)
    weight_row = levels * sides * parts * taps
    start_row = weight_row + parts * width

    def band(ref, level, side):
        first = ((level * sides + side) * parts) * taps
        tables = [ref[first + p * taps : first + (p + 1) * taps].astype(F32) for p in range(parts)]
        start = ref[start_row : start_row + ceil_to(levels * sides, 16)].astype(F32)
        start = start[level * sides + side : level * sides + side + 1].astype(jnp.int32)
        found = [[], []]
        for c in range(0, beams, SUBL):
            column = lax.broadcasted_iota(jnp.int32, (SUBL, beams), 0) + c
            offset = column - start
            spot = offset & (SUBL - 1)
            for p in range(parts):
                value = jnp.zeros((SUBL, beams), F32)
                for t in range(0, taps, SUBL):
                    got = jnp.take_along_axis(
                        tables[p][t : t + SUBL], spot, axis=0, mode="promise_in_bounds"
                    )
                    value = jnp.where((offset >= t) & (offset < t + SUBL), got, value)
                found[p].append(value)
        return [jnp.concatenate(f, axis=0) for f in found]

    def complex_operand(real, imag):
        top = jnp.concatenate([real, imag], axis=1)
        low = jnp.concatenate([-imag, real], axis=1)
        return jnp.concatenate([top, low], axis=0).astype(BF16)

    section = index_ref[0]
    images = []
    for a in range(2):
        for p in range(parts):
            weights[...] = refs[a][weight_row + p * width : weight_row + (p + 1) * width].astype(F32)
            rows = []
            for j in range(sections):
                at = pl.multiple_of((section ^ j) * group, group)
                rows.append(weights[pl.ds(at, group)])
            images.append(jnp.concatenate(rows, axis=0))
    zero = jnp.zeros((width, 2 * beams), F32)
    own = jnp.concatenate([jnp.concatenate(images[0:2], axis=1), zero], axis=0)
    partner = jnp.concatenate([zero, jnp.concatenate(images[2:4], axis=1)], axis=0)
    for level in range(levels):
        own_high, own_low = split_two(own)
        partner_high, partner_low = split_two(partner)
        own_rows = jnp.concatenate([own_high, own_low], axis=0)
        partner_rows = jnp.concatenate([partner_high, partner_low], axis=0)

        def merged(ref, mine, other):
            product = jnp.dot(
                mine, complex_operand(*band(ref, level, 0)), preferred_element_type=F32
            ) + jnp.dot(other, complex_operand(*band(ref, level, 1)), preferred_element_type=F32)
            return product[: 2 * width] + product[2 * width :]

        following = merged(own_ref, own_rows, partner_rows)
        if level < levels - 1:
            partner = merged(partner_ref, partner_rows, own_rows)
        own = following
    blocks = []
    for j in range(2 * sections):
        real = own[j * group : (j + 1) * group, :beams]
        imag = own[j * group : (j + 1) * group, beams:]
        blocks.append(jnp.concatenate([real, imag], axis=1))
        blocks.append(jnp.concatenate([-imag, real], axis=1))
    whole = jnp.concatenate(blocks, axis=0).T
    high, low = split_two(whole)
    out_ref[...] = jnp.concatenate([high, low], axis=1)


def fold_operator(index, own, partner, dims, sections, group):
    beams = dims[-1]
    width = sections * group
    return pl.pallas_call(
        functools.partial(operator_kernel, dims=dims, sections=sections, group=group),
        out_shape=jax.ShapeDtypeStruct((2 * beams, 8 * width), BF16),
        in_specs=[
            pl.BlockSpec(memory_space=pltpu.SMEM),
            pl.BlockSpec(memory_space=pltpu.VMEM),
            pl.BlockSpec(memory_space=pltpu.VMEM),
        ],
        scratch_shapes=[pltpu.VMEM((width, beams), F32)],
        compiler_params=pltpu.CompilerParams(vmem_limit_bytes=16 * 1024 * 1024),
        name="fold_operator",
    )(index, own, partner)


def correlate(rows, even, odd, table, blocks, extra, group):
    total = blocks + extra
    held = [
        jnp.concatenate(
            [rows[:group, b * LANE : (b + 1) * LANE], rows[group:, b * LANE : (b + 1) * LANE]], axis=1
        )
        for b in range(total)
    ]
    for b in range(0, total, 2):
        even[b * group : (b + 2) * group] = jnp.concatenate(held[b : b + 2], axis=0).astype(BF16)
    for b in range(1, total - 1, 2):
        odd[(b - 1) * group : (b + 1) * group] = jnp.concatenate(held[b : b + 2], axis=0).astype(BF16)
    window = blocks * group
    pieces = []
    for lag in range(extra + 1):
        source, at = (even, lag) if lag % 2 == 0 else (odd, lag - 1)
        pieces.append(source[at * group : at * group + window])
    return jnp.dot(jnp.concatenate(pieces, axis=1), table[...], preferred_element_type=F32)


def as_chunk(done, s, chunk, group):
    return jnp.concatenate(
        [
            jnp.concatenate(
                [
                    done[(s * chunk + b) * group : (s * chunk + b + 1) * group, c * LANE : (c + 1) * LANE]
                    for b in range(chunk)
                ],
                axis=1,
            )
            for c in range(2)
        ],
        axis=0,
    ).astype(BF16)


def begin_kernel(echo_ref, chirp_ref, out_ref, late_ref, table, rows, even, odd, *, group):
    pulses, _, length = echo_ref.shape
    extra = chirp_ref.shape[1] // LANE
    reverse = LANE - 1 - lax.broadcasted_iota(jnp.int32, (2, LANE), 1)
    below = lax.broadcasted_iota(jnp.int32, (LANE, LANE), 1) <= lax.broadcasted_iota(
        jnp.int32, (LANE, LANE), 0
    )
    before = [jnp.zeros((LANE, LANE), F32)] * 2
    for lag in range(extra + 1):
        if lag < extra:
            piece = chirp_ref[:, lag * LANE : (lag + 1) * LANE].astype(F32)
            piece = jnp.take_along_axis(piece, reverse, axis=1, mode="promise_in_bounds")
            turned = [
                pltpu.roll(
                    jnp.broadcast_to(piece[c : c + 1], (LANE, LANE)), 1, 1, stride=1, stride_axis=0
                )
                for c in range(2)
            ]
        else:
            turned = [jnp.zeros((LANE, LANE), F32)] * 2
        real, imag = [jnp.where(below, turned[c], before[c]) for c in range(2)]
        before = turned
        at = lag * 2 * LANE
        table[at : at + LANE, :LANE] = real.astype(BF16)
        table[at : at + LANE, LANE:] = (-imag).astype(BF16)
        table[at + LANE : at + 2 * LANE, :LANE] = imag.astype(BF16)
        table[at + LANE : at + 2 * LANE, LANE:] = real.astype(BF16)
    rows[...] = jnp.zeros_like(rows)
    for p in range(pulses):
        near = echo_ref[p].astype(F32)
        for c in range(2):
            rows[c * group + p : c * group + p + 1, :] = near[c : c + 1]
    late_ref[...] = rows[:, length - late_ref.shape[1] :]
    done = correlate(rows, even, odd, table, length // LANE - extra, extra, group)
    for s in range(out_ref.shape[0]):
        out_ref[s] = as_chunk(done, s, out_ref.shape[2] // LANE, group)


def finish_kernel(
    index_ref, early_ref, late_ref, halo_ref, halo_odd_ref, table, out_ref, rows, even, odd, *, group
):
    section, is_odd, has_next = index_ref[0], index_ref[1] != 0, index_ref[2] != 0
    pulses = halo_ref.shape[0]
    span = late_ref.shape[1]
    extra = even.shape[0] // group - span // LANE
    taps = extra * LANE
    rows[:, :span] = late_ref[...]
    rows[:, span:] = jnp.zeros((2 * group, taps), F32)
    for p in range(pulses):
        far = halo_ref[p, :, :taps].astype(F32)
        far = jnp.where(is_odd, halo_odd_ref[p, :, :taps].astype(F32), far)
        far = jnp.where(has_next, far, 0.0)
        for c in range(2):
            rows[c * group + p : c * group + p + 1, span:] = far[c : c + 1]
    done = correlate(rows, even, odd, table, span // LANE, extra, group)
    ready = early_ref.shape[0]
    for s in range(ready):
        out_ref[section ^ s] = early_ref[s]
    for s in range(ready, out_ref.shape[0]):
        out_ref[section ^ s] = as_chunk(done, s - ready, out_ref.shape[2] // LANE, group)


def row_scratch(blocks, group):
    return [
        pltpu.VMEM((2 * group, blocks * LANE), F32),
        pltpu.VMEM((blocks * group, 2 * LANE), BF16),
        pltpu.VMEM((blocks * group, 2 * LANE), BF16),
    ]


def begin_compression(echo, chirp, sections, group):
    _, _, length = echo.shape
    taps = chirp.shape[1]
    extra = taps // LANE
    chunk = length // sections
    early = (length - taps) // chunk
    return pl.pallas_call(
        functools.partial(begin_kernel, group=group),
        out_shape=(
            jax.ShapeDtypeStruct((early, 2 * group, chunk), BF16),
            jax.ShapeDtypeStruct((2 * group, length - early * chunk), F32),
            jax.ShapeDtypeStruct(((extra + 1) * 2 * LANE, 2 * LANE), BF16),
        ),
        scratch_shapes=row_scratch(length // LANE, group),
        compiler_params=pltpu.CompilerParams(vmem_limit_bytes=24 * 1024 * 1024),
        name="begin_compression",
    )(echo, chirp)


def finish_compression(index, early, late, halos, table, sections, group):
    _, height, chunk = early.shape
    blocks = late.shape[1] // LANE + table.shape[0] // (2 * LANE) - 1
    return pl.pallas_call(
        functools.partial(finish_kernel, group=group),
        out_shape=jax.ShapeDtypeStruct((sections, height, chunk), BF16),
        in_specs=[pl.BlockSpec(memory_space=pltpu.SMEM)] + [pl.BlockSpec(memory_space=pltpu.VMEM)] * 5,
        scratch_shapes=row_scratch(blocks, group),
        compiler_params=pltpu.CompilerParams(vmem_limit_bytes=24 * 1024 * 1024),
        name="finish_compression",
    )(index, early, late, *halos, table)


def image_kernel(operator_ref, *refs):
    chunks, (out_ref, parts, sems) = refs[:-3], refs[-3:]
    count, _, tile = parts.shape
    operator = operator_ref[...]
    copies = []
    for i in range(count):
        pulses = [chunk[:, i * tile : (i + 1) * tile] for chunk in chunks]
        result = jnp.dot(operator, jnp.concatenate(pulses + pulses, axis=0), preferred_element_type=F32)
        parts[i] = result.astype(BF16)
        copy = pltpu.make_async_copy(parts.at[i], out_ref.at[:, i * tile : (i + 1) * tile], sems.at[i])
        copy.start()
        copies.append(copy)
    for copy in copies:
        copy.wait()


def form_image(operator, chunks):
    height, width = operator.shape[0], chunks[0].shape[1]
    tile = 256 if width % 256 == 0 else width
    return pl.pallas_call(
        image_kernel,
        out_shape=jax.ShapeDtypeStruct((height, width), BF16),
        in_specs=[pl.BlockSpec(memory_space=pltpu.VMEM)] * (1 + len(chunks)),
        out_specs=pl.BlockSpec(memory_space=pl.ANY),
        scratch_shapes=[
            pltpu.VMEM((width // tile, height, tile), BF16),
            pltpu.SemaphoreType.DMA((width // tile,)),
        ],
        compiler_params=pltpu.CompilerParams(vmem_limit_bytes=16 * 1024 * 1024),
        name="form_image",
    )(operator, *chunks)


def swap(value, axis, by):
    count = lax.axis_size(axis)
    return lax.ppermute(value, axis, [(i, i ^ by) for i in range(count)])


def swap_both(value, by_section, by_sub):
    sections, subs = lax.axis_size("section"), lax.axis_size("sub")
    pairs = [
        (s * subs + a, (s ^ by_section) * subs + (a ^ by_sub)) for s in range(sections) for a in range(subs)
    ]
    return lax.ppermute(value, ("section", "sub"), pairs)


def from_next(value, axis):
    count = lax.axis_size(axis)
    results = []
    for parity in range(2):
        peers = [min(max(((i + parity) ^ 1) - parity, 0), count - 1) for i in range(count)]
        results.append(lax.ppermute(value, axis, list(enumerate(peers))))
    return results


def on_device(echoes, chirp, steer, pulse_order, band_coef, band_start, band_width):
    sections, subs = lax.axis_size("section"), lax.axis_size("sub")
    pulses_each = echoes.shape[2]
    group = ceil_to(pulses_each, SUBL)
    coef = jnp.swapaxes(band_coef, 4, 5)
    weights = jnp.swapaxes(steer, 2, 3)
    levels, _, sides, parts, taps, beams = coef.shape
    dims = (levels, sides, parts, taps, beams)

    section = lax.axis_index("section").astype(jnp.int32)
    place, last = lax.axis_index("rng").astype(jnp.int32), lax.axis_size("rng") - 1
    index = jnp.stack([section, place & 1, (place < last).astype(jnp.int32)])
    echo = jnp.transpose(echoes[:, 0], (1, 0, 2))
    halos = from_next(echo, "rng")
    packed = pack_parameters(coef, band_start, band_width, weights, pulse_order, sections, group)
    packed_partner = swap(packed, "sub", 1) if subs == 2 else packed
    early, late, table = begin_compression(echo, chirp, sections, group)
    *halos, packed_partner = lax.optimization_barrier((*halos, packed_partner))
    compressed = finish_compression(index, early, late, halos, table, sections, group)
    chunks = [compressed[0]] + [swap(compressed[j], "section", j) for j in range(1, sections)]
    if subs != 2:
        return merge_images(section, chunks, packed, dims, sections, group)
    chunks += [swap_both(compressed[j], j, 1) for j in range(sections)]
    operator = fold_operator(index, packed, packed_partner, dims, sections, group)
    image = form_image(operator, chunks)
    return image.reshape(2, beams, 1, image.shape[1])


def merge_images(section, chunks, packed, dims, sections, group):
    levels, sides, parts, taps, beams = dims
    width = sections * group
    first = levels * sides * parts * taps
    table = packed[first : first + parts * width].reshape(parts, sections, group, beams)
    table = jnp.take(table, section ^ jnp.arange(sections), axis=1)
    real, imag = table[0], table[1]
    rows = jnp.concatenate(
        [jnp.concatenate([real, -imag], axis=1), jnp.concatenate([imag, real], axis=1)], axis=2
    ).reshape(sections * 2 * group, 2 * beams)
    image = lax.dot_general(
        rows, jnp.concatenate(chunks, axis=0), (((0,), (0,)), ((), ())), preferred_element_type=F32
    ).astype(BF16)
    starts = packed[first + parts * width :].astype(jnp.int32)
    column = jnp.arange(beams, dtype=jnp.int32)
    bits = lax.axis_size("sub").bit_length() - 1
    for level in range(levels):
        partner = swap(image, "sub", 1 << (level % bits))
        operands = []
        for side in range(sides):
            at = (level * sides + side) * parts * taps
            coef = packed[at : at + parts * taps].reshape(parts, taps, beams)
            offset = column[:, None] - starts[level * sides + side][None, :]
            hits = (offset[None] == jnp.arange(taps, dtype=jnp.int32)[:, None, None]).astype(BF16)
            operands.append(jnp.einsum("ptq,tcq->pqc", coef, hits, preferred_element_type=F32).astype(BF16))
        top = jnp.concatenate([operands[0][0], -operands[0][1], operands[1][0], -operands[1][1]], axis=1)
        low = jnp.concatenate([operands[0][1], operands[0][0], operands[1][1], operands[1][0]], axis=1)
        image = jnp.dot(
            jnp.concatenate([top, low], axis=0),
            jnp.concatenate([image, partner], axis=0),
            preferred_element_type=F32,
        ).astype(BF16)
    return image.reshape(2, beams, 1, image.shape[1])


def solution(mesh):
    return jax.shard_map(
        on_device,
        mesh=mesh,
        in_specs=(
            P(None, "sub", "section", "rng"),
            P(),
            P(None, "sub", None, None),
            P("sub", None),
            P(None, "sub", None, None, None, None),
            P(None, "sub", None, None),
            P(None, "sub", None, None),
        ),
        out_specs=P(None, "sub", "rng", "section"),
        check_vma=False,
    )
```

```python
import functools

import jax
import jax.numpy as jnp
from jax import lax
from jax.experimental import pallas as pl
from jax.experimental.pallas import tpu as pltpu
from jax.sharding import PartitionSpec as P

LANE = 128
SUBL = 8
F32 = jnp.float32
BF16 = jnp.bfloat16


def ceil_to(value, unit):
    return -(-value // unit) * unit


def pack_kernel(coef_ref, start_ref, width_ref, steer_ref, order_ref, pack_ref, starts, *, sections, group):
    levels, _, sides, parts, taps, beams = coef_ref.shape
    tap = lax.broadcasted_iota(jnp.int32, (taps, beams), 0)
    row = 0
    for level in range(levels):
        for side in range(sides):
            used = tap < width_ref[level, 0, side : side + 1, :]
            for part in range(parts):
                entries = coef_ref[level, 0, side, part].astype(F32)
                pack_ref[row : row + taps] = jnp.where(used, entries, 0.0).astype(BF16)
                row += taps
    pulses = order_ref.shape[1]
    each = pulses // sections
    position = lax.broadcasted_iota(jnp.int32, (pulses, pulses), 0)
    hit = (position == order_ref[0:1, :]).astype(F32)
    slot = lax.broadcasted_iota(jnp.int32, (sections * group, pulses), 0)
    pulse = lax.broadcasted_iota(jnp.int32, (sections * group, pulses), 1)
    place = jnp.zeros((sections * group, pulses), F32)
    for s in range(sections):
        inside = (pulse >= s * each) & (pulse < (s + 1) * each)
        place = jnp.where(inside & (slot - s * group == pulse - s * each), 1.0, place)
    pick = lax.dot_general(
        place.astype(BF16), hit.astype(BF16), (((1,), (1,)), ((), ())), preferred_element_type=F32
    )
    for part in range(parts):
        chosen = jnp.dot(pick.astype(BF16), steer_ref[part, 0], preferred_element_type=F32)
        pack_ref[row : row + sections * group] = chosen.astype(BF16)
        row += sections * group
    starts[...] = jnp.zeros_like(starts)
    for level in range(levels):
        starts[sides * level : sides * level + sides] = start_ref[level, 0].astype(F32)
    pack_ref[row : row + starts.shape[0]] = starts[...].astype(BF16)


def pack_rows(levels, sides, parts, taps, sections, group):
    return levels * sides * parts * taps + parts * sections * group + ceil_to(levels * sides, 16)


def pack_parameters(coef, start, width, steer, order, sections, group):
    levels, _, sides, parts, taps, beams = coef.shape
    return pl.pallas_call(
        functools.partial(pack_kernel, sections=sections, group=group),
        out_shape=jax.ShapeDtypeStruct((pack_rows(levels, sides, parts, taps, sections, group), beams), BF16),
        scratch_shapes=[pltpu.VMEM((ceil_to(levels * sides, 16), beams), F32)],
        name="pack_parameters",
    )(coef, start, width, steer, order)


def split_two(value):
    high = value.astype(BF16)
    return high, (value - high.astype(F32)).astype(BF16)


def operator_kernel(index_ref, own_ref, partner_ref, out_ref, weights, *, dims, sections, group):
    levels, sides, parts, taps, beams = dims
    width = sections * group
    refs = (own_ref, partner_ref)
    weight_row = levels * sides * parts * taps
    start_row = weight_row + parts * width

    def band(ref, level, side):
        first = ((level * sides + side) * parts) * taps
        tables = [ref[first + p * taps : first + (p + 1) * taps].astype(F32) for p in range(parts)]
        start = ref[start_row : start_row + ceil_to(levels * sides, 16)].astype(F32)
        start = start[level * sides + side : level * sides + side + 1].astype(jnp.int32)
        found = [[], []]
        for c in range(0, beams, SUBL):
            column = lax.broadcasted_iota(jnp.int32, (SUBL, beams), 0) + c
            offset = column - start
            spot = offset & (SUBL - 1)
            for p in range(parts):
                value = jnp.zeros((SUBL, beams), F32)
                for t in range(0, taps, SUBL):
                    got = jnp.take_along_axis(
                        tables[p][t : t + SUBL], spot, axis=0, mode="promise_in_bounds"
                    )
                    value = jnp.where((offset >= t) & (offset < t + SUBL), got, value)
                found[p].append(value)
        return [jnp.concatenate(f, axis=0) for f in found]

    def complex_operand(real, imag):
        top = jnp.concatenate([real, imag], axis=1)
        low = jnp.concatenate([-imag, real], axis=1)
        return jnp.concatenate([top, low], axis=0).astype(BF16)

    section = index_ref[0]
    images = []
    for a in range(2):
        for p in range(parts):
            weights[...] = refs[a][weight_row + p * width : weight_row + (p + 1) * width].astype(F32)
            rows = []
            for j in range(sections):
                at = pl.multiple_of((section ^ j) * group, group)
                rows.append(weights[pl.ds(at, group)])
            images.append(jnp.concatenate(rows, axis=0))
    zero = jnp.zeros((width, 2 * beams), F32)
    own = jnp.concatenate([jnp.concatenate(images[0:2], axis=1), zero], axis=0)
    partner = jnp.concatenate([zero, jnp.concatenate(images[2:4], axis=1)], axis=0)
    for level in range(levels):
        own_high, own_low = split_two(own)
        partner_high, partner_low = split_two(partner)
        own_rows = jnp.concatenate([own_high, own_low], axis=0)
        partner_rows = jnp.concatenate([partner_high, partner_low], axis=0)

        def merged(ref, mine, other):
            product = jnp.dot(
                mine, complex_operand(*band(ref, level, 0)), preferred_element_type=F32
            ) + jnp.dot(other, complex_operand(*band(ref, level, 1)), preferred_element_type=F32)
            return product[: 2 * width] + product[2 * width :]

        following = merged(own_ref, own_rows, partner_rows)
        if level < levels - 1:
            partner = merged(partner_ref, partner_rows, own_rows)
        own = following
    blocks = []
    for j in range(2 * sections):
        real = own[j * group : (j + 1) * group, :beams]
        imag = own[j * group : (j + 1) * group, beams:]
        blocks.append(jnp.concatenate([real, imag], axis=1))
        blocks.append(jnp.concatenate([-imag, real], axis=1))
    whole = jnp.concatenate(blocks, axis=0).T
    high, low = split_two(whole)
    out_ref[...] = jnp.concatenate([high, low], axis=1)


def fold_operator(section, own, partner, dims, sections, group):
    beams = dims[-1]
    width = sections * group
    return pl.pallas_call(
        functools.partial(operator_kernel, dims=dims, sections=sections, group=group),
        out_shape=jax.ShapeDtypeStruct((2 * beams, 8 * width), BF16),
        in_specs=[
            pl.BlockSpec(memory_space=pltpu.SMEM),
            pl.BlockSpec(memory_space=pltpu.VMEM),
            pl.BlockSpec(memory_space=pltpu.VMEM),
        ],
        scratch_shapes=[pltpu.VMEM((width, beams), F32)],
        compiler_params=pltpu.CompilerParams(vmem_limit_bytes=16 * 1024 * 1024),
        name="fold_operator",
    )(section, own, partner)


def compress_kernel(
    index_ref, echo_ref, halo_ref, chirp_ref, keep_ref, give_ref, rows, even, odd, table, *, sections, group
):
    pulses, _, length = echo_ref.shape
    taps = chirp_ref.shape[1]
    blocks, extra = length // LANE, taps // LANE
    total = blocks + extra
    reverse = LANE - 1 - lax.broadcasted_iota(jnp.int32, (2, LANE), 1)
    below = lax.broadcasted_iota(jnp.int32, (LANE, LANE), 1) <= lax.broadcasted_iota(
        jnp.int32, (LANE, LANE), 0
    )
    before = [jnp.zeros((LANE, LANE), F32)] * 2
    for lag in range(extra + 1):
        if lag < extra:
            piece = chirp_ref[:, lag * LANE : (lag + 1) * LANE].astype(F32)
            piece = jnp.take_along_axis(piece, reverse, axis=1, mode="promise_in_bounds")
            turned = [
                pltpu.roll(
                    jnp.broadcast_to(piece[c : c + 1], (LANE, LANE)), 1, 1, stride=1, stride_axis=0
                )
                for c in range(2)
            ]
        else:
            turned = [jnp.zeros((LANE, LANE), F32)] * 2
        real, imag = [jnp.where(below, turned[c], before[c]) for c in range(2)]
        before = turned
        at = lag * 2 * LANE
        table[at : at + LANE, :LANE] = real.astype(BF16)
        table[at : at + LANE, LANE:] = (-imag).astype(BF16)
        table[at + LANE : at + 2 * LANE, :LANE] = imag.astype(BF16)
        table[at + LANE : at + 2 * LANE, LANE:] = real.astype(BF16)
    rows[...] = jnp.zeros_like(rows)
    for p in range(pulses):
        near = echo_ref[p].astype(F32)
        far = halo_ref[p, :, :taps].astype(F32)
        for c in range(2):
            rows[c * group + p : c * group + p + 1, :length] = near[c : c + 1]
            rows[c * group + p : c * group + p + 1, length:] = far[c : c + 1]
    held = [
        jnp.concatenate(
            [rows[:group, b * LANE : (b + 1) * LANE], rows[group:, b * LANE : (b + 1) * LANE]], axis=1
        )
        for b in range(total)
    ]
    for b in range(0, total, 2):
        even[b * group : (b + 2) * group] = jnp.concatenate(held[b : b + 2], axis=0).astype(BF16)
    for b in range(1, total - 1, 2):
        odd[(b - 1) * group : (b + 1) * group] = jnp.concatenate(held[b : b + 2], axis=0).astype(BF16)
    window = blocks * group
    pieces = []
    for lag in range(extra + 1):
        source, at = (even, lag) if lag % 2 == 0 else (odd, lag - 1)
        pieces.append(source[at * group : at * group + window])
    done = jnp.dot(jnp.concatenate(pieces, axis=1), table[...], preferred_element_type=F32)
    section = index_ref[0]
    chunk = blocks // sections
    for s in range(sections):
        real = [done[(s * chunk + b) * group : (s * chunk + b + 1) * group, :LANE] for b in range(chunk)]
        imag = [done[(s * chunk + b) * group : (s * chunk + b + 1) * group, LANE:] for b in range(chunk)]
        stacked = jnp.concatenate(
            [jnp.concatenate(real, axis=1), jnp.concatenate(imag, axis=1)], axis=0
        )
        slot = section ^ s

        @pl.when(slot % 2 == 0)
        def _():
            keep_ref[slot // 2] = stacked.astype(BF16)

        @pl.when(slot % 2 == 1)
        def _():
            give_ref[slot // 2] = stacked.astype(BF16)


def compress_pulses(section, echo, halo, chirp, sections, group):
    pulses, _, length = echo.shape
    taps = chirp.shape[1]
    blocks, extra = length // LANE, taps // LANE
    total = blocks + extra
    return pl.pallas_call(
        functools.partial(compress_kernel, sections=sections, group=group),
        out_shape=[jax.ShapeDtypeStruct((sections // 2, 2 * group, length // sections), BF16)] * 2,
        in_specs=[pl.BlockSpec(memory_space=pltpu.SMEM)] + [pl.BlockSpec(memory_space=pltpu.VMEM)] * 3,
        scratch_shapes=[
            pltpu.VMEM((2 * group, total * LANE), F32),
            pltpu.VMEM((total * group, 2 * LANE), BF16),
            pltpu.VMEM((total * group, 2 * LANE), BF16),
            pltpu.VMEM(((extra + 1) * 2 * LANE, 2 * LANE), BF16),
        ],
        compiler_params=pltpu.CompilerParams(vmem_limit_bytes=24 * 1024 * 1024),
        name="compress_pulses",
    )(section, echo, halo, chirp)


def image_kernel(operator_ref, *refs):
    chunks, (out_ref, parts, sems) = refs[:-3], refs[-3:]
    count, _, tile = parts.shape
    operator = operator_ref[...]
    copies = []
    for i in range(count):
        pulses = [chunk[:, i * tile : (i + 1) * tile] for chunk in chunks]
        result = jnp.dot(operator, jnp.concatenate(pulses + pulses, axis=0), preferred_element_type=F32)
        parts[i] = result.astype(BF16)
        copy = pltpu.make_async_copy(parts.at[i], out_ref.at[:, i * tile : (i + 1) * tile], sems.at[i])
        copy.start()
        copies.append(copy)
    for copy in copies:
        copy.wait()


def form_image(operator, chunks):
    height, width = operator.shape[0], chunks[0].shape[1]
    tile = 256 if width % 256 == 0 else width
    return pl.pallas_call(
        image_kernel,
        out_shape=jax.ShapeDtypeStruct((height, width), BF16),
        in_specs=[pl.BlockSpec(memory_space=pltpu.VMEM)] * (1 + len(chunks)),
        out_specs=pl.BlockSpec(memory_space=pl.ANY),
        scratch_shapes=[
            pltpu.VMEM((width // tile, height, tile), BF16),
            pltpu.SemaphoreType.DMA((width // tile,)),
        ],
        compiler_params=pltpu.CompilerParams(vmem_limit_bytes=16 * 1024 * 1024),
        name="form_image",
    )(operator, *chunks)


def swap(value, axis, by):
    count = lax.axis_size(axis)
    return lax.ppermute(value, axis, [(i, i ^ by) for i in range(count)])


def swap_both(value, by_section, by_sub):
    sections, subs = lax.axis_size("section"), lax.axis_size("sub")
    pairs = [
        (s * subs + a, (s ^ by_section) * subs + (a ^ by_sub)) for s in range(sections) for a in range(subs)
    ]
    return lax.ppermute(value, ("section", "sub"), pairs)


def from_behind(value, axis, by):
    size = lax.axis_size(axis)
    pairs = [(i, i + by) for i in range(size) if 0 <= i + by < size]
    return lax.ppermute(value, axis, pairs)


def on_device(echoes, chirp, steer, pulse_order, band_coef, band_start, band_width):
    sections, subs = lax.axis_size("section"), lax.axis_size("sub")
    pulses_each = echoes.shape[2]
    group = ceil_to(pulses_each, SUBL)
    section = lax.axis_index("section").astype(jnp.int32).reshape(1)
    coef = jnp.swapaxes(band_coef, 4, 5)
    weights = jnp.swapaxes(steer, 2, 3)
    levels, _, sides, parts, taps, beams = coef.shape
    dims = (levels, sides, parts, taps, beams)

    echo = jnp.transpose(echoes[:, 0], (1, 0, 2))
    halo = from_behind(echo, "rng", -1)
    packed = pack_parameters(coef, band_start, band_width, weights, pulse_order, sections, group)
    if subs == 2:
        packed_partner = swap(packed, "sub", 1)
    keep, give = compress_pulses(section, echo, halo, chirp, sections, group)
    both = jnp.concatenate([keep, swap(give, "section", 1)], axis=1)
    chunks = [both[0]] + [swap(both[j], "section", 2 * j) for j in range(1, sections // 2)]
    if subs != 2:
        return merge_images(section, chunks, packed, dims, sections, group)
    chunks += [swap_both(both[j], 2 * j, 1) for j in range(sections // 2)]
    operator = fold_operator(section, packed, packed_partner, dims, sections, group)
    image = form_image(operator, chunks)
    return image.reshape(2, beams, 1, image.shape[1])


def merge_images(section, chunks, packed, dims, sections, group):
    levels, sides, parts, taps, beams = dims
    width = sections * group
    first = levels * sides * parts * taps
    table = packed[first : first + parts * width].reshape(parts, sections, group, beams)
    table = jnp.take(table, section[0] ^ jnp.arange(sections), axis=1)
    real, imag = table[0], table[1]
    rows = jnp.concatenate(
        [jnp.concatenate([real, -imag], axis=1), jnp.concatenate([imag, real], axis=1)], axis=2
    ).reshape(sections * 2 * group, 2 * beams)
    image = lax.dot_general(
        rows, jnp.concatenate(chunks, axis=0), (((0,), (0,)), ((), ())), preferred_element_type=F32
    ).astype(BF16)
    starts = packed[first + parts * width :].astype(jnp.int32)
    column = jnp.arange(beams, dtype=jnp.int32)
    bits = lax.axis_size("sub").bit_length() - 1
    for level in range(levels):
        partner = swap(image, "sub", 1 << (level % bits))
        operands = []
        for side in range(sides):
            at = (level * sides + side) * parts * taps
            coef = packed[at : at + parts * taps].reshape(parts, taps, beams)
            offset = column[:, None] - starts[level * sides + side][None, :]
            hits = (offset[None] == jnp.arange(taps, dtype=jnp.int32)[:, None, None]).astype(BF16)
            operands.append(jnp.einsum("ptq,tcq->pqc", coef, hits, preferred_element_type=F32).astype(BF16))
        top = jnp.concatenate([operands[0][0], -operands[0][1], operands[1][0], -operands[1][1]], axis=1)
        low = jnp.concatenate([operands[0][1], operands[0][0], operands[1][1], operands[1][0]], axis=1)
        image = jnp.dot(
            jnp.concatenate([top, low], axis=0),
            jnp.concatenate([image, partner], axis=0),
            preferred_element_type=F32,
        ).astype(BF16)
    return image.reshape(2, beams, 1, image.shape[1])


def solution(mesh):
    return jax.shard_map(
        on_device,
        mesh=mesh,
        in_specs=(
            P(None, "sub", "section", "rng"),
            P(),
            P(None, "sub", None, None),
            P("sub", None),
            P(None, "sub", None, None, None, None),
            P(None, "sub", None, None),
            P(None, "sub", None, None),
        ),
        out_specs=P(None, "sub", "rng", "section"),
        check_vma=False,
    )
```

```python
import functools

import jax
import jax.numpy as jnp
from jax import lax
from jax.experimental import pallas as pl
from jax.experimental.pallas import tpu as pltpu
from jax.sharding import PartitionSpec as P

LANE = 128
SUBL = 8
F32 = jnp.float32
BF16 = jnp.bfloat16


def ceil_to(value, unit):
    return -(-value // unit) * unit


def pack_kernel(coef_ref, start_ref, width_ref, steer_ref, order_ref, pack_ref, starts, *, sections, group):
    levels, _, sides, parts, taps, beams = coef_ref.shape
    tap = lax.broadcasted_iota(jnp.int32, (taps, beams), 0)
    row = 0
    for level in range(levels):
        for side in range(sides):
            used = tap < width_ref[level, 0, side : side + 1, :]
            for part in range(parts):
                entries = coef_ref[level, 0, side, part].astype(F32)
                pack_ref[row : row + taps] = jnp.where(used, entries, 0.0).astype(BF16)
                row += taps
    pulses = order_ref.shape[1]
    each = pulses // sections
    position = lax.broadcasted_iota(jnp.int32, (pulses, pulses), 0)
    hit = (position == order_ref[0:1, :]).astype(F32)
    slot = lax.broadcasted_iota(jnp.int32, (sections * group, pulses), 0)
    pulse = lax.broadcasted_iota(jnp.int32, (sections * group, pulses), 1)
    place = jnp.zeros((sections * group, pulses), F32)
    for s in range(sections):
        inside = (pulse >= s * each) & (pulse < (s + 1) * each)
        place = jnp.where(inside & (slot - s * group == pulse - s * each), 1.0, place)
    pick = lax.dot_general(
        place.astype(BF16), hit.astype(BF16), (((1,), (1,)), ((), ())), preferred_element_type=F32
    )
    for part in range(parts):
        chosen = jnp.dot(pick.astype(BF16), steer_ref[part, 0], preferred_element_type=F32)
        pack_ref[row : row + sections * group] = chosen.astype(BF16)
        row += sections * group
    starts[...] = jnp.zeros_like(starts)
    for level in range(levels):
        starts[sides * level : sides * level + sides] = start_ref[level, 0].astype(F32)
    pack_ref[row : row + starts.shape[0]] = starts[...].astype(BF16)


def pack_rows(levels, sides, parts, taps, sections, group):
    return levels * sides * parts * taps + parts * sections * group + ceil_to(levels * sides, 16)


def pack_parameters(coef, start, width, steer, order, sections, group):
    levels, _, sides, parts, taps, beams = coef.shape
    return pl.pallas_call(
        functools.partial(pack_kernel, sections=sections, group=group),
        out_shape=jax.ShapeDtypeStruct((pack_rows(levels, sides, parts, taps, sections, group), beams), BF16),
        scratch_shapes=[pltpu.VMEM((ceil_to(levels * sides, 16), beams), F32)],
        name="pack_parameters",
    )(coef, start, width, steer, order)


def pack_rows_of(real, imag, each):
    group = real.shape[0]
    row = lax.broadcasted_iota(jnp.int32, real.shape, 0)
    return jnp.where(row < each, real, pltpu.roll(imag, each, 0)), group - each


def split_two(value):
    high = value.astype(BF16)
    return high, (value - high.astype(F32)).astype(BF16)


def operator_kernel(index_ref, own_ref, partner_ref, out_ref, weights, *, dims, sections, group, each):
    levels, sides, parts, taps, beams = dims
    width = sections * group
    refs = (own_ref, partner_ref)
    weight_row = levels * sides * parts * taps
    start_row = weight_row + parts * width

    def band(ref, level, side):
        first = ((level * sides + side) * parts) * taps
        tables = [ref[first + p * taps : first + (p + 1) * taps].astype(F32) for p in range(parts)]
        start = ref[start_row : start_row + ceil_to(levels * sides, 16)].astype(F32)
        start = start[level * sides + side : level * sides + side + 1].astype(jnp.int32)
        found = [[], []]
        for c in range(0, beams, SUBL):
            column = lax.broadcasted_iota(jnp.int32, (SUBL, beams), 0) + c
            offset = column - start
            spot = offset & (SUBL - 1)
            for p in range(parts):
                value = jnp.zeros((SUBL, beams), F32)
                for t in range(0, taps, SUBL):
                    got = jnp.take_along_axis(
                        tables[p][t : t + SUBL], spot, axis=0, mode="promise_in_bounds"
                    )
                    value = jnp.where((offset >= t) & (offset < t + SUBL), got, value)
                found[p].append(value)
        return [jnp.concatenate(f, axis=0) for f in found]

    def complex_operand(real, imag):
        top = jnp.concatenate([real, imag], axis=1)
        low = jnp.concatenate([-imag, real], axis=1)
        return jnp.concatenate([top, low], axis=0).astype(BF16)

    section = index_ref[0]
    images = []
    for a in range(2):
        for p in range(parts):
            weights[...] = refs[a][weight_row + p * width : weight_row + (p + 1) * width].astype(F32)
            rows = []
            for j in range(sections):
                at = pl.multiple_of((section ^ j) * group, group)
                rows.append(weights[pl.ds(at, group)])
            images.append(jnp.concatenate(rows, axis=0))
    zero = jnp.zeros((width, 2 * beams), F32)
    own = jnp.concatenate([jnp.concatenate(images[0:2], axis=1), zero], axis=0)
    partner = jnp.concatenate([zero, jnp.concatenate(images[2:4], axis=1)], axis=0)
    for level in range(levels):
        own_high, own_low = split_two(own)
        partner_high, partner_low = split_two(partner)
        own_rows = jnp.concatenate([own_high, own_low], axis=0)
        partner_rows = jnp.concatenate([partner_high, partner_low], axis=0)

        def merged(ref, mine, other):
            product = jnp.dot(
                mine, complex_operand(*band(ref, level, 0)), preferred_element_type=F32
            ) + jnp.dot(other, complex_operand(*band(ref, level, 1)), preferred_element_type=F32)
            return product[: 2 * width] + product[2 * width :]

        following = merged(own_ref, own_rows, partner_rows)
        if level < levels - 1:
            partner = merged(partner_ref, partner_rows, own_rows)
        own = following
    full, left, right = [], [], []
    for j in range(2 * sections):
        real = own[j * group : (j + 1) * group, :beams]
        imag = own[j * group : (j + 1) * group, beams:]
        straight = jnp.concatenate([real, imag], axis=1)
        turned = jnp.concatenate([-imag, real], axis=1)
        lead, moved = pack_rows_of(straight, turned, each)
        row = lax.broadcasted_iota(jnp.int32, lead.shape, 0)
        full.append(lead)
        left.append(jnp.where(row < group // 2, pltpu.roll(turned, group - moved, 0), 0.0))
        right.append(jnp.where(row >= group // 2, pltpu.roll(turned, group // 2 - moved, 0), 0.0))
    pairs = sections // 2
    first_core = section % 2 == 0
    for half, rest in enumerate((left, right)):
        sources = [jnp.concatenate([full[j], rest[j]], axis=0) for j in range(2 * sections)]
        quarters = [jnp.concatenate(sources[q * pairs : (q + 1) * pairs], axis=0) for q in range(4)]
        quarters[1:3] = [
            jnp.where(first_core, quarters[1], quarters[2]),
            jnp.where(first_core, quarters[2], quarters[1]),
        ]
        high, low = split_two(jnp.concatenate(quarters, axis=0).T)
        out_ref[half] = jnp.concatenate([high, low], axis=1)


def fold_operator(section, own, partner, dims, sections, group, each):
    beams = dims[-1]
    width = sections * group
    return pl.pallas_call(
        functools.partial(operator_kernel, dims=dims, sections=sections, group=group, each=each),
        out_shape=jax.ShapeDtypeStruct((2, 2 * beams, 8 * width), BF16),
        in_specs=[
            pl.BlockSpec(memory_space=pltpu.SMEM),
            pl.BlockSpec(memory_space=pltpu.VMEM),
            pl.BlockSpec(memory_space=pltpu.VMEM),
        ],
        scratch_shapes=[pltpu.VMEM((width, beams), F32)],
        compiler_params=pltpu.CompilerParams(vmem_limit_bytes=16 * 1024 * 1024),
        name="fold_operator",
    )(section, own, partner)


def compress_kernel(
    index_ref, echo_ref, halo_ref, chirp_ref, keep_ref, give_ref, rows, even, odd, table, *, sections, group
):
    pulses, _, length = echo_ref.shape
    taps = chirp_ref.shape[1]
    blocks, extra = length // LANE, taps // LANE
    total = blocks + extra
    reverse = LANE - 1 - lax.broadcasted_iota(jnp.int32, (2, LANE), 1)
    below = lax.broadcasted_iota(jnp.int32, (LANE, LANE), 1) <= lax.broadcasted_iota(
        jnp.int32, (LANE, LANE), 0
    )
    before = [jnp.zeros((LANE, LANE), F32)] * 2
    for lag in range(extra + 1):
        if lag < extra:
            piece = chirp_ref[:, lag * LANE : (lag + 1) * LANE].astype(F32)
            piece = jnp.take_along_axis(piece, reverse, axis=1, mode="promise_in_bounds")
            turned = [
                pltpu.roll(
                    jnp.broadcast_to(piece[c : c + 1], (LANE, LANE)), 1, 1, stride=1, stride_axis=0
                )
                for c in range(2)
            ]
        else:
            turned = [jnp.zeros((LANE, LANE), F32)] * 2
        real, imag = [jnp.where(below, turned[c], before[c]) for c in range(2)]
        before = turned
        at = lag * 2 * LANE
        table[at : at + LANE, :LANE] = real.astype(BF16)
        table[at : at + LANE, LANE:] = (-imag).astype(BF16)
        table[at + LANE : at + 2 * LANE, :LANE] = imag.astype(BF16)
        table[at + LANE : at + 2 * LANE, LANE:] = real.astype(BF16)
    rows[...] = jnp.zeros_like(rows)
    for p in range(pulses):
        near = echo_ref[p].astype(F32)
        far = halo_ref[p, :, :taps].astype(F32)
        for c in range(2):
            rows[c * group + p : c * group + p + 1, :length] = near[c : c + 1]
            rows[c * group + p : c * group + p + 1, length:] = far[c : c + 1]
    held = [
        jnp.concatenate(
            [rows[:group, b * LANE : (b + 1) * LANE], rows[group:, b * LANE : (b + 1) * LANE]], axis=1
        )
        for b in range(total)
    ]
    for b in range(0, total, 2):
        even[b * group : (b + 2) * group] = jnp.concatenate(held[b : b + 2], axis=0).astype(BF16)
    for b in range(1, total - 1, 2):
        odd[(b - 1) * group : (b + 1) * group] = jnp.concatenate(held[b : b + 2], axis=0).astype(BF16)
    window = blocks * group
    pieces = []
    for lag in range(extra + 1):
        source, at = (even, lag) if lag % 2 == 0 else (odd, lag - 1)
        pieces.append(source[at * group : at * group + window])
    done = jnp.dot(jnp.concatenate(pieces, axis=1), table[...], preferred_element_type=F32)
    section = index_ref[0]
    chunk = blocks // sections
    for s in range(sections):
        real, imag = [
            jnp.concatenate(
                [
                    done[(s * chunk + b) * group : (s * chunk + b + 1) * group, c * LANE : (c + 1) * LANE]
                    for b in range(chunk)
                ],
                axis=1,
            )
            for c in range(2)
        ]
        middle = chunk * LANE // 2
        lead, moved = pack_rows_of(real, imag, pulses)
        row = lax.broadcasted_iota(jnp.int32, (group, middle), 0)
        rest = jnp.where(
            row < group // 2,
            pltpu.roll(imag[:, :middle], group - moved, 0),
            pltpu.roll(imag[:, middle:], group // 2 - moved, 0),
        )
        stacked = jnp.concatenate([lead[:, :middle], lead[:, middle:], rest], axis=0).astype(BF16)
        slot = section ^ s
        far, other_core = slot // 2, slot % 2
        place = far ^ 1 ^ (section % 2) ^ other_core

        @pl.when(other_core == 0)
        def _():
            keep_ref[place] = stacked

        @pl.when(other_core == 1)
        def _():
            give_ref[place] = stacked


def compress_pulses(section, echo, halo, chirp, sections, group):
    pulses, _, length = echo.shape
    taps = chirp.shape[1]
    blocks, extra = length // LANE, taps // LANE
    total = blocks + extra
    return pl.pallas_call(
        functools.partial(compress_kernel, sections=sections, group=group),
        out_shape=[jax.ShapeDtypeStruct((2, 3 * group, length // sections // 2), BF16)] * 2,
        in_specs=[pl.BlockSpec(memory_space=pltpu.SMEM)] + [pl.BlockSpec(memory_space=pltpu.VMEM)] * 3,
        scratch_shapes=[
            pltpu.VMEM((2 * group, total * LANE), F32),
            pltpu.VMEM((total * group, 2 * LANE), BF16),
            pltpu.VMEM((total * group, 2 * LANE), BF16),
            pltpu.VMEM(((extra + 1) * 2 * LANE, 2 * LANE), BF16),
        ],
        compiler_params=pltpu.CompilerParams(vmem_limit_bytes=24 * 1024 * 1024),
        name="compress_pulses",
    )(section, echo, halo, chirp)


def image_kernel(index_ref, operator_ref, both_ref, *refs, group):
    chunks, (out_ref, parts, sems) = refs[:-3], refs[-3:]
    count, _, tile = parts.shape
    width = both_ref.shape[2]
    near = 1 - index_ref[0] % 2
    held = [both_ref[near]] + [chunk[...] for chunk in chunks]
    held = [value.astype(F32) for value in held]
    copies = []
    for i in range(count):
        half, at = divmod(i * tile, width)
        rows = []
        for value in held:
            for first in range(0, value.shape[0], 3 * group):
                rows.append(value[first + half * group : first + (half + 1) * group, at : at + tile])
                rows.append(value[first + 2 * group : first + 3 * group, at : at + tile])
        pulses = jnp.concatenate(rows, axis=0).astype(BF16)
        result = jnp.dot(
            operator_ref[half], jnp.concatenate([pulses, pulses], axis=0), preferred_element_type=F32
        )
        parts[i] = result.astype(BF16)
        copy = pltpu.make_async_copy(parts.at[i], out_ref.at[:, i * tile : (i + 1) * tile], sems.at[i])
        copy.start()
        copies.append(copy)
    for copy in copies:
        copy.wait()


def form_image(section, operator, both, chunks, group):
    height, half = operator.shape[1], both.shape[2]
    tile = 256 if half % 256 == 0 else half
    count = 2 * half // tile
    return pl.pallas_call(
        functools.partial(image_kernel, group=group),
        out_shape=jax.ShapeDtypeStruct((height, 2 * half), BF16),
        in_specs=[pl.BlockSpec(memory_space=pltpu.SMEM)]
        + [pl.BlockSpec(memory_space=pltpu.VMEM)] * (2 + len(chunks)),
        out_specs=pl.BlockSpec(memory_space=pl.ANY),
        scratch_shapes=[
            pltpu.VMEM((count, height, tile), BF16),
            pltpu.SemaphoreType.DMA((count,)),
        ],
        compiler_params=pltpu.CompilerParams(vmem_limit_bytes=16 * 1024 * 1024),
        name="form_image",
    )(section, operator, both, *chunks)


def swap(value, axis, by):
    count = lax.axis_size(axis)
    return lax.ppermute(value, axis, [(i, i ^ by) for i in range(count)])


def swap_by(value, move):
    sections, subs = lax.axis_size("section"), lax.axis_size("sub")
    pairs = []
    for s in range(sections):
        for a in range(subs):
            to_s, to_a = move(s, a)
            pairs.append((s * subs + a, to_s * subs + to_a))
    return lax.ppermute(value, ("section", "sub"), pairs)


def from_behind(value, axis, by):
    size = lax.axis_size(axis)
    pairs = [(i, i + by) for i in range(size) if 0 <= i + by < size]
    return lax.ppermute(value, axis, pairs)


def on_device(echoes, chirp, steer, pulse_order, band_coef, band_start, band_width):
    sections, subs = lax.axis_size("section"), lax.axis_size("sub")
    pulses_each = echoes.shape[2]
    group = ceil_to(pulses_each, SUBL)
    section = lax.axis_index("section").astype(jnp.int32).reshape(1)
    coef = jnp.swapaxes(band_coef, 4, 5)
    weights = jnp.swapaxes(steer, 2, 3)
    levels, _, sides, parts, taps, beams = coef.shape
    dims = (levels, sides, parts, taps, beams)

    echo = jnp.transpose(echoes[:, 0], (1, 0, 2))
    halo = from_behind(echo, "rng", -1)
    packed = pack_parameters(coef, band_start, band_width, weights, pulse_order, sections, group)
    if subs == 2:
        packed_partner = swap(packed, "sub", 1)
    keep, give = compress_pulses(section, echo, halo, chirp, sections, group)
    both = jnp.concatenate([keep, swap(give, "section", 1)], axis=1)
    far = lax.dynamic_index_in_dim(both, section[0] % 2, 0, keepdims=False)
    if subs != 2:
        near = lax.dynamic_index_in_dim(both, 1 - section[0] % 2, 0, keepdims=False)
        chunks = [near, swap(far, "section", 2)]
        return merge_images(section, chunks, packed, dims, sections, group, pulses_each)
    chunks = [
        swap_by(both[0], lambda s, a: (s, a ^ 1) if s % 2 else (s ^ 2, a)),
        swap_by(both[1], lambda s, a: (s ^ 2, a) if s % 2 else (s, a ^ 1)),
        swap_by(far, lambda s, a: (s ^ 2, a ^ 1)),
    ]
    operator = fold_operator(section, packed, packed_partner, dims, sections, group, pulses_each)
    image = form_image(section, operator, both, chunks, group)
    return image.reshape(2, beams, 1, image.shape[1])


def unpack(chunk, group, each):
    lead = jnp.concatenate([chunk[:group], chunk[group : 2 * group]], axis=1)
    moved, rest = group - each, chunk[2 * group :]
    tail = jnp.concatenate([rest[: each - moved], rest[group // 2 : group // 2 + each - moved]], axis=1)
    return jnp.concatenate([lead, tail], axis=0)


def merge_images(section, chunks, packed, dims, sections, group, each):
    levels, sides, parts, taps, beams = dims
    width = sections * group
    first = levels * sides * parts * taps
    table = packed[first : first + parts * width].reshape(parts, sections, group, beams)
    table = jnp.take(table, section[0] ^ jnp.arange(sections), axis=1)[:, :, :each]
    chunks = [
        unpack(chunk[first : first + 3 * group], group, each)
        for chunk in chunks
        for first in range(0, chunk.shape[0], 3 * group)
    ]
    real, imag = table[0], table[1]
    rows = jnp.concatenate(
        [jnp.concatenate([real, -imag], axis=1), jnp.concatenate([imag, real], axis=1)], axis=2
    )
    image = lax.dot_general(
        rows.reshape(-1, 2 * beams), jnp.concatenate(chunks, axis=0), (((0,), (0,)), ((), ())), preferred_element_type=F32
    ).astype(BF16)
    starts = packed[first + parts * width :].astype(jnp.int32)
    column = jnp.arange(beams, dtype=jnp.int32)
    bits = lax.axis_size("sub").bit_length() - 1
    for level in range(levels):
        partner = swap(image, "sub", 1 << (level % bits))
        operands = []
        for side in range(sides):
            at = (level * sides + side) * parts * taps
            coef = packed[at : at + parts * taps].reshape(parts, taps, beams)
            offset = column[:, None] - starts[level * sides + side][None, :]
            hits = (offset[None] == jnp.arange(taps, dtype=jnp.int32)[:, None, None]).astype(BF16)
            operands.append(jnp.einsum("ptq,tcq->pqc", coef, hits, preferred_element_type=F32).astype(BF16))
        top = jnp.concatenate([operands[0][0], -operands[0][1], operands[1][0], -operands[1][1]], axis=1)
        low = jnp.concatenate([operands[0][1], operands[0][0], operands[1][1], operands[1][0]], axis=1)
        image = jnp.dot(
            jnp.concatenate([top, low], axis=0),
            jnp.concatenate([image, partner], axis=0),
            preferred_element_type=F32,
        ).astype(BF16)
    return image.reshape(2, beams, 1, image.shape[1])


def solution(mesh):
    return jax.shard_map(
        on_device,
        mesh=mesh,
        in_specs=(
            P(None, "sub", "section", "rng"),
            P(),
            P(None, "sub", None, None),
            P("sub", None),
            P(None, "sub", None, None, None, None),
            P(None, "sub", None, None),
            P(None, "sub", None, None),
        ),
        out_specs=P(None, "sub", "rng", "section"),
        check_vma=False,
    )
```

```python
import functools

import jax
import jax.numpy as jnp
from jax import lax
from jax.experimental import pallas as pl
from jax.experimental.pallas import tpu as pltpu
from jax.sharding import PartitionSpec as P

LANE = 128
SUBL = 8
F32 = jnp.float32
BF16 = jnp.bfloat16


def ceil_to(value, unit):
    return -(-value // unit) * unit


def pack_kernel(coef_ref, start_ref, width_ref, steer_ref, order_ref, pack_ref, starts, *, sections, group):
    levels, _, sides, parts, taps, beams = coef_ref.shape
    tap = lax.broadcasted_iota(jnp.int32, (taps, beams), 0)
    row = 0
    for level in range(levels):
        for side in range(sides):
            used = tap < width_ref[level, 0, side : side + 1, :]
            for part in range(parts):
                entries = coef_ref[level, 0, side, part].astype(F32)
                pack_ref[row : row + taps] = jnp.where(used, entries, 0.0).astype(BF16)
                row += taps
    pulses = order_ref.shape[1]
    each = pulses // sections
    position = lax.broadcasted_iota(jnp.int32, (pulses, pulses), 0)
    hit = (position == order_ref[0:1, :]).astype(F32)
    slot = lax.broadcasted_iota(jnp.int32, (sections * group, pulses), 0)
    pulse = lax.broadcasted_iota(jnp.int32, (sections * group, pulses), 1)
    place = jnp.zeros((sections * group, pulses), F32)
    for s in range(sections):
        inside = (pulse >= s * each) & (pulse < (s + 1) * each)
        place = jnp.where(inside & (slot - s * group == pulse - s * each), 1.0, place)
    pick = lax.dot_general(
        place.astype(BF16), hit.astype(BF16), (((1,), (1,)), ((), ())), preferred_element_type=F32
    )
    for part in range(parts):
        chosen = jnp.dot(pick.astype(BF16), steer_ref[part, 0], preferred_element_type=F32)
        pack_ref[row : row + sections * group] = chosen.astype(BF16)
        row += sections * group
    starts[...] = jnp.zeros_like(starts)
    for level in range(levels):
        starts[sides * level : sides * level + sides] = start_ref[level, 0].astype(F32)
    pack_ref[row : row + starts.shape[0]] = starts[...].astype(BF16)


def pack_rows(levels, sides, parts, taps, sections, group):
    return levels * sides * parts * taps + parts * sections * group + ceil_to(levels * sides, 16)


def pack_parameters(coef, start, width, steer, order, sections, group):
    levels, _, sides, parts, taps, beams = coef.shape
    return pl.pallas_call(
        functools.partial(pack_kernel, sections=sections, group=group),
        out_shape=jax.ShapeDtypeStruct((pack_rows(levels, sides, parts, taps, sections, group), beams), BF16),
        scratch_shapes=[pltpu.VMEM((ceil_to(levels * sides, 16), beams), F32)],
        name="pack_parameters",
    )(coef, start, width, steer, order)


def pack_rows_of(real, imag, each):
    group = real.shape[0]
    row = lax.broadcasted_iota(jnp.int32, real.shape, 0)
    return jnp.where(row < each, real, pltpu.roll(imag, each, 0)), group - each


def split_two(value):
    high = value.astype(BF16)
    return high, (value - high.astype(F32)).astype(BF16)


def operator_kernel(index_ref, own_ref, partner_ref, out_ref, weights, *, dims, sections, group, each):
    levels, sides, parts, taps, beams = dims
    width = sections * group
    refs = (own_ref, partner_ref)
    weight_row = levels * sides * parts * taps
    start_row = weight_row + parts * width

    def band(ref, level, side):
        first = ((level * sides + side) * parts) * taps
        tables = [ref[first + p * taps : first + (p + 1) * taps].astype(F32) for p in range(parts)]
        start = ref[start_row : start_row + ceil_to(levels * sides, 16)].astype(F32)
        start = start[level * sides + side : level * sides + side + 1].astype(jnp.int32)
        found = [[], []]
        for c in range(0, beams, SUBL):
            column = lax.broadcasted_iota(jnp.int32, (SUBL, beams), 0) + c
            offset = column - start
            spot = offset & (SUBL - 1)
            for p in range(parts):
                value = jnp.zeros((SUBL, beams), F32)
                for t in range(0, taps, SUBL):
                    got = jnp.take_along_axis(
                        tables[p][t : t + SUBL], spot, axis=0, mode="promise_in_bounds"
                    )
                    value = jnp.where((offset >= t) & (offset < t + SUBL), got, value)
                found[p].append(value)
        return [jnp.concatenate(f, axis=0) for f in found]

    def complex_operand(real, imag):
        top = jnp.concatenate([real, imag], axis=1)
        low = jnp.concatenate([-imag, real], axis=1)
        return jnp.concatenate([top, low], axis=0).astype(BF16)

    section = index_ref[0]
    images = []
    for a in range(2):
        for p in range(parts):
            weights[...] = refs[a][weight_row + p * width : weight_row + (p + 1) * width].astype(F32)
            rows = []
            for j in range(sections):
                at = pl.multiple_of((section ^ j) * group, group)
                rows.append(weights[pl.ds(at, group)])
            images.append(jnp.concatenate(rows, axis=0))
    zero = jnp.zeros((width, 2 * beams), F32)
    own = jnp.concatenate([jnp.concatenate(images[0:2], axis=1), zero], axis=0)
    partner = jnp.concatenate([zero, jnp.concatenate(images[2:4], axis=1)], axis=0)
    for level in range(levels):
        own_high, own_low = split_two(own)
        partner_high, partner_low = split_two(partner)
        own_rows = jnp.concatenate([own_high, own_low], axis=0)
        partner_rows = jnp.concatenate([partner_high, partner_low], axis=0)

        def merged(ref, mine, other):
            product = jnp.dot(
                mine, complex_operand(*band(ref, level, 0)), preferred_element_type=F32
            ) + jnp.dot(other, complex_operand(*band(ref, level, 1)), preferred_element_type=F32)
            return product[: 2 * width] + product[2 * width :]

        following = merged(own_ref, own_rows, partner_rows)
        if level < levels - 1:
            partner = merged(partner_ref, partner_rows, own_rows)
        own = following
    full, left, right = [], [], []
    for j in range(2 * sections):
        real = own[j * group : (j + 1) * group, :beams]
        imag = own[j * group : (j + 1) * group, beams:]
        straight = jnp.concatenate([real, imag], axis=1)
        turned = jnp.concatenate([-imag, real], axis=1)
        lead, moved = pack_rows_of(straight, turned, each)
        row = lax.broadcasted_iota(jnp.int32, lead.shape, 0)
        full.append(lead)
        left.append(jnp.where(row < group // 2, pltpu.roll(turned, group - moved, 0), 0.0))
        right.append(jnp.where(row >= group // 2, pltpu.roll(turned, group // 2 - moved, 0), 0.0))
    pairs = sections // 2
    first_core = section % 2 == 0
    for half, rest in enumerate((left, right)):
        sources = [jnp.concatenate([full[j], rest[j]], axis=0) for j in range(2 * sections)]
        quarters = [jnp.concatenate(sources[q * pairs : (q + 1) * pairs], axis=0) for q in range(4)]
        quarters[1:3] = [
            jnp.where(first_core, quarters[1], quarters[2]),
            jnp.where(first_core, quarters[2], quarters[1]),
        ]
        high, low = split_two(jnp.concatenate(quarters, axis=0).T)
        out_ref[half] = jnp.concatenate([high, low], axis=1)


def fold_operator(section, own, partner, dims, sections, group, each):
    beams = dims[-1]
    width = sections * group
    return pl.pallas_call(
        functools.partial(operator_kernel, dims=dims, sections=sections, group=group, each=each),
        out_shape=jax.ShapeDtypeStruct((2, 2 * beams, 8 * width), BF16),
        in_specs=[
            pl.BlockSpec(memory_space=pltpu.SMEM),
            pl.BlockSpec(memory_space=pltpu.VMEM),
            pl.BlockSpec(memory_space=pltpu.VMEM),
        ],
        scratch_shapes=[pltpu.VMEM((width, beams), F32)],
        compiler_params=pltpu.CompilerParams(vmem_limit_bytes=16 * 1024 * 1024),
        name="fold_operator",
    )(section, own, partner)


def correlate(rows, even, odd, table, blocks, group):
    extra = table.shape[0] // (2 * LANE) - 1
    total = blocks + extra
    held = [
        jnp.concatenate(
            [rows[:group, b * LANE : (b + 1) * LANE], rows[group:, b * LANE : (b + 1) * LANE]], axis=1
        )
        for b in range(total)
    ]
    for b in range(0, total, 2):
        even[b * group : (b + 2) * group] = jnp.concatenate(held[b : b + 2], axis=0).astype(BF16)
    for b in range(1, total - 1, 2):
        odd[(b - 1) * group : (b + 1) * group] = jnp.concatenate(held[b : b + 2], axis=0).astype(BF16)
    window = blocks * group
    pieces = []
    for lag in range(extra + 1):
        source, at = (even, lag) if lag % 2 == 0 else (odd, lag - 1)
        pieces.append(source[at * group : at * group + window])
    return jnp.dot(jnp.concatenate(pieces, axis=1), table[...], preferred_element_type=F32)


def as_chunk(done, s, chunk, group, each):
    real, imag = [
        jnp.concatenate(
            [
                done[(s * chunk + b) * group : (s * chunk + b + 1) * group, c * LANE : (c + 1) * LANE]
                for b in range(chunk)
            ],
            axis=1,
        )
        for c in range(2)
    ]
    middle = chunk * LANE // 2
    lead, moved = pack_rows_of(real, imag, each)
    row = lax.broadcasted_iota(jnp.int32, (group, middle), 0)
    rest = jnp.where(
        row < group // 2,
        pltpu.roll(imag[:, :middle], group - moved, 0),
        pltpu.roll(imag[:, middle:], group // 2 - moved, 0),
    )
    return jnp.concatenate([lead[:, :middle], lead[:, middle:], rest], axis=0).astype(BF16)


def begin_kernel(echo_ref, chirp_ref, early_ref, late_ref, table, rows, even, odd, *, group):
    pulses, _, length = echo_ref.shape
    extra = chirp_ref.shape[1] // LANE
    reverse = LANE - 1 - lax.broadcasted_iota(jnp.int32, (2, LANE), 1)
    below = lax.broadcasted_iota(jnp.int32, (LANE, LANE), 1) <= lax.broadcasted_iota(
        jnp.int32, (LANE, LANE), 0
    )
    before = [jnp.zeros((LANE, LANE), F32)] * 2
    for lag in range(extra + 1):
        if lag < extra:
            piece = chirp_ref[:, lag * LANE : (lag + 1) * LANE].astype(F32)
            piece = jnp.take_along_axis(piece, reverse, axis=1, mode="promise_in_bounds")
            turned = [
                pltpu.roll(
                    jnp.broadcast_to(piece[c : c + 1], (LANE, LANE)), 1, 1, stride=1, stride_axis=0
                )
                for c in range(2)
            ]
        else:
            turned = [jnp.zeros((LANE, LANE), F32)] * 2
        real, imag = [jnp.where(below, turned[c], before[c]) for c in range(2)]
        before = turned
        at = lag * 2 * LANE
        table[at : at + LANE, :LANE] = real.astype(BF16)
        table[at : at + LANE, LANE:] = (-imag).astype(BF16)
        table[at + LANE : at + 2 * LANE, :LANE] = imag.astype(BF16)
        table[at + LANE : at + 2 * LANE, LANE:] = real.astype(BF16)
    rows[...] = jnp.zeros_like(rows)
    for p in range(pulses):
        near = echo_ref[p].astype(F32)
        for c in range(2):
            rows[c * group + p : c * group + p + 1, :] = near[c : c + 1]
    late_ref[...] = rows[:, length - late_ref.shape[1] :]
    done = correlate(rows, even, odd, table, length // LANE - extra, group)
    for s in range(early_ref.shape[0]):
        early_ref[s] = as_chunk(done, s, 2 * early_ref.shape[2] // LANE, group, pulses)


def finish_kernel(index_ref, early_ref, late_ref, halo_ref, table, keep_ref, give_ref, rows, even, odd, *, group):
    pulses = halo_ref.shape[0]
    span = late_ref.shape[1]
    taps = rows.shape[1] - span
    rows[:, :span] = late_ref[...]
    rows[:, span:] = jnp.zeros((2 * group, taps), F32)
    for p in range(pulses):
        far = halo_ref[p, :, :taps].astype(F32)
        for c in range(2):
            rows[c * group + p : c * group + p + 1, span:] = far[c : c + 1]
    done = correlate(rows, even, odd, table, span // LANE, group)
    ready = early_ref.shape[0]
    chunk = 2 * early_ref.shape[2]
    section = index_ref[0]
    for s in range(ready + span // chunk):
        stacked = early_ref[s] if s < ready else as_chunk(done, s - ready, chunk // LANE, group, pulses)
        slot = section ^ s
        far_chunk, other_core = slot // 2, slot % 2
        place = far_chunk ^ 1 ^ (section % 2) ^ other_core

        @pl.when(other_core == 0)
        def _():
            keep_ref[place] = stacked

        @pl.when(other_core == 1)
        def _():
            give_ref[place] = stacked


def row_scratch(blocks, group):
    return [
        pltpu.VMEM((2 * group, blocks * LANE), F32),
        pltpu.VMEM((blocks * group, 2 * LANE), BF16),
        pltpu.VMEM((blocks * group, 2 * LANE), BF16),
    ]


def begin_compression(echo, chirp, sections, group):
    _, _, length = echo.shape
    taps = chirp.shape[1]
    chunk = length // sections
    early = (length - taps) // chunk
    return pl.pallas_call(
        functools.partial(begin_kernel, group=group),
        out_shape=(
            jax.ShapeDtypeStruct((early, 3 * group, chunk // 2), BF16),
            jax.ShapeDtypeStruct((2 * group, length - early * chunk), F32),
            jax.ShapeDtypeStruct(((taps // LANE + 1) * 2 * LANE, 2 * LANE), BF16),
        ),
        scratch_shapes=row_scratch(length // LANE, group),
        compiler_params=pltpu.CompilerParams(vmem_limit_bytes=24 * 1024 * 1024),
        name="begin_compression",
    )(echo, chirp)


def finish_compression(section, early, late, halo, table, group):
    blocks = late.shape[1] // LANE + table.shape[0] // (2 * LANE) - 1
    return pl.pallas_call(
        functools.partial(finish_kernel, group=group),
        out_shape=[jax.ShapeDtypeStruct((2, *early.shape[1:]), BF16)] * 2,
        in_specs=[pl.BlockSpec(memory_space=pltpu.SMEM)] + [pl.BlockSpec(memory_space=pltpu.VMEM)] * 4,
        scratch_shapes=row_scratch(blocks, group),
        compiler_params=pltpu.CompilerParams(vmem_limit_bytes=24 * 1024 * 1024),
        name="finish_compression",
    )(section, early, late, halo, table)


def image_kernel(index_ref, operator_ref, both_ref, *refs, group):
    chunks, (out_ref, parts, sems) = refs[:-3], refs[-3:]
    count, _, tile = parts.shape
    width = both_ref.shape[2]
    near = 1 - index_ref[0] % 2
    held = [both_ref[near]] + [chunk[...] for chunk in chunks]
    held = [value.astype(F32) for value in held]
    copies = []
    for i in range(count):
        half, at = divmod(i * tile, width)
        rows = []
        for value in held:
            for first in range(0, value.shape[0], 3 * group):
                rows.append(value[first + half * group : first + (half + 1) * group, at : at + tile])
                rows.append(value[first + 2 * group : first + 3 * group, at : at + tile])
        pulses = jnp.concatenate(rows, axis=0).astype(BF16)
        result = jnp.dot(
            operator_ref[half], jnp.concatenate([pulses, pulses], axis=0), preferred_element_type=F32
        )
        parts[i] = result.astype(BF16)
        copy = pltpu.make_async_copy(parts.at[i], out_ref.at[:, i * tile : (i + 1) * tile], sems.at[i])
        copy.start()
        copies.append(copy)
    for copy in copies:
        copy.wait()


def form_image(section, operator, both, chunks, group):
    height, half = operator.shape[1], both.shape[2]
    tile = 256 if half % 256 == 0 else half
    count = 2 * half // tile
    return pl.pallas_call(
        functools.partial(image_kernel, group=group),
        out_shape=jax.ShapeDtypeStruct((height, 2 * half), BF16),
        in_specs=[pl.BlockSpec(memory_space=pltpu.SMEM)]
        + [pl.BlockSpec(memory_space=pltpu.VMEM)] * (2 + len(chunks)),
        out_specs=pl.BlockSpec(memory_space=pl.ANY),
        scratch_shapes=[
            pltpu.VMEM((count, height, tile), BF16),
            pltpu.SemaphoreType.DMA((count,)),
        ],
        compiler_params=pltpu.CompilerParams(vmem_limit_bytes=16 * 1024 * 1024),
        name="form_image",
    )(section, operator, both, *chunks)


def swap(value, axis, by):
    count = lax.axis_size(axis)
    return lax.ppermute(value, axis, [(i, i ^ by) for i in range(count)])


def swap_by(value, move):
    sections, subs = lax.axis_size("section"), lax.axis_size("sub")
    pairs = []
    for s in range(sections):
        for a in range(subs):
            to_s, to_a = move(s, a)
            pairs.append((s * subs + a, to_s * subs + to_a))
    return lax.ppermute(value, ("section", "sub"), pairs)


def from_behind(value, axis, by):
    size = lax.axis_size(axis)
    pairs = [(i, i + by) for i in range(size) if 0 <= i + by < size]
    return lax.ppermute(value, axis, pairs)


def on_device(echoes, chirp, steer, pulse_order, band_coef, band_start, band_width):
    sections, subs = lax.axis_size("section"), lax.axis_size("sub")
    pulses_each = echoes.shape[2]
    group = ceil_to(pulses_each, SUBL)
    section = lax.axis_index("section").astype(jnp.int32).reshape(1)
    coef = jnp.swapaxes(band_coef, 4, 5)
    weights = jnp.swapaxes(steer, 2, 3)
    levels, _, sides, parts, taps, beams = coef.shape
    dims = (levels, sides, parts, taps, beams)

    echo = jnp.transpose(echoes[:, 0], (1, 0, 2))
    halo = from_behind(echo, "rng", -1)
    packed = pack_parameters(coef, band_start, band_width, weights, pulse_order, sections, group)
    if subs == 2:
        packed_partner = swap(packed, "sub", 1)
    early, late, table = begin_compression(echo, chirp, sections, group)
    keep, give = finish_compression(section, early, late, halo, table, group)
    both = jnp.concatenate([keep, swap(give, "section", 1)], axis=1)
    far = lax.dynamic_index_in_dim(both, section[0] % 2, 0, keepdims=False)
    if subs != 2:
        near = lax.dynamic_index_in_dim(both, 1 - section[0] % 2, 0, keepdims=False)
        chunks = [near, swap(far, "section", 2)]
        return merge_images(section, chunks, packed, dims, sections, group, pulses_each)
    chunks = [
        swap_by(both[0], lambda s, a: (s, a ^ 1) if s % 2 else (s ^ 2, a)),
        swap_by(both[1], lambda s, a: (s ^ 2, a) if s % 2 else (s, a ^ 1)),
        swap_by(far, lambda s, a: (s ^ 2, a ^ 1)),
    ]
    operator = fold_operator(section, packed, packed_partner, dims, sections, group, pulses_each)
    image = form_image(section, operator, both, chunks, group)
    return image.reshape(2, beams, 1, image.shape[1])


def unpack(chunk, group, each):
    lead = jnp.concatenate([chunk[:group], chunk[group : 2 * group]], axis=1)
    moved, rest = group - each, chunk[2 * group :]
    tail = jnp.concatenate([rest[: each - moved], rest[group // 2 : group // 2 + each - moved]], axis=1)
    return jnp.concatenate([lead, tail], axis=0)


def merge_images(section, chunks, packed, dims, sections, group, each):
    levels, sides, parts, taps, beams = dims
    width = sections * group
    first = levels * sides * parts * taps
    table = packed[first : first + parts * width].reshape(parts, sections, group, beams)
    table = jnp.take(table, section[0] ^ jnp.arange(sections), axis=1)[:, :, :each]
    chunks = [
        unpack(chunk[first : first + 3 * group], group, each)
        for chunk in chunks
        for first in range(0, chunk.shape[0], 3 * group)
    ]
    real, imag = table[0], table[1]
    rows = jnp.concatenate(
        [jnp.concatenate([real, -imag], axis=1), jnp.concatenate([imag, real], axis=1)], axis=2
    )
    image = lax.dot_general(
        rows.reshape(-1, 2 * beams), jnp.concatenate(chunks, axis=0), (((0,), (0,)), ((), ())), preferred_element_type=F32
    ).astype(BF16)
    starts = packed[first + parts * width :].astype(jnp.int32)
    column = jnp.arange(beams, dtype=jnp.int32)
    bits = lax.axis_size("sub").bit_length() - 1
    for level in range(levels):
        partner = swap(image, "sub", 1 << (level % bits))
        operands = []
        for side in range(sides):
            at = (level * sides + side) * parts * taps
            coef = packed[at : at + parts * taps].reshape(parts, taps, beams)
            offset = column[:, None] - starts[level * sides + side][None, :]
            hits = (offset[None] == jnp.arange(taps, dtype=jnp.int32)[:, None, None]).astype(BF16)
            operands.append(jnp.einsum("ptq,tcq->pqc", coef, hits, preferred_element_type=F32).astype(BF16))
        top = jnp.concatenate([operands[0][0], -operands[0][1], operands[1][0], -operands[1][1]], axis=1)
        low = jnp.concatenate([operands[0][1], operands[0][0], operands[1][1], operands[1][0]], axis=1)
        image = jnp.dot(
            jnp.concatenate([top, low], axis=0),
            jnp.concatenate([image, partner], axis=0),
            preferred_element_type=F32,
        ).astype(BF16)
    return image.reshape(2, beams, 1, image.shape[1])


def solution(mesh):
    return jax.shard_map(
        on_device,
        mesh=mesh,
        in_specs=(
            P(None, "sub", "section", "rng"),
            P(),
            P(None, "sub", None, None),
            P("sub", None),
            P(None, "sub", None, None, None, None),
            P(None, "sub", None, None),
            P(None, "sub", None, None),
        ),
        out_specs=P(None, "sub", "rng", "section"),
        check_vma=False,
    )
```

```python
import functools

import jax
import jax.numpy as jnp
from jax import lax
from jax.experimental import pallas as pl
from jax.experimental.pallas import tpu as pltpu
from jax.sharding import PartitionSpec as P

LANE = 128
SUBL = 8
F32 = jnp.float32
BF16 = jnp.bfloat16


def cost(macs, moved):
    return pl.CostEstimate(flops=2 * macs, bytes_accessed=moved, transcendentals=0)


def ceil_to(value, unit):
    return -(-value // unit) * unit


def pack_kernel(coef_ref, start_ref, width_ref, steer_ref, order_ref, pack_ref, starts, *, sections, group):
    levels, _, sides, parts, taps, beams = coef_ref.shape
    tap = lax.broadcasted_iota(jnp.int32, (taps, beams), 0)
    row = 0
    for level in range(levels):
        for side in range(sides):
            used = tap < width_ref[level, 0, side : side + 1, :]
            for part in range(parts):
                entries = coef_ref[level, 0, side, part].astype(F32)
                pack_ref[row : row + taps] = jnp.where(used, entries, 0.0).astype(BF16)
                row += taps
    pulses = order_ref.shape[1]
    each = pulses // sections
    position = lax.broadcasted_iota(jnp.int32, (pulses, pulses), 0)
    hit = (position == order_ref[0:1, :]).astype(F32)
    slot = lax.broadcasted_iota(jnp.int32, (sections * group, pulses), 0)
    pulse = lax.broadcasted_iota(jnp.int32, (sections * group, pulses), 1)
    place = jnp.zeros((sections * group, pulses), F32)
    for s in range(sections):
        inside = (pulse >= s * each) & (pulse < (s + 1) * each)
        place = jnp.where(inside & (slot - s * group == pulse - s * each), 1.0, place)
    pick = lax.dot_general(
        place.astype(BF16), hit.astype(BF16), (((1,), (1,)), ((), ())), preferred_element_type=F32
    )
    for part in range(parts):
        chosen = jnp.dot(pick.astype(BF16), steer_ref[part, 0], preferred_element_type=F32)
        pack_ref[row : row + sections * group] = chosen.astype(BF16)
        row += sections * group
    starts[...] = jnp.zeros_like(starts)
    for level in range(levels):
        starts[sides * level : sides * level + sides] = start_ref[level, 0].astype(F32)
    pack_ref[row : row + starts.shape[0]] = starts[...].astype(BF16)


def pack_rows(levels, sides, parts, taps, sections, group):
    return levels * sides * parts * taps + parts * sections * group + ceil_to(levels * sides, 16)


def pack_parameters(coef, start, width, steer, order, sections, group):
    levels, _, sides, parts, taps, beams = coef.shape
    return pl.pallas_call(
        functools.partial(pack_kernel, sections=sections, group=group),
        out_shape=jax.ShapeDtypeStruct((pack_rows(levels, sides, parts, taps, sections, group), beams), BF16),
        scratch_shapes=[pltpu.VMEM((ceil_to(levels * sides, 16), beams), F32)],
        cost_estimate=cost(0, 6 << 20),
        name="pack_parameters",
    )(coef, start, width, steer, order)


def pack_rows_of(real, imag, each):
    group = real.shape[0]
    row = lax.broadcasted_iota(jnp.int32, real.shape, 0)
    return jnp.where(row < each, real, pltpu.roll(imag, each, 0)), group - each


def split_two(value):
    high = value.astype(BF16)
    return high, (value - high.astype(F32)).astype(BF16)


def operator_kernel(index_ref, own_ref, partner_ref, out_ref, weights, *, dims, sections, group, each):
    levels, sides, parts, taps, beams = dims
    width = sections * group
    refs = (own_ref, partner_ref)
    weight_row = levels * sides * parts * taps
    start_row = weight_row + parts * width

    def band(ref, level, side):
        first = ((level * sides + side) * parts) * taps
        tables = [ref[first + p * taps : first + (p + 1) * taps].astype(F32) for p in range(parts)]
        start = ref[start_row : start_row + ceil_to(levels * sides, 16)].astype(F32)
        start = start[level * sides + side : level * sides + side + 1].astype(jnp.int32)
        found = [[], []]
        for c in range(0, beams, SUBL):
            column = lax.broadcasted_iota(jnp.int32, (SUBL, beams), 0) + c
            offset = column - start
            spot = offset & (SUBL - 1)
            for p in range(parts):
                value = jnp.zeros((SUBL, beams), F32)
                for t in range(0, taps, SUBL):
                    got = jnp.take_along_axis(
                        tables[p][t : t + SUBL], spot, axis=0, mode="promise_in_bounds"
                    )
                    value = jnp.where((offset >= t) & (offset < t + SUBL), got, value)
                found[p].append(value)
        return [jnp.concatenate(f, axis=0) for f in found]

    def complex_operand(real, imag):
        top = jnp.concatenate([real, imag], axis=1)
        low = jnp.concatenate([-imag, real], axis=1)
        return jnp.concatenate([top, low], axis=0).astype(BF16)

    section = index_ref[0]
    images = []
    for a in range(2):
        for p in range(parts):
            weights[...] = refs[a][weight_row + p * width : weight_row + (p + 1) * width].astype(F32)
            rows = []
            for j in range(sections):
                at = pl.multiple_of((section ^ j) * group, group)
                rows.append(weights[pl.ds(at, group)])
            images.append(jnp.concatenate(rows, axis=0))
    zero = jnp.zeros((width, 2 * beams), F32)
    own = jnp.concatenate([jnp.concatenate(images[0:2], axis=1), zero], axis=0)
    partner = jnp.concatenate([zero, jnp.concatenate(images[2:4], axis=1)], axis=0)
    for level in range(levels):
        own_high, own_low = split_two(own)
        partner_high, partner_low = split_two(partner)
        own_rows = jnp.concatenate([own_high, own_low], axis=0)
        partner_rows = jnp.concatenate([partner_high, partner_low], axis=0)

        def merged(ref, mine, other):
            product = jnp.dot(
                mine, complex_operand(*band(ref, level, 0)), preferred_element_type=F32
            ) + jnp.dot(other, complex_operand(*band(ref, level, 1)), preferred_element_type=F32)
            return product[: 2 * width] + product[2 * width :]

        following = merged(own_ref, own_rows, partner_rows)
        if level < levels - 1:
            partner = merged(partner_ref, partner_rows, own_rows)
        own = following
    full, left, right = [], [], []
    for j in range(2 * sections):
        real = own[j * group : (j + 1) * group, :beams]
        imag = own[j * group : (j + 1) * group, beams:]
        straight = jnp.concatenate([real, imag], axis=1)
        turned = jnp.concatenate([-imag, real], axis=1)
        lead, moved = pack_rows_of(straight, turned, each)
        row = lax.broadcasted_iota(jnp.int32, lead.shape, 0)
        full.append(lead)
        left.append(jnp.where(row < group // 2, pltpu.roll(turned, group - moved, 0), 0.0))
        right.append(jnp.where(row >= group // 2, pltpu.roll(turned, group // 2 - moved, 0), 0.0))
    pairs = sections // 2
    first_core = section % 2 == 0
    for half, rest in enumerate((left, right)):
        sources = [jnp.concatenate([full[j], rest[j]], axis=0) for j in range(2 * sections)]
        quarters = [jnp.concatenate(sources[q * pairs : (q + 1) * pairs], axis=0) for q in range(4)]
        quarters[1:3] = [
            jnp.where(first_core, quarters[1], quarters[2]),
            jnp.where(first_core, quarters[2], quarters[1]),
        ]
        high, low = split_two(jnp.concatenate(quarters, axis=0).T)
        out_ref[half] = jnp.concatenate([high, low], axis=1)


def fold_operator(section, own, partner, dims, sections, group, each):
    levels, beams = dims[0], dims[-1]
    width = sections * group
    return pl.pallas_call(
        functools.partial(operator_kernel, dims=dims, sections=sections, group=group, each=each),
        out_shape=jax.ShapeDtypeStruct((2, 2 * beams, 8 * width), BF16),
        in_specs=[
            pl.BlockSpec(memory_space=pltpu.SMEM),
            pl.BlockSpec(memory_space=pltpu.VMEM),
            pl.BlockSpec(memory_space=pltpu.VMEM),
        ],
        scratch_shapes=[pltpu.VMEM((width, beams), F32)],
        compiler_params=pltpu.CompilerParams(vmem_limit_bytes=16 * 1024 * 1024),
        cost_estimate=cost(levels * 2 * 16 * width * beams * beams, 4 << 20),
        name="fold_operator",
    )(section, own, partner)


def correlate(rows, even, odd, table, blocks, group):
    extra = table.shape[0] // (2 * LANE) - 1
    total = blocks + extra
    held = [
        jnp.concatenate(
            [rows[:group, b * LANE : (b + 1) * LANE], rows[group:, b * LANE : (b + 1) * LANE]], axis=1
        )
        for b in range(total)
    ]
    for b in range(0, total, 2):
        even[b * group : (b + 2) * group] = jnp.concatenate(held[b : b + 2], axis=0).astype(BF16)
    for b in range(1, total - 1, 2):
        odd[(b - 1) * group : (b + 1) * group] = jnp.concatenate(held[b : b + 2], axis=0).astype(BF16)
    window = blocks * group
    pieces = []
    for lag in range(extra + 1):
        source, at = (even, lag) if lag % 2 == 0 else (odd, lag - 1)
        pieces.append(source[at * group : at * group + window])
    return jnp.dot(jnp.concatenate(pieces, axis=1), table[...], preferred_element_type=F32)


def as_chunk(done, s, chunk, group, each):
    real, imag = [
        jnp.concatenate(
            [
                done[(s * chunk + b) * group : (s * chunk + b + 1) * group, c * LANE : (c + 1) * LANE]
                for b in range(chunk)
            ],
            axis=1,
        )
        for c in range(2)
    ]
    middle = chunk * LANE // 2
    lead, moved = pack_rows_of(real, imag, each)
    row = lax.broadcasted_iota(jnp.int32, (group, middle), 0)
    rest = jnp.where(
        row < group // 2,
        pltpu.roll(imag[:, :middle], group - moved, 0),
        pltpu.roll(imag[:, middle:], group // 2 - moved, 0),
    )
    return jnp.concatenate([lead[:, :middle], lead[:, middle:], rest], axis=0).astype(BF16)


def begin_kernel(echo_ref, chirp_ref, early_ref, late_ref, table, rows, even, odd, *, group):
    pulses, _, length = echo_ref.shape
    extra = chirp_ref.shape[1] // LANE
    reverse = LANE - 1 - lax.broadcasted_iota(jnp.int32, (2, LANE), 1)
    below = lax.broadcasted_iota(jnp.int32, (LANE, LANE), 1) <= lax.broadcasted_iota(
        jnp.int32, (LANE, LANE), 0
    )
    before = [jnp.zeros((LANE, LANE), F32)] * 2
    for lag in range(extra + 1):
        if lag < extra:
            piece = chirp_ref[:, lag * LANE : (lag + 1) * LANE].astype(F32)
            piece = jnp.take_along_axis(piece, reverse, axis=1, mode="promise_in_bounds")
            turned = [
                pltpu.roll(
                    jnp.broadcast_to(piece[c : c + 1], (LANE, LANE)), 1, 1, stride=1, stride_axis=0
                )
                for c in range(2)
            ]
        else:
            turned = [jnp.zeros((LANE, LANE), F32)] * 2
        real, imag = [jnp.where(below, turned[c], before[c]) for c in range(2)]
        before = turned
        at = lag * 2 * LANE
        table[at : at + LANE, :LANE] = real.astype(BF16)
        table[at : at + LANE, LANE:] = (-imag).astype(BF16)
        table[at + LANE : at + 2 * LANE, :LANE] = imag.astype(BF16)
        table[at + LANE : at + 2 * LANE, LANE:] = real.astype(BF16)
    rows[...] = jnp.zeros_like(rows)
    for p in range(pulses):
        near = echo_ref[p].astype(F32)
        for c in range(2):
            rows[c * group + p : c * group + p + 1, :] = near[c : c + 1]
    late_ref[...] = rows[:, length - late_ref.shape[1] :]
    done = correlate(rows, even, odd, table, length // LANE - extra, group)
    for s in range(early_ref.shape[0]):
        early_ref[s] = as_chunk(done, s, 2 * early_ref.shape[2] // LANE, group, pulses)


def finish_kernel(index_ref, early_ref, late_ref, halo_ref, table, keep_ref, give_ref, rows, even, odd, *, group):
    pulses = halo_ref.shape[0]
    span = late_ref.shape[1]
    taps = rows.shape[1] - span
    rows[:, :span] = late_ref[...]
    rows[:, span:] = jnp.zeros((2 * group, taps), F32)
    for p in range(pulses):
        far = halo_ref[p, :, :taps].astype(F32)
        for c in range(2):
            rows[c * group + p : c * group + p + 1, span:] = far[c : c + 1]
    done = correlate(rows, even, odd, table, span // LANE, group)
    ready = early_ref.shape[0]
    chunk = 2 * early_ref.shape[2]
    section = index_ref[0]
    for s in range(ready + span // chunk):
        stacked = early_ref[s] if s < ready else as_chunk(done, s - ready, chunk // LANE, group, pulses)
        slot = section ^ s
        far_chunk, other_core = slot // 2, slot % 2
        place = far_chunk ^ 1 ^ (section % 2) ^ other_core

        @pl.when(other_core == 0)
        def _():
            keep_ref[place] = stacked

        @pl.when(other_core == 1)
        def _():
            give_ref[place] = stacked


def pulses_macs(echo, taps):
    pulses, _, length = echo.shape
    return 4 * pulses * length * taps


def row_scratch(blocks, group):
    return [
        pltpu.VMEM((2 * group, blocks * LANE), F32),
        pltpu.VMEM((blocks * group, 2 * LANE), BF16),
        pltpu.VMEM((blocks * group, 2 * LANE), BF16),
    ]


def begin_compression(echo, chirp, sections, group):
    _, _, length = echo.shape
    taps = chirp.shape[1]
    chunk = length // sections
    early = (length - taps) // chunk
    return pl.pallas_call(
        functools.partial(begin_kernel, group=group),
        out_shape=(
            jax.ShapeDtypeStruct((early, 3 * group, chunk // 2), BF16),
            jax.ShapeDtypeStruct((2 * group, length - early * chunk), F32),
            jax.ShapeDtypeStruct(((taps // LANE + 1) * 2 * LANE, 2 * LANE), BF16),
        ),
        scratch_shapes=row_scratch(length // LANE, group),
        compiler_params=pltpu.CompilerParams(vmem_limit_bytes=24 * 1024 * 1024),
        cost_estimate=cost(pulses_macs(echo, taps) // 2, 4 << 20),
        name="begin_compression",
    )(echo, chirp)


def finish_compression(section, early, late, halo, table, group):
    blocks = late.shape[1] // LANE + table.shape[0] // (2 * LANE) - 1
    return pl.pallas_call(
        functools.partial(finish_kernel, group=group),
        out_shape=[jax.ShapeDtypeStruct((2, *early.shape[1:]), BF16)] * 2,
        in_specs=[pl.BlockSpec(memory_space=pltpu.SMEM)] + [pl.BlockSpec(memory_space=pltpu.VMEM)] * 4,
        scratch_shapes=row_scratch(blocks, group),
        compiler_params=pltpu.CompilerParams(vmem_limit_bytes=24 * 1024 * 1024),
        cost_estimate=cost(pulses_macs(halo, halo.shape[2] // 2) // 2, 2 << 20),
        name="finish_compression",
    )(section, early, late, halo, table)


def image_kernel(index_ref, operator_ref, both_ref, *refs, group):
    chunks, (out_ref, parts, sems) = refs[:-3], refs[-3:]
    count, _, tile = parts.shape
    width = both_ref.shape[2]
    near = 1 - index_ref[0] % 2
    held = [both_ref[near]] + [chunk[...] for chunk in chunks]
    held = [value.astype(F32) for value in held]
    copies = []
    for i in range(count):
        half, at = divmod(i * tile, width)
        rows = []
        for value in held:
            for first in range(0, value.shape[0], 3 * group):
                rows.append(value[first + half * group : first + (half + 1) * group, at : at + tile])
                rows.append(value[first + 2 * group : first + 3 * group, at : at + tile])
        pulses = jnp.concatenate(rows, axis=0).astype(BF16)
        result = jnp.dot(
            operator_ref[half], jnp.concatenate([pulses, pulses], axis=0), preferred_element_type=F32
        )
        parts[i] = result.astype(BF16)
        copy = pltpu.make_async_copy(parts.at[i], out_ref.at[:, i * tile : (i + 1) * tile], sems.at[i])
        copy.start()
        copies.append(copy)
    for copy in copies:
        copy.wait()


def form_image(section, operator, both, chunks, group):
    height, half = operator.shape[1], both.shape[2]
    tile = 256 if half % 256 == 0 else half
    count = 2 * half // tile
    return pl.pallas_call(
        functools.partial(image_kernel, group=group),
        out_shape=jax.ShapeDtypeStruct((height, 2 * half), BF16),
        in_specs=[pl.BlockSpec(memory_space=pltpu.SMEM)]
        + [pl.BlockSpec(memory_space=pltpu.VMEM)] * (2 + len(chunks)),
        out_specs=pl.BlockSpec(memory_space=pl.ANY),
        scratch_shapes=[
            pltpu.VMEM((count, height, tile), BF16),
            pltpu.SemaphoreType.DMA((count,)),
        ],
        compiler_params=pltpu.CompilerParams(vmem_limit_bytes=16 * 1024 * 1024),
        cost_estimate=cost(height * height * 2 * half, 4 << 20),
        name="form_image",
    )(section, operator, both, *chunks)


def swap(value, axis, by):
    count = lax.axis_size(axis)
    return lax.ppermute(value, axis, [(i, i ^ by) for i in range(count)])


def swap_by(value, move):
    sections, subs = lax.axis_size("section"), lax.axis_size("sub")
    pairs = []
    for s in range(sections):
        for a in range(subs):
            to_s, to_a = move(s, a)
            pairs.append((s * subs + a, to_s * subs + to_a))
    return lax.ppermute(value, ("section", "sub"), pairs)


def from_behind(value, axis, by):
    size = lax.axis_size(axis)
    pairs = [(i, i + by) for i in range(size) if 0 <= i + by < size]
    return lax.ppermute(value, axis, pairs)


def on_device(echoes, chirp, steer, pulse_order, band_coef, band_start, band_width):
    sections, subs = lax.axis_size("section"), lax.axis_size("sub")
    pulses_each = echoes.shape[2]
    group = ceil_to(pulses_each, SUBL)
    section = lax.axis_index("section").astype(jnp.int32).reshape(1)
    coef = jnp.swapaxes(band_coef, 4, 5)
    weights = jnp.swapaxes(steer, 2, 3)
    levels, _, sides, parts, taps, beams = coef.shape
    dims = (levels, sides, parts, taps, beams)

    echo = jnp.transpose(echoes[:, 0], (1, 0, 2))
    halo = from_behind(echo, "rng", -1)
    packed = pack_parameters(coef, band_start, band_width, weights, pulse_order, sections, group)
    if subs == 2:
        packed_partner = swap(packed, "sub", 1)
    early, late, table = begin_compression(echo, chirp, sections, group)
    keep, give = finish_compression(section, early, late, halo, table, group)
    both = jnp.concatenate([keep, swap(give, "section", 1)], axis=1)
    far = lax.dynamic_index_in_dim(both, section[0] % 2, 0, keepdims=False)
    if subs != 2:
        near = lax.dynamic_index_in_dim(both, 1 - section[0] % 2, 0, keepdims=False)
        chunks = [near, swap(far, "section", 2)]
        return merge_images(section, chunks, packed, dims, sections, group, pulses_each)
    chunks = [
        swap_by(both[0], lambda s, a: (s, a ^ 1) if s % 2 else (s ^ 2, a)),
        swap_by(both[1], lambda s, a: (s ^ 2, a) if s % 2 else (s, a ^ 1)),
        swap_by(far, lambda s, a: (s ^ 2, a ^ 1)),
    ]
    operator = fold_operator(section, packed, packed_partner, dims, sections, group, pulses_each)
    image = form_image(section, operator, both, chunks, group)
    return image.reshape(2, beams, 1, image.shape[1])


def unpack(chunk, group, each):
    lead = jnp.concatenate([chunk[:group], chunk[group : 2 * group]], axis=1)
    moved, rest = group - each, chunk[2 * group :]
    tail = jnp.concatenate([rest[: each - moved], rest[group // 2 : group // 2 + each - moved]], axis=1)
    return jnp.concatenate([lead, tail], axis=0)


def merge_images(section, chunks, packed, dims, sections, group, each):
    levels, sides, parts, taps, beams = dims
    width = sections * group
    first = levels * sides * parts * taps
    table = packed[first : first + parts * width].reshape(parts, sections, group, beams)
    table = jnp.take(table, section[0] ^ jnp.arange(sections), axis=1)[:, :, :each]
    chunks = [
        unpack(chunk[first : first + 3 * group], group, each)
        for chunk in chunks
        for first in range(0, chunk.shape[0], 3 * group)
    ]
    real, imag = table[0], table[1]
    rows = jnp.concatenate(
        [jnp.concatenate([real, -imag], axis=1), jnp.concatenate([imag, real], axis=1)], axis=2
    )
    image = lax.dot_general(
        rows.reshape(-1, 2 * beams), jnp.concatenate(chunks, axis=0), (((0,), (0,)), ((), ())), preferred_element_type=F32
    ).astype(BF16)
    starts = packed[first + parts * width :].astype(jnp.int32)
    column = jnp.arange(beams, dtype=jnp.int32)
    bits = lax.axis_size("sub").bit_length() - 1
    for level in range(levels):
        partner = swap(image, "sub", 1 << (level % bits))
        operands = []
        for side in range(sides):
            at = (level * sides + side) * parts * taps
            coef = packed[at : at + parts * taps].reshape(parts, taps, beams)
            offset = column[:, None] - starts[level * sides + side][None, :]
            hits = (offset[None] == jnp.arange(taps, dtype=jnp.int32)[:, None, None]).astype(BF16)
            operands.append(jnp.einsum("ptq,tcq->pqc", coef, hits, preferred_element_type=F32).astype(BF16))
        top = jnp.concatenate([operands[0][0], -operands[0][1], operands[1][0], -operands[1][1]], axis=1)
        low = jnp.concatenate([operands[0][1], operands[0][0], operands[1][1], operands[1][0]], axis=1)
        image = jnp.dot(
            jnp.concatenate([top, low], axis=0),
            jnp.concatenate([image, partner], axis=0),
            preferred_element_type=F32,
        ).astype(BF16)
    return image.reshape(2, beams, 1, image.shape[1])


def solution(mesh):
    return jax.shard_map(
        on_device,
        mesh=mesh,
        in_specs=(
            P(None, "sub", "section", "rng"),
            P(),
            P(None, "sub", None, None),
            P("sub", None),
            P(None, "sub", None, None, None, None),
            P(None, "sub", None, None),
            P(None, "sub", None, None),
        ),
        out_specs=P(None, "sub", "rng", "section"),
        check_vma=False,
    )
```

```python
import functools

import jax
import jax.numpy as jnp
from jax import lax
from jax.experimental import pallas as pl
from jax.experimental.pallas import tpu as pltpu
from jax.sharding import PartitionSpec as P

LANE = 128
SUBL = 8
F32 = jnp.float32
BF16 = jnp.bfloat16


def ceil_to(value, unit):
    return -(-value // unit) * unit


def prepare_kernel(*refs, sections, group):
    sources, (echo_out, chirp_out, pack_ref), scratch = refs[:7], refs[7:10], refs[10:]
    coef_ref, start_ref, width_ref, steer_ref, order_ref, starts, sems = scratch
    targets = (coef_ref, start_ref, width_ref, steer_ref, order_ref, chirp_out, echo_out)
    loads = [
        pltpu.make_async_copy(source, target, sems.at[i])
        for i, (source, target) in enumerate(zip(sources, targets))
    ]
    for load in loads:
        load.start()
    for load in loads:
        load.wait()
    levels, _, sides, parts, taps, beams = coef_ref.shape
    tap = lax.broadcasted_iota(jnp.int32, (taps, beams), 0)
    row = 0
    for level in range(levels):
        for side in range(sides):
            used = tap < width_ref[level, 0, side : side + 1, :]
            for part in range(parts):
                entries = coef_ref[level, 0, side, part].astype(F32)
                pack_ref[row : row + taps] = jnp.where(used, entries, 0.0).astype(BF16)
                row += taps
    pulses = order_ref.shape[1]
    each = pulses // sections
    position = lax.broadcasted_iota(jnp.int32, (pulses, pulses), 0)
    hit = (position == order_ref[0:1, :]).astype(F32)
    slot = lax.broadcasted_iota(jnp.int32, (sections * group, pulses), 0)
    pulse = lax.broadcasted_iota(jnp.int32, (sections * group, pulses), 1)
    place = jnp.zeros((sections * group, pulses), F32)
    for s in range(sections):
        inside = (pulse >= s * each) & (pulse < (s + 1) * each)
        place = jnp.where(inside & (slot - s * group == pulse - s * each), 1.0, place)
    pick = lax.dot_general(
        place.astype(BF16), hit.astype(BF16), (((1,), (1,)), ((), ())), preferred_element_type=F32
    )
    for part in range(parts):
        chosen = jnp.dot(pick.astype(BF16), steer_ref[part, 0], preferred_element_type=F32)
        pack_ref[row : row + sections * group] = chosen.astype(BF16)
        row += sections * group
    starts[...] = jnp.zeros_like(starts)
    for level in range(levels):
        starts[sides * level : sides * level + sides] = start_ref[level, 0].astype(F32)
    pack_ref[row : row + starts.shape[0]] = starts[...].astype(BF16)


def pack_rows(levels, sides, parts, taps, sections, group):
    return levels * sides * parts * taps + parts * sections * group + ceil_to(levels * sides, 16)


def prepare(echo, chirp, coef, start, width, steer, order, sections, group):
    levels, _, sides, parts, taps, beams = coef.shape
    sources = (coef, start, width, steer, order, chirp, echo)
    return pl.pallas_call(
        functools.partial(prepare_kernel, sections=sections, group=group),
        out_shape=(
            jax.ShapeDtypeStruct(echo.shape, BF16),
            jax.ShapeDtypeStruct(chirp.shape, BF16),
            jax.ShapeDtypeStruct((pack_rows(levels, sides, parts, taps, sections, group), beams), BF16),
        ),
        in_specs=[pl.BlockSpec(memory_space=pl.ANY)] * len(sources),
        scratch_shapes=[pltpu.VMEM(x.shape, x.dtype) for x in sources[:5]]
        + [pltpu.VMEM((ceil_to(levels * sides, 16), beams), F32), pltpu.SemaphoreType.DMA((len(sources),))],
        compiler_params=pltpu.CompilerParams(vmem_limit_bytes=16 * 1024 * 1024),
        name="prepare",
    )(*[pltpu.with_memory_space_constraint(x, pltpu.HBM) for x in sources])


def pack_rows_of(real, imag, each):
    group = real.shape[0]
    row = lax.broadcasted_iota(jnp.int32, real.shape, 0)
    return jnp.where(row < each, real, pltpu.roll(imag, each, 0)), group - each


def split_two(value):
    high = value.astype(BF16)
    return high, (value - high.astype(F32)).astype(BF16)


def operator_kernel(index_ref, own_ref, partner_ref, out_ref, weights, *, dims, sections, group, each):
    levels, sides, parts, taps, beams = dims
    width = sections * group
    refs = (own_ref, partner_ref)
    weight_row = levels * sides * parts * taps
    start_row = weight_row + parts * width

    def band(ref, level, side):
        first = ((level * sides + side) * parts) * taps
        tables = [ref[first + p * taps : first + (p + 1) * taps].astype(F32) for p in range(parts)]
        start = ref[start_row : start_row + ceil_to(levels * sides, 16)].astype(F32)
        start = start[level * sides + side : level * sides + side + 1].astype(jnp.int32)
        found = [[], []]
        for c in range(0, beams, SUBL):
            column = lax.broadcasted_iota(jnp.int32, (SUBL, beams), 0) + c
            offset = column - start
            spot = offset & (SUBL - 1)
            for p in range(parts):
                value = jnp.zeros((SUBL, beams), F32)
                for t in range(0, taps, SUBL):
                    got = jnp.take_along_axis(
                        tables[p][t : t + SUBL], spot, axis=0, mode="promise_in_bounds"
                    )
                    value = jnp.where((offset >= t) & (offset < t + SUBL), got, value)
                found[p].append(value)
        return [jnp.concatenate(f, axis=0) for f in found]

    def complex_operand(real, imag):
        top = jnp.concatenate([real, imag], axis=1)
        low = jnp.concatenate([-imag, real], axis=1)
        return jnp.concatenate([top, low], axis=0).astype(BF16)

    section = index_ref[0]
    images = []
    for a in range(2):
        for p in range(parts):
            weights[...] = refs[a][weight_row + p * width : weight_row + (p + 1) * width].astype(F32)
            rows = []
            for j in range(sections):
                at = pl.multiple_of((section ^ j) * group, group)
                rows.append(weights[pl.ds(at, group)])
            images.append(jnp.concatenate(rows, axis=0))
    zero = jnp.zeros((width, 2 * beams), F32)
    own = jnp.concatenate([jnp.concatenate(images[0:2], axis=1), zero], axis=0)
    partner = jnp.concatenate([zero, jnp.concatenate(images[2:4], axis=1)], axis=0)
    for level in range(levels):
        own_high, own_low = split_two(own)
        partner_high, partner_low = split_two(partner)
        own_rows = jnp.concatenate([own_high, own_low], axis=0)
        partner_rows = jnp.concatenate([partner_high, partner_low], axis=0)

        def merged(ref, mine, other):
            product = jnp.dot(
                mine, complex_operand(*band(ref, level, 0)), preferred_element_type=F32
            ) + jnp.dot(other, complex_operand(*band(ref, level, 1)), preferred_element_type=F32)
            return product[: 2 * width] + product[2 * width :]

        following = merged(own_ref, own_rows, partner_rows)
        if level < levels - 1:
            partner = merged(partner_ref, partner_rows, own_rows)
        own = following
    full, left, right = [], [], []
    for j in range(2 * sections):
        real = own[j * group : (j + 1) * group, :beams]
        imag = own[j * group : (j + 1) * group, beams:]
        straight = jnp.concatenate([real, imag], axis=1)
        turned = jnp.concatenate([-imag, real], axis=1)
        lead, moved = pack_rows_of(straight, turned, each)
        row = lax.broadcasted_iota(jnp.int32, lead.shape, 0)
        full.append(lead)
        left.append(jnp.where(row < group // 2, pltpu.roll(turned, group - moved, 0), 0.0))
        right.append(jnp.where(row >= group // 2, pltpu.roll(turned, group // 2 - moved, 0), 0.0))
    pairs = sections // 2
    first_core = section % 2 == 0
    for half, rest in enumerate((left, right)):
        sources = [jnp.concatenate([full[j], rest[j]], axis=0) for j in range(2 * sections)]
        quarters = [jnp.concatenate(sources[q * pairs : (q + 1) * pairs], axis=0) for q in range(4)]
        quarters[1:3] = [
            jnp.where(first_core, quarters[1], quarters[2]),
            jnp.where(first_core, quarters[2], quarters[1]),
        ]
        high, low = split_two(jnp.concatenate(quarters, axis=0).T)
        out_ref[half] = jnp.concatenate([high, low], axis=1)


def fold_operator(section, own, partner, dims, sections, group, each):
    beams = dims[-1]
    width = sections * group
    return pl.pallas_call(
        functools.partial(operator_kernel, dims=dims, sections=sections, group=group, each=each),
        out_shape=jax.ShapeDtypeStruct((2, 2 * beams, 8 * width), BF16),
        in_specs=[
            pl.BlockSpec(memory_space=pltpu.SMEM),
            pl.BlockSpec(memory_space=pltpu.VMEM),
            pl.BlockSpec(memory_space=pltpu.VMEM),
        ],
        scratch_shapes=[pltpu.VMEM((width, beams), F32)],
        compiler_params=pltpu.CompilerParams(vmem_limit_bytes=16 * 1024 * 1024),
        name="fold_operator",
    )(section, own, partner)


def correlate(rows, even, odd, table, blocks, group):
    extra = table.shape[0] // (2 * LANE) - 1
    total = blocks + extra
    held = [
        jnp.concatenate(
            [rows[:group, b * LANE : (b + 1) * LANE], rows[group:, b * LANE : (b + 1) * LANE]], axis=1
        )
        for b in range(total)
    ]
    for b in range(0, total, 2):
        even[b * group : (b + 2) * group] = jnp.concatenate(held[b : b + 2], axis=0).astype(BF16)
    for b in range(1, total - 1, 2):
        odd[(b - 1) * group : (b + 1) * group] = jnp.concatenate(held[b : b + 2], axis=0).astype(BF16)
    window = blocks * group
    pieces = []
    for lag in range(extra + 1):
        source, at = (even, lag) if lag % 2 == 0 else (odd, lag - 1)
        pieces.append(source[at * group : at * group + window])
    return jnp.dot(jnp.concatenate(pieces, axis=1), table[...], preferred_element_type=F32)


def as_chunk(done, s, chunk, group, each):
    real, imag = [
        jnp.concatenate(
            [
                done[(s * chunk + b) * group : (s * chunk + b + 1) * group, c * LANE : (c + 1) * LANE]
                for b in range(chunk)
            ],
            axis=1,
        )
        for c in range(2)
    ]
    middle = chunk * LANE // 2
    lead, moved = pack_rows_of(real, imag, each)
    row = lax.broadcasted_iota(jnp.int32, (group, middle), 0)
    rest = jnp.where(
        row < group // 2,
        pltpu.roll(imag[:, :middle], group - moved, 0),
        pltpu.roll(imag[:, middle:], group // 2 - moved, 0),
    )
    return jnp.concatenate([lead[:, :middle], lead[:, middle:], rest], axis=0).astype(BF16)


def begin_kernel(echo_ref, chirp_ref, early_ref, late_ref, table, rows, even, odd, *, group):
    pulses, _, length = echo_ref.shape
    extra = chirp_ref.shape[1] // LANE
    reverse = LANE - 1 - lax.broadcasted_iota(jnp.int32, (2, LANE), 1)
    below = lax.broadcasted_iota(jnp.int32, (LANE, LANE), 1) <= lax.broadcasted_iota(
        jnp.int32, (LANE, LANE), 0
    )
    before = [jnp.zeros((LANE, LANE), F32)] * 2
    for lag in range(extra + 1):
        if lag < extra:
            piece = chirp_ref[:, lag * LANE : (lag + 1) * LANE].astype(F32)
            piece = jnp.take_along_axis(piece, reverse, axis=1, mode="promise_in_bounds")
            turned = [
                pltpu.roll(
                    jnp.broadcast_to(piece[c : c + 1], (LANE, LANE)), 1, 1, stride=1, stride_axis=0
                )
                for c in range(2)
            ]
        else:
            turned = [jnp.zeros((LANE, LANE), F32)] * 2
        real, imag = [jnp.where(below, turned[c], before[c]) for c in range(2)]
        before = turned
        at = lag * 2 * LANE
        table[at : at + LANE, :LANE] = real.astype(BF16)
        table[at : at + LANE, LANE:] = (-imag).astype(BF16)
        table[at + LANE : at + 2 * LANE, :LANE] = imag.astype(BF16)
        table[at + LANE : at + 2 * LANE, LANE:] = real.astype(BF16)
    rows[...] = jnp.zeros_like(rows)
    for p in range(pulses):
        near = echo_ref[p].astype(F32)
        for c in range(2):
            rows[c * group + p : c * group + p + 1, :] = near[c : c + 1]
    late_ref[...] = rows[:, length - late_ref.shape[1] :]
    done = correlate(rows, even, odd, table, length // LANE - extra, group)
    for s in range(early_ref.shape[0]):
        early_ref[s] = as_chunk(done, s, 2 * early_ref.shape[2] // LANE, group, pulses)


def finish_kernel(index_ref, early_ref, late_ref, halo_ref, table, keep_ref, give_ref, rows, even, odd, *, group):
    pulses = halo_ref.shape[0]
    span = late_ref.shape[1]
    taps = rows.shape[1] - span
    rows[:, :span] = late_ref[...]
    rows[:, span:] = jnp.zeros((2 * group, taps), F32)
    for p in range(pulses):
        far = halo_ref[p, :, :taps].astype(F32)
        for c in range(2):
            rows[c * group + p : c * group + p + 1, span:] = far[c : c + 1]
    done = correlate(rows, even, odd, table, span // LANE, group)
    ready = early_ref.shape[0]
    chunk = 2 * early_ref.shape[2]
    section = index_ref[0]
    for s in range(ready + span // chunk):
        stacked = early_ref[s] if s < ready else as_chunk(done, s - ready, chunk // LANE, group, pulses)
        slot = section ^ s
        far_chunk, other_core = slot // 2, slot % 2
        place = far_chunk ^ 1 ^ (section % 2) ^ other_core

        @pl.when(other_core == 0)
        def _():
            keep_ref[place] = stacked

        @pl.when(other_core == 1)
        def _():
            give_ref[place] = stacked


def row_scratch(blocks, group):
    return [
        pltpu.VMEM((2 * group, blocks * LANE), F32),
        pltpu.VMEM((blocks * group, 2 * LANE), BF16),
        pltpu.VMEM((blocks * group, 2 * LANE), BF16),
    ]


def begin_compression(echo, chirp, sections, group):
    _, _, length = echo.shape
    taps = chirp.shape[1]
    chunk = length // sections
    early = (length - taps) // chunk
    return pl.pallas_call(
        functools.partial(begin_kernel, group=group),
        out_shape=(
            jax.ShapeDtypeStruct((early, 3 * group, chunk // 2), BF16),
            jax.ShapeDtypeStruct((2 * group, length - early * chunk), F32),
            jax.ShapeDtypeStruct(((taps // LANE + 1) * 2 * LANE, 2 * LANE), BF16),
        ),
        scratch_shapes=row_scratch(length // LANE, group),
        compiler_params=pltpu.CompilerParams(vmem_limit_bytes=24 * 1024 * 1024),
        name="begin_compression",
    )(echo, chirp)


def finish_compression(section, early, late, halo, table, group):
    blocks = late.shape[1] // LANE + table.shape[0] // (2 * LANE) - 1
    return pl.pallas_call(
        functools.partial(finish_kernel, group=group),
        out_shape=[jax.ShapeDtypeStruct((2, *early.shape[1:]), BF16)] * 2,
        in_specs=[pl.BlockSpec(memory_space=pltpu.SMEM)] + [pl.BlockSpec(memory_space=pltpu.VMEM)] * 4,
        scratch_shapes=row_scratch(blocks, group),
        compiler_params=pltpu.CompilerParams(vmem_limit_bytes=24 * 1024 * 1024),
        name="finish_compression",
    )(section, early, late, halo, table)


def image_kernel(index_ref, operator_ref, both_ref, *refs, group):
    chunks, (out_ref, parts, sems) = refs[:-3], refs[-3:]
    count, _, tile = parts.shape
    width = both_ref.shape[2]
    near = 1 - index_ref[0] % 2
    held = [both_ref[near]] + [chunk[...] for chunk in chunks]
    held = [value.astype(F32) for value in held]
    copies = []
    for i in range(count):
        half, at = divmod(i * tile, width)
        rows = []
        for value in held:
            for first in range(0, value.shape[0], 3 * group):
                rows.append(value[first + half * group : first + (half + 1) * group, at : at + tile])
                rows.append(value[first + 2 * group : first + 3 * group, at : at + tile])
        pulses = jnp.concatenate(rows, axis=0).astype(BF16)
        result = jnp.dot(
            operator_ref[half], jnp.concatenate([pulses, pulses], axis=0), preferred_element_type=F32
        )
        parts[i] = result.astype(BF16)
        copy = pltpu.make_async_copy(parts.at[i], out_ref.at[:, i * tile : (i + 1) * tile], sems.at[i])
        copy.start()
        copies.append(copy)
    for copy in copies:
        copy.wait()


def form_image(section, operator, both, chunks, group):
    height, half = operator.shape[1], both.shape[2]
    tile = 256 if half % 256 == 0 else half
    count = 2 * half // tile
    return pl.pallas_call(
        functools.partial(image_kernel, group=group),
        out_shape=jax.ShapeDtypeStruct((height, 2 * half), BF16),
        in_specs=[pl.BlockSpec(memory_space=pltpu.SMEM)]
        + [pl.BlockSpec(memory_space=pltpu.VMEM)] * (2 + len(chunks)),
        out_specs=pl.BlockSpec(memory_space=pl.ANY),
        scratch_shapes=[
            pltpu.VMEM((count, height, tile), BF16),
            pltpu.SemaphoreType.DMA((count,)),
        ],
        compiler_params=pltpu.CompilerParams(vmem_limit_bytes=16 * 1024 * 1024),
        name="form_image",
    )(section, operator, both, *chunks)


def swap(value, axis, by):
    count = lax.axis_size(axis)
    return lax.ppermute(value, axis, [(i, i ^ by) for i in range(count)])


def swap_by(value, move):
    sections, subs = lax.axis_size("section"), lax.axis_size("sub")
    pairs = []
    for s in range(sections):
        for a in range(subs):
            to_s, to_a = move(s, a)
            pairs.append((s * subs + a, to_s * subs + to_a))
    return lax.ppermute(value, ("section", "sub"), pairs)


def from_behind(value, axis, by):
    size = lax.axis_size(axis)
    pairs = [(i, i + by) for i in range(size) if 0 <= i + by < size]
    return lax.ppermute(value, axis, pairs)


def on_device(echoes, chirp, steer, pulse_order, band_coef, band_start, band_width):
    sections, subs = lax.axis_size("section"), lax.axis_size("sub")
    pulses_each = echoes.shape[2]
    group = ceil_to(pulses_each, SUBL)
    section = lax.axis_index("section").astype(jnp.int32).reshape(1)
    coef = jnp.swapaxes(band_coef, 4, 5)
    weights = jnp.swapaxes(steer, 2, 3)
    levels, _, sides, parts, taps, beams = coef.shape
    dims = (levels, sides, parts, taps, beams)

    echo = jnp.transpose(echoes[:, 0], (1, 0, 2))
    halo = from_behind(echo, "rng", -1)
    echo, chirp, packed = prepare(
        echo, chirp, coef, band_start, band_width, weights, pulse_order, sections, group
    )
    if subs == 2:
        packed_partner = swap(packed, "sub", 1)
    early, late, table = begin_compression(echo, chirp, sections, group)
    keep, give = finish_compression(section, early, late, halo, table, group)
    both = jnp.concatenate([keep, swap(give, "section", 1)], axis=1)
    far = lax.dynamic_index_in_dim(both, section[0] % 2, 0, keepdims=False)
    if subs != 2:
        near = lax.dynamic_index_in_dim(both, 1 - section[0] % 2, 0, keepdims=False)
        chunks = [near, swap(far, "section", 2)]
        return merge_images(section, chunks, packed, dims, sections, group, pulses_each)
    chunks = [
        swap_by(both[0], lambda s, a: (s, a ^ 1) if s % 2 else (s ^ 2, a)),
        swap_by(both[1], lambda s, a: (s ^ 2, a) if s % 2 else (s, a ^ 1)),
        swap_by(far, lambda s, a: (s ^ 2, a ^ 1)),
    ]
    operator = fold_operator(section, packed, packed_partner, dims, sections, group, pulses_each)
    image = form_image(section, operator, both, chunks, group)
    return image.reshape(2, beams, 1, image.shape[1])


def unpack(chunk, group, each):
    lead = jnp.concatenate([chunk[:group], chunk[group : 2 * group]], axis=1)
    moved, rest = group - each, chunk[2 * group :]
    tail = jnp.concatenate([rest[: each - moved], rest[group // 2 : group // 2 + each - moved]], axis=1)
    return jnp.concatenate([lead, tail], axis=0)


def merge_images(section, chunks, packed, dims, sections, group, each):
    levels, sides, parts, taps, beams = dims
    width = sections * group
    first = levels * sides * parts * taps
    table = packed[first : first + parts * width].reshape(parts, sections, group, beams)
    table = jnp.take(table, section[0] ^ jnp.arange(sections), axis=1)[:, :, :each]
    chunks = [
        unpack(chunk[first : first + 3 * group], group, each)
        for chunk in chunks
        for first in range(0, chunk.shape[0], 3 * group)
    ]
    real, imag = table[0], table[1]
    rows = jnp.concatenate(
        [jnp.concatenate([real, -imag], axis=1), jnp.concatenate([imag, real], axis=1)], axis=2
    )
    image = lax.dot_general(
        rows.reshape(-1, 2 * beams), jnp.concatenate(chunks, axis=0), (((0,), (0,)), ((), ())), preferred_element_type=F32
    ).astype(BF16)
    starts = packed[first + parts * width :].astype(jnp.int32)
    column = jnp.arange(beams, dtype=jnp.int32)
    bits = lax.axis_size("sub").bit_length() - 1
    for level in range(levels):
        partner = swap(image, "sub", 1 << (level % bits))
        operands = []
        for side in range(sides):
            at = (level * sides + side) * parts * taps
            coef = packed[at : at + parts * taps].reshape(parts, taps, beams)
            offset = column[:, None] - starts[level * sides + side][None, :]
            hits = (offset[None] == jnp.arange(taps, dtype=jnp.int32)[:, None, None]).astype(BF16)
            operands.append(jnp.einsum("ptq,tcq->pqc", coef, hits, preferred_element_type=F32).astype(BF16))
        top = jnp.concatenate([operands[0][0], -operands[0][1], operands[1][0], -operands[1][1]], axis=1)
        low = jnp.concatenate([operands[0][1], operands[0][0], operands[1][1], operands[1][0]], axis=1)
        image = jnp.dot(
            jnp.concatenate([top, low], axis=0),
            jnp.concatenate([image, partner], axis=0),
            preferred_element_type=F32,
        ).astype(BF16)
    return image.reshape(2, beams, 1, image.shape[1])


def solution(mesh):
    return jax.shard_map(
        on_device,
        mesh=mesh,
        in_specs=(
            P(None, "sub", "section", "rng"),
            P(),
            P(None, "sub", None, None),
            P("sub", None),
            P(None, "sub", None, None, None, None),
            P(None, "sub", None, None),
            P(None, "sub", None, None),
        ),
        out_specs=P(None, "sub", "rng", "section"),
        check_vma=False,
    )
```

```python
import functools

import jax
import jax.numpy as jnp
from jax import lax
from jax.experimental import pallas as pl
from jax.experimental.pallas import tpu as pltpu
from jax.sharding import PartitionSpec as P

LANE = 128
SUBL = 8
F32 = jnp.float32
BF16 = jnp.bfloat16


def ceil_to(value, unit):
    return -(-value // unit) * unit


def prepare_kernel(*refs, sections, group):
    sources, (echo_out, chirp_out, pack_ref), scratch = refs[:7], refs[7:10], refs[10:]
    coef_ref, start_ref, width_ref, steer_ref, order_ref, starts, sems = scratch
    targets = (coef_ref, start_ref, width_ref, steer_ref, order_ref, chirp_out, echo_out)
    loads = [
        pltpu.make_async_copy(source, target, sems.at[i])
        for i, (source, target) in enumerate(zip(sources, targets))
    ]
    for load in loads:
        load.start()
    for load in loads:
        load.wait()
    levels, _, sides, parts, taps, beams = coef_ref.shape
    tap = lax.broadcasted_iota(jnp.int32, (taps, beams), 0)
    row = 0
    for level in range(levels):
        for side in range(sides):
            used = tap < width_ref[level, 0, side : side + 1, :]
            for part in range(parts):
                entries = coef_ref[level, 0, side, part].astype(F32)
                pack_ref[row : row + taps] = jnp.where(used, entries, 0.0).astype(BF16)
                row += taps
    pulses = order_ref.shape[1]
    each = pulses // sections
    position = lax.broadcasted_iota(jnp.int32, (pulses, pulses), 0)
    hit = (position == order_ref[0:1, :]).astype(F32)
    slot = lax.broadcasted_iota(jnp.int32, (sections * group, pulses), 0)
    pulse = lax.broadcasted_iota(jnp.int32, (sections * group, pulses), 1)
    place = jnp.zeros((sections * group, pulses), F32)
    for s in range(sections):
        inside = (pulse >= s * each) & (pulse < (s + 1) * each)
        place = jnp.where(inside & (slot - s * group == pulse - s * each), 1.0, place)
    pick = lax.dot_general(
        place.astype(BF16), hit.astype(BF16), (((1,), (1,)), ((), ())), preferred_element_type=F32
    )
    for part in range(parts):
        chosen = jnp.dot(pick.astype(BF16), steer_ref[part, 0], preferred_element_type=F32)
        pack_ref[row : row + sections * group] = chosen.astype(BF16)
        row += sections * group
    starts[...] = jnp.zeros_like(starts)
    for level in range(levels):
        starts[sides * level : sides * level + sides] = start_ref[level, 0].astype(F32)
    pack_ref[row : row + starts.shape[0]] = starts[...].astype(BF16)


def pack_rows(levels, sides, parts, taps, sections, group):
    return levels * sides * parts * taps + parts * sections * group + ceil_to(levels * sides, 16)


def prepare(echo, chirp, coef, start, width, steer, order, sections, group):
    levels, _, sides, parts, taps, beams = coef.shape
    sources = (coef, start, width, steer, order, chirp, echo)
    return pl.pallas_call(
        functools.partial(prepare_kernel, sections=sections, group=group),
        out_shape=(
            jax.ShapeDtypeStruct(echo.shape, BF16),
            jax.ShapeDtypeStruct(chirp.shape, BF16),
            jax.ShapeDtypeStruct((pack_rows(levels, sides, parts, taps, sections, group), beams), BF16),
        ),
        in_specs=[pl.BlockSpec(memory_space=pl.ANY)] * len(sources),
        scratch_shapes=[pltpu.VMEM(x.shape, x.dtype) for x in sources[:5]]
        + [pltpu.VMEM((ceil_to(levels * sides, 16), beams), F32), pltpu.SemaphoreType.DMA((len(sources),))],
        compiler_params=pltpu.CompilerParams(vmem_limit_bytes=16 * 1024 * 1024),
        name="prepare",
    )(*[pltpu.with_memory_space_constraint(x, pltpu.HBM) for x in sources])


def pack_rows_of(real, imag, each):
    group = real.shape[0]
    row = lax.broadcasted_iota(jnp.int32, real.shape, 0)
    return jnp.where(row < each, real, pltpu.roll(imag, each, 0)), group - each


def split_two(value):
    high = value.astype(BF16)
    return high, (value - high.astype(F32)).astype(BF16)


def operator_kernel(index_ref, own_ref, partner_ref, out_ref, weights, *, dims, sections, group, each):
    levels, sides, parts, taps, beams = dims
    width = sections * group
    refs = (own_ref, partner_ref)
    weight_row = levels * sides * parts * taps
    start_row = weight_row + parts * width

    def band(ref, level, side):
        first = ((level * sides + side) * parts) * taps
        tables = [ref[first + p * taps : first + (p + 1) * taps].astype(F32) for p in range(parts)]
        start = ref[start_row : start_row + ceil_to(levels * sides, 16)].astype(F32)
        start = start[level * sides + side : level * sides + side + 1].astype(jnp.int32)
        found = [[], []]
        for c in range(0, beams, SUBL):
            column = lax.broadcasted_iota(jnp.int32, (SUBL, beams), 0) + c
            offset = column - start
            spot = offset & (SUBL - 1)
            for p in range(parts):
                value = jnp.zeros((SUBL, beams), F32)
                for t in range(0, taps, SUBL):
                    got = jnp.take_along_axis(
                        tables[p][t : t + SUBL], spot, axis=0, mode="promise_in_bounds"
                    )
                    value = jnp.where((offset >= t) & (offset < t + SUBL), got, value)
                found[p].append(value)
        return [jnp.concatenate(f, axis=0) for f in found]

    def complex_operand(real, imag):
        top = jnp.concatenate([real, imag], axis=1)
        low = jnp.concatenate([-imag, real], axis=1)
        return jnp.concatenate([top, low], axis=0).astype(BF16)

    section = index_ref[0]
    images = []
    for a in range(2):
        for p in range(parts):
            weights[...] = refs[a][weight_row + p * width : weight_row + (p + 1) * width].astype(F32)
            rows = []
            for j in range(sections):
                at = pl.multiple_of((section ^ j) * group, group)
                rows.append(weights[pl.ds(at, group)])
            images.append(jnp.concatenate(rows, axis=0))
    zero = jnp.zeros((width, 2 * beams), F32)
    own = jnp.concatenate([jnp.concatenate(images[0:2], axis=1), zero], axis=0)
    partner = jnp.concatenate([zero, jnp.concatenate(images[2:4], axis=1)], axis=0)
    for level in range(levels):
        own_high, own_low = split_two(own)
        partner_high, partner_low = split_two(partner)
        own_rows = jnp.concatenate([own_high, own_low], axis=0)
        partner_rows = jnp.concatenate([partner_high, partner_low], axis=0)

        def merged(ref, mine, other):
            product = jnp.dot(
                mine, complex_operand(*band(ref, level, 0)), preferred_element_type=F32
            ) + jnp.dot(other, complex_operand(*band(ref, level, 1)), preferred_element_type=F32)
            return product[: 2 * width] + product[2 * width :]

        following = merged(own_ref, own_rows, partner_rows)
        if level < levels - 1:
            partner = merged(partner_ref, partner_rows, own_rows)
        own = following
    full, left, right = [], [], []
    for j in range(2 * sections):
        real = own[j * group : (j + 1) * group, :beams]
        imag = own[j * group : (j + 1) * group, beams:]
        straight = jnp.concatenate([real, imag], axis=1)
        turned = jnp.concatenate([-imag, real], axis=1)
        lead, moved = pack_rows_of(straight, turned, each)
        row = lax.broadcasted_iota(jnp.int32, lead.shape, 0)
        full.append(lead)
        left.append(jnp.where(row < group // 2, pltpu.roll(turned, group - moved, 0), 0.0))
        right.append(jnp.where(row >= group // 2, pltpu.roll(turned, group // 2 - moved, 0), 0.0))
    pairs = sections // 2
    first_core = section % 2 == 0
    for half, rest in enumerate((left, right)):
        sources = [jnp.concatenate([full[j], rest[j]], axis=0) for j in range(2 * sections)]
        quarters = [jnp.concatenate(sources[q * pairs : (q + 1) * pairs], axis=0) for q in range(4)]
        quarters = [
            quarters[0],
            quarters[3],
            jnp.where(first_core, quarters[1], quarters[2]),
            jnp.where(first_core, quarters[2], quarters[1]),
        ]
        high, low = split_two(jnp.concatenate(quarters, axis=0).T)
        out_ref[half] = jnp.concatenate([high, low], axis=1)


def fold_operator(section, own, partner, dims, sections, group, each):
    beams = dims[-1]
    width = sections * group
    return pl.pallas_call(
        functools.partial(operator_kernel, dims=dims, sections=sections, group=group, each=each),
        out_shape=jax.ShapeDtypeStruct((2, 2 * beams, 8 * width), BF16),
        in_specs=[
            pl.BlockSpec(memory_space=pltpu.SMEM),
            pl.BlockSpec(memory_space=pltpu.VMEM),
            pl.BlockSpec(memory_space=pltpu.VMEM),
        ],
        scratch_shapes=[pltpu.VMEM((width, beams), F32)],
        compiler_params=pltpu.CompilerParams(vmem_limit_bytes=16 * 1024 * 1024),
        name="fold_operator",
    )(section, own, partner)


def correlate(rows, even, odd, table, blocks, group):
    extra = table.shape[0] // (2 * LANE) - 1
    total = blocks + extra
    held = [
        jnp.concatenate(
            [rows[:group, b * LANE : (b + 1) * LANE], rows[group:, b * LANE : (b + 1) * LANE]], axis=1
        )
        for b in range(total)
    ]
    for b in range(0, total, 2):
        even[b * group : (b + 2) * group] = jnp.concatenate(held[b : b + 2], axis=0).astype(BF16)
    for b in range(1, total - 1, 2):
        odd[(b - 1) * group : (b + 1) * group] = jnp.concatenate(held[b : b + 2], axis=0).astype(BF16)
    window = blocks * group
    pieces = []
    for lag in range(extra + 1):
        source, at = (even, lag) if lag % 2 == 0 else (odd, lag - 1)
        pieces.append(source[at * group : at * group + window])
    return jnp.dot(jnp.concatenate(pieces, axis=1), table[...], preferred_element_type=F32)


def as_chunk(done, s, chunk, group, each):
    real, imag = [
        jnp.concatenate(
            [
                done[(s * chunk + b) * group : (s * chunk + b + 1) * group, c * LANE : (c + 1) * LANE]
                for b in range(chunk)
            ],
            axis=1,
        )
        for c in range(2)
    ]
    middle = chunk * LANE // 2
    lead, moved = pack_rows_of(real, imag, each)
    row = lax.broadcasted_iota(jnp.int32, (group, middle), 0)
    rest = jnp.where(
        row < group // 2,
        pltpu.roll(imag[:, :middle], group - moved, 0),
        pltpu.roll(imag[:, middle:], group // 2 - moved, 0),
    )
    return jnp.concatenate([lead[:, :middle], lead[:, middle:], rest], axis=0).astype(BF16)


def begin_kernel(echo_ref, chirp_ref, early_ref, late_ref, table, rows, even, odd, *, group):
    pulses, _, length = echo_ref.shape
    extra = chirp_ref.shape[1] // LANE
    reverse = LANE - 1 - lax.broadcasted_iota(jnp.int32, (2, LANE), 1)
    below = lax.broadcasted_iota(jnp.int32, (LANE, LANE), 1) <= lax.broadcasted_iota(
        jnp.int32, (LANE, LANE), 0
    )
    before = [jnp.zeros((LANE, LANE), F32)] * 2
    for lag in range(extra + 1):
        if lag < extra:
            piece = chirp_ref[:, lag * LANE : (lag + 1) * LANE].astype(F32)
            piece = jnp.take_along_axis(piece, reverse, axis=1, mode="promise_in_bounds")
            turned = [
                pltpu.roll(
                    jnp.broadcast_to(piece[c : c + 1], (LANE, LANE)), 1, 1, stride=1, stride_axis=0
                )
                for c in range(2)
            ]
        else:
            turned = [jnp.zeros((LANE, LANE), F32)] * 2
        real, imag = [jnp.where(below, turned[c], before[c]) for c in range(2)]
        before = turned
        at = lag * 2 * LANE
        table[at : at + LANE, :LANE] = real.astype(BF16)
        table[at : at + LANE, LANE:] = (-imag).astype(BF16)
        table[at + LANE : at + 2 * LANE, :LANE] = imag.astype(BF16)
        table[at + LANE : at + 2 * LANE, LANE:] = real.astype(BF16)
    rows[...] = jnp.zeros_like(rows)
    for p in range(pulses):
        near = echo_ref[p].astype(F32)
        for c in range(2):
            rows[c * group + p : c * group + p + 1, :] = near[c : c + 1]
    late_ref[...] = rows[:, length - late_ref.shape[1] :]
    done = correlate(rows, even, odd, table, length // LANE - extra, group)
    for s in range(early_ref.shape[0]):
        early_ref[s] = as_chunk(done, s, 2 * early_ref.shape[2] // LANE, group, pulses)


def finish_kernel(index_ref, early_ref, late_ref, halo_ref, table, keep_ref, give_ref, rows, even, odd, *, group):
    pulses = halo_ref.shape[0]
    span = late_ref.shape[1]
    taps = rows.shape[1] - span
    rows[:, :span] = late_ref[...]
    rows[:, span:] = jnp.zeros((2 * group, taps), F32)
    for p in range(pulses):
        far = jnp.where(index_ref[1] != 0, halo_ref[p, :, :taps].astype(F32), 0.0)
        for c in range(2):
            rows[c * group + p : c * group + p + 1, span:] = far[c : c + 1]
    done = correlate(rows, even, odd, table, span // LANE, group)
    ready = early_ref.shape[0]
    chunk = 2 * early_ref.shape[2]
    section = index_ref[0]
    for s in range(ready + span // chunk):
        stacked = early_ref[s] if s < ready else as_chunk(done, s - ready, chunk // LANE, group, pulses)
        slot = section ^ s
        far_chunk, other_core = slot // 2, slot % 2
        place = far_chunk ^ 1 ^ (section % 2) ^ other_core

        @pl.when(other_core == 0)
        def _():
            keep_ref[place] = stacked

        @pl.when(other_core == 1)
        def _():
            give_ref[place] = stacked


def row_scratch(blocks, group):
    return [
        pltpu.VMEM((2 * group, blocks * LANE), F32),
        pltpu.VMEM((blocks * group, 2 * LANE), BF16),
        pltpu.VMEM((blocks * group, 2 * LANE), BF16),
    ]


def begin_compression(echo, chirp, sections, group):
    _, _, length = echo.shape
    taps = chirp.shape[1]
    chunk = length // sections
    early = (length - taps) // chunk
    return pl.pallas_call(
        functools.partial(begin_kernel, group=group),
        out_shape=(
            jax.ShapeDtypeStruct((early, 3 * group, chunk // 2), BF16),
            jax.ShapeDtypeStruct((2 * group, length - early * chunk), F32),
            jax.ShapeDtypeStruct(((taps // LANE + 1) * 2 * LANE, 2 * LANE), BF16),
        ),
        scratch_shapes=row_scratch(length // LANE, group),
        compiler_params=pltpu.CompilerParams(vmem_limit_bytes=24 * 1024 * 1024),
        name="begin_compression",
    )(echo, chirp)


def finish_compression(place, early, late, halo, table, group):
    blocks = late.shape[1] // LANE + table.shape[0] // (2 * LANE) - 1
    return pl.pallas_call(
        functools.partial(finish_kernel, group=group),
        out_shape=[jax.ShapeDtypeStruct((2, *early.shape[1:]), BF16)] * 2,
        in_specs=[pl.BlockSpec(memory_space=pltpu.SMEM)] + [pl.BlockSpec(memory_space=pltpu.VMEM)] * 4,
        scratch_shapes=row_scratch(blocks, group),
        compiler_params=pltpu.CompilerParams(vmem_limit_bytes=24 * 1024 * 1024),
        name="finish_compression",
    )(place, early, late, halo, table)


def image_kernel(index_ref, operator_ref, both_ref, *refs, group):
    chunks, (out_ref, parts, sems) = refs[:-3], refs[-3:]
    count, _, tile = parts.shape
    width = both_ref.shape[2]
    near = 1 - index_ref[0] % 2
    held = [both_ref[near]] + [chunk[...] for chunk in chunks]
    held = [value.astype(F32) for value in held]
    copies = []
    for i in range(count):
        half, at = divmod(i * tile, width)
        rows = []
        for value in held:
            for first in range(0, value.shape[0], 3 * group):
                rows.append(value[first + half * group : first + (half + 1) * group, at : at + tile])
                rows.append(value[first + 2 * group : first + 3 * group, at : at + tile])
        pulses = jnp.concatenate(rows, axis=0).astype(BF16)
        result = jnp.dot(
            operator_ref[half], jnp.concatenate([pulses, pulses], axis=0), preferred_element_type=F32
        )
        parts[i] = result.astype(BF16)
        copy = pltpu.make_async_copy(parts.at[i], out_ref.at[:, i * tile : (i + 1) * tile], sems.at[i])
        copy.start()
        copies.append(copy)
    for copy in copies:
        copy.wait()


def form_image(section, operator, both, chunks, group):
    height, half = operator.shape[1], both.shape[2]
    tile = 256 if half % 256 == 0 else half
    count = 2 * half // tile
    return pl.pallas_call(
        functools.partial(image_kernel, group=group),
        out_shape=jax.ShapeDtypeStruct((height, 2 * half), BF16),
        in_specs=[pl.BlockSpec(memory_space=pltpu.SMEM)]
        + [pl.BlockSpec(memory_space=pltpu.VMEM)] * (2 + len(chunks)),
        out_specs=pl.BlockSpec(memory_space=pl.ANY),
        scratch_shapes=[
            pltpu.VMEM((count, height, tile), BF16),
            pltpu.SemaphoreType.DMA((count,)),
        ],
        compiler_params=pltpu.CompilerParams(vmem_limit_bytes=16 * 1024 * 1024),
        name="form_image",
    )(section, operator, both, *chunks)


def swap(value, axis, by):
    count = lax.axis_size(axis)
    return lax.ppermute(value, axis, [(i, i ^ by) for i in range(count)])


def swap_by(value, move):
    sections, subs = lax.axis_size("section"), lax.axis_size("sub")
    pairs = []
    for s in range(sections):
        for a in range(subs):
            to_s, to_a = move(s, a)
            pairs.append((s * subs + a, to_s * subs + to_a))
    return lax.ppermute(value, ("section", "sub"), pairs)


def from_next(value):
    sections, others, count = lax.axis_size("section"), lax.axis_size("sub"), lax.axis_size("rng")
    pairs = []
    for s in range(sections):
        for a in range(others):
            first = (s * others + a) * count
            pairs += [(first + i, first + i - 1) for i in range(1, count)]
            if s:
                pairs.append((first, first + count - 1))
    return lax.ppermute(value, ("section", "sub", "rng"), pairs)


def on_device(echoes, chirp, steer, pulse_order, band_coef, band_start, band_width):
    sections, subs = lax.axis_size("section"), lax.axis_size("sub")
    pulses_each = echoes.shape[2]
    group = ceil_to(pulses_each, SUBL)
    section = lax.axis_index("section").astype(jnp.int32).reshape(1)
    coef = jnp.swapaxes(band_coef, 4, 5)
    weights = jnp.swapaxes(steer, 2, 3)
    levels, _, sides, parts, taps, beams = coef.shape
    dims = (levels, sides, parts, taps, beams)

    echo = jnp.transpose(echoes[:, 0], (1, 0, 2))
    halo = from_next(echo)
    has_next = (lax.axis_index("rng") < lax.axis_size("rng") - 1).astype(jnp.int32)
    echo, chirp, packed = prepare(
        echo, chirp, coef, band_start, band_width, weights, pulse_order, sections, group
    )
    if subs == 2:
        packed_partner = swap(packed, "sub", 1)
    early, late, table = begin_compression(echo, chirp, sections, group)
    place = jnp.stack([section[0], has_next])
    keep, give = finish_compression(place, early, late, halo, table, group)
    both = jnp.concatenate([keep, swap(give, "section", 1)], axis=1)
    far = lax.dynamic_index_in_dim(both, section[0] % 2, 0, keepdims=False)
    if subs != 2:
        near = lax.dynamic_index_in_dim(both, 1 - section[0] % 2, 0, keepdims=False)
        chunks = [near, swap(far, "section", 2)]
        return merge_images(section, chunks, packed, dims, sections, group, pulses_each)
    chunks = [
        swap_by(far, lambda s, a: (s ^ 2, a ^ 1)),
        swap_by(both[0], lambda s, a: (s, a ^ 1) if s % 2 else (s ^ 2, a)),
        swap_by(both[1], lambda s, a: (s ^ 2, a) if s % 2 else (s, a ^ 1)),
    ]
    operator = fold_operator(section, packed, packed_partner, dims, sections, group, pulses_each)
    image = form_image(section, operator, both, chunks, group)
    return image.reshape(2, beams, 1, image.shape[1])


def unpack(chunk, group, each):
    lead = jnp.concatenate([chunk[:group], chunk[group : 2 * group]], axis=1)
    moved, rest = group - each, chunk[2 * group :]
    tail = jnp.concatenate([rest[: each - moved], rest[group // 2 : group // 2 + each - moved]], axis=1)
    return jnp.concatenate([lead, tail], axis=0)


def merge_images(section, chunks, packed, dims, sections, group, each):
    levels, sides, parts, taps, beams = dims
    width = sections * group
    first = levels * sides * parts * taps
    table = packed[first : first + parts * width].reshape(parts, sections, group, beams)
    table = jnp.take(table, section[0] ^ jnp.arange(sections), axis=1)[:, :, :each]
    chunks = [
        unpack(chunk[first : first + 3 * group], group, each)
        for chunk in chunks
        for first in range(0, chunk.shape[0], 3 * group)
    ]
    real, imag = table[0], table[1]
    rows = jnp.concatenate(
        [jnp.concatenate([real, -imag], axis=1), jnp.concatenate([imag, real], axis=1)], axis=2
    )
    image = lax.dot_general(
        rows.reshape(-1, 2 * beams), jnp.concatenate(chunks, axis=0), (((0,), (0,)), ((), ())), preferred_element_type=F32
    ).astype(BF16)
    starts = packed[first + parts * width :].astype(jnp.int32)
    column = jnp.arange(beams, dtype=jnp.int32)
    bits = lax.axis_size("sub").bit_length() - 1
    for level in range(levels):
        partner = swap(image, "sub", 1 << (level % bits))
        operands = []
        for side in range(sides):
            at = (level * sides + side) * parts * taps
            coef = packed[at : at + parts * taps].reshape(parts, taps, beams)
            offset = column[:, None] - starts[level * sides + side][None, :]
            hits = (offset[None] == jnp.arange(taps, dtype=jnp.int32)[:, None, None]).astype(BF16)
            operands.append(jnp.einsum("ptq,tcq->pqc", coef, hits, preferred_element_type=F32).astype(BF16))
        top = jnp.concatenate([operands[0][0], -operands[0][1], operands[1][0], -operands[1][1]], axis=1)
        low = jnp.concatenate([operands[0][1], operands[0][0], operands[1][1], operands[1][0]], axis=1)
        image = jnp.dot(
            jnp.concatenate([top, low], axis=0),
            jnp.concatenate([image, partner], axis=0),
            preferred_element_type=F32,
        ).astype(BF16)
    return image.reshape(2, beams, 1, image.shape[1])


def solution(mesh):
    return jax.shard_map(
        on_device,
        mesh=mesh,
        in_specs=(
            P(None, "sub", "section", "rng"),
            P(),
            P(None, "sub", None, None),
            P("sub", None),
            P(None, "sub", None, None, None, None),
            P(None, "sub", None, None),
            P(None, "sub", None, None),
        ),
        out_specs=P(None, "sub", "rng", "section"),
        check_vma=False,
    )
```

```python
import functools

import jax
import jax.numpy as jnp
from jax import lax
from jax.experimental import pallas as pl
from jax.experimental.pallas import tpu as pltpu
from jax.sharding import PartitionSpec as P

LANE = 128
SUBL = 8
F32 = jnp.float32
BF16 = jnp.bfloat16


def ceil_to(value, unit):
    return -(-value // unit) * unit


def prepare_kernel(*refs, sections, group):
    sources, (echo_out, rim_ref, chirp_out, pack_ref), scratch = refs[:7], refs[7:11], refs[11:]
    coef_ref, start_ref, width_ref, steer_ref, order_ref, starts, sems = scratch
    targets = (echo_out, coef_ref, start_ref, width_ref, steer_ref, order_ref, chirp_out)
    loads = [
        pltpu.make_async_copy(source, target, sems.at[i])
        for i, (source, target) in enumerate(zip(sources, targets))
    ]
    for load in loads:
        load.start()
    for load in loads:
        load.wait()
    rim_ref[...] = echo_out[:, :, : rim_ref.shape[2]]
    levels, _, sides, parts, taps, beams = coef_ref.shape
    tap = lax.broadcasted_iota(jnp.int32, (taps, beams), 0)
    row = 0
    for level in range(levels):
        for side in range(sides):
            used = tap < width_ref[level, 0, side : side + 1, :]
            for part in range(parts):
                entries = coef_ref[level, 0, side, part].astype(F32)
                pack_ref[row : row + taps] = jnp.where(used, entries, 0.0).astype(BF16)
                row += taps
    pulses = order_ref.shape[1]
    each = pulses // sections
    position = lax.broadcasted_iota(jnp.int32, (pulses, pulses), 0)
    hit = (position == order_ref[0:1, :]).astype(F32)
    slot = lax.broadcasted_iota(jnp.int32, (sections * group, pulses), 0)
    pulse = lax.broadcasted_iota(jnp.int32, (sections * group, pulses), 1)
    place = jnp.zeros((sections * group, pulses), F32)
    for s in range(sections):
        inside = (pulse >= s * each) & (pulse < (s + 1) * each)
        place = jnp.where(inside & (slot - s * group == pulse - s * each), 1.0, place)
    pick = lax.dot_general(
        place.astype(BF16), hit.astype(BF16), (((1,), (1,)), ((), ())), preferred_element_type=F32
    )
    for part in range(parts):
        chosen = jnp.dot(pick.astype(BF16), steer_ref[part, 0], preferred_element_type=F32)
        pack_ref[row : row + sections * group] = chosen.astype(BF16)
        row += sections * group
    starts[...] = jnp.zeros_like(starts)
    for level in range(levels):
        starts[sides * level : sides * level + sides] = start_ref[level, 0].astype(F32)
    pack_ref[row : row + starts.shape[0]] = starts[...].astype(BF16)


def pack_rows(levels, sides, parts, taps, sections, group):
    return levels * sides * parts * taps + parts * sections * group + ceil_to(levels * sides, 16)


def prepare(echo, chirp, coef, start, width, steer, order, sections, group):
    levels, _, sides, parts, taps, beams = coef.shape
    sources = (echo, coef, start, width, steer, order, chirp)
    return pl.pallas_call(
        functools.partial(prepare_kernel, sections=sections, group=group),
        out_shape=(
            jax.ShapeDtypeStruct(echo.shape, BF16),
            jax.ShapeDtypeStruct((*echo.shape[:2], chirp.shape[1]), BF16),
            jax.ShapeDtypeStruct(chirp.shape, BF16),
            jax.ShapeDtypeStruct((pack_rows(levels, sides, parts, taps, sections, group), beams), BF16),
        ),
        in_specs=[pl.BlockSpec(memory_space=pl.ANY)] * len(sources),
        scratch_shapes=[pltpu.VMEM(x.shape, x.dtype) for x in sources[1:6]]
        + [pltpu.VMEM((ceil_to(levels * sides, 16), beams), F32), pltpu.SemaphoreType.DMA((len(sources),))],
        compiler_params=pltpu.CompilerParams(vmem_limit_bytes=16 * 1024 * 1024),
        name="prepare",
    )(*[pltpu.with_memory_space_constraint(x, pltpu.HBM) for x in sources])


def pack_rows_of(real, imag, each):
    group = real.shape[0]
    row = lax.broadcasted_iota(jnp.int32, real.shape, 0)
    return jnp.where(row < each, real, pltpu.roll(imag, each, 0)), group - each


def split_two(value):
    high = value.astype(BF16)
    return high, (value - high.astype(F32)).astype(BF16)


def operator_kernel(index_ref, own_ref, partner_ref, out_ref, weights, *, dims, sections, group, each):
    levels, sides, parts, taps, beams = dims
    width = sections * group
    refs = (own_ref, partner_ref)
    weight_row = levels * sides * parts * taps
    start_row = weight_row + parts * width

    def band(ref, level, side):
        first = ((level * sides + side) * parts) * taps
        tables = [ref[first + p * taps : first + (p + 1) * taps].astype(F32) for p in range(parts)]
        start = ref[start_row : start_row + ceil_to(levels * sides, 16)].astype(F32)
        start = start[level * sides + side : level * sides + side + 1].astype(jnp.int32)
        found = [[], []]
        for c in range(0, beams, SUBL):
            column = lax.broadcasted_iota(jnp.int32, (SUBL, beams), 0) + c
            offset = column - start
            spot = offset & (SUBL - 1)
            for p in range(parts):
                value = jnp.zeros((SUBL, beams), F32)
                for t in range(0, taps, SUBL):
                    got = jnp.take_along_axis(
                        tables[p][t : t + SUBL], spot, axis=0, mode="promise_in_bounds"
                    )
                    value = jnp.where((offset >= t) & (offset < t + SUBL), got, value)
                found[p].append(value)
        return [jnp.concatenate(f, axis=0) for f in found]

    def complex_operand(real, imag):
        top = jnp.concatenate([real, imag], axis=1)
        low = jnp.concatenate([-imag, real], axis=1)
        return jnp.concatenate([top, low], axis=0).astype(BF16)

    section = index_ref[0]
    images = []
    for a in range(2):
        for p in range(parts):
            weights[...] = refs[a][weight_row + p * width : weight_row + (p + 1) * width].astype(F32)
            rows = []
            for j in range(sections):
                at = pl.multiple_of((section ^ j) * group, group)
                rows.append(weights[pl.ds(at, group)])
            images.append(jnp.concatenate(rows, axis=0))
    zero = jnp.zeros((width, 2 * beams), F32)
    own = jnp.concatenate([jnp.concatenate(images[0:2], axis=1), zero], axis=0)
    partner = jnp.concatenate([zero, jnp.concatenate(images[2:4], axis=1)], axis=0)
    for level in range(levels):
        own_high, own_low = split_two(own)
        partner_high, partner_low = split_two(partner)
        own_rows = jnp.concatenate([own_high, own_low], axis=0)
        partner_rows = jnp.concatenate([partner_high, partner_low], axis=0)

        def merged(ref, mine, other):
            product = jnp.dot(
                mine, complex_operand(*band(ref, level, 0)), preferred_element_type=F32
            ) + jnp.dot(other, complex_operand(*band(ref, level, 1)), preferred_element_type=F32)
            return product[: 2 * width] + product[2 * width :]

        following = merged(own_ref, own_rows, partner_rows)
        if level < levels - 1:
            partner = merged(partner_ref, partner_rows, own_rows)
        own = following
    full, left, right = [], [], []
    for j in range(2 * sections):
        real = own[j * group : (j + 1) * group, :beams]
        imag = own[j * group : (j + 1) * group, beams:]
        straight = jnp.concatenate([real, imag], axis=1)
        turned = jnp.concatenate([-imag, real], axis=1)
        lead, moved = pack_rows_of(straight, turned, each)
        row = lax.broadcasted_iota(jnp.int32, lead.shape, 0)
        full.append(lead)
        left.append(jnp.where(row < group // 2, pltpu.roll(turned, group - moved, 0), 0.0))
        right.append(jnp.where(row >= group // 2, pltpu.roll(turned, group // 2 - moved, 0), 0.0))
    pairs = sections // 2
    first_core = section % 2 == 0
    for half, rest in enumerate((left, right)):
        sources = [jnp.concatenate([full[j], rest[j]], axis=0) for j in range(2 * sections)]
        quarters = [jnp.concatenate(sources[q * pairs : (q + 1) * pairs], axis=0) for q in range(4)]
        quarters = [
            quarters[0],
            quarters[3],
            jnp.where(first_core, quarters[1], quarters[2]),
            jnp.where(first_core, quarters[2], quarters[1]),
        ]
        high, low = split_two(jnp.concatenate(quarters, axis=0).T)
        out_ref[half] = jnp.concatenate([high, low], axis=1)


def fold_operator(section, own, partner, dims, sections, group, each):
    beams = dims[-1]
    width = sections * group
    return pl.pallas_call(
        functools.partial(operator_kernel, dims=dims, sections=sections, group=group, each=each),
        out_shape=jax.ShapeDtypeStruct((2, 2 * beams, 8 * width), BF16),
        in_specs=[
            pl.BlockSpec(memory_space=pltpu.SMEM),
            pl.BlockSpec(memory_space=pltpu.VMEM),
            pl.BlockSpec(memory_space=pltpu.VMEM),
        ],
        scratch_shapes=[pltpu.VMEM((width, beams), F32)],
        compiler_params=pltpu.CompilerParams(vmem_limit_bytes=16 * 1024 * 1024),
        name="fold_operator",
    )(section, own, partner)


def correlate(rows, even, odd, table, blocks, group):
    extra = table.shape[0] // (2 * LANE) - 1
    total = blocks + extra
    held = [
        jnp.concatenate(
            [rows[:group, b * LANE : (b + 1) * LANE], rows[group:, b * LANE : (b + 1) * LANE]], axis=1
        )
        for b in range(total)
    ]
    for b in range(0, total, 2):
        even[b * group : (b + 2) * group] = jnp.concatenate(held[b : b + 2], axis=0).astype(BF16)
    for b in range(1, total - 1, 2):
        odd[(b - 1) * group : (b + 1) * group] = jnp.concatenate(held[b : b + 2], axis=0).astype(BF16)
    window = blocks * group
    pieces = []
    for lag in range(extra + 1):
        source, at = (even, lag) if lag % 2 == 0 else (odd, lag - 1)
        pieces.append(source[at * group : at * group + window])
    return jnp.dot(jnp.concatenate(pieces, axis=1), table[...], preferred_element_type=F32)


def as_chunk(done, s, chunk, group, each):
    real, imag = [
        jnp.concatenate(
            [
                done[(s * chunk + b) * group : (s * chunk + b + 1) * group, c * LANE : (c + 1) * LANE]
                for b in range(chunk)
            ],
            axis=1,
        )
        for c in range(2)
    ]
    middle = chunk * LANE // 2
    lead, moved = pack_rows_of(real, imag, each)
    row = lax.broadcasted_iota(jnp.int32, (group, middle), 0)
    rest = jnp.where(
        row < group // 2,
        pltpu.roll(imag[:, :middle], group - moved, 0),
        pltpu.roll(imag[:, middle:], group // 2 - moved, 0),
    )
    return jnp.concatenate([lead[:, :middle], lead[:, middle:], rest], axis=0).astype(BF16)


def begin_kernel(echo_ref, chirp_ref, early_ref, late_ref, table, rows, even, odd, *, group):
    pulses, _, length = echo_ref.shape
    extra = chirp_ref.shape[1] // LANE
    reverse = LANE - 1 - lax.broadcasted_iota(jnp.int32, (2, LANE), 1)
    below = lax.broadcasted_iota(jnp.int32, (LANE, LANE), 1) <= lax.broadcasted_iota(
        jnp.int32, (LANE, LANE), 0
    )
    before = [jnp.zeros((LANE, LANE), F32)] * 2
    for lag in range(extra + 1):
        if lag < extra:
            piece = chirp_ref[:, lag * LANE : (lag + 1) * LANE].astype(F32)
            piece = jnp.take_along_axis(piece, reverse, axis=1, mode="promise_in_bounds")
            turned = [
                pltpu.roll(
                    jnp.broadcast_to(piece[c : c + 1], (LANE, LANE)), 1, 1, stride=1, stride_axis=0
                )
                for c in range(2)
            ]
        else:
            turned = [jnp.zeros((LANE, LANE), F32)] * 2
        real, imag = [jnp.where(below, turned[c], before[c]) for c in range(2)]
        before = turned
        at = lag * 2 * LANE
        table[at : at + LANE, :LANE] = real.astype(BF16)
        table[at : at + LANE, LANE:] = (-imag).astype(BF16)
        table[at + LANE : at + 2 * LANE, :LANE] = imag.astype(BF16)
        table[at + LANE : at + 2 * LANE, LANE:] = real.astype(BF16)
    rows[...] = jnp.zeros_like(rows)
    for p in range(pulses):
        near = echo_ref[p].astype(F32)
        for c in range(2):
            rows[c * group + p : c * group + p + 1, :] = near[c : c + 1]
    late_ref[...] = rows[:, length - late_ref.shape[1] :]
    done = correlate(rows, even, odd, table, length // LANE - extra, group)
    for s in range(early_ref.shape[0]):
        early_ref[s] = as_chunk(done, s, 2 * early_ref.shape[2] // LANE, group, pulses)


def finish_kernel(index_ref, early_ref, late_ref, halo_ref, table, keep_ref, give_ref, rows, even, odd, *, group):
    pulses = halo_ref.shape[0]
    span = late_ref.shape[1]
    taps = halo_ref.shape[2]
    ready = early_ref.shape[0]
    chunk = 2 * early_ref.shape[2]
    sections = ready + span // chunk
    section = lax.rem(index_ref[0], sections)
    has_next = index_ref[0] >= sections
    rows[:, :span] = late_ref[...]
    rows[:, span:] = jnp.zeros((2 * group, taps), F32)
    for p in range(pulses):
        far = jnp.where(has_next, halo_ref[p].astype(F32), 0.0)
        for c in range(2):
            rows[c * group + p : c * group + p + 1, span:] = far[c : c + 1]
    done = correlate(rows, even, odd, table, span // LANE, group)
    for s in range(sections):
        stacked = early_ref[s] if s < ready else as_chunk(done, s - ready, chunk // LANE, group, pulses)
        slot = section ^ s
        far_chunk, other_core = slot // 2, slot % 2
        place = far_chunk ^ 1 ^ (section % 2) ^ other_core

        @pl.when(other_core == 0)
        def _():
            keep_ref[place] = stacked

        @pl.when(other_core == 1)
        def _():
            give_ref[place] = stacked


def row_scratch(blocks, group):
    return [
        pltpu.VMEM((2 * group, blocks * LANE), F32),
        pltpu.VMEM((blocks * group, 2 * LANE), BF16),
        pltpu.VMEM((blocks * group, 2 * LANE), BF16),
    ]


def begin_compression(echo, chirp, sections, group):
    _, _, length = echo.shape
    taps = chirp.shape[1]
    chunk = length // sections
    early = (length - taps) // chunk
    return pl.pallas_call(
        functools.partial(begin_kernel, group=group),
        out_shape=(
            jax.ShapeDtypeStruct((early, 3 * group, chunk // 2), BF16),
            jax.ShapeDtypeStruct((2 * group, length - early * chunk), F32),
            jax.ShapeDtypeStruct(((taps // LANE + 1) * 2 * LANE, 2 * LANE), BF16),
        ),
        scratch_shapes=row_scratch(length // LANE, group),
        compiler_params=pltpu.CompilerParams(vmem_limit_bytes=24 * 1024 * 1024),
        name="begin_compression",
    )(echo, chirp)


def finish_compression(place, early, late, halo, table, group):
    blocks = late.shape[1] // LANE + table.shape[0] // (2 * LANE) - 1
    return pl.pallas_call(
        functools.partial(finish_kernel, group=group),
        out_shape=[jax.ShapeDtypeStruct((2, *early.shape[1:]), BF16)] * 2,
        in_specs=[pl.BlockSpec(memory_space=pltpu.SMEM)] + [pl.BlockSpec(memory_space=pltpu.VMEM)] * 4,
        scratch_shapes=row_scratch(blocks, group),
        compiler_params=pltpu.CompilerParams(vmem_limit_bytes=24 * 1024 * 1024),
        name="finish_compression",
    )(place, early, late, halo, table)


def image_kernel(index_ref, operator_ref, both_ref, *refs, group):
    chunks, (out_ref, parts, sems) = refs[:-3], refs[-3:]
    count, _, tile = parts.shape
    width = both_ref.shape[2]
    near = 1 - index_ref[0] % 2
    held = [both_ref[near]] + [chunk[...] for chunk in chunks]
    held = [value.astype(F32) for value in held]
    copies = []
    for i in range(count):
        half, at = divmod(i * tile, width)
        rows = []
        for value in held:
            for first in range(0, value.shape[0], 3 * group):
                rows.append(value[first + half * group : first + (half + 1) * group, at : at + tile])
                rows.append(value[first + 2 * group : first + 3 * group, at : at + tile])
        pulses = jnp.concatenate(rows, axis=0).astype(BF16)
        result = jnp.dot(
            operator_ref[half], jnp.concatenate([pulses, pulses], axis=0), preferred_element_type=F32
        )
        parts[i] = result.astype(BF16)
        copy = pltpu.make_async_copy(parts.at[i], out_ref.at[:, i * tile : (i + 1) * tile], sems.at[i])
        copy.start()
        copies.append(copy)
    for copy in copies:
        copy.wait()


def form_image(section, operator, both, chunks, group):
    height, half = operator.shape[1], both.shape[2]
    tile = 256 if half % 256 == 0 else half
    count = 2 * half // tile
    return pl.pallas_call(
        functools.partial(image_kernel, group=group),
        out_shape=jax.ShapeDtypeStruct((height, 2 * half), BF16),
        in_specs=[pl.BlockSpec(memory_space=pltpu.SMEM)]
        + [pl.BlockSpec(memory_space=pltpu.VMEM)] * (2 + len(chunks)),
        out_specs=pl.BlockSpec(memory_space=pl.ANY),
        scratch_shapes=[
            pltpu.VMEM((count, height, tile), BF16),
            pltpu.SemaphoreType.DMA((count,)),
        ],
        compiler_params=pltpu.CompilerParams(vmem_limit_bytes=16 * 1024 * 1024),
        name="form_image",
    )(section, operator, both, *chunks)


def swap(value, axis, by):
    count = lax.axis_size(axis)
    return lax.ppermute(value, axis, [(i, i ^ by) for i in range(count)])


def swap_by(value, move):
    sections, subs = lax.axis_size("section"), lax.axis_size("sub")
    pairs = []
    for s in range(sections):
        for a in range(subs):
            to_s, to_a = move(s, a)
            pairs.append((s * subs + a, to_s * subs + to_a))
    return lax.ppermute(value, ("section", "sub"), pairs)


def from_next(value, axis):
    count = lax.axis_size(axis)
    return lax.ppermute(value, axis, [(i, (i - 1) % count) for i in range(count)])


def on_device(echoes, chirp, steer, pulse_order, band_coef, band_start, band_width):
    sections, subs = lax.axis_size("section"), lax.axis_size("sub")
    pulses_each = echoes.shape[2]
    group = ceil_to(pulses_each, SUBL)
    section = lax.axis_index("section").astype(jnp.int32).reshape(1)
    coef = jnp.swapaxes(band_coef, 4, 5)
    weights = jnp.swapaxes(steer, 2, 3)
    levels, _, sides, parts, taps, beams = coef.shape
    dims = (levels, sides, parts, taps, beams)

    echo = jnp.transpose(echoes[:, 0], (1, 0, 2))
    echo, rim, chirp, packed = prepare(
        echo, chirp, coef, band_start, band_width, weights, pulse_order, sections, group
    )
    halo = from_next(rim, "rng")
    has_next = (lax.axis_index("rng") < lax.axis_size("rng") - 1).astype(jnp.int32)
    if subs == 2:
        packed_partner = swap(packed, "sub", 1)
    early, late, table = begin_compression(echo, chirp, sections, group)
    place = section + sections * has_next
    keep, give = finish_compression(place, early, late, halo, table, group)
    both = jnp.concatenate([keep, swap(give, "section", 1)], axis=1)
    far = lax.dynamic_index_in_dim(both, section[0] % 2, 0, keepdims=False)
    if subs != 2:
        near = lax.dynamic_index_in_dim(both, 1 - section[0] % 2, 0, keepdims=False)
        chunks = [near, swap(far, "section", 2)]
        return merge_images(section, chunks, packed, dims, sections, group, pulses_each)
    chunks = [
        swap_by(far, lambda s, a: (s ^ 2, a ^ 1)),
        swap_by(both[0], lambda s, a: (s, a ^ 1) if s % 2 else (s ^ 2, a)),
        swap_by(both[1], lambda s, a: (s ^ 2, a) if s % 2 else (s, a ^ 1)),
    ]
    operator = fold_operator(section, packed, packed_partner, dims, sections, group, pulses_each)
    image = form_image(section, operator, both, chunks, group)
    return image.reshape(2, beams, 1, image.shape[1])


def unpack(chunk, group, each):
    lead = jnp.concatenate([chunk[:group], chunk[group : 2 * group]], axis=1)
    moved, rest = group - each, chunk[2 * group :]
    tail = jnp.concatenate([rest[: each - moved], rest[group // 2 : group // 2 + each - moved]], axis=1)
    return jnp.concatenate([lead, tail], axis=0)


def merge_images(section, chunks, packed, dims, sections, group, each):
    levels, sides, parts, taps, beams = dims
    width = sections * group
    first = levels * sides * parts * taps
    table = packed[first : first + parts * width].reshape(parts, sections, group, beams)
    table = jnp.take(table, section[0] ^ jnp.arange(sections), axis=1)[:, :, :each]
    chunks = [
        unpack(chunk[first : first + 3 * group], group, each)
        for chunk in chunks
        for first in range(0, chunk.shape[0], 3 * group)
    ]
    real, imag = table[0], table[1]
    rows = jnp.concatenate(
        [jnp.concatenate([real, -imag], axis=1), jnp.concatenate([imag, real], axis=1)], axis=2
    )
    image = lax.dot_general(
        rows.reshape(-1, 2 * beams), jnp.concatenate(chunks, axis=0), (((0,), (0,)), ((), ())), preferred_element_type=F32
    ).astype(BF16)
    starts = packed[first + parts * width :].astype(jnp.int32)
    column = jnp.arange(beams, dtype=jnp.int32)
    bits = lax.axis_size("sub").bit_length() - 1
    for level in range(levels):
        partner = swap(image, "sub", 1 << (level % bits))
        operands = []
        for side in range(sides):
            at = (level * sides + side) * parts * taps
            coef = packed[at : at + parts * taps].reshape(parts, taps, beams)
            offset = column[:, None] - starts[level * sides + side][None, :]
            hits = (offset[None] == jnp.arange(taps, dtype=jnp.int32)[:, None, None]).astype(BF16)
            operands.append(jnp.einsum("ptq,tcq->pqc", coef, hits, preferred_element_type=F32).astype(BF16))
        top = jnp.concatenate([operands[0][0], -operands[0][1], operands[1][0], -operands[1][1]], axis=1)
        low = jnp.concatenate([operands[0][1], operands[0][0], operands[1][1], operands[1][0]], axis=1)
        image = jnp.dot(
            jnp.concatenate([top, low], axis=0),
            jnp.concatenate([image, partner], axis=0),
            preferred_element_type=F32,
        ).astype(BF16)
    return image.reshape(2, beams, 1, image.shape[1])


def solution(mesh):
    return jax.shard_map(
        on_device,
        mesh=mesh,
        in_specs=(
            P(None, "sub", "section", "rng"),
            P(),
            P(None, "sub", None, None),
            P("sub", None),
            P(None, "sub", None, None, None, None),
            P(None, "sub", None, None),
            P(None, "sub", None, None),
        ),
        out_specs=P(None, "sub", "rng", "section"),
        check_vma=False,
    )
```

```python
import functools

import jax
import jax.numpy as jnp
from jax import lax
from jax.experimental import pallas as pl
from jax.experimental.pallas import tpu as pltpu
from jax.sharding import PartitionSpec as P

LANE = 128
SUBL = 8
F32 = jnp.float32
BF16 = jnp.bfloat16


def ceil_to(value, unit):
    return -(-value // unit) * unit


def prepare_kernel(*refs, sections, group):
    sources, (echo_out, chirp_out, pack_ref), scratch = refs[:7], refs[7:10], refs[10:]
    coef_ref, start_ref, width_ref, steer_ref, order_ref, starts, sems = scratch
    targets = (echo_out, coef_ref, start_ref, width_ref, steer_ref, order_ref, chirp_out)
    loads = [
        pltpu.make_async_copy(source, target, sems.at[i])
        for i, (source, target) in enumerate(zip(sources, targets))
    ]
    for load in loads:
        load.start()
    for load in loads:
        load.wait()
    levels, _, sides, parts, taps, beams = coef_ref.shape
    tap = lax.broadcasted_iota(jnp.int32, (taps, beams), 0)
    row = 0
    for level in range(levels):
        for side in range(sides):
            used = tap < width_ref[level, 0, side : side + 1, :]
            for part in range(parts):
                entries = coef_ref[level, 0, side, part].astype(F32)
                pack_ref[row : row + taps] = jnp.where(used, entries, 0.0).astype(BF16)
                row += taps
    pulses = order_ref.shape[1]
    each = pulses // sections
    position = lax.broadcasted_iota(jnp.int32, (pulses, pulses), 0)
    hit = (position == order_ref[0:1, :]).astype(F32)
    slot = lax.broadcasted_iota(jnp.int32, (sections * group, pulses), 0)
    pulse = lax.broadcasted_iota(jnp.int32, (sections * group, pulses), 1)
    place = jnp.zeros((sections * group, pulses), F32)
    for s in range(sections):
        inside = (pulse >= s * each) & (pulse < (s + 1) * each)
        place = jnp.where(inside & (slot - s * group == pulse - s * each), 1.0, place)
    pick = lax.dot_general(
        place.astype(BF16), hit.astype(BF16), (((1,), (1,)), ((), ())), preferred_element_type=F32
    )
    for part in range(parts):
        chosen = jnp.dot(pick.astype(BF16), steer_ref[part, 0], preferred_element_type=F32)
        pack_ref[row : row + sections * group] = chosen.astype(BF16)
        row += sections * group
    starts[...] = jnp.zeros_like(starts)
    for level in range(levels):
        starts[sides * level : sides * level + sides] = start_ref[level, 0].astype(F32)
    pack_ref[row : row + starts.shape[0]] = starts[...].astype(BF16)


def pack_rows(levels, sides, parts, taps, sections, group):
    return levels * sides * parts * taps + parts * sections * group + ceil_to(levels * sides, 16)


def prepare(echo, chirp, coef, start, width, steer, order, sections, group):
    levels, _, sides, parts, taps, beams = coef.shape
    sources = (echo, coef, start, width, steer, order, chirp)
    return pl.pallas_call(
        functools.partial(prepare_kernel, sections=sections, group=group),
        out_shape=(
            jax.ShapeDtypeStruct(echo.shape, BF16),
            jax.ShapeDtypeStruct(chirp.shape, BF16),
            jax.ShapeDtypeStruct((pack_rows(levels, sides, parts, taps, sections, group), beams), BF16),
        ),
        in_specs=[pl.BlockSpec(memory_space=pl.ANY)] * len(sources),
        scratch_shapes=[pltpu.VMEM(x.shape, x.dtype) for x in sources[1:6]]
        + [pltpu.VMEM((ceil_to(levels * sides, 16), beams), F32), pltpu.SemaphoreType.DMA((len(sources),))],
        compiler_params=pltpu.CompilerParams(vmem_limit_bytes=16 * 1024 * 1024),
        name="prepare",
    )(*[pltpu.with_memory_space_constraint(x, pltpu.HBM) for x in sources])


def pack_rows_of(real, imag, each):
    group = real.shape[0]
    row = lax.broadcasted_iota(jnp.int32, real.shape, 0)
    return jnp.where(row < each, real, pltpu.roll(imag, each, 0)), group - each


def split_two(value):
    high = value.astype(BF16)
    return high, (value - high.astype(F32)).astype(BF16)


def operator_kernel(index_ref, own_ref, partner_ref, out_ref, weights, *, dims, sections, group, each):
    levels, sides, parts, taps, beams = dims
    width = sections * group
    refs = (own_ref, partner_ref)
    weight_row = levels * sides * parts * taps
    start_row = weight_row + parts * width

    def band(ref, level, side):
        first = ((level * sides + side) * parts) * taps
        tables = [ref[first + p * taps : first + (p + 1) * taps].astype(F32) for p in range(parts)]
        start = ref[start_row : start_row + ceil_to(levels * sides, 16)].astype(F32)
        start = start[level * sides + side : level * sides + side + 1].astype(jnp.int32)
        found = [[], []]
        for c in range(0, beams, SUBL):
            column = lax.broadcasted_iota(jnp.int32, (SUBL, beams), 0) + c
            offset = column - start
            spot = offset & (SUBL - 1)
            for p in range(parts):
                value = jnp.zeros((SUBL, beams), F32)
                for t in range(0, taps, SUBL):
                    got = jnp.take_along_axis(
                        tables[p][t : t + SUBL], spot, axis=0, mode="promise_in_bounds"
                    )
                    value = jnp.where((offset >= t) & (offset < t + SUBL), got, value)
                found[p].append(value)
        return [jnp.concatenate(f, axis=0) for f in found]

    def complex_operand(real, imag):
        top = jnp.concatenate([real, imag], axis=1)
        low = jnp.concatenate([-imag, real], axis=1)
        return jnp.concatenate([top, low], axis=0).astype(BF16)

    section = index_ref[0]
    images = []
    for a in range(2):
        for p in range(parts):
            weights[...] = refs[a][weight_row + p * width : weight_row + (p + 1) * width].astype(F32)
            rows = []
            for j in range(sections):
                at = pl.multiple_of((section ^ j) * group, group)
                rows.append(weights[pl.ds(at, group)])
            images.append(jnp.concatenate(rows, axis=0))
    zero = jnp.zeros((width, 2 * beams), F32)
    own = jnp.concatenate([jnp.concatenate(images[0:2], axis=1), zero], axis=0)
    partner = jnp.concatenate([zero, jnp.concatenate(images[2:4], axis=1)], axis=0)
    for level in range(levels):
        own_high, own_low = split_two(own)
        partner_high, partner_low = split_two(partner)
        own_rows = jnp.concatenate([own_high, own_low], axis=0)
        partner_rows = jnp.concatenate([partner_high, partner_low], axis=0)

        def merged(ref, mine, other):
            product = jnp.dot(
                mine, complex_operand(*band(ref, level, 0)), preferred_element_type=F32
            ) + jnp.dot(other, complex_operand(*band(ref, level, 1)), preferred_element_type=F32)
            return product[: 2 * width] + product[2 * width :]

        following = merged(own_ref, own_rows, partner_rows)
        if level < levels - 1:
            partner = merged(partner_ref, partner_rows, own_rows)
        own = following
    full, left, right = [], [], []
    for j in range(2 * sections):
        real = own[j * group : (j + 1) * group, :beams]
        imag = own[j * group : (j + 1) * group, beams:]
        straight = jnp.concatenate([real, imag], axis=1)
        turned = jnp.concatenate([-imag, real], axis=1)
        lead, moved = pack_rows_of(straight, turned, each)
        row = lax.broadcasted_iota(jnp.int32, lead.shape, 0)
        full.append(lead)
        left.append(jnp.where(row < group // 2, pltpu.roll(turned, group - moved, 0), 0.0))
        right.append(jnp.where(row >= group // 2, pltpu.roll(turned, group // 2 - moved, 0), 0.0))
    pairs = sections // 2
    first_core = section % 2 == 0
    for half, rest in enumerate((left, right)):
        sources = [jnp.concatenate([full[j], rest[j]], axis=0) for j in range(2 * sections)]
        quarters = [jnp.concatenate(sources[q * pairs : (q + 1) * pairs], axis=0) for q in range(4)]
        quarters = [
            quarters[0],
            quarters[3],
            jnp.where(first_core, quarters[1], quarters[2]),
            jnp.where(first_core, quarters[2], quarters[1]),
        ]
        high, low = split_two(jnp.concatenate(quarters, axis=0).T)
        out_ref[half] = jnp.concatenate([high, low], axis=1)


def fold_operator(section, own, partner, dims, sections, group, each):
    beams = dims[-1]
    width = sections * group
    return pl.pallas_call(
        functools.partial(operator_kernel, dims=dims, sections=sections, group=group, each=each),
        out_shape=jax.ShapeDtypeStruct((2, 2 * beams, 8 * width), BF16),
        in_specs=[
            pl.BlockSpec(memory_space=pltpu.SMEM),
            pl.BlockSpec(memory_space=pltpu.VMEM),
            pl.BlockSpec(memory_space=pltpu.VMEM),
        ],
        scratch_shapes=[pltpu.VMEM((width, beams), F32)],
        compiler_params=pltpu.CompilerParams(vmem_limit_bytes=16 * 1024 * 1024),
        name="fold_operator",
    )(section, own, partner)


def correlate(rows, even, odd, table, blocks, group):
    extra = table.shape[0] // (2 * LANE) - 1
    total = blocks + extra
    held = [
        jnp.concatenate(
            [rows[:group, b * LANE : (b + 1) * LANE], rows[group:, b * LANE : (b + 1) * LANE]], axis=1
        )
        for b in range(total)
    ]
    for b in range(0, total, 2):
        even[b * group : (b + 2) * group] = jnp.concatenate(held[b : b + 2], axis=0).astype(BF16)
    for b in range(1, total - 1, 2):
        odd[(b - 1) * group : (b + 1) * group] = jnp.concatenate(held[b : b + 2], axis=0).astype(BF16)
    window = blocks * group
    pieces = []
    for lag in range(extra + 1):
        source, at = (even, lag) if lag % 2 == 0 else (odd, lag - 1)
        pieces.append(source[at * group : at * group + window])
    return jnp.dot(jnp.concatenate(pieces, axis=1), table[...], preferred_element_type=F32)


def as_chunk(done, s, chunk, group, each):
    real, imag = [
        jnp.concatenate(
            [
                done[(s * chunk + b) * group : (s * chunk + b + 1) * group, c * LANE : (c + 1) * LANE]
                for b in range(chunk)
            ],
            axis=1,
        )
        for c in range(2)
    ]
    middle = chunk * LANE // 2
    lead, moved = pack_rows_of(real, imag, each)
    row = lax.broadcasted_iota(jnp.int32, (group, middle), 0)
    rest = jnp.where(
        row < group // 2,
        pltpu.roll(imag[:, :middle], group - moved, 0),
        pltpu.roll(imag[:, middle:], group // 2 - moved, 0),
    )
    return jnp.concatenate([lead[:, :middle], lead[:, middle:], rest], axis=0).astype(BF16)


def begin_kernel(echo_ref, chirp_ref, early_ref, late_ref, table, rows, even, odd, *, group):
    pulses, _, length = echo_ref.shape
    extra = chirp_ref.shape[1] // LANE
    reverse = LANE - 1 - lax.broadcasted_iota(jnp.int32, (2, LANE), 1)
    below = lax.broadcasted_iota(jnp.int32, (LANE, LANE), 1) <= lax.broadcasted_iota(
        jnp.int32, (LANE, LANE), 0
    )
    before = [jnp.zeros((LANE, LANE), F32)] * 2
    for lag in range(extra + 1):
        if lag < extra:
            piece = chirp_ref[:, lag * LANE : (lag + 1) * LANE].astype(F32)
            piece = jnp.take_along_axis(piece, reverse, axis=1, mode="promise_in_bounds")
            turned = [
                pltpu.roll(
                    jnp.broadcast_to(piece[c : c + 1], (LANE, LANE)), 1, 1, stride=1, stride_axis=0
                )
                for c in range(2)
            ]
        else:
            turned = [jnp.zeros((LANE, LANE), F32)] * 2
        real, imag = [jnp.where(below, turned[c], before[c]) for c in range(2)]
        before = turned
        at = lag * 2 * LANE
        table[at : at + LANE, :LANE] = real.astype(BF16)
        table[at : at + LANE, LANE:] = (-imag).astype(BF16)
        table[at + LANE : at + 2 * LANE, :LANE] = imag.astype(BF16)
        table[at + LANE : at + 2 * LANE, LANE:] = real.astype(BF16)
    rows[...] = jnp.zeros_like(rows)
    for p in range(pulses):
        near = echo_ref[p].astype(F32)
        for c in range(2):
            rows[c * group + p : c * group + p + 1, :] = near[c : c + 1]
    late_ref[...] = rows[:, length - late_ref.shape[1] :]
    done = correlate(rows, even, odd, table, length // LANE - extra, group)
    for s in range(early_ref.shape[0]):
        early_ref[s] = as_chunk(done, s, 2 * early_ref.shape[2] // LANE, group, pulses)


def finish_kernel(index_ref, early_ref, late_ref, halo_ref, table, keep_ref, give_ref, rows, even, odd, *, group):
    pulses = halo_ref.shape[0]
    span = late_ref.shape[1]
    taps = rows.shape[1] - span
    ready = early_ref.shape[0]
    chunk = 2 * early_ref.shape[2]
    sections = ready + span // chunk
    section = lax.rem(index_ref[0], sections)
    has_next = index_ref[0] >= sections
    rows[:, :span] = late_ref[...]
    rows[:, span:] = jnp.zeros((2 * group, taps), F32)
    for p in range(pulses):
        far = jnp.where(has_next, halo_ref[p, :, :taps].astype(F32), 0.0)
        for c in range(2):
            rows[c * group + p : c * group + p + 1, span:] = far[c : c + 1]
    done = correlate(rows, even, odd, table, span // LANE, group)
    for s in range(sections):
        stacked = early_ref[s] if s < ready else as_chunk(done, s - ready, chunk // LANE, group, pulses)
        slot = section ^ s
        far_chunk, other_core = slot // 2, slot % 2
        place = far_chunk ^ 1 ^ (section % 2) ^ other_core

        @pl.when(other_core == 0)
        def _():
            keep_ref[place] = stacked

        @pl.when(other_core == 1)
        def _():
            give_ref[place] = stacked


def row_scratch(blocks, group):
    return [
        pltpu.VMEM((2 * group, blocks * LANE), F32),
        pltpu.VMEM((blocks * group, 2 * LANE), BF16),
        pltpu.VMEM((blocks * group, 2 * LANE), BF16),
    ]


def begin_compression(echo, chirp, sections, group):
    _, _, length = echo.shape
    taps = chirp.shape[1]
    chunk = length // sections
    early = (length - taps) // chunk
    return pl.pallas_call(
        functools.partial(begin_kernel, group=group),
        out_shape=(
            jax.ShapeDtypeStruct((early, 3 * group, chunk // 2), BF16),
            jax.ShapeDtypeStruct((2 * group, length - early * chunk), F32),
            jax.ShapeDtypeStruct(((taps // LANE + 1) * 2 * LANE, 2 * LANE), BF16),
        ),
        scratch_shapes=row_scratch(length // LANE, group),
        compiler_params=pltpu.CompilerParams(vmem_limit_bytes=24 * 1024 * 1024),
        name="begin_compression",
    )(echo, chirp)


def finish_compression(place, early, late, halo, table, group):
    blocks = late.shape[1] // LANE + table.shape[0] // (2 * LANE) - 1
    return pl.pallas_call(
        functools.partial(finish_kernel, group=group),
        out_shape=[jax.ShapeDtypeStruct((2, *early.shape[1:]), BF16)] * 2,
        in_specs=[pl.BlockSpec(memory_space=pltpu.SMEM)] + [pl.BlockSpec(memory_space=pltpu.VMEM)] * 4,
        scratch_shapes=row_scratch(blocks, group),
        compiler_params=pltpu.CompilerParams(vmem_limit_bytes=24 * 1024 * 1024),
        name="finish_compression",
    )(place, early, late, halo, table)


def image_kernel(index_ref, operator_ref, both_ref, *refs, group):
    chunks, (out_ref, parts, sems) = refs[:-3], refs[-3:]
    count, _, tile = parts.shape
    width = both_ref.shape[2]
    near = 1 - index_ref[0] % 2
    held = [both_ref[near]] + [chunk[...] for chunk in chunks]
    held = [value.astype(F32) for value in held]
    copies = []
    for i in range(count):
        half, at = divmod(i * tile, width)
        rows = []
        for value in held:
            for first in range(0, value.shape[0], 3 * group):
                rows.append(value[first + half * group : first + (half + 1) * group, at : at + tile])
                rows.append(value[first + 2 * group : first + 3 * group, at : at + tile])
        pulses = jnp.concatenate(rows, axis=0).astype(BF16)
        result = jnp.dot(
            operator_ref[half], jnp.concatenate([pulses, pulses], axis=0), preferred_element_type=F32
        )
        parts[i] = result.astype(BF16)
        copy = pltpu.make_async_copy(parts.at[i], out_ref.at[:, i * tile : (i + 1) * tile], sems.at[i])
        copy.start()
        copies.append(copy)
    for copy in copies:
        copy.wait()


def form_image(section, operator, both, chunks, group):
    height, half = operator.shape[1], both.shape[2]
    tile = 256 if half % 256 == 0 else half
    count = 2 * half // tile
    return pl.pallas_call(
        functools.partial(image_kernel, group=group),
        out_shape=jax.ShapeDtypeStruct((height, 2 * half), BF16),
        in_specs=[pl.BlockSpec(memory_space=pltpu.SMEM)]
        + [pl.BlockSpec(memory_space=pltpu.VMEM)] * (2 + len(chunks)),
        out_specs=pl.BlockSpec(memory_space=pl.ANY),
        scratch_shapes=[
            pltpu.VMEM((count, height, tile), BF16),
            pltpu.SemaphoreType.DMA((count,)),
        ],
        compiler_params=pltpu.CompilerParams(vmem_limit_bytes=16 * 1024 * 1024),
        name="form_image",
    )(section, operator, both, *chunks)


def swap(value, axis, by):
    count = lax.axis_size(axis)
    return lax.ppermute(value, axis, [(i, i ^ by) for i in range(count)])


def swap_by(value, move):
    sections, subs = lax.axis_size("section"), lax.axis_size("sub")
    pairs = []
    for s in range(sections):
        for a in range(subs):
            to_s, to_a = move(s, a)
            pairs.append((s * subs + a, to_s * subs + to_a))
    return lax.ppermute(value, ("section", "sub"), pairs)


def from_next(value, axis):
    count = lax.axis_size(axis)
    return lax.ppermute(value, axis, [(i, (i - 1) % count) for i in range(count)])


def on_device(echoes, chirp, steer, pulse_order, band_coef, band_start, band_width):
    sections, subs = lax.axis_size("section"), lax.axis_size("sub")
    pulses_each = echoes.shape[2]
    group = ceil_to(pulses_each, SUBL)
    section = lax.axis_index("section").astype(jnp.int32).reshape(1)
    coef = jnp.swapaxes(band_coef, 4, 5)
    weights = jnp.swapaxes(steer, 2, 3)
    levels, _, sides, parts, taps, beams = coef.shape
    dims = (levels, sides, parts, taps, beams)

    echo = jnp.transpose(echoes[:, 0], (1, 0, 2))
    halo = from_next(echo, "rng")
    echo, chirp, packed = prepare(
        echo, chirp, coef, band_start, band_width, weights, pulse_order, sections, group
    )
    has_next = (lax.axis_index("rng") < lax.axis_size("rng") - 1).astype(jnp.int32)
    if subs == 2:
        packed_partner = swap(packed, "sub", 1)
    early, late, table = begin_compression(echo, chirp, sections, group)
    place = section + sections * has_next
    keep, give = finish_compression(place, early, late, halo, table, group)
    both = jnp.concatenate([keep, swap(give, "section", 1)], axis=1)
    far = lax.dynamic_index_in_dim(both, section[0] % 2, 0, keepdims=False)
    if subs != 2:
        near = lax.dynamic_index_in_dim(both, 1 - section[0] % 2, 0, keepdims=False)
        chunks = [near, swap(far, "section", 2)]
        return merge_images(section, chunks, packed, dims, sections, group, pulses_each)
    chunks = [
        swap_by(far, lambda s, a: (s ^ 2, a ^ 1)),
        swap_by(both[0], lambda s, a: (s, a ^ 1) if s % 2 else (s ^ 2, a)),
        swap_by(both[1], lambda s, a: (s ^ 2, a) if s % 2 else (s, a ^ 1)),
    ]
    operator = fold_operator(section, packed, packed_partner, dims, sections, group, pulses_each)
    image = form_image(section, operator, both, chunks, group)
    return image.reshape(2, beams, 1, image.shape[1])


def unpack(chunk, group, each):
    lead = jnp.concatenate([chunk[:group], chunk[group : 2 * group]], axis=1)
    moved, rest = group - each, chunk[2 * group :]
    tail = jnp.concatenate([rest[: each - moved], rest[group // 2 : group // 2 + each - moved]], axis=1)
    return jnp.concatenate([lead, tail], axis=0)


def merge_images(section, chunks, packed, dims, sections, group, each):
    levels, sides, parts, taps, beams = dims
    width = sections * group
    first = levels * sides * parts * taps
    table = packed[first : first + parts * width].reshape(parts, sections, group, beams)
    table = jnp.take(table, section[0] ^ jnp.arange(sections), axis=1)[:, :, :each]
    chunks = [
        unpack(chunk[first : first + 3 * group], group, each)
        for chunk in chunks
        for first in range(0, chunk.shape[0], 3 * group)
    ]
    real, imag = table[0], table[1]
    rows = jnp.concatenate(
        [jnp.concatenate([real, -imag], axis=1), jnp.concatenate([imag, real], axis=1)], axis=2
    )
    image = lax.dot_general(
        rows.reshape(-1, 2 * beams), jnp.concatenate(chunks, axis=0), (((0,), (0,)), ((), ())), preferred_element_type=F32
    ).astype(BF16)
    starts = packed[first + parts * width :].astype(jnp.int32)
    column = jnp.arange(beams, dtype=jnp.int32)
    bits = lax.axis_size("sub").bit_length() - 1
    for level in range(levels):
        partner = swap(image, "sub", 1 << (level % bits))
        operands = []
        for side in range(sides):
            at = (level * sides + side) * parts * taps
            coef = packed[at : at + parts * taps].reshape(parts, taps, beams)
            offset = column[:, None] - starts[level * sides + side][None, :]
            hits = (offset[None] == jnp.arange(taps, dtype=jnp.int32)[:, None, None]).astype(BF16)
            operands.append(jnp.einsum("ptq,tcq->pqc", coef, hits, preferred_element_type=F32).astype(BF16))
        top = jnp.concatenate([operands[0][0], -operands[0][1], operands[1][0], -operands[1][1]], axis=1)
        low = jnp.concatenate([operands[0][1], operands[0][0], operands[1][1], operands[1][0]], axis=1)
        image = jnp.dot(
            jnp.concatenate([top, low], axis=0),
            jnp.concatenate([image, partner], axis=0),
            preferred_element_type=F32,
        ).astype(BF16)
    return image.reshape(2, beams, 1, image.shape[1])


def solution(mesh):
    return jax.shard_map(
        on_device,
        mesh=mesh,
        in_specs=(
            P(None, "sub", "section", "rng"),
            P(),
            P(None, "sub", None, None),
            P("sub", None),
            P(None, "sub", None, None, None, None),
            P(None, "sub", None, None),
            P(None, "sub", None, None),
        ),
        out_specs=P(None, "sub", "rng", "section"),
        check_vma=False,
    )
```

```python
import functools

import jax
import jax.numpy as jnp
from jax import lax
from jax.experimental import pallas as pl
from jax.experimental.pallas import tpu as pltpu
from jax.sharding import PartitionSpec as P

LANE = 128
SUBL = 8
F32 = jnp.float32
BF16 = jnp.bfloat16


def ceil_to(value, unit):
    return -(-value // unit) * unit


def prepare_kernel(*refs, sections, group):
    sources, (echo_out, chirp_out, pack_ref), scratch = refs[:7], refs[7:10], refs[10:]
    coef_ref, start_ref, width_ref, steer_ref, order_ref, starts, sems = scratch
    targets = (echo_out, coef_ref, start_ref, width_ref, steer_ref, order_ref, chirp_out)
    loads = [
        pltpu.make_async_copy(source, target, sems.at[i])
        for i, (source, target) in enumerate(zip(sources, targets))
    ]
    for load in loads:
        load.start()
    for load in loads:
        load.wait()
    levels, _, sides, parts, taps, beams = coef_ref.shape
    tap = lax.broadcasted_iota(jnp.int32, (taps, beams), 0)
    row = 0
    for level in range(levels):
        for side in range(sides):
            used = tap < width_ref[level, 0, side : side + 1, :]
            for part in range(parts):
                entries = coef_ref[level, 0, side, part].astype(F32)
                pack_ref[row : row + taps] = jnp.where(used, entries, 0.0).astype(BF16)
                row += taps
    pulses = order_ref.shape[1]
    each = pulses // sections
    position = lax.broadcasted_iota(jnp.int32, (pulses, pulses), 0)
    hit = (position == order_ref[0:1, :]).astype(F32)
    slot = lax.broadcasted_iota(jnp.int32, (sections * group, pulses), 0)
    pulse = lax.broadcasted_iota(jnp.int32, (sections * group, pulses), 1)
    place = jnp.zeros((sections * group, pulses), F32)
    for s in range(sections):
        inside = (pulse >= s * each) & (pulse < (s + 1) * each)
        place = jnp.where(inside & (slot - s * group == pulse - s * each), 1.0, place)
    pick = lax.dot_general(
        place.astype(BF16), hit.astype(BF16), (((1,), (1,)), ((), ())), preferred_element_type=F32
    )
    for part in range(parts):
        chosen = jnp.dot(pick.astype(BF16), steer_ref[part, 0], preferred_element_type=F32)
        pack_ref[row : row + sections * group] = chosen.astype(BF16)
        row += sections * group
    starts[...] = jnp.zeros_like(starts)
    for level in range(levels):
        starts[sides * level : sides * level + sides] = start_ref[level, 0].astype(F32)
    pack_ref[row : row + starts.shape[0]] = starts[...].astype(BF16)


def pack_rows(levels, sides, parts, taps, sections, group):
    return levels * sides * parts * taps + parts * sections * group + ceil_to(levels * sides, 16)


def prepare(echo, chirp, coef, start, width, steer, order, sections, group):
    levels, _, sides, parts, taps, beams = coef.shape
    sources = (echo, coef, start, width, steer, order, chirp)
    return pl.pallas_call(
        functools.partial(prepare_kernel, sections=sections, group=group),
        out_shape=(
            jax.ShapeDtypeStruct(echo.shape, BF16),
            jax.ShapeDtypeStruct(chirp.shape, BF16),
            jax.ShapeDtypeStruct((pack_rows(levels, sides, parts, taps, sections, group), beams), BF16),
        ),
        in_specs=[pl.BlockSpec(memory_space=pl.ANY)] * len(sources),
        scratch_shapes=[pltpu.VMEM(x.shape, x.dtype) for x in sources[1:6]]
        + [pltpu.VMEM((ceil_to(levels * sides, 16), beams), F32), pltpu.SemaphoreType.DMA((len(sources),))],
        compiler_params=pltpu.CompilerParams(vmem_limit_bytes=16 * 1024 * 1024),
        name="prepare",
    )(*[pltpu.with_memory_space_constraint(x, pltpu.HBM) for x in sources])


def pack_rows_of(real, imag, each):
    group = real.shape[0]
    row = lax.broadcasted_iota(jnp.int32, real.shape, 0)
    return jnp.where(row < each, real, pltpu.roll(imag, each, 0)), group - each


def split_two(value):
    high = value.astype(BF16)
    return high, (value - high.astype(F32)).astype(BF16)


def operator_kernel(index_ref, own_ref, partner_ref, out_ref, weights, *, dims, sections, group, each):
    levels, sides, parts, taps, beams = dims
    width = sections * group
    refs = (own_ref, partner_ref)
    weight_row = levels * sides * parts * taps
    start_row = weight_row + parts * width

    def band(ref, level, side):
        first = ((level * sides + side) * parts) * taps
        tables = [ref[first + p * taps : first + (p + 1) * taps].astype(F32) for p in range(parts)]
        start = ref[start_row : start_row + ceil_to(levels * sides, 16)].astype(F32)
        start = start[level * sides + side : level * sides + side + 1].astype(jnp.int32)
        found = [[], []]
        for c in range(0, beams, SUBL):
            column = lax.broadcasted_iota(jnp.int32, (SUBL, beams), 0) + c
            offset = column - start
            spot = offset & (SUBL - 1)
            for p in range(parts):
                value = jnp.zeros((SUBL, beams), F32)
                for t in range(0, taps, SUBL):
                    got = jnp.take_along_axis(
                        tables[p][t : t + SUBL], spot, axis=0, mode="promise_in_bounds"
                    )
                    value = jnp.where((offset >= t) & (offset < t + SUBL), got, value)
                found[p].append(value)
        return [jnp.concatenate(f, axis=0) for f in found]

    def complex_operand(real, imag):
        top = jnp.concatenate([real, imag], axis=1)
        low = jnp.concatenate([-imag, real], axis=1)
        return jnp.concatenate([top, low], axis=0).astype(BF16)

    section = index_ref[0]
    images = []
    for a in range(2):
        for p in range(parts):
            weights[...] = refs[a][weight_row + p * width : weight_row + (p + 1) * width].astype(F32)
            rows = []
            for j in range(sections):
                at = pl.multiple_of((section ^ j) * group, group)
                rows.append(weights[pl.ds(at, group)])
            images.append(jnp.concatenate(rows, axis=0))
    zero = jnp.zeros((width, 2 * beams), F32)
    own = jnp.concatenate([jnp.concatenate(images[0:2], axis=1), zero], axis=0)
    partner = jnp.concatenate([zero, jnp.concatenate(images[2:4], axis=1)], axis=0)
    for level in range(levels):
        own_high, own_low = split_two(own)
        partner_high, partner_low = split_two(partner)
        own_rows = jnp.concatenate([own_high, own_low], axis=0)
        partner_rows = jnp.concatenate([partner_high, partner_low], axis=0)

        def merged(ref, mine, other):
            product = jnp.dot(
                mine, complex_operand(*band(ref, level, 0)), preferred_element_type=F32
            ) + jnp.dot(other, complex_operand(*band(ref, level, 1)), preferred_element_type=F32)
            return product[: 2 * width] + product[2 * width :]

        following = merged(own_ref, own_rows, partner_rows)
        if level < levels - 1:
            partner = merged(partner_ref, partner_rows, own_rows)
        own = following
    full, left, right = [], [], []
    for j in range(2 * sections):
        real = own[j * group : (j + 1) * group, :beams]
        imag = own[j * group : (j + 1) * group, beams:]
        straight = jnp.concatenate([real, imag], axis=1)
        turned = jnp.concatenate([-imag, real], axis=1)
        lead, moved = pack_rows_of(straight, turned, each)
        row = lax.broadcasted_iota(jnp.int32, lead.shape, 0)
        full.append(lead)
        left.append(jnp.where(row < group // 2, pltpu.roll(turned, group - moved, 0), 0.0))
        right.append(jnp.where(row >= group // 2, pltpu.roll(turned, group // 2 - moved, 0), 0.0))
    pairs = sections // 2
    first_core = section % 2 == 0
    for half, rest in enumerate((left, right)):
        sources = [jnp.concatenate([full[j], rest[j]], axis=0) for j in range(2 * sections)]
        quarters = [jnp.concatenate(sources[q * pairs : (q + 1) * pairs], axis=0) for q in range(4)]
        quarters = [
            quarters[0],
            quarters[3],
            jnp.where(first_core, quarters[1], quarters[2]),
            jnp.where(first_core, quarters[2], quarters[1]),
        ]
        high, low = split_two(jnp.concatenate(quarters, axis=0).T)
        out_ref[half] = jnp.concatenate([high, low], axis=1)


def fold_operator(section, own, partner, dims, sections, group, each):
    beams = dims[-1]
    width = sections * group
    return pl.pallas_call(
        functools.partial(operator_kernel, dims=dims, sections=sections, group=group, each=each),
        out_shape=jax.ShapeDtypeStruct((2, 2 * beams, 8 * width), BF16),
        in_specs=[
            pl.BlockSpec(memory_space=pltpu.SMEM),
            pl.BlockSpec(memory_space=pltpu.VMEM),
            pl.BlockSpec(memory_space=pltpu.VMEM),
        ],
        scratch_shapes=[pltpu.VMEM((width, beams), F32)],
        compiler_params=pltpu.CompilerParams(vmem_limit_bytes=16 * 1024 * 1024),
        name="fold_operator",
    )(section, own, partner)


def correlate(rows, even, odd, table, blocks, group):
    extra = table.shape[0] // (2 * LANE) - 1
    total = blocks + extra
    held = [
        jnp.concatenate(
            [rows[:group, b * LANE : (b + 1) * LANE], rows[group:, b * LANE : (b + 1) * LANE]], axis=1
        )
        for b in range(total)
    ]
    for b in range(0, total, 2):
        even[b * group : (b + 2) * group] = jnp.concatenate(held[b : b + 2], axis=0).astype(BF16)
    for b in range(1, total - 1, 2):
        odd[(b - 1) * group : (b + 1) * group] = jnp.concatenate(held[b : b + 2], axis=0).astype(BF16)
    window = blocks * group
    pieces = []
    for lag in range(extra + 1):
        source, at = (even, lag) if lag % 2 == 0 else (odd, lag - 1)
        pieces.append(source[at * group : at * group + window])
    return jnp.dot(jnp.concatenate(pieces, axis=1), table[...], preferred_element_type=F32)


def as_chunk(done, s, chunk, group, each):
    real, imag = [
        jnp.concatenate(
            [
                done[(s * chunk + b) * group : (s * chunk + b + 1) * group, c * LANE : (c + 1) * LANE]
                for b in range(chunk)
            ],
            axis=1,
        )
        for c in range(2)
    ]
    middle = chunk * LANE // 2
    lead, moved = pack_rows_of(real, imag, each)
    row = lax.broadcasted_iota(jnp.int32, (group, middle), 0)
    rest = jnp.where(
        row < group // 2,
        pltpu.roll(imag[:, :middle], group - moved, 0),
        pltpu.roll(imag[:, middle:], group // 2 - moved, 0),
    )
    return jnp.concatenate([lead[:, :middle], lead[:, middle:], rest], axis=0).astype(BF16)


def begin_kernel(echo_ref, chirp_ref, early_ref, late_ref, table, rows, even, odd, *, group):
    pulses, _, length = echo_ref.shape
    extra = chirp_ref.shape[1] // LANE
    reverse = LANE - 1 - lax.broadcasted_iota(jnp.int32, (2, LANE), 1)
    below = lax.broadcasted_iota(jnp.int32, (LANE, LANE), 1) <= lax.broadcasted_iota(
        jnp.int32, (LANE, LANE), 0
    )
    before = [jnp.zeros((LANE, LANE), F32)] * 2
    for lag in range(extra + 1):
        if lag < extra:
            piece = chirp_ref[:, lag * LANE : (lag + 1) * LANE].astype(F32)
            piece = jnp.take_along_axis(piece, reverse, axis=1, mode="promise_in_bounds")
            turned = [
                pltpu.roll(
                    jnp.broadcast_to(piece[c : c + 1], (LANE, LANE)), 1, 1, stride=1, stride_axis=0
                )
                for c in range(2)
            ]
        else:
            turned = [jnp.zeros((LANE, LANE), F32)] * 2
        real, imag = [jnp.where(below, turned[c], before[c]) for c in range(2)]
        before = turned
        at = lag * 2 * LANE
        table[at : at + LANE, :LANE] = real.astype(BF16)
        table[at : at + LANE, LANE:] = (-imag).astype(BF16)
        table[at + LANE : at + 2 * LANE, :LANE] = imag.astype(BF16)
        table[at + LANE : at + 2 * LANE, LANE:] = real.astype(BF16)
    rows[...] = jnp.zeros_like(rows)
    for p in range(pulses):
        near = echo_ref[p].astype(F32)
        for c in range(2):
            rows[c * group + p : c * group + p + 1, :] = near[c : c + 1]
    late_ref[...] = rows[:, length - late_ref.shape[1] :]
    done = correlate(rows, even, odd, table, length // LANE - extra, group)
    for s in range(early_ref.shape[0]):
        early_ref[s] = as_chunk(done, s, 2 * early_ref.shape[2] // LANE, group, pulses)


def finish_kernel(index_ref, early_ref, late_ref, halo_ref, table, keep_ref, give_ref, rows, even, odd, *, group):
    pulses = halo_ref.shape[0]
    span = late_ref.shape[1]
    taps = rows.shape[1] - span
    ready = early_ref.shape[0]
    chunk = 2 * early_ref.shape[2]
    sections = ready + span // chunk
    section = index_ref[0]
    rows[:, :span] = late_ref[...]
    rows[:, span:] = jnp.zeros((2 * group, taps), F32)
    for p in range(pulses):
        far = halo_ref[p, :, :taps].astype(F32)
        for c in range(2):
            rows[c * group + p : c * group + p + 1, span:] = far[c : c + 1]
    done = correlate(rows, even, odd, table, span // LANE, group)
    for s in range(sections):
        stacked = early_ref[s] if s < ready else as_chunk(done, s - ready, chunk // LANE, group, pulses)
        slot = section ^ s
        far_chunk, other_core = slot // 2, slot % 2
        place = far_chunk ^ 1 ^ (section % 2) ^ other_core

        @pl.when(other_core == 0)
        def _():
            keep_ref[place] = stacked

        @pl.when(other_core == 1)
        def _():
            give_ref[place] = stacked


def row_scratch(blocks, group):
    return [
        pltpu.VMEM((2 * group, blocks * LANE), F32),
        pltpu.VMEM((blocks * group, 2 * LANE), BF16),
        pltpu.VMEM((blocks * group, 2 * LANE), BF16),
    ]


def begin_compression(echo, chirp, sections, group):
    _, _, length = echo.shape
    taps = chirp.shape[1]
    chunk = length // sections
    early = (length - taps) // chunk
    return pl.pallas_call(
        functools.partial(begin_kernel, group=group),
        out_shape=(
            jax.ShapeDtypeStruct((early, 3 * group, chunk // 2), BF16),
            jax.ShapeDtypeStruct((2 * group, length - early * chunk), F32),
            jax.ShapeDtypeStruct(((taps // LANE + 1) * 2 * LANE, 2 * LANE), BF16),
        ),
        scratch_shapes=row_scratch(length // LANE, group),
        compiler_params=pltpu.CompilerParams(vmem_limit_bytes=24 * 1024 * 1024),
        name="begin_compression",
    )(echo, chirp)


def finish_compression(section, early, late, halo, table, group):
    blocks = late.shape[1] // LANE + table.shape[0] // (2 * LANE) - 1
    return pl.pallas_call(
        functools.partial(finish_kernel, group=group),
        out_shape=[jax.ShapeDtypeStruct((2, *early.shape[1:]), BF16)] * 2,
        in_specs=[pl.BlockSpec(memory_space=pltpu.SMEM)] + [pl.BlockSpec(memory_space=pltpu.VMEM)] * 4,
        scratch_shapes=row_scratch(blocks, group),
        compiler_params=pltpu.CompilerParams(vmem_limit_bytes=24 * 1024 * 1024),
        name="finish_compression",
    )(section, early, late, halo, table)


def image_kernel(index_ref, operator_ref, both_ref, *refs, group):
    chunks, (out_ref, parts, sems) = refs[:-3], refs[-3:]
    count, _, tile = parts.shape
    width = both_ref.shape[2]
    near = 1 - index_ref[0] % 2
    held = [both_ref[near]] + [chunk[...] for chunk in chunks]
    held = [value.astype(F32) for value in held]
    copies = []
    for i in range(count):
        half, at = divmod(i * tile, width)
        rows = []
        for value in held:
            for first in range(0, value.shape[0], 3 * group):
                rows.append(value[first + half * group : first + (half + 1) * group, at : at + tile])
                rows.append(value[first + 2 * group : first + 3 * group, at : at + tile])
        pulses = jnp.concatenate(rows, axis=0).astype(BF16)
        result = jnp.dot(
            operator_ref[half], jnp.concatenate([pulses, pulses], axis=0), preferred_element_type=F32
        )
        parts[i] = result.astype(BF16)
        copy = pltpu.make_async_copy(parts.at[i], out_ref.at[:, i * tile : (i + 1) * tile], sems.at[i])
        copy.start()
        copies.append(copy)
    for copy in copies:
        copy.wait()


def form_image(section, operator, both, chunks, group):
    height, half = operator.shape[1], both.shape[2]
    tile = 256 if half % 256 == 0 else half
    count = 2 * half // tile
    return pl.pallas_call(
        functools.partial(image_kernel, group=group),
        out_shape=jax.ShapeDtypeStruct((height, 2 * half), BF16),
        in_specs=[pl.BlockSpec(memory_space=pltpu.SMEM)]
        + [pl.BlockSpec(memory_space=pltpu.VMEM)] * (2 + len(chunks)),
        out_specs=pl.BlockSpec(memory_space=pl.ANY),
        scratch_shapes=[
            pltpu.VMEM((count, height, tile), BF16),
            pltpu.SemaphoreType.DMA((count,)),
        ],
        compiler_params=pltpu.CompilerParams(vmem_limit_bytes=16 * 1024 * 1024),
        name="form_image",
    )(section, operator, both, *chunks)


def swap(value, axis, by):
    count = lax.axis_size(axis)
    return lax.ppermute(value, axis, [(i, i ^ by) for i in range(count)])


def swap_by(value, move):
    sections, subs = lax.axis_size("section"), lax.axis_size("sub")
    pairs = []
    for s in range(sections):
        for a in range(subs):
            to_s, to_a = move(s, a)
            pairs.append((s * subs + a, to_s * subs + to_a))
    return lax.ppermute(value, ("section", "sub"), pairs)


def from_next(value, axis):
    return lax.ppermute(value, axis, [(i, i - 1) for i in range(1, lax.axis_size(axis))])


def on_device(echoes, chirp, steer, pulse_order, band_coef, band_start, band_width):
    sections, subs = lax.axis_size("section"), lax.axis_size("sub")
    pulses_each = echoes.shape[2]
    group = ceil_to(pulses_each, SUBL)
    section = lax.axis_index("section").astype(jnp.int32).reshape(1)
    coef = jnp.swapaxes(band_coef, 4, 5)
    weights = jnp.swapaxes(steer, 2, 3)
    levels, _, sides, parts, taps, beams = coef.shape
    dims = (levels, sides, parts, taps, beams)

    echo = jnp.transpose(echoes[:, 0], (1, 0, 2))
    halo = from_next(echo, "rng")
    echo, chirp, packed = prepare(
        echo, chirp, coef, band_start, band_width, weights, pulse_order, sections, group
    )
    if subs == 2:
        packed_partner = swap(packed, "sub", 1)
    early, late, table = begin_compression(echo, chirp, sections, group)
    keep, give = finish_compression(section, early, late, halo, table, group)
    both = jnp.concatenate([keep, swap(give, "section", 1)], axis=1)
    far = lax.dynamic_index_in_dim(both, section[0] % 2, 0, keepdims=False)
    if subs != 2:
        near = lax.dynamic_index_in_dim(both, 1 - section[0] % 2, 0, keepdims=False)
        chunks = [near, swap(far, "section", 2)]
        return merge_images(section, chunks, packed, dims, sections, group, pulses_each)
    chunks = [
        swap_by(far, lambda s, a: (s ^ 2, a ^ 1)),
        swap_by(both[0], lambda s, a: (s, a ^ 1) if s % 2 else (s ^ 2, a)),
        swap_by(both[1], lambda s, a: (s ^ 2, a) if s % 2 else (s, a ^ 1)),
    ]
    operator = fold_operator(section, packed, packed_partner, dims, sections, group, pulses_each)
    image = form_image(section, operator, both, chunks, group)
    return image.reshape(2, beams, 1, image.shape[1])


def unpack(chunk, group, each):
    lead = jnp.concatenate([chunk[:group], chunk[group : 2 * group]], axis=1)
    moved, rest = group - each, chunk[2 * group :]
    tail = jnp.concatenate([rest[: each - moved], rest[group // 2 : group // 2 + each - moved]], axis=1)
    return jnp.concatenate([lead, tail], axis=0)


def merge_images(section, chunks, packed, dims, sections, group, each):
    levels, sides, parts, taps, beams = dims
    width = sections * group
    first = levels * sides * parts * taps
    table = packed[first : first + parts * width].reshape(parts, sections, group, beams)
    table = jnp.take(table, section[0] ^ jnp.arange(sections), axis=1)[:, :, :each]
    chunks = [
        unpack(chunk[first : first + 3 * group], group, each)
        for chunk in chunks
        for first in range(0, chunk.shape[0], 3 * group)
    ]
    real, imag = table[0], table[1]
    rows = jnp.concatenate(
        [jnp.concatenate([real, -imag], axis=1), jnp.concatenate([imag, real], axis=1)], axis=2
    )
    image = lax.dot_general(
        rows.reshape(-1, 2 * beams), jnp.concatenate(chunks, axis=0), (((0,), (0,)), ((), ())), preferred_element_type=F32
    ).astype(BF16)
    starts = packed[first + parts * width :].astype(jnp.int32)
    column = jnp.arange(beams, dtype=jnp.int32)
    bits = lax.axis_size("sub").bit_length() - 1
    for level in range(levels):
        partner = swap(image, "sub", 1 << (level % bits))
        operands = []
        for side in range(sides):
            at = (level * sides + side) * parts * taps
            coef = packed[at : at + parts * taps].reshape(parts, taps, beams)
            offset = column[:, None] - starts[level * sides + side][None, :]
            hits = (offset[None] == jnp.arange(taps, dtype=jnp.int32)[:, None, None]).astype(BF16)
            operands.append(jnp.einsum("ptq,tcq->pqc", coef, hits, preferred_element_type=F32).astype(BF16))
        top = jnp.concatenate([operands[0][0], -operands[0][1], operands[1][0], -operands[1][1]], axis=1)
        low = jnp.concatenate([operands[0][1], operands[0][0], operands[1][1], operands[1][0]], axis=1)
        image = jnp.dot(
            jnp.concatenate([top, low], axis=0),
            jnp.concatenate([image, partner], axis=0),
            preferred_element_type=F32,
        ).astype(BF16)
    return image.reshape(2, beams, 1, image.shape[1])


def solution(mesh):
    return jax.shard_map(
        on_device,
        mesh=mesh,
        in_specs=(
            P(None, "sub", "section", "rng"),
            P(),
            P(None, "sub", None, None),
            P("sub", None),
            P(None, "sub", None, None, None, None),
            P(None, "sub", None, None),
            P(None, "sub", None, None),
        ),
        out_specs=P(None, "sub", "rng", "section"),
        check_vma=False,
    )
```

```python
import functools

import jax
import jax.numpy as jnp
from jax import lax
from jax.experimental import pallas as pl
from jax.experimental.pallas import tpu as pltpu
from jax.sharding import PartitionSpec as P

LANE = 128
SUBL = 8
F32 = jnp.float32
BF16 = jnp.bfloat16


def ceil_to(value, unit):
    return -(-value // unit) * unit


def prepare_kernel(*refs, sections, group):
    sources, (echo_out, chirp_out, pack_ref), scratch = refs[:7], refs[7:10], refs[10:]
    coef_ref, start_ref, width_ref, steer_ref, order_ref, starts, sems = scratch
    targets = (echo_out, coef_ref, start_ref, width_ref, steer_ref, order_ref, chirp_out)
    loads = [
        pltpu.make_async_copy(source, target, sems.at[i])
        for i, (source, target) in enumerate(zip(sources, targets))
    ]
    for load in loads:
        load.start()
    for load in loads:
        load.wait()
    levels, _, sides, parts, taps, beams = coef_ref.shape
    tap = lax.broadcasted_iota(jnp.int32, (taps, beams), 0)
    row = 0
    for level in range(levels):
        for side in range(sides):
            used = tap < width_ref[level, 0, side : side + 1, :]
            for part in range(parts):
                entries = coef_ref[level, 0, side, part].astype(F32)
                pack_ref[row : row + taps] = jnp.where(used, entries, 0.0).astype(BF16)
                row += taps
    pulses = order_ref.shape[1]
    each = pulses // sections
    position = lax.broadcasted_iota(jnp.int32, (pulses, pulses), 0)
    hit = (position == order_ref[0:1, :]).astype(F32)
    slot = lax.broadcasted_iota(jnp.int32, (sections * group, pulses), 0)
    pulse = lax.broadcasted_iota(jnp.int32, (sections * group, pulses), 1)
    place = jnp.zeros((sections * group, pulses), F32)
    for s in range(sections):
        inside = (pulse >= s * each) & (pulse < (s + 1) * each)
        place = jnp.where(inside & (slot - s * group == pulse - s * each), 1.0, place)
    pick = lax.dot_general(
        place.astype(BF16), hit.astype(BF16), (((1,), (1,)), ((), ())), preferred_element_type=F32
    )
    for part in range(parts):
        chosen = jnp.dot(pick.astype(BF16), steer_ref[part, 0], preferred_element_type=F32)
        pack_ref[row : row + sections * group] = chosen.astype(BF16)
        row += sections * group
    starts[...] = jnp.zeros_like(starts)
    for level in range(levels):
        starts[sides * level : sides * level + sides] = start_ref[level, 0].astype(F32)
    pack_ref[row : row + starts.shape[0]] = starts[...].astype(BF16)


def pack_rows(levels, sides, parts, taps, sections, group):
    return levels * sides * parts * taps + parts * sections * group + ceil_to(levels * sides, 16)


def prepare(echo, chirp, coef, start, width, steer, order, sections, group):
    levels, _, sides, parts, taps, beams = coef.shape
    sources = (echo, coef, start, width, steer, order, chirp)
    return pl.pallas_call(
        functools.partial(prepare_kernel, sections=sections, group=group),
        out_shape=(
            jax.ShapeDtypeStruct(echo.shape, BF16),
            jax.ShapeDtypeStruct(chirp.shape, BF16),
            jax.ShapeDtypeStruct((pack_rows(levels, sides, parts, taps, sections, group), beams), BF16),
        ),
        in_specs=[pl.BlockSpec(memory_space=pl.ANY)] * len(sources),
        scratch_shapes=[pltpu.VMEM(x.shape, x.dtype) for x in sources[1:6]]
        + [pltpu.VMEM((ceil_to(levels * sides, 16), beams), F32), pltpu.SemaphoreType.DMA((len(sources),))],
        compiler_params=pltpu.CompilerParams(vmem_limit_bytes=16 * 1024 * 1024),
        name="prepare",
    )(*[pltpu.with_memory_space_constraint(x, pltpu.HBM) for x in sources])


def pack_rows_of(real, imag, each):
    group = real.shape[0]
    row = lax.broadcasted_iota(jnp.int32, real.shape, 0)
    return jnp.where(row < each, real, pltpu.roll(imag, each, 0)), group - each


def split_two(value):
    high = value.astype(BF16)
    return high, (value - high.astype(F32)).astype(BF16)


def operator_kernel(index_ref, own_ref, partner_ref, out_ref, weights, *, dims, sections, group, each):
    levels, sides, parts, taps, beams = dims
    width = sections * group
    refs = (own_ref, partner_ref)
    weight_row = levels * sides * parts * taps
    start_row = weight_row + parts * width

    def band(ref, level, side):
        first = ((level * sides + side) * parts) * taps
        tables = [ref[first + p * taps : first + (p + 1) * taps].astype(F32) for p in range(parts)]
        start = ref[start_row : start_row + ceil_to(levels * sides, 16)].astype(F32)
        start = start[level * sides + side : level * sides + side + 1].astype(jnp.int32)
        found = [[], []]
        for c in range(0, beams, SUBL):
            column = lax.broadcasted_iota(jnp.int32, (SUBL, beams), 0) + c
            offset = column - start
            spot = offset & (SUBL - 1)
            for p in range(parts):
                value = jnp.zeros((SUBL, beams), F32)
                for t in range(0, taps, SUBL):
                    got = jnp.take_along_axis(
                        tables[p][t : t + SUBL], spot, axis=0, mode="promise_in_bounds"
                    )
                    value = jnp.where((offset >= t) & (offset < t + SUBL), got, value)
                found[p].append(value)
        return [jnp.concatenate(f, axis=0) for f in found]

    def complex_operand(real, imag):
        top = jnp.concatenate([real, imag], axis=1)
        low = jnp.concatenate([-imag, real], axis=1)
        return jnp.concatenate([top, low], axis=0).astype(BF16)

    section = index_ref[0]
    images = []
    for a in range(2):
        for p in range(parts):
            weights[...] = refs[a][weight_row + p * width : weight_row + (p + 1) * width].astype(F32)
            rows = []
            for j in range(sections):
                at = pl.multiple_of((section ^ j) * group, group)
                rows.append(weights[pl.ds(at, group)])
            images.append(jnp.concatenate(rows, axis=0))
    zero = jnp.zeros((width, 2 * beams), F32)
    own = jnp.concatenate([jnp.concatenate(images[0:2], axis=1), zero], axis=0)
    partner = jnp.concatenate([zero, jnp.concatenate(images[2:4], axis=1)], axis=0)
    for level in range(levels):
        own_high, own_low = split_two(own)
        partner_high, partner_low = split_two(partner)
        own_rows = jnp.concatenate([own_high, own_low], axis=0)
        partner_rows = jnp.concatenate([partner_high, partner_low], axis=0)

        def merged(ref, mine, other):
            product = jnp.dot(
                mine, complex_operand(*band(ref, level, 0)), preferred_element_type=F32
            ) + jnp.dot(other, complex_operand(*band(ref, level, 1)), preferred_element_type=F32)
            return product[: 2 * width] + product[2 * width :]

        following = merged(own_ref, own_rows, partner_rows)
        if level < levels - 1:
            partner = merged(partner_ref, partner_rows, own_rows)
        own = following
    full, left, right = [], [], []
    for j in range(2 * sections):
        real = own[j * group : (j + 1) * group, :beams]
        imag = own[j * group : (j + 1) * group, beams:]
        straight = jnp.concatenate([real, imag], axis=1)
        turned = jnp.concatenate([-imag, real], axis=1)
        lead, moved = pack_rows_of(straight, turned, each)
        row = lax.broadcasted_iota(jnp.int32, lead.shape, 0)
        full.append(lead)
        left.append(jnp.where(row < group // 2, pltpu.roll(turned, group - moved, 0), 0.0))
        right.append(jnp.where(row >= group // 2, pltpu.roll(turned, group // 2 - moved, 0), 0.0))
    pairs = sections // 2
    first_core = section % 2 == 0
    for half, rest in enumerate((left, right)):
        sources = [jnp.concatenate([full[j], rest[j]], axis=0) for j in range(2 * sections)]
        quarters = [jnp.concatenate(sources[q * pairs : (q + 1) * pairs], axis=0) for q in range(4)]
        quarters = [
            quarters[0],
            quarters[3],
            jnp.where(first_core, quarters[1], quarters[2]),
            jnp.where(first_core, quarters[2], quarters[1]),
        ]
        high, low = split_two(jnp.concatenate(quarters, axis=0).T)
        out_ref[half] = jnp.concatenate([high, low], axis=1)


def fold_operator(section, own, partner, dims, sections, group, each):
    beams = dims[-1]
    width = sections * group
    return pl.pallas_call(
        functools.partial(operator_kernel, dims=dims, sections=sections, group=group, each=each),
        out_shape=jax.ShapeDtypeStruct((2, 2 * beams, 8 * width), BF16),
        in_specs=[
            pl.BlockSpec(memory_space=pltpu.SMEM),
            pl.BlockSpec(memory_space=pltpu.VMEM),
            pl.BlockSpec(memory_space=pltpu.VMEM),
        ],
        scratch_shapes=[pltpu.VMEM((width, beams), F32)],
        compiler_params=pltpu.CompilerParams(vmem_limit_bytes=16 * 1024 * 1024),
        name="fold_operator",
    )(section, own, partner)


def correlate(rows, even, odd, table, blocks, group):
    extra = table.shape[0] // (2 * LANE) - 1
    total = blocks + extra
    held = [
        jnp.concatenate(
            [rows[:group, b * LANE : (b + 1) * LANE], rows[group:, b * LANE : (b + 1) * LANE]], axis=1
        )
        for b in range(total)
    ]
    for b in range(0, total, 2):
        even[b * group : (b + 2) * group] = jnp.concatenate(held[b : b + 2], axis=0).astype(BF16)
    for b in range(1, total - 1, 2):
        odd[(b - 1) * group : (b + 1) * group] = jnp.concatenate(held[b : b + 2], axis=0).astype(BF16)
    window = blocks * group
    pieces = []
    for lag in range(extra + 1):
        source, at = (even, lag) if lag % 2 == 0 else (odd, lag - 1)
        pieces.append(source[at * group : at * group + window])
    return jnp.dot(jnp.concatenate(pieces, axis=1), table[...], preferred_element_type=F32)


def as_chunk(done, s, chunk, group, each):
    real, imag = [
        jnp.concatenate(
            [
                done[(s * chunk + b) * group : (s * chunk + b + 1) * group, c * LANE : (c + 1) * LANE]
                for b in range(chunk)
            ],
            axis=1,
        )
        for c in range(2)
    ]
    middle = chunk * LANE // 2
    lead, moved = pack_rows_of(real, imag, each)
    row = lax.broadcasted_iota(jnp.int32, (group, middle), 0)
    rest = jnp.where(
        row < group // 2,
        pltpu.roll(imag[:, :middle], group - moved, 0),
        pltpu.roll(imag[:, middle:], group // 2 - moved, 0),
    )
    return jnp.concatenate([lead[:, :middle], lead[:, middle:], rest], axis=0).astype(BF16)


def begin_kernel(echo_ref, chirp_ref, early_ref, late_ref, table, rows, even, odd, *, group):
    pulses, _, length = echo_ref.shape
    extra = chirp_ref.shape[1] // LANE
    reverse = LANE - 1 - lax.broadcasted_iota(jnp.int32, (2, LANE), 1)
    below = lax.broadcasted_iota(jnp.int32, (LANE, LANE), 1) <= lax.broadcasted_iota(
        jnp.int32, (LANE, LANE), 0
    )
    before = [jnp.zeros((LANE, LANE), F32)] * 2
    for lag in range(extra + 1):
        if lag < extra:
            piece = chirp_ref[:, lag * LANE : (lag + 1) * LANE].astype(F32)
            piece = jnp.take_along_axis(piece, reverse, axis=1, mode="promise_in_bounds")
            turned = [
                pltpu.roll(
                    jnp.broadcast_to(piece[c : c + 1], (LANE, LANE)), 1, 1, stride=1, stride_axis=0
                )
                for c in range(2)
            ]
        else:
            turned = [jnp.zeros((LANE, LANE), F32)] * 2
        real, imag = [jnp.where(below, turned[c], before[c]) for c in range(2)]
        before = turned
        at = lag * 2 * LANE
        table[at : at + LANE, :LANE] = real.astype(BF16)
        table[at : at + LANE, LANE:] = (-imag).astype(BF16)
        table[at + LANE : at + 2 * LANE, :LANE] = imag.astype(BF16)
        table[at + LANE : at + 2 * LANE, LANE:] = real.astype(BF16)
    rows[...] = jnp.zeros_like(rows)
    for p in range(pulses):
        near = echo_ref[p].astype(F32)
        for c in range(2):
            rows[c * group + p : c * group + p + 1, :] = near[c : c + 1]
    late_ref[...] = rows[:, length - late_ref.shape[1] :]
    done = correlate(rows, even, odd, table, length // LANE - extra, group)
    for s in range(early_ref.shape[0]):
        early_ref[s] = as_chunk(done, s, 2 * early_ref.shape[2] // LANE, group, pulses)


def finish_kernel(index_ref, early_ref, late_ref, halo_ref, table, keep_ref, give_ref, rows, even, odd, *, group):
    pulses = halo_ref.shape[0]
    span = late_ref.shape[1]
    taps = rows.shape[1] - span
    ready = early_ref.shape[0]
    chunk = 2 * early_ref.shape[2]
    sections = ready + span // chunk
    section = lax.rem(index_ref[0], sections)
    has_next = index_ref[0] >= sections
    rows[:, :span] = late_ref[...]
    rows[:, span:] = jnp.zeros((2 * group, taps), F32)
    for p in range(pulses):
        far = jnp.where(has_next, halo_ref[p, :, :taps].astype(F32), 0.0)
        for c in range(2):
            rows[c * group + p : c * group + p + 1, span:] = far[c : c + 1]
    done = correlate(rows, even, odd, table, span // LANE, group)
    for s in range(sections):
        stacked = early_ref[s] if s < ready else as_chunk(done, s - ready, chunk // LANE, group, pulses)
        slot = section ^ s
        far_chunk, other_core = slot // 2, slot % 2
        place = far_chunk ^ 1 ^ (section % 2) ^ other_core

        @pl.when(other_core == 0)
        def _():
            keep_ref[place] = stacked

        @pl.when(other_core == 1)
        def _():
            give_ref[place] = stacked


def row_scratch(blocks, group):
    return [
        pltpu.VMEM((2 * group, blocks * LANE), F32),
        pltpu.VMEM((blocks * group, 2 * LANE), BF16),
        pltpu.VMEM((blocks * group, 2 * LANE), BF16),
    ]


def begin_compression(echo, chirp, sections, group):
    _, _, length = echo.shape
    taps = chirp.shape[1]
    chunk = length // sections
    early = (length - taps) // chunk
    return pl.pallas_call(
        functools.partial(begin_kernel, group=group),
        out_shape=(
            jax.ShapeDtypeStruct((early, 3 * group, chunk // 2), BF16),
            jax.ShapeDtypeStruct((2 * group, length - early * chunk), F32),
            jax.ShapeDtypeStruct(((taps // LANE + 1) * 2 * LANE, 2 * LANE), BF16),
        ),
        scratch_shapes=row_scratch(length // LANE, group),
        compiler_params=pltpu.CompilerParams(vmem_limit_bytes=24 * 1024 * 1024),
        name="begin_compression",
    )(echo, chirp)


def finish_compression(place, early, late, halo, table, group):
    blocks = late.shape[1] // LANE + table.shape[0] // (2 * LANE) - 1
    return pl.pallas_call(
        functools.partial(finish_kernel, group=group),
        out_shape=[jax.ShapeDtypeStruct((2, *early.shape[1:]), BF16)] * 2,
        in_specs=[pl.BlockSpec(memory_space=pltpu.SMEM)] + [pl.BlockSpec(memory_space=pltpu.VMEM)] * 4,
        scratch_shapes=row_scratch(blocks, group),
        compiler_params=pltpu.CompilerParams(vmem_limit_bytes=24 * 1024 * 1024),
        name="finish_compression",
    )(place, early, late, halo, table)


def image_kernel(index_ref, operator_ref, both_ref, *refs, group):
    chunks, (out_ref, parts, sems) = refs[:-3], refs[-3:]
    count, _, tile = parts.shape
    width = both_ref.shape[2]
    near = 1 - index_ref[0] % 2
    held = [both_ref[near]] + [chunk[...] for chunk in chunks]
    held = [value.astype(F32) for value in held]
    copies = []
    for i in range(count):
        half, at = divmod(i * tile, width)
        rows = []
        for value in held:
            for first in range(0, value.shape[0], 3 * group):
                rows.append(value[first + half * group : first + (half + 1) * group, at : at + tile])
                rows.append(value[first + 2 * group : first + 3 * group, at : at + tile])
        pulses = jnp.concatenate(rows, axis=0).astype(BF16)
        result = jnp.dot(
            operator_ref[half], jnp.concatenate([pulses, pulses], axis=0), preferred_element_type=F32
        )
        parts[i] = result.astype(BF16)
        copy = pltpu.make_async_copy(parts.at[i], out_ref.at[:, i * tile : (i + 1) * tile], sems.at[i])
        copy.start()
        copies.append(copy)
    for copy in copies:
        copy.wait()


def form_image(section, operator, both, chunks, group):
    height, half = operator.shape[1], both.shape[2]
    tile = 256 if half % 256 == 0 else half
    count = 2 * half // tile
    return pl.pallas_call(
        functools.partial(image_kernel, group=group),
        out_shape=jax.ShapeDtypeStruct((height, 2 * half), BF16),
        in_specs=[pl.BlockSpec(memory_space=pltpu.SMEM)]
        + [pl.BlockSpec(memory_space=pltpu.VMEM)] * (2 + len(chunks)),
        out_specs=pl.BlockSpec(memory_space=pl.ANY),
        scratch_shapes=[
            pltpu.VMEM((count, height, tile), BF16),
            pltpu.SemaphoreType.DMA((count,)),
        ],
        compiler_params=pltpu.CompilerParams(vmem_limit_bytes=16 * 1024 * 1024),
        name="form_image",
    )(section, operator, both, *chunks)


def swap(value, axis, by):
    count = lax.axis_size(axis)
    return lax.ppermute(value, axis, [(i, i ^ by) for i in range(count)])


def swap_by(value, move):
    sections, subs = lax.axis_size("section"), lax.axis_size("sub")
    pairs = []
    for s in range(sections):
        for a in range(subs):
            to_s, to_a = move(s, a)
            pairs.append((s * subs + a, to_s * subs + to_a))
    return lax.ppermute(value, ("section", "sub"), pairs)


def from_next(value, axis):
    count = lax.axis_size(axis)
    return lax.ppermute(value, axis, [(i, (i - 1) % count) for i in range(count)])


def on_device(echoes, chirp, steer, pulse_order, band_coef, band_start, band_width):
    sections, subs = lax.axis_size("section"), lax.axis_size("sub")
    pulses_each = echoes.shape[2]
    group = ceil_to(pulses_each, SUBL)
    section = lax.axis_index("section").astype(jnp.int32).reshape(1)
    coef = jnp.swapaxes(band_coef, 4, 5)
    weights = jnp.swapaxes(steer, 2, 3)
    levels, _, sides, parts, taps, beams = coef.shape
    dims = (levels, sides, parts, taps, beams)

    echo = jnp.transpose(echoes[:, 0], (1, 0, 2))
    halo = from_next(echo, "rng")
    echo, chirp, packed = prepare(
        echo, chirp, coef, band_start, band_width, weights, pulse_order, sections, group
    )
    has_next = (lax.axis_index("rng") < lax.axis_size("rng") - 1).astype(jnp.int32)
    early, late, table = begin_compression(echo, chirp, sections, group)
    place = section + sections * has_next
    keep, give = finish_compression(place, early, late, halo, table, group)
    give, packed = lax.optimization_barrier((give, packed))
    both = jnp.concatenate([keep, swap(give, "section", 1)], axis=1)
    packed_partner = swap(packed, "sub", 1) if subs == 2 else packed
    far = lax.dynamic_index_in_dim(both, section[0] % 2, 0, keepdims=False)
    if subs != 2:
        near = lax.dynamic_index_in_dim(both, 1 - section[0] % 2, 0, keepdims=False)
        chunks = [near, swap(far, "section", 2)]
        return merge_images(section, chunks, packed, dims, sections, group, pulses_each)
    chunks = [
        swap_by(far, lambda s, a: (s ^ 2, a ^ 1)),
        swap_by(both[0], lambda s, a: (s, a ^ 1) if s % 2 else (s ^ 2, a)),
        swap_by(both[1], lambda s, a: (s ^ 2, a) if s % 2 else (s, a ^ 1)),
    ]
    operator = fold_operator(section, packed, packed_partner, dims, sections, group, pulses_each)
    image = form_image(section, operator, both, chunks, group)
    return image.reshape(2, beams, 1, image.shape[1])


def unpack(chunk, group, each):
    lead = jnp.concatenate([chunk[:group], chunk[group : 2 * group]], axis=1)
    moved, rest = group - each, chunk[2 * group :]
    tail = jnp.concatenate([rest[: each - moved], rest[group // 2 : group // 2 + each - moved]], axis=1)
    return jnp.concatenate([lead, tail], axis=0)


def merge_images(section, chunks, packed, dims, sections, group, each):
    levels, sides, parts, taps, beams = dims
    width = sections * group
    first = levels * sides * parts * taps
    table = packed[first : first + parts * width].reshape(parts, sections, group, beams)
    table = jnp.take(table, section[0] ^ jnp.arange(sections), axis=1)[:, :, :each]
    chunks = [
        unpack(chunk[first : first + 3 * group], group, each)
        for chunk in chunks
        for first in range(0, chunk.shape[0], 3 * group)
    ]
    real, imag = table[0], table[1]
    rows = jnp.concatenate(
        [jnp.concatenate([real, -imag], axis=1), jnp.concatenate([imag, real], axis=1)], axis=2
    )
    image = lax.dot_general(
        rows.reshape(-1, 2 * beams), jnp.concatenate(chunks, axis=0), (((0,), (0,)), ((), ())), preferred_element_type=F32
    ).astype(BF16)
    starts = packed[first + parts * width :].astype(jnp.int32)
    column = jnp.arange(beams, dtype=jnp.int32)
    bits = lax.axis_size("sub").bit_length() - 1
    for level in range(levels):
        partner = swap(image, "sub", 1 << (level % bits))
        operands = []
        for side in range(sides):
            at = (level * sides + side) * parts * taps
            coef = packed[at : at + parts * taps].reshape(parts, taps, beams)
            offset = column[:, None] - starts[level * sides + side][None, :]
            hits = (offset[None] == jnp.arange(taps, dtype=jnp.int32)[:, None, None]).astype(BF16)
            operands.append(jnp.einsum("ptq,tcq->pqc", coef, hits, preferred_element_type=F32).astype(BF16))
        top = jnp.concatenate([operands[0][0], -operands[0][1], operands[1][0], -operands[1][1]], axis=1)
        low = jnp.concatenate([operands[0][1], operands[0][0], operands[1][1], operands[1][0]], axis=1)
        image = jnp.dot(
            jnp.concatenate([top, low], axis=0),
            jnp.concatenate([image, partner], axis=0),
            preferred_element_type=F32,
        ).astype(BF16)
    return image.reshape(2, beams, 1, image.shape[1])


def solution(mesh):
    return jax.shard_map(
        on_device,
        mesh=mesh,
        in_specs=(
            P(None, "sub", "section", "rng"),
            P(),
            P(None, "sub", None, None),
            P("sub", None),
            P(None, "sub", None, None, None, None),
            P(None, "sub", None, None),
            P(None, "sub", None, None),
        ),
        out_specs=P(None, "sub", "rng", "section"),
        check_vma=False,
    )
```

```python
import functools

import jax
import jax.numpy as jnp
from jax import lax
from jax.experimental import pallas as pl
from jax.experimental.pallas import tpu as pltpu
from jax.sharding import PartitionSpec as P

LANE = 128
SUBL = 8
F32 = jnp.float32
BF16 = jnp.bfloat16


def ceil_to(value, unit):
    return -(-value // unit) * unit


def prepare_kernel(*refs, sections, group):
    sources, (echo_out, chirp_out, pack_ref), scratch = refs[:7], refs[7:10], refs[10:]
    coef_ref, start_ref, width_ref, steer_ref, order_ref, starts, sems = scratch
    targets = (echo_out, coef_ref, start_ref, width_ref, steer_ref, order_ref, chirp_out)
    loads = [
        pltpu.make_async_copy(source, target, sems.at[i])
        for i, (source, target) in enumerate(zip(sources, targets))
    ]
    for load in loads:
        load.start()
    for load in loads:
        load.wait()
    levels, _, sides, parts, taps, beams = coef_ref.shape
    tap = lax.broadcasted_iota(jnp.int32, (taps, beams), 0)
    row = 0
    for level in range(levels):
        for side in range(sides):
            used = tap < width_ref[level, 0, side : side + 1, :]
            for part in range(parts):
                entries = coef_ref[level, 0, side, part].astype(F32)
                pack_ref[row : row + taps] = jnp.where(used, entries, 0.0).astype(BF16)
                row += taps
    pulses = order_ref.shape[1]
    each = pulses // sections
    position = lax.broadcasted_iota(jnp.int32, (pulses, pulses), 0)
    hit = (position == order_ref[0:1, :]).astype(F32)
    slot = lax.broadcasted_iota(jnp.int32, (sections * group, pulses), 0)
    pulse = lax.broadcasted_iota(jnp.int32, (sections * group, pulses), 1)
    place = jnp.zeros((sections * group, pulses), F32)
    for s in range(sections):
        inside = (pulse >= s * each) & (pulse < (s + 1) * each)
        place = jnp.where(inside & (slot - s * group == pulse - s * each), 1.0, place)
    pick = lax.dot_general(
        place.astype(BF16), hit.astype(BF16), (((1,), (1,)), ((), ())), preferred_element_type=F32
    )
    for part in range(parts):
        chosen = jnp.dot(pick.astype(BF16), steer_ref[part, 0], preferred_element_type=F32)
        pack_ref[row : row + sections * group] = chosen.astype(BF16)
        row += sections * group
    starts[...] = jnp.zeros_like(starts)
    for level in range(levels):
        starts[sides * level : sides * level + sides] = start_ref[level, 0].astype(F32)
    pack_ref[row : row + starts.shape[0]] = starts[...].astype(BF16)


def pack_rows(levels, sides, parts, taps, sections, group):
    return levels * sides * parts * taps + parts * sections * group + ceil_to(levels * sides, 16)


def prepare(echo, chirp, coef, start, width, steer, order, sections, group):
    levels, _, sides, parts, taps, beams = coef.shape
    sources = (echo, coef, start, width, steer, order, chirp)
    return pl.pallas_call(
        functools.partial(prepare_kernel, sections=sections, group=group),
        out_shape=(
            jax.ShapeDtypeStruct(echo.shape, BF16),
            jax.ShapeDtypeStruct(chirp.shape, BF16),
            jax.ShapeDtypeStruct((pack_rows(levels, sides, parts, taps, sections, group), beams), BF16),
        ),
        in_specs=[pl.BlockSpec(memory_space=pl.ANY)] * len(sources),
        scratch_shapes=[pltpu.VMEM(x.shape, x.dtype) for x in sources[1:6]]
        + [pltpu.VMEM((ceil_to(levels * sides, 16), beams), F32), pltpu.SemaphoreType.DMA((len(sources),))],
        compiler_params=pltpu.CompilerParams(vmem_limit_bytes=16 * 1024 * 1024),
        name="prepare",
    )(*[pltpu.with_memory_space_constraint(x, pltpu.HBM) for x in sources])


def pack_rows_of(real, imag, each):
    group = real.shape[0]
    row = lax.broadcasted_iota(jnp.int32, real.shape, 0)
    return jnp.where(row < each, real, pltpu.roll(imag, each, 0)), group - each


def split_two(value):
    high = value.astype(BF16)
    return high, (value - high.astype(F32)).astype(BF16)


def operator_kernel(index_ref, own_ref, partner_ref, out_ref, weights, *, dims, sections, group, each):
    levels, sides, parts, taps, beams = dims
    width = sections * group
    refs = (own_ref, partner_ref)
    weight_row = levels * sides * parts * taps
    start_row = weight_row + parts * width

    def band(ref, level, side):
        first = ((level * sides + side) * parts) * taps
        tables = [ref[first + p * taps : first + (p + 1) * taps].astype(F32) for p in range(parts)]
        start = ref[start_row : start_row + ceil_to(levels * sides, 16)].astype(F32)
        start = start[level * sides + side : level * sides + side + 1].astype(jnp.int32)
        found = [[], []]
        for c in range(0, beams, SUBL):
            column = lax.broadcasted_iota(jnp.int32, (SUBL, beams), 0) + c
            offset = column - start
            spot = offset & (SUBL - 1)
            for p in range(parts):
                value = jnp.zeros((SUBL, beams), F32)
                for t in range(0, taps, SUBL):
                    got = jnp.take_along_axis(
                        tables[p][t : t + SUBL], spot, axis=0, mode="promise_in_bounds"
                    )
                    value = jnp.where((offset >= t) & (offset < t + SUBL), got, value)
                found[p].append(value)
        return [jnp.concatenate(f, axis=0) for f in found]

    def complex_operand(real, imag):
        top = jnp.concatenate([real, imag], axis=1)
        low = jnp.concatenate([-imag, real], axis=1)
        return jnp.concatenate([top, low], axis=0).astype(BF16)

    section = index_ref[0]
    images = []
    for a in range(2):
        for p in range(parts):
            weights[...] = refs[a][weight_row + p * width : weight_row + (p + 1) * width].astype(F32)
            rows = []
            for j in range(sections):
                at = pl.multiple_of((section ^ j) * group, group)
                rows.append(weights[pl.ds(at, group)])
            images.append(jnp.concatenate(rows, axis=0))
    zero = jnp.zeros((width, 2 * beams), F32)
    own = jnp.concatenate([jnp.concatenate(images[0:2], axis=1), zero], axis=0)
    partner = jnp.concatenate([zero, jnp.concatenate(images[2:4], axis=1)], axis=0)
    for level in range(levels):
        own_high, own_low = split_two(own)
        partner_high, partner_low = split_two(partner)
        own_rows = jnp.concatenate([own_high, own_low], axis=0)
        partner_rows = jnp.concatenate([partner_high, partner_low], axis=0)

        def merged(ref, mine, other):
            product = jnp.dot(
                mine, complex_operand(*band(ref, level, 0)), preferred_element_type=F32
            ) + jnp.dot(other, complex_operand(*band(ref, level, 1)), preferred_element_type=F32)
            return product[: 2 * width] + product[2 * width :]

        following = merged(own_ref, own_rows, partner_rows)
        if level < levels - 1:
            partner = merged(partner_ref, partner_rows, own_rows)
        own = following
    full, left, right = [], [], []
    for j in range(2 * sections):
        real = own[j * group : (j + 1) * group, :beams]
        imag = own[j * group : (j + 1) * group, beams:]
        straight = jnp.concatenate([real, imag], axis=1)
        turned = jnp.concatenate([-imag, real], axis=1)
        lead, moved = pack_rows_of(straight, turned, each)
        row = lax.broadcasted_iota(jnp.int32, lead.shape, 0)
        full.append(lead)
        left.append(jnp.where(row < group // 2, pltpu.roll(turned, group - moved, 0), 0.0))
        right.append(jnp.where(row >= group // 2, pltpu.roll(turned, group // 2 - moved, 0), 0.0))
    pairs = sections // 2
    first_core = section % 2 == 0
    for half, rest in enumerate((left, right)):
        sources = [jnp.concatenate([full[j], rest[j]], axis=0) for j in range(2 * sections)]
        quarters = [jnp.concatenate(sources[q * pairs : (q + 1) * pairs], axis=0) for q in range(4)]
        quarters = [
            quarters[0],
            jnp.where(first_core, quarters[3], quarters[2]),
            jnp.where(first_core, quarters[1], quarters[3]),
            jnp.where(first_core, quarters[2], quarters[1]),
        ]
        high, low = split_two(jnp.concatenate(quarters, axis=0).T)
        out_ref[half] = jnp.concatenate([high, low], axis=1)


def fold_operator(section, own, partner, dims, sections, group, each):
    beams = dims[-1]
    width = sections * group
    return pl.pallas_call(
        functools.partial(operator_kernel, dims=dims, sections=sections, group=group, each=each),
        out_shape=jax.ShapeDtypeStruct((2, 2 * beams, 8 * width), BF16),
        in_specs=[
            pl.BlockSpec(memory_space=pltpu.SMEM),
            pl.BlockSpec(memory_space=pltpu.VMEM),
            pl.BlockSpec(memory_space=pltpu.VMEM),
        ],
        scratch_shapes=[pltpu.VMEM((width, beams), F32)],
        compiler_params=pltpu.CompilerParams(vmem_limit_bytes=16 * 1024 * 1024),
        name="fold_operator",
    )(section, own, partner)


def correlate(rows, even, odd, table, blocks, group):
    extra = table.shape[0] // (2 * LANE) - 1
    total = blocks + extra
    held = [
        jnp.concatenate(
            [rows[:group, b * LANE : (b + 1) * LANE], rows[group:, b * LANE : (b + 1) * LANE]], axis=1
        )
        for b in range(total)
    ]
    for b in range(0, total, 2):
        even[b * group : (b + 2) * group] = jnp.concatenate(held[b : b + 2], axis=0).astype(BF16)
    for b in range(1, total - 1, 2):
        odd[(b - 1) * group : (b + 1) * group] = jnp.concatenate(held[b : b + 2], axis=0).astype(BF16)
    window = blocks * group
    pieces = []
    for lag in range(extra + 1):
        source, at = (even, lag) if lag % 2 == 0 else (odd, lag - 1)
        pieces.append(source[at * group : at * group + window])
    return jnp.dot(jnp.concatenate(pieces, axis=1), table[...], preferred_element_type=F32)


def as_chunk(done, s, chunk, group, each):
    real, imag = [
        jnp.concatenate(
            [
                done[(s * chunk + b) * group : (s * chunk + b + 1) * group, c * LANE : (c + 1) * LANE]
                for b in range(chunk)
            ],
            axis=1,
        )
        for c in range(2)
    ]
    middle = chunk * LANE // 2
    lead, moved = pack_rows_of(real, imag, each)
    row = lax.broadcasted_iota(jnp.int32, (group, middle), 0)
    rest = jnp.where(
        row < group // 2,
        pltpu.roll(imag[:, :middle], group - moved, 0),
        pltpu.roll(imag[:, middle:], group // 2 - moved, 0),
    )
    return jnp.concatenate([lead[:, :middle], lead[:, middle:], rest], axis=0).astype(BF16)


def begin_kernel(echo_ref, chirp_ref, early_ref, late_ref, table, rows, even, odd, *, group):
    pulses, _, length = echo_ref.shape
    extra = chirp_ref.shape[1] // LANE
    reverse = LANE - 1 - lax.broadcasted_iota(jnp.int32, (2, LANE), 1)
    below = lax.broadcasted_iota(jnp.int32, (LANE, LANE), 1) <= lax.broadcasted_iota(
        jnp.int32, (LANE, LANE), 0
    )
    before = [jnp.zeros((LANE, LANE), F32)] * 2
    for lag in range(extra + 1):
        if lag < extra:
            piece = chirp_ref[:, lag * LANE : (lag + 1) * LANE].astype(F32)
            piece = jnp.take_along_axis(piece, reverse, axis=1, mode="promise_in_bounds")
            turned = [
                pltpu.roll(
                    jnp.broadcast_to(piece[c : c + 1], (LANE, LANE)), 1, 1, stride=1, stride_axis=0
                )
                for c in range(2)
            ]
        else:
            turned = [jnp.zeros((LANE, LANE), F32)] * 2
        real, imag = [jnp.where(below, turned[c], before[c]) for c in range(2)]
        before = turned
        at = lag * 2 * LANE
        table[at : at + LANE, :LANE] = real.astype(BF16)
        table[at : at + LANE, LANE:] = (-imag).astype(BF16)
        table[at + LANE : at + 2 * LANE, :LANE] = imag.astype(BF16)
        table[at + LANE : at + 2 * LANE, LANE:] = real.astype(BF16)
    rows[...] = jnp.zeros_like(rows)
    for p in range(pulses):
        near = echo_ref[p].astype(F32)
        for c in range(2):
            rows[c * group + p : c * group + p + 1, :] = near[c : c + 1]
    late_ref[...] = rows[:, length - late_ref.shape[1] :]
    done = correlate(rows, even, odd, table, length // LANE - extra, group)
    for s in range(early_ref.shape[0]):
        early_ref[s] = as_chunk(done, s, 2 * early_ref.shape[2] // LANE, group, pulses)


def finish_kernel(index_ref, early_ref, late_ref, halo_ref, table, keep_ref, give_ref, rows, even, odd, *, group):
    pulses = halo_ref.shape[0]
    span = late_ref.shape[1]
    taps = rows.shape[1] - span
    ready = early_ref.shape[0]
    chunk = 2 * early_ref.shape[2]
    sections = ready + span // chunk
    section = lax.rem(index_ref[0], sections)
    has_next = index_ref[0] >= sections
    rows[:, :span] = late_ref[...]
    rows[:, span:] = jnp.zeros((2 * group, taps), F32)
    for p in range(pulses):
        far = jnp.where(has_next, halo_ref[p, :, :taps].astype(F32), 0.0)
        for c in range(2):
            rows[c * group + p : c * group + p + 1, span:] = far[c : c + 1]
    done = correlate(rows, even, odd, table, span // LANE, group)
    for s in range(sections):
        stacked = early_ref[s] if s < ready else as_chunk(done, s - ready, chunk // LANE, group, pulses)
        slot = section ^ s
        far_chunk, other_core = slot // 2, slot % 2
        place = far_chunk ^ 1 ^ (section % 2) ^ other_core

        @pl.when(other_core == 0)
        def _():
            keep_ref[place] = stacked

        @pl.when(other_core == 1)
        def _():
            give_ref[place] = stacked


def row_scratch(blocks, group):
    return [
        pltpu.VMEM((2 * group, blocks * LANE), F32),
        pltpu.VMEM((blocks * group, 2 * LANE), BF16),
        pltpu.VMEM((blocks * group, 2 * LANE), BF16),
    ]


def begin_compression(echo, chirp, sections, group):
    _, _, length = echo.shape
    taps = chirp.shape[1]
    chunk = length // sections
    early = (length - taps) // chunk
    return pl.pallas_call(
        functools.partial(begin_kernel, group=group),
        out_shape=(
            jax.ShapeDtypeStruct((early, 3 * group, chunk // 2), BF16),
            jax.ShapeDtypeStruct((2 * group, length - early * chunk), F32),
            jax.ShapeDtypeStruct(((taps // LANE + 1) * 2 * LANE, 2 * LANE), BF16),
        ),
        scratch_shapes=row_scratch(length // LANE, group),
        compiler_params=pltpu.CompilerParams(vmem_limit_bytes=24 * 1024 * 1024),
        name="begin_compression",
    )(echo, chirp)


def finish_compression(place, early, late, halo, table, group):
    blocks = late.shape[1] // LANE + table.shape[0] // (2 * LANE) - 1
    return pl.pallas_call(
        functools.partial(finish_kernel, group=group),
        out_shape=[jax.ShapeDtypeStruct((2, *early.shape[1:]), BF16)] * 2,
        in_specs=[pl.BlockSpec(memory_space=pltpu.SMEM)] + [pl.BlockSpec(memory_space=pltpu.VMEM)] * 4,
        scratch_shapes=row_scratch(blocks, group),
        compiler_params=pltpu.CompilerParams(vmem_limit_bytes=24 * 1024 * 1024),
        name="finish_compression",
    )(place, early, late, halo, table)


def image_kernel(index_ref, operator_ref, both_ref, *refs, group):
    chunks, (out_ref, parts, sems) = refs[:-3], refs[-3:]
    count, _, tile = parts.shape
    width = both_ref.shape[2]
    near = 1 - index_ref[0] % 2
    held = [both_ref[near]] + [chunk[...] for chunk in chunks]
    held = [value.astype(F32) for value in held]
    copies = []
    for i in range(count):
        half, at = divmod(i * tile, width)
        rows = []
        for value in held:
            for first in range(0, value.shape[0], 3 * group):
                rows.append(value[first + half * group : first + (half + 1) * group, at : at + tile])
                rows.append(value[first + 2 * group : first + 3 * group, at : at + tile])
        pulses = jnp.concatenate(rows, axis=0).astype(BF16)
        result = jnp.dot(
            operator_ref[half], jnp.concatenate([pulses, pulses], axis=0), preferred_element_type=F32
        )
        parts[i] = result.astype(BF16)
        copy = pltpu.make_async_copy(parts.at[i], out_ref.at[:, i * tile : (i + 1) * tile], sems.at[i])
        copy.start()
        copies.append(copy)
    for copy in copies:
        copy.wait()


def form_image(section, operator, both, chunks, group):
    height, half = operator.shape[1], both.shape[2]
    tile = 256 if half % 256 == 0 else half
    count = 2 * half // tile
    return pl.pallas_call(
        functools.partial(image_kernel, group=group),
        out_shape=jax.ShapeDtypeStruct((height, 2 * half), BF16),
        in_specs=[pl.BlockSpec(memory_space=pltpu.SMEM)]
        + [pl.BlockSpec(memory_space=pltpu.VMEM)] * (2 + len(chunks)),
        out_specs=pl.BlockSpec(memory_space=pl.ANY),
        scratch_shapes=[
            pltpu.VMEM((count, height, tile), BF16),
            pltpu.SemaphoreType.DMA((count,)),
        ],
        compiler_params=pltpu.CompilerParams(vmem_limit_bytes=16 * 1024 * 1024),
        name="form_image",
    )(section, operator, both, *chunks)


def swap(value, axis, by):
    count = lax.axis_size(axis)
    return lax.ppermute(value, axis, [(i, i ^ by) for i in range(count)])


def swap_by(value, move):
    sections, subs = lax.axis_size("section"), lax.axis_size("sub")
    pairs = []
    for s in range(sections):
        for a in range(subs):
            to_s, to_a = move(s, a)
            pairs.append((s * subs + a, to_s * subs + to_a))
    return lax.ppermute(value, ("section", "sub"), pairs)


def from_next(value, axis):
    count = lax.axis_size(axis)
    return lax.ppermute(value, axis, [(i, (i - 1) % count) for i in range(count)])


def on_device(echoes, chirp, steer, pulse_order, band_coef, band_start, band_width):
    sections, subs = lax.axis_size("section"), lax.axis_size("sub")
    pulses_each = echoes.shape[2]
    group = ceil_to(pulses_each, SUBL)
    section = lax.axis_index("section").astype(jnp.int32).reshape(1)
    coef = jnp.swapaxes(band_coef, 4, 5)
    weights = jnp.swapaxes(steer, 2, 3)
    levels, _, sides, parts, taps, beams = coef.shape
    dims = (levels, sides, parts, taps, beams)

    echo = jnp.transpose(echoes[:, 0], (1, 0, 2))
    halo = from_next(echo, "rng")
    echo, chirp, packed = prepare(
        echo, chirp, coef, band_start, band_width, weights, pulse_order, sections, group
    )
    has_next = (lax.axis_index("rng") < lax.axis_size("rng") - 1).astype(jnp.int32)
    if subs == 2:
        packed_partner = swap(packed, "sub", 1)
    early, late, table = begin_compression(echo, chirp, sections, group)
    place = section + sections * has_next
    keep, give = finish_compression(place, early, late, halo, table, group)
    both = jnp.concatenate([keep, swap(give, "section", 1)], axis=1)
    far = lax.dynamic_index_in_dim(both, section[0] % 2, 0, keepdims=False)
    if subs != 2:
        near = lax.dynamic_index_in_dim(both, 1 - section[0] % 2, 0, keepdims=False)
        chunks = [near, swap(far, "section", 2)]
        return merge_images(section, chunks, packed, dims, sections, group, pulses_each)
    chunks = [
        swap_by(both[0], lambda s, a: (s, a ^ 1) if s % 2 else (s ^ 2, a ^ 1)),
        swap_by(far, lambda s, a: (s ^ 2, a ^ 1) if s % 2 else (s ^ 2, a)),
        swap_by(both[1], lambda s, a: (s ^ 2, a) if s % 2 else (s, a ^ 1)),
    ]
    operator = fold_operator(section, packed, packed_partner, dims, sections, group, pulses_each)
    image = form_image(section, operator, both, chunks, group)
    return image.reshape(2, beams, 1, image.shape[1])


def unpack(chunk, group, each):
    lead = jnp.concatenate([chunk[:group], chunk[group : 2 * group]], axis=1)
    moved, rest = group - each, chunk[2 * group :]
    tail = jnp.concatenate([rest[: each - moved], rest[group // 2 : group // 2 + each - moved]], axis=1)
    return jnp.concatenate([lead, tail], axis=0)


def merge_images(section, chunks, packed, dims, sections, group, each):
    levels, sides, parts, taps, beams = dims
    width = sections * group
    first = levels * sides * parts * taps
    table = packed[first : first + parts * width].reshape(parts, sections, group, beams)
    table = jnp.take(table, section[0] ^ jnp.arange(sections), axis=1)[:, :, :each]
    chunks = [
        unpack(chunk[first : first + 3 * group], group, each)
        for chunk in chunks
        for first in range(0, chunk.shape[0], 3 * group)
    ]
    real, imag = table[0], table[1]
    rows = jnp.concatenate(
        [jnp.concatenate([real, -imag], axis=1), jnp.concatenate([imag, real], axis=1)], axis=2
    )
    image = lax.dot_general(
        rows.reshape(-1, 2 * beams), jnp.concatenate(chunks, axis=0), (((0,), (0,)), ((), ())), preferred_element_type=F32
    ).astype(BF16)
    starts = packed[first + parts * width :].astype(jnp.int32)
    column = jnp.arange(beams, dtype=jnp.int32)
    bits = lax.axis_size("sub").bit_length() - 1
    for level in range(levels):
        partner = swap(image, "sub", 1 << (level % bits))
        operands = []
        for side in range(sides):
            at = (level * sides + side) * parts * taps
            coef = packed[at : at + parts * taps].reshape(parts, taps, beams)
            offset = column[:, None] - starts[level * sides + side][None, :]
            hits = (offset[None] == jnp.arange(taps, dtype=jnp.int32)[:, None, None]).astype(BF16)
            operands.append(jnp.einsum("ptq,tcq->pqc", coef, hits, preferred_element_type=F32).astype(BF16))
        top = jnp.concatenate([operands[0][0], -operands[0][1], operands[1][0], -operands[1][1]], axis=1)
        low = jnp.concatenate([operands[0][1], operands[0][0], operands[1][1], operands[1][0]], axis=1)
        image = jnp.dot(
            jnp.concatenate([top, low], axis=0),
            jnp.concatenate([image, partner], axis=0),
            preferred_element_type=F32,
        ).astype(BF16)
    return image.reshape(2, beams, 1, image.shape[1])


def solution(mesh):
    return jax.shard_map(
        on_device,
        mesh=mesh,
        in_specs=(
            P(None, "sub", "section", "rng"),
            P(),
            P(None, "sub", None, None),
            P("sub", None),
            P(None, "sub", None, None, None, None),
            P(None, "sub", None, None),
            P(None, "sub", None, None),
        ),
        out_specs=P(None, "sub", "rng", "section"),
        check_vma=False,
    )
```

```python
import functools

import jax
import jax.numpy as jnp
from jax import lax
from jax.experimental import pallas as pl
from jax.experimental.pallas import tpu as pltpu
from jax.sharding import PartitionSpec as P

LANE = 128
SUBL = 8
F32 = jnp.float32
BF16 = jnp.bfloat16


def ceil_to(value, unit):
    return -(-value // unit) * unit


def prepare_kernel(*refs, sections, group):
    sources, (echo_out, chirp_out, pack_ref), scratch = refs[:7], refs[7:10], refs[10:]
    coef_ref, start_ref, width_ref, steer_ref, order_ref, starts, sems = scratch
    targets = (echo_out, coef_ref, start_ref, width_ref, steer_ref, order_ref, chirp_out)
    loads = [
        pltpu.make_async_copy(source, target, sems.at[i])
        for i, (source, target) in enumerate(zip(sources, targets))
    ]
    for load in loads:
        load.start()
    for load in loads:
        load.wait()
    levels, _, sides, parts, taps, beams = coef_ref.shape
    tap = lax.broadcasted_iota(jnp.int32, (taps, beams), 0)
    row = 0
    for level in range(levels):
        for side in range(sides):
            used = tap < width_ref[level, 0, side : side + 1, :]
            for part in range(parts):
                entries = coef_ref[level, 0, side, part].astype(F32)
                pack_ref[row : row + taps] = jnp.where(used, entries, 0.0).astype(BF16)
                row += taps
    pulses = order_ref.shape[1]
    each = pulses // sections
    position = lax.broadcasted_iota(jnp.int32, (pulses, pulses), 0)
    hit = (position == order_ref[0:1, :]).astype(F32)
    slot = lax.broadcasted_iota(jnp.int32, (sections * group, pulses), 0)
    pulse = lax.broadcasted_iota(jnp.int32, (sections * group, pulses), 1)
    place = jnp.zeros((sections * group, pulses), F32)
    for s in range(sections):
        inside = (pulse >= s * each) & (pulse < (s + 1) * each)
        place = jnp.where(inside & (slot - s * group == pulse - s * each), 1.0, place)
    pick = lax.dot_general(
        place.astype(BF16), hit.astype(BF16), (((1,), (1,)), ((), ())), preferred_element_type=F32
    )
    for part in range(parts):
        chosen = jnp.dot(pick.astype(BF16), steer_ref[part, 0], preferred_element_type=F32)
        pack_ref[row : row + sections * group] = chosen.astype(BF16)
        row += sections * group
    starts[...] = jnp.zeros_like(starts)
    for level in range(levels):
        starts[sides * level : sides * level + sides] = start_ref[level, 0].astype(F32)
    pack_ref[row : row + starts.shape[0]] = starts[...].astype(BF16)


def pack_rows(levels, sides, parts, taps, sections, group):
    return levels * sides * parts * taps + parts * sections * group + ceil_to(levels * sides, 16)


def prepare(echo, chirp, coef, start, width, steer, order, sections, group):
    levels, _, sides, parts, taps, beams = coef.shape
    sources = (echo, coef, start, width, steer, order, chirp)
    return pl.pallas_call(
        functools.partial(prepare_kernel, sections=sections, group=group),
        out_shape=(
            jax.ShapeDtypeStruct(echo.shape, BF16),
            jax.ShapeDtypeStruct(chirp.shape, BF16),
            jax.ShapeDtypeStruct((pack_rows(levels, sides, parts, taps, sections, group), beams), BF16),
        ),
        in_specs=[pl.BlockSpec(memory_space=pl.ANY)] * len(sources),
        scratch_shapes=[pltpu.VMEM(x.shape, x.dtype) for x in sources[1:6]]
        + [pltpu.VMEM((ceil_to(levels * sides, 16), beams), F32), pltpu.SemaphoreType.DMA((len(sources),))],
        compiler_params=pltpu.CompilerParams(vmem_limit_bytes=16 * 1024 * 1024),
        name="prepare",
    )(*[pltpu.with_memory_space_constraint(x, pltpu.HBM) for x in sources])


def pack_rows_of(real, imag, each):
    group = real.shape[0]
    row = lax.broadcasted_iota(jnp.int32, real.shape, 0)
    return jnp.where(row < each, real, pltpu.roll(imag, each, 0)), group - each


def split_two(value):
    high = value.astype(BF16)
    return high, (value - high.astype(F32)).astype(BF16)


def operator_kernel(index_ref, own_ref, partner_ref, out_ref, weights, *, dims, sections, group, each):
    levels, sides, parts, taps, beams = dims
    width = sections * group
    refs = (own_ref, partner_ref)
    weight_row = levels * sides * parts * taps
    start_row = weight_row + parts * width

    def band(ref, level, side):
        first = ((level * sides + side) * parts) * taps
        tables = [ref[first + p * taps : first + (p + 1) * taps].astype(F32) for p in range(parts)]
        start = ref[start_row : start_row + ceil_to(levels * sides, 16)].astype(F32)
        start = start[level * sides + side : level * sides + side + 1].astype(jnp.int32)
        found = [[], []]
        for c in range(0, beams, SUBL):
            column = lax.broadcasted_iota(jnp.int32, (SUBL, beams), 0) + c
            offset = column - start
            spot = offset & (SUBL - 1)
            for p in range(parts):
                value = jnp.zeros((SUBL, beams), F32)
                for t in range(0, taps, SUBL):
                    got = jnp.take_along_axis(
                        tables[p][t : t + SUBL], spot, axis=0, mode="promise_in_bounds"
                    )
                    value = jnp.where((offset >= t) & (offset < t + SUBL), got, value)
                found[p].append(value)
        return [jnp.concatenate(f, axis=0) for f in found]

    def complex_operand(real, imag):
        top = jnp.concatenate([real, imag], axis=1)
        low = jnp.concatenate([-imag, real], axis=1)
        return jnp.concatenate([top, low], axis=0).astype(BF16)

    section = index_ref[0]
    images = []
    for a in range(2):
        for p in range(parts):
            weights[...] = refs[a][weight_row + p * width : weight_row + (p + 1) * width].astype(F32)
            rows = []
            for j in range(sections):
                at = pl.multiple_of((section ^ j) * group, group)
                rows.append(weights[pl.ds(at, group)])
            images.append(jnp.concatenate(rows, axis=0))
    zero = jnp.zeros((width, 2 * beams), F32)
    own = jnp.concatenate([jnp.concatenate(images[0:2], axis=1), zero], axis=0)
    partner = jnp.concatenate([zero, jnp.concatenate(images[2:4], axis=1)], axis=0)
    for level in range(levels):
        own_high, own_low = split_two(own)
        partner_high, partner_low = split_two(partner)
        own_rows = jnp.concatenate([own_high, own_low], axis=0)
        partner_rows = jnp.concatenate([partner_high, partner_low], axis=0)

        def merged(ref, mine, other):
            product = jnp.dot(
                mine, complex_operand(*band(ref, level, 0)), preferred_element_type=F32
            ) + jnp.dot(other, complex_operand(*band(ref, level, 1)), preferred_element_type=F32)
            return product[: 2 * width] + product[2 * width :]

        following = merged(own_ref, own_rows, partner_rows)
        if level < levels - 1:
            partner = merged(partner_ref, partner_rows, own_rows)
        own = following
    full, left, right = [], [], []
    for j in range(2 * sections):
        real = own[j * group : (j + 1) * group, :beams]
        imag = own[j * group : (j + 1) * group, beams:]
        straight = jnp.concatenate([real, imag], axis=1)
        turned = jnp.concatenate([-imag, real], axis=1)
        lead, moved = pack_rows_of(straight, turned, each)
        row = lax.broadcasted_iota(jnp.int32, lead.shape, 0)
        full.append(lead)
        left.append(jnp.where(row < group // 2, pltpu.roll(turned, group - moved, 0), 0.0))
        right.append(jnp.where(row >= group // 2, pltpu.roll(turned, group // 2 - moved, 0), 0.0))
    pairs = sections // 2
    first_core = section % 2 == 0
    for half, rest in enumerate((left, right)):
        sources = [jnp.concatenate([full[j], rest[j]], axis=0) for j in range(2 * sections)]
        quarters = [jnp.concatenate(sources[q * pairs : (q + 1) * pairs], axis=0) for q in range(4)]
        quarters = [
            quarters[0],
            quarters[3],
            jnp.where(first_core, quarters[1], quarters[2]),
            jnp.where(first_core, quarters[2], quarters[1]),
        ]
        high, low = split_two(jnp.concatenate(quarters, axis=0).T)
        out_ref[half] = jnp.concatenate([high, low], axis=1)


def fold_operator(section, own, partner, dims, sections, group, each):
    beams = dims[-1]
    width = sections * group
    return pl.pallas_call(
        functools.partial(operator_kernel, dims=dims, sections=sections, group=group, each=each),
        out_shape=jax.ShapeDtypeStruct((2, 2 * beams, 8 * width), BF16),
        in_specs=[
            pl.BlockSpec(memory_space=pltpu.SMEM),
            pl.BlockSpec(memory_space=pltpu.VMEM),
            pl.BlockSpec(memory_space=pltpu.VMEM),
        ],
        scratch_shapes=[pltpu.VMEM((width, beams), F32)],
        compiler_params=pltpu.CompilerParams(vmem_limit_bytes=16 * 1024 * 1024),
        name="fold_operator",
    )(section, own, partner)


def lay_out(rows, refs, held, first, blocks, group, keep):
    span = blocks * LANE
    rows[...] = jnp.zeros_like(rows)
    for m, ref in enumerate(refs):
        for p in range(ref.shape[0]):
            samples = ref[p, :, :span].astype(F32)
            samples = samples if keep is None else jnp.where(keep, samples, 0.0)
            for c in range(2):
                rows[c, m * group + p : m * group + p + 1, :] = samples[c : c + 1]
    stack = rows.shape[1]
    for b in range(blocks):
        for c in range(2):
            held[(first + b) * stack : (first + b + 1) * stack, c * LANE : (c + 1) * LANE] = rows[
                c, :, b * LANE : (b + 1) * LANE
            ].astype(BF16)


def correlate(held, table, first, blocks, stack):
    lags = table.shape[0] // (2 * LANE)
    pieces = []
    for lag in range(lags):
        at = pl.multiple_of((first + lag) * stack, stack)
        pieces.append(held[pl.ds(at, blocks * stack)])
    return jnp.dot(jnp.concatenate(pieces, axis=1), table[...], preferred_element_type=F32)


def as_chunk(done, source, chunk, stack, group, each):
    real, imag = [
        jnp.concatenate(
            [
                done[b * stack + source * group : b * stack + (source + 1) * group, c * LANE : (c + 1) * LANE]
                for b in range(chunk)
            ],
            axis=1,
        )
        for c in range(2)
    ]
    middle = chunk * LANE // 2
    lead, moved = pack_rows_of(real, imag, each)
    row = lax.broadcasted_iota(jnp.int32, (group, middle), 0)
    rest = jnp.where(
        row < group // 2,
        pltpu.roll(imag[:, :middle], group - moved, 0),
        pltpu.roll(imag[:, middle:], group // 2 - moved, 0),
    )
    return jnp.concatenate([lead[:, :middle], lead[:, middle:], rest], axis=0).astype(BF16)


def begin_kernel(index_ref, echo_ref, other_ref, chirp_ref, early_ref, late_ref, table, rows, held, *, group):
    pulses, _, length = echo_ref.shape
    extra = chirp_ref.shape[1] // LANE
    reverse = LANE - 1 - lax.broadcasted_iota(jnp.int32, (2, LANE), 1)
    below = lax.broadcasted_iota(jnp.int32, (LANE, LANE), 1) <= lax.broadcasted_iota(
        jnp.int32, (LANE, LANE), 0
    )
    before = [jnp.zeros((LANE, LANE), F32)] * 2
    for lag in range(extra + 1):
        if lag < extra:
            piece = chirp_ref[:, lag * LANE : (lag + 1) * LANE].astype(F32)
            piece = jnp.take_along_axis(piece, reverse, axis=1, mode="promise_in_bounds")
            turned = [
                pltpu.roll(
                    jnp.broadcast_to(piece[c : c + 1], (LANE, LANE)), 1, 1, stride=1, stride_axis=0
                )
                for c in range(2)
            ]
        else:
            turned = [jnp.zeros((LANE, LANE), F32)] * 2
        real, imag = [jnp.where(below, turned[c], before[c]) for c in range(2)]
        before = turned
        at = lag * 2 * LANE
        table[at : at + LANE, :LANE] = real.astype(BF16)
        table[at : at + LANE, LANE:] = (-imag).astype(BF16)
        table[at + LANE : at + 2 * LANE, :LANE] = imag.astype(BF16)
        table[at + LANE : at + 2 * LANE, LANE:] = real.astype(BF16)
    blocks, stack = length // LANE, rows.shape[1]
    lay_out(rows, (echo_ref, other_ref), held, 0, blocks, group, None)
    kept = late_ref.shape[0]
    late_ref[...] = held[blocks * stack - kept :]
    chunk = 2 * early_ref.shape[1] // LANE
    done = correlate(held, table, index_ref[0] % 2 * chunk, chunk, stack)
    early_ref[...] = jnp.concatenate(
        [as_chunk(done, m, chunk, stack, group, pulses) for m in range(2)], axis=0
    )


def finish_kernel(
    index_ref, early_ref, late_ref, halo_ref, other_ref, table,
    near_ref, far_ref, first_ref, second_ref, rows, held, *, group, sections
):
    pulses = halo_ref.shape[0]
    section = lax.rem(index_ref[0], sections)
    side, core = section // 2, section % 2
    stack = rows.shape[1]
    kept, taps = late_ref.shape[0], rows.shape[2]
    held[:kept] = late_ref[...]
    lay_out(rows, (halo_ref, other_ref), held, kept // stack, taps // LANE, group, index_ref[0] >= sections)
    chunk = 2 * early_ref.shape[1] // LANE
    done = correlate(held, table, core * chunk, chunk, stack)
    early = early_ref[...]
    late = jnp.concatenate([as_chunk(done, m, chunk, stack, group, pulses) for m in range(2)], axis=0)

    def put(ref, is_late):
        @pl.when(is_late)
        def _():
            ref[...] = late

        @pl.when(jnp.logical_not(is_late))
        def _():
            ref[...] = early

    put(near_ref, side == 1)
    put(far_ref, side == 0)
    put(first_ref, side == core)
    put(second_ref, side != core)


def begin_compression(section, echo, other, chirp, sections, group):
    _, _, length = echo.shape
    taps = chirp.shape[1]
    chunk, stack = length // sections, 2 * group
    return pl.pallas_call(
        functools.partial(begin_kernel, group=group),
        out_shape=(
            jax.ShapeDtypeStruct((6 * group, chunk // 2), BF16),
            jax.ShapeDtypeStruct((length // 2 // LANE * stack, 2 * LANE), BF16),
            jax.ShapeDtypeStruct(((taps // LANE + 1) * 2 * LANE, 2 * LANE), BF16),
        ),
        in_specs=[pl.BlockSpec(memory_space=pltpu.SMEM)] + [pl.BlockSpec(memory_space=pltpu.VMEM)] * 3,
        scratch_shapes=[
            pltpu.VMEM((2, stack, length), F32),
            pltpu.VMEM((length // LANE * stack, 2 * LANE), BF16),
        ],
        compiler_params=pltpu.CompilerParams(vmem_limit_bytes=24 * 1024 * 1024),
        name="begin_compression",
    )(section, echo, other, chirp)


def finish_compression(place, early, late, halo, other, table, sections, group):
    stack, taps = 2 * group, table.shape[0] // 2 - LANE
    return pl.pallas_call(
        functools.partial(finish_kernel, group=group, sections=sections),
        out_shape=[jax.ShapeDtypeStruct(early.shape, BF16)] * 4,
        in_specs=[pl.BlockSpec(memory_space=pltpu.SMEM)] + [pl.BlockSpec(memory_space=pltpu.VMEM)] * 5,
        scratch_shapes=[
            pltpu.VMEM((2, stack, taps), F32),
            pltpu.VMEM((late.shape[0] + taps // LANE * stack, 2 * LANE), BF16),
        ],
        compiler_params=pltpu.CompilerParams(vmem_limit_bytes=24 * 1024 * 1024),
        name="finish_compression",
    )(place, early, late, halo, other, table)


def image_kernel(operator_ref, *refs, group):
    chunks, (out_ref, parts, sems) = refs[:-3], refs[-3:]
    count, _, tile = parts.shape
    width = chunks[0].shape[1]
    held = [chunk[...].astype(F32) for chunk in chunks]
    copies = []
    for i in range(count):
        half, at = divmod(i * tile, width)
        rows = []
        for value in held:
            for first in range(0, value.shape[0], 3 * group):
                rows.append(value[first + half * group : first + (half + 1) * group, at : at + tile])
                rows.append(value[first + 2 * group : first + 3 * group, at : at + tile])
        pulses = jnp.concatenate(rows, axis=0).astype(BF16)
        result = jnp.dot(
            operator_ref[half], jnp.concatenate([pulses, pulses], axis=0), preferred_element_type=F32
        )
        parts[i] = result.astype(BF16)
        copy = pltpu.make_async_copy(parts.at[i], out_ref.at[:, i * tile : (i + 1) * tile], sems.at[i])
        copy.start()
        copies.append(copy)
    for copy in copies:
        copy.wait()


def form_image(operator, chunks, group):
    height, half = operator.shape[1], chunks[0].shape[1]
    tile = 256 if half % 256 == 0 else half
    count = 2 * half // tile
    return pl.pallas_call(
        functools.partial(image_kernel, group=group),
        out_shape=jax.ShapeDtypeStruct((height, 2 * half), BF16),
        in_specs=[pl.BlockSpec(memory_space=pltpu.VMEM)] * (1 + len(chunks)),
        out_specs=pl.BlockSpec(memory_space=pl.ANY),
        scratch_shapes=[
            pltpu.VMEM((count, height, tile), BF16),
            pltpu.SemaphoreType.DMA((count,)),
        ],
        compiler_params=pltpu.CompilerParams(vmem_limit_bytes=16 * 1024 * 1024),
        name="form_image",
    )(operator, *chunks)


def swap(value, axis, by):
    count = lax.axis_size(axis)
    return lax.ppermute(value, axis, [(i, i ^ by) for i in range(count)])


def swap_by(value, move):
    sections, subs = lax.axis_size("section"), lax.axis_size("sub")
    pairs = []
    for s in range(sections):
        for a in range(subs):
            to_s, to_a = move(s, a)
            pairs.append((s * subs + a, to_s * subs + to_a))
    return lax.ppermute(value, ("section", "sub"), pairs)


def from_next(value, axis):
    count = lax.axis_size(axis)
    return lax.ppermute(value, axis, [(i, (i - 1) % count) for i in range(count)])


def on_device(echoes, chirp, steer, pulse_order, band_coef, band_start, band_width):
    sections, subs = lax.axis_size("section"), lax.axis_size("sub")
    pulses_each = echoes.shape[2]
    group = ceil_to(pulses_each, SUBL)
    section = lax.axis_index("section").astype(jnp.int32).reshape(1)
    coef = jnp.swapaxes(band_coef, 4, 5)
    weights = jnp.swapaxes(steer, 2, 3)
    levels, _, sides, parts, taps, beams = coef.shape
    dims = (levels, sides, parts, taps, beams)

    echo = jnp.transpose(echoes[:, 0], (1, 0, 2))
    halo = from_next(echo, "rng")
    other = swap(echo, "section", 1)
    has_next = (lax.axis_index("rng") < lax.axis_size("rng") - 1).astype(jnp.int32)
    echo, chirp, packed = prepare(
        echo, chirp, coef, band_start, band_width, weights, pulse_order, sections, group
    )
    packed_partner = swap(packed, "sub", 1) if subs == 2 else packed
    halo, chirp = lax.optimization_barrier((halo, chirp))
    early, late, table = begin_compression(section, echo, other, chirp, sections, group)
    place = section + sections * has_next
    near, far, first, second = finish_compression(
        place, early, late, halo, swap(halo, "section", 1), table, sections, group
    )
    if subs != 2:
        chunks = [near, swap(far, "section", 2)]
        return merge_images(section, chunks, packed, dims, sections, group, pulses_each)
    chunks = [
        near,
        swap_by(far, lambda s, a: (s ^ 2, a ^ 1)),
        swap_by(first, lambda s, a: (s, a ^ 1) if s % 2 else (s ^ 2, a)),
        swap_by(second, lambda s, a: (s ^ 2, a) if s % 2 else (s, a ^ 1)),
    ]
    operator = fold_operator(section, packed, packed_partner, dims, sections, group, pulses_each)
    image = form_image(operator, chunks, group)
    return image.reshape(2, beams, 1, image.shape[1])


def unpack(chunk, group, each):
    lead = jnp.concatenate([chunk[:group], chunk[group : 2 * group]], axis=1)
    moved, rest = group - each, chunk[2 * group :]
    tail = jnp.concatenate([rest[: each - moved], rest[group // 2 : group // 2 + each - moved]], axis=1)
    return jnp.concatenate([lead, tail], axis=0)


def merge_images(section, chunks, packed, dims, sections, group, each):
    levels, sides, parts, taps, beams = dims
    width = sections * group
    first = levels * sides * parts * taps
    table = packed[first : first + parts * width].reshape(parts, sections, group, beams)
    table = jnp.take(table, section[0] ^ jnp.arange(sections), axis=1)[:, :, :each]
    chunks = [
        unpack(chunk[first : first + 3 * group], group, each)
        for chunk in chunks
        for first in range(0, chunk.shape[0], 3 * group)
    ]
    real, imag = table[0], table[1]
    rows = jnp.concatenate(
        [jnp.concatenate([real, -imag], axis=1), jnp.concatenate([imag, real], axis=1)], axis=2
    )
    image = lax.dot_general(
        rows.reshape(-1, 2 * beams), jnp.concatenate(chunks, axis=0), (((0,), (0,)), ((), ())), preferred_element_type=F32
    ).astype(BF16)
    starts = packed[first + parts * width :].astype(jnp.int32)
    column = jnp.arange(beams, dtype=jnp.int32)
    bits = lax.axis_size("sub").bit_length() - 1
    for level in range(levels):
        partner = swap(image, "sub", 1 << (level % bits))
        operands = []
        for side in range(sides):
            at = (level * sides + side) * parts * taps
            coef = packed[at : at + parts * taps].reshape(parts, taps, beams)
            offset = column[:, None] - starts[level * sides + side][None, :]
            hits = (offset[None] == jnp.arange(taps, dtype=jnp.int32)[:, None, None]).astype(BF16)
            operands.append(jnp.einsum("ptq,tcq->pqc", coef, hits, preferred_element_type=F32).astype(BF16))
        top = jnp.concatenate([operands[0][0], -operands[0][1], operands[1][0], -operands[1][1]], axis=1)
        low = jnp.concatenate([operands[0][1], operands[0][0], operands[1][1], operands[1][0]], axis=1)
        image = jnp.dot(
            jnp.concatenate([top, low], axis=0),
            jnp.concatenate([image, partner], axis=0),
            preferred_element_type=F32,
        ).astype(BF16)
    return image.reshape(2, beams, 1, image.shape[1])


def solution(mesh):
    return jax.shard_map(
        on_device,
        mesh=mesh,
        in_specs=(
            P(None, "sub", "section", "rng"),
            P(),
            P(None, "sub", None, None),
            P("sub", None),
            P(None, "sub", None, None, None, None),
            P(None, "sub", None, None),
            P(None, "sub", None, None),
        ),
        out_specs=P(None, "sub", "rng", "section"),
        check_vma=False,
    )
```

```python
import functools

import jax
import jax.numpy as jnp
from jax import lax
from jax.experimental import pallas as pl
from jax.experimental.pallas import tpu as pltpu
from jax.sharding import PartitionSpec as P

LANE = 128
SUBL = 8
F32 = jnp.float32
BF16 = jnp.bfloat16


def ceil_to(value, unit):
    return -(-value // unit) * unit


def prepare_kernel(*refs, sections, group):
    sources, (echo_out, chirp_out, pack_ref), scratch = refs[:7], refs[7:10], refs[10:]
    coef_ref, start_ref, width_ref, steer_ref, order_ref, starts, sems = scratch
    targets = (echo_out, coef_ref, start_ref, width_ref, steer_ref, order_ref, chirp_out)
    loads = [
        pltpu.make_async_copy(source, target, sems.at[i])
        for i, (source, target) in enumerate(zip(sources, targets))
    ]
    for load in loads:
        load.start()
    for load in loads:
        load.wait()
    levels, _, sides, parts, taps, beams = coef_ref.shape
    tap = lax.broadcasted_iota(jnp.int32, (taps, beams), 0)
    row = 0
    for level in range(levels):
        for side in range(sides):
            used = tap < width_ref[level, 0, side : side + 1, :]
            for part in range(parts):
                entries = coef_ref[level, 0, side, part].astype(F32)
                pack_ref[row : row + taps] = jnp.where(used, entries, 0.0).astype(BF16)
                row += taps
    pulses = order_ref.shape[1]
    each = pulses // sections
    position = lax.broadcasted_iota(jnp.int32, (pulses, pulses), 0)
    hit = (position == order_ref[0:1, :]).astype(F32)
    slot = lax.broadcasted_iota(jnp.int32, (sections * group, pulses), 0)
    pulse = lax.broadcasted_iota(jnp.int32, (sections * group, pulses), 1)
    place = jnp.zeros((sections * group, pulses), F32)
    for s in range(sections):
        inside = (pulse >= s * each) & (pulse < (s + 1) * each)
        place = jnp.where(inside & (slot - s * group == pulse - s * each), 1.0, place)
    pick = lax.dot_general(
        place.astype(BF16), hit.astype(BF16), (((1,), (1,)), ((), ())), preferred_element_type=F32
    )
    for part in range(parts):
        chosen = jnp.dot(pick.astype(BF16), steer_ref[part, 0], preferred_element_type=F32)
        pack_ref[row : row + sections * group] = chosen.astype(BF16)
        row += sections * group
    starts[...] = jnp.zeros_like(starts)
    for level in range(levels):
        starts[sides * level : sides * level + sides] = start_ref[level, 0].astype(F32)
    pack_ref[row : row + starts.shape[0]] = starts[...].astype(BF16)


def pack_rows(levels, sides, parts, taps, sections, group):
    return levels * sides * parts * taps + parts * sections * group + ceil_to(levels * sides, 16)


def prepare(echo, chirp, coef, start, width, steer, order, sections, group):
    levels, _, sides, parts, taps, beams = coef.shape
    sources = (echo, coef, start, width, steer, order, chirp)
    return pl.pallas_call(
        functools.partial(prepare_kernel, sections=sections, group=group),
        out_shape=(
            jax.ShapeDtypeStruct(echo.shape, BF16),
            jax.ShapeDtypeStruct(chirp.shape, BF16),
            jax.ShapeDtypeStruct((pack_rows(levels, sides, parts, taps, sections, group), beams), BF16),
        ),
        in_specs=[pl.BlockSpec(memory_space=pl.ANY)] * len(sources),
        scratch_shapes=[pltpu.VMEM(x.shape, x.dtype) for x in sources[1:6]]
        + [pltpu.VMEM((ceil_to(levels * sides, 16), beams), F32), pltpu.SemaphoreType.DMA((len(sources),))],
        compiler_params=pltpu.CompilerParams(vmem_limit_bytes=16 * 1024 * 1024),
        name="prepare",
    )(*[pltpu.with_memory_space_constraint(x, pltpu.HBM) for x in sources])


def pack_rows_of(real, imag, each):
    group = real.shape[0]
    row = lax.broadcasted_iota(jnp.int32, real.shape, 0)
    return jnp.where(row < each, real, pltpu.roll(imag, each, 0)), group - each


def split_two(value):
    high = value.astype(BF16)
    return high, (value - high.astype(F32)).astype(BF16)


def operator_kernel(index_ref, own_ref, partner_ref, out_ref, weights, *, dims, sections, group, each):
    levels, sides, parts, taps, beams = dims
    width = sections * group
    refs = (own_ref, partner_ref)
    weight_row = levels * sides * parts * taps
    start_row = weight_row + parts * width

    def band(ref, level, side):
        first = ((level * sides + side) * parts) * taps
        tables = [ref[first + p * taps : first + (p + 1) * taps].astype(F32) for p in range(parts)]
        start = ref[start_row : start_row + ceil_to(levels * sides, 16)].astype(F32)
        start = start[level * sides + side : level * sides + side + 1].astype(jnp.int32)
        found = [[], []]
        for c in range(0, beams, SUBL):
            column = lax.broadcasted_iota(jnp.int32, (SUBL, beams), 0) + c
            offset = column - start
            spot = offset & (SUBL - 1)
            for p in range(parts):
                value = jnp.zeros((SUBL, beams), F32)
                for t in range(0, taps, SUBL):
                    got = jnp.take_along_axis(
                        tables[p][t : t + SUBL], spot, axis=0, mode="promise_in_bounds"
                    )
                    value = jnp.where((offset >= t) & (offset < t + SUBL), got, value)
                found[p].append(value)
        return [jnp.concatenate(f, axis=0) for f in found]

    def complex_operand(real, imag):
        top = jnp.concatenate([real, imag], axis=1)
        low = jnp.concatenate([-imag, real], axis=1)
        return jnp.concatenate([top, low], axis=0).astype(BF16)

    section = index_ref[0]
    images = []
    for a in range(2):
        for p in range(parts):
            weights[...] = refs[a][weight_row + p * width : weight_row + (p + 1) * width].astype(F32)
            rows = []
            for j in range(sections):
                at = pl.multiple_of((section ^ j) * group, group)
                rows.append(weights[pl.ds(at, group)])
            images.append(jnp.concatenate(rows, axis=0))
    zero = jnp.zeros((width, 2 * beams), F32)
    own = jnp.concatenate([jnp.concatenate(images[0:2], axis=1), zero], axis=0)
    partner = jnp.concatenate([zero, jnp.concatenate(images[2:4], axis=1)], axis=0)
    for level in range(levels):
        own_high, own_low = split_two(own)
        partner_high, partner_low = split_two(partner)
        own_rows = jnp.concatenate([own_high, own_low], axis=0)
        partner_rows = jnp.concatenate([partner_high, partner_low], axis=0)

        def merged(ref, mine, other):
            product = jnp.dot(
                mine, complex_operand(*band(ref, level, 0)), preferred_element_type=F32
            ) + jnp.dot(other, complex_operand(*band(ref, level, 1)), preferred_element_type=F32)
            return product[: 2 * width] + product[2 * width :]

        following = merged(own_ref, own_rows, partner_rows)
        if level < levels - 1:
            partner = merged(partner_ref, partner_rows, own_rows)
        own = following
    full, left, right = [], [], []
    for j in range(2 * sections):
        real = own[j * group : (j + 1) * group, :beams]
        imag = own[j * group : (j + 1) * group, beams:]
        straight = jnp.concatenate([real, imag], axis=1)
        turned = jnp.concatenate([-imag, real], axis=1)
        lead, moved = pack_rows_of(straight, turned, each)
        row = lax.broadcasted_iota(jnp.int32, lead.shape, 0)
        full.append(lead)
        left.append(jnp.where(row < group // 2, pltpu.roll(turned, group - moved, 0), 0.0))
        right.append(jnp.where(row >= group // 2, pltpu.roll(turned, group // 2 - moved, 0), 0.0))
    pairs = sections // 2
    first_core = section % 2 == 0
    for half, rest in enumerate((left, right)):
        sources = [jnp.concatenate([full[j], rest[j]], axis=0) for j in range(2 * sections)]
        quarters = [jnp.concatenate(sources[q * pairs : (q + 1) * pairs], axis=0) for q in range(4)]
        quarters = [
            quarters[0],
            quarters[3],
            jnp.where(first_core, quarters[1], quarters[2]),
            jnp.where(first_core, quarters[2], quarters[1]),
        ]
        high, low = split_two(jnp.concatenate(quarters, axis=0).T)
        out_ref[half] = jnp.concatenate([high, low], axis=1)


def fold_operator(section, own, partner, dims, sections, group, each):
    beams = dims[-1]
    width = sections * group
    return pl.pallas_call(
        functools.partial(operator_kernel, dims=dims, sections=sections, group=group, each=each),
        out_shape=jax.ShapeDtypeStruct((2, 2 * beams, 8 * width), BF16),
        in_specs=[
            pl.BlockSpec(memory_space=pltpu.SMEM),
            pl.BlockSpec(memory_space=pltpu.VMEM),
            pl.BlockSpec(memory_space=pltpu.VMEM),
        ],
        scratch_shapes=[pltpu.VMEM((width, beams), F32)],
        compiler_params=pltpu.CompilerParams(vmem_limit_bytes=16 * 1024 * 1024),
        name="fold_operator",
    )(section, own, partner)


def correlate(rows, even, odd, table, blocks, group):
    extra = table.shape[0] // (2 * LANE) - 1
    total = blocks + extra
    held = [
        jnp.concatenate(
            [rows[:group, b * LANE : (b + 1) * LANE], rows[group:, b * LANE : (b + 1) * LANE]], axis=1
        )
        for b in range(total)
    ]
    for b in range(0, total, 2):
        even[b * group : (b + 2) * group] = jnp.concatenate(held[b : b + 2], axis=0).astype(BF16)
    for b in range(1, total - 1, 2):
        odd[(b - 1) * group : (b + 1) * group] = jnp.concatenate(held[b : b + 2], axis=0).astype(BF16)
    window = blocks * group
    pieces = []
    for lag in range(extra + 1):
        source, at = (even, lag) if lag % 2 == 0 else (odd, lag - 1)
        pieces.append(source[at * group : at * group + window])
    return jnp.dot(jnp.concatenate(pieces, axis=1), table[...], preferred_element_type=F32)


def as_chunk(done, s, chunk, group, each):
    real, imag = [
        jnp.concatenate(
            [
                done[(s * chunk + b) * group : (s * chunk + b + 1) * group, c * LANE : (c + 1) * LANE]
                for b in range(chunk)
            ],
            axis=1,
        )
        for c in range(2)
    ]
    middle = chunk * LANE // 2
    lead, moved = pack_rows_of(real, imag, each)
    row = lax.broadcasted_iota(jnp.int32, (group, middle), 0)
    rest = jnp.where(
        row < group // 2,
        pltpu.roll(imag[:, :middle], group - moved, 0),
        pltpu.roll(imag[:, middle:], group // 2 - moved, 0),
    )
    return jnp.concatenate([lead[:, :middle], lead[:, middle:], rest], axis=0).astype(BF16)


def begin_kernel(echo_ref, chirp_ref, early_ref, late_ref, table, rows, even, odd, *, group):
    pulses, _, length = echo_ref.shape
    extra = chirp_ref.shape[1] // LANE
    reverse = LANE - 1 - lax.broadcasted_iota(jnp.int32, (2, LANE), 1)
    below = lax.broadcasted_iota(jnp.int32, (LANE, LANE), 1) <= lax.broadcasted_iota(
        jnp.int32, (LANE, LANE), 0
    )
    before = [jnp.zeros((LANE, LANE), F32)] * 2
    for lag in range(extra + 1):
        if lag < extra:
            piece = chirp_ref[:, lag * LANE : (lag + 1) * LANE].astype(F32)
            piece = jnp.take_along_axis(piece, reverse, axis=1, mode="promise_in_bounds")
            turned = [
                pltpu.roll(
                    jnp.broadcast_to(piece[c : c + 1], (LANE, LANE)), 1, 1, stride=1, stride_axis=0
                )
                for c in range(2)
            ]
        else:
            turned = [jnp.zeros((LANE, LANE), F32)] * 2
        real, imag = [jnp.where(below, turned[c], before[c]) for c in range(2)]
        before = turned
        at = lag * 2 * LANE
        table[at : at + LANE, :LANE] = real.astype(BF16)
        table[at : at + LANE, LANE:] = (-imag).astype(BF16)
        table[at + LANE : at + 2 * LANE, :LANE] = imag.astype(BF16)
        table[at + LANE : at + 2 * LANE, LANE:] = real.astype(BF16)
    rows[...] = jnp.zeros_like(rows)
    for p in range(pulses):
        near = echo_ref[p].astype(F32)
        for c in range(2):
            rows[c * group + p : c * group + p + 1, :] = near[c : c + 1]
    late_ref[...] = rows[:, length - late_ref.shape[1] :]
    done = correlate(rows, even, odd, table, length // LANE - extra, group)
    for s in range(early_ref.shape[0]):
        early_ref[s] = as_chunk(done, s, 2 * early_ref.shape[2] // LANE, group, pulses)


def finish_kernel(
    index_ref, early_ref, late_ref, odd_halo_ref, halo_ref, table, keep_ref, give_ref, rows, even, odd, *, group
):
    pulses = halo_ref.shape[0]
    span = late_ref.shape[1]
    taps = rows.shape[1] - span
    ready = early_ref.shape[0]
    chunk = 2 * early_ref.shape[2]
    sections = ready + span // chunk
    section = lax.rem(index_ref[0], sections)
    kind = index_ref[0] // sections
    rows[:, :span] = late_ref[...]
    rows[:, span:] = jnp.zeros((2 * group, taps), F32)
    for p in range(pulses):
        far = jnp.where(kind == 1, halo_ref[p, :, :taps].astype(F32), 0.0)
        far = jnp.where(kind == 2, odd_halo_ref[p, :, :taps].astype(F32), far)
        for c in range(2):
            rows[c * group + p : c * group + p + 1, span:] = far[c : c + 1]
    done = correlate(rows, even, odd, table, span // LANE, group)
    for s in range(sections):
        stacked = early_ref[s] if s < ready else as_chunk(done, s - ready, chunk // LANE, group, pulses)
        slot = section ^ s
        far_chunk, other_core = slot // 2, slot % 2
        place = far_chunk ^ 1 ^ (section % 2) ^ other_core

        @pl.when(other_core == 0)
        def _():
            keep_ref[place] = stacked

        @pl.when(other_core == 1)
        def _():
            give_ref[place] = stacked


def row_scratch(blocks, group):
    return [
        pltpu.VMEM((2 * group, blocks * LANE), F32),
        pltpu.VMEM((blocks * group, 2 * LANE), BF16),
        pltpu.VMEM((blocks * group, 2 * LANE), BF16),
    ]


def begin_compression(echo, chirp, sections, group):
    _, _, length = echo.shape
    taps = chirp.shape[1]
    chunk = length // sections
    early = (length - taps) // chunk
    return pl.pallas_call(
        functools.partial(begin_kernel, group=group),
        out_shape=(
            jax.ShapeDtypeStruct((early, 3 * group, chunk // 2), BF16),
            jax.ShapeDtypeStruct((2 * group, length - early * chunk), F32),
            jax.ShapeDtypeStruct(((taps // LANE + 1) * 2 * LANE, 2 * LANE), BF16),
        ),
        scratch_shapes=row_scratch(length // LANE, group),
        compiler_params=pltpu.CompilerParams(vmem_limit_bytes=24 * 1024 * 1024),
        name="begin_compression",
    )(echo, chirp)


def finish_compression(place, early, late, halos, table, group):
    blocks = late.shape[1] // LANE + table.shape[0] // (2 * LANE) - 1
    return pl.pallas_call(
        functools.partial(finish_kernel, group=group),
        out_shape=[jax.ShapeDtypeStruct((2, *early.shape[1:]), BF16)] * 2,
        in_specs=[pl.BlockSpec(memory_space=pltpu.SMEM)] + [pl.BlockSpec(memory_space=pltpu.VMEM)] * 5,
        scratch_shapes=row_scratch(blocks, group),
        compiler_params=pltpu.CompilerParams(vmem_limit_bytes=24 * 1024 * 1024),
        name="finish_compression",
    )(place, early, late, *halos, table)


def image_kernel(index_ref, operator_ref, both_ref, *refs, group):
    chunks, (out_ref, parts, sems) = refs[:-3], refs[-3:]
    count, _, tile = parts.shape
    width = both_ref.shape[2]
    near = 1 - index_ref[0] % 2
    held = [both_ref[near]] + [chunk[...] for chunk in chunks]
    held = [value.astype(F32) for value in held]
    copies = []
    for i in range(count):
        half, at = divmod(i * tile, width)
        rows = []
        for value in held:
            for first in range(0, value.shape[0], 3 * group):
                rows.append(value[first + half * group : first + (half + 1) * group, at : at + tile])
                rows.append(value[first + 2 * group : first + 3 * group, at : at + tile])
        pulses = jnp.concatenate(rows, axis=0).astype(BF16)
        result = jnp.dot(
            operator_ref[half], jnp.concatenate([pulses, pulses], axis=0), preferred_element_type=F32
        )
        parts[i] = result.astype(BF16)
        copy = pltpu.make_async_copy(parts.at[i], out_ref.at[:, i * tile : (i + 1) * tile], sems.at[i])
        copy.start()
        copies.append(copy)
    for copy in copies:
        copy.wait()


def form_image(section, operator, both, chunks, group):
    height, half = operator.shape[1], both.shape[2]
    tile = 256 if half % 256 == 0 else half
    count = 2 * half // tile
    return pl.pallas_call(
        functools.partial(image_kernel, group=group),
        out_shape=jax.ShapeDtypeStruct((height, 2 * half), BF16),
        in_specs=[pl.BlockSpec(memory_space=pltpu.SMEM)]
        + [pl.BlockSpec(memory_space=pltpu.VMEM)] * (2 + len(chunks)),
        out_specs=pl.BlockSpec(memory_space=pl.ANY),
        scratch_shapes=[
            pltpu.VMEM((count, height, tile), BF16),
            pltpu.SemaphoreType.DMA((count,)),
        ],
        compiler_params=pltpu.CompilerParams(vmem_limit_bytes=16 * 1024 * 1024),
        name="form_image",
    )(section, operator, both, *chunks)


def swap(value, axis, by):
    count = lax.axis_size(axis)
    return lax.ppermute(value, axis, [(i, i ^ by) for i in range(count)])


def swap_by(value, move):
    sections, subs = lax.axis_size("section"), lax.axis_size("sub")
    pairs = []
    for s in range(sections):
        for a in range(subs):
            to_s, to_a = move(s, a)
            pairs.append((s * subs + a, to_s * subs + to_a))
    return lax.ppermute(value, ("section", "sub"), pairs)


def from_next(value, axis):
    count = lax.axis_size(axis)
    results = []
    for parity in (0, 1):
        peers = [min(max(((i + parity) ^ 1) - parity, 0), count - 1) for i in range(count)]
        results.append(lax.ppermute(value, axis, list(enumerate(peers))))
    return results[::-1]


def on_device(echoes, chirp, steer, pulse_order, band_coef, band_start, band_width):
    sections, subs = lax.axis_size("section"), lax.axis_size("sub")
    pulses_each = echoes.shape[2]
    group = ceil_to(pulses_each, SUBL)
    section = lax.axis_index("section").astype(jnp.int32).reshape(1)
    coef = jnp.swapaxes(band_coef, 4, 5)
    weights = jnp.swapaxes(steer, 2, 3)
    levels, _, sides, parts, taps, beams = coef.shape
    dims = (levels, sides, parts, taps, beams)

    echo = jnp.transpose(echoes[:, 0], (1, 0, 2))
    halos = from_next(echo, "rng")
    echo, chirp, packed = prepare(
        echo, chirp, coef, band_start, band_width, weights, pulse_order, sections, group
    )
    rng, last = lax.axis_index("rng").astype(jnp.int32), lax.axis_size("rng") - 1
    kind = jnp.where(rng < last, 1 + rng % 2, 0)
    if subs == 2:
        packed_partner = swap(packed, "sub", 1)
    early, late, table = begin_compression(echo, chirp, sections, group)
    place = section + sections * kind
    keep, give = finish_compression(place, early, late, halos, table, group)
    both = jnp.concatenate([keep, swap(give, "section", 1)], axis=1)
    far = lax.dynamic_index_in_dim(both, section[0] % 2, 0, keepdims=False)
    if subs != 2:
        near = lax.dynamic_index_in_dim(both, 1 - section[0] % 2, 0, keepdims=False)
        chunks = [near, swap(far, "section", 2)]
        return merge_images(section, chunks, packed, dims, sections, group, pulses_each)
    chunks = [
        swap_by(far, lambda s, a: (s ^ 2, a ^ 1)),
        swap_by(both[0], lambda s, a: (s, a ^ 1) if s % 2 else (s ^ 2, a)),
        swap_by(both[1], lambda s, a: (s ^ 2, a) if s % 2 else (s, a ^ 1)),
    ]
    operator = fold_operator(section, packed, packed_partner, dims, sections, group, pulses_each)
    image = form_image(section, operator, both, chunks, group)
    return image.reshape(2, beams, 1, image.shape[1])


def unpack(chunk, group, each):
    lead = jnp.concatenate([chunk[:group], chunk[group : 2 * group]], axis=1)
    moved, rest = group - each, chunk[2 * group :]
    tail = jnp.concatenate([rest[: each - moved], rest[group // 2 : group // 2 + each - moved]], axis=1)
    return jnp.concatenate([lead, tail], axis=0)


def merge_images(section, chunks, packed, dims, sections, group, each):
    levels, sides, parts, taps, beams = dims
    width = sections * group
    first = levels * sides * parts * taps
    table = packed[first : first + parts * width].reshape(parts, sections, group, beams)
    table = jnp.take(table, section[0] ^ jnp.arange(sections), axis=1)[:, :, :each]
    chunks = [
        unpack(chunk[first : first + 3 * group], group, each)
        for chunk in chunks
        for first in range(0, chunk.shape[0], 3 * group)
    ]
    real, imag = table[0], table[1]
    rows = jnp.concatenate(
        [jnp.concatenate([real, -imag], axis=1), jnp.concatenate([imag, real], axis=1)], axis=2
    )
    image = lax.dot_general(
        rows.reshape(-1, 2 * beams), jnp.concatenate(chunks, axis=0), (((0,), (0,)), ((), ())), preferred_element_type=F32
    ).astype(BF16)
    starts = packed[first + parts * width :].astype(jnp.int32)
    column = jnp.arange(beams, dtype=jnp.int32)
    bits = lax.axis_size("sub").bit_length() - 1
    for level in range(levels):
        partner = swap(image, "sub", 1 << (level % bits))
        operands = []
        for side in range(sides):
            at = (level * sides + side) * parts * taps
            coef = packed[at : at + parts * taps].reshape(parts, taps, beams)
            offset = column[:, None] - starts[level * sides + side][None, :]
            hits = (offset[None] == jnp.arange(taps, dtype=jnp.int32)[:, None, None]).astype(BF16)
            operands.append(jnp.einsum("ptq,tcq->pqc", coef, hits, preferred_element_type=F32).astype(BF16))
        top = jnp.concatenate([operands[0][0], -operands[0][1], operands[1][0], -operands[1][1]], axis=1)
        low = jnp.concatenate([operands[0][1], operands[0][0], operands[1][1], operands[1][0]], axis=1)
        image = jnp.dot(
            jnp.concatenate([top, low], axis=0),
            jnp.concatenate([image, partner], axis=0),
            preferred_element_type=F32,
        ).astype(BF16)
    return image.reshape(2, beams, 1, image.shape[1])


def solution(mesh):
    return jax.shard_map(
        on_device,
        mesh=mesh,
        in_specs=(
            P(None, "sub", "section", "rng"),
            P(),
            P(None, "sub", None, None),
            P("sub", None),
            P(None, "sub", None, None, None, None),
            P(None, "sub", None, None),
            P(None, "sub", None, None),
        ),
        out_specs=P(None, "sub", "rng", "section"),
        check_vma=False,
    )
```

```python
import functools

import jax
import jax.numpy as jnp
from jax import lax
from jax.experimental import pallas as pl
from jax.experimental.pallas import tpu as pltpu
from jax.sharding import PartitionSpec as P

LANE = 128
SUBL = 8
F32 = jnp.float32
BF16 = jnp.bfloat16


def ceil_to(value, unit):
    return -(-value // unit) * unit


def prepare_kernel(*refs, sections, group):
    sources, (echo_out, chirp_out, pack_ref), scratch = refs[:7], refs[7:10], refs[10:]
    coef_ref, start_ref, width_ref, steer_ref, order_ref, starts, sems = scratch
    targets = (echo_out, coef_ref, start_ref, width_ref, steer_ref, order_ref, chirp_out)
    loads = [
        pltpu.make_async_copy(source, target, sems.at[i])
        for i, (source, target) in enumerate(zip(sources, targets))
    ]
    for load in loads:
        load.start()
    for load in loads:
        load.wait()
    levels, _, sides, parts, taps, beams = coef_ref.shape
    tap = lax.broadcasted_iota(jnp.int32, (taps, beams), 0)
    row = 0
    for level in range(levels):
        for side in range(sides):
            used = tap < width_ref[level, 0, side : side + 1, :]
            for part in range(parts):
                entries = coef_ref[level, 0, side, part].astype(F32)
                pack_ref[row : row + taps] = jnp.where(used, entries, 0.0).astype(BF16)
                row += taps
    pulses = order_ref.shape[1]
    each = pulses // sections
    position = lax.broadcasted_iota(jnp.int32, (pulses, pulses), 0)
    hit = (position == order_ref[0:1, :]).astype(F32)
    slot = lax.broadcasted_iota(jnp.int32, (sections * group, pulses), 0)
    pulse = lax.broadcasted_iota(jnp.int32, (sections * group, pulses), 1)
    place = jnp.zeros((sections * group, pulses), F32)
    for s in range(sections):
        inside = (pulse >= s * each) & (pulse < (s + 1) * each)
        place = jnp.where(inside & (slot - s * group == pulse - s * each), 1.0, place)
    pick = lax.dot_general(
        place.astype(BF16), hit.astype(BF16), (((1,), (1,)), ((), ())), preferred_element_type=F32
    )
    for part in range(parts):
        chosen = jnp.dot(pick.astype(BF16), steer_ref[part, 0], preferred_element_type=F32)
        pack_ref[row : row + sections * group] = chosen.astype(BF16)
        row += sections * group
    starts[...] = jnp.zeros_like(starts)
    for level in range(levels):
        starts[sides * level : sides * level + sides] = start_ref[level, 0].astype(F32)
    pack_ref[row : row + starts.shape[0]] = starts[...].astype(BF16)


def pack_rows(levels, sides, parts, taps, sections, group):
    return levels * sides * parts * taps + parts * sections * group + ceil_to(levels * sides, 16)


def prepare(echo, chirp, coef, start, width, steer, order, sections, group):
    levels, _, sides, parts, taps, beams = coef.shape
    sources = (echo, coef, start, width, steer, order, chirp)
    return pl.pallas_call(
        functools.partial(prepare_kernel, sections=sections, group=group),
        out_shape=(
            jax.ShapeDtypeStruct(echo.shape, BF16),
            jax.ShapeDtypeStruct(chirp.shape, BF16),
            jax.ShapeDtypeStruct((pack_rows(levels, sides, parts, taps, sections, group), beams), BF16),
        ),
        in_specs=[pl.BlockSpec(memory_space=pl.ANY)] * len(sources),
        scratch_shapes=[pltpu.VMEM(x.shape, x.dtype) for x in sources[1:6]]
        + [pltpu.VMEM((ceil_to(levels * sides, 16), beams), F32), pltpu.SemaphoreType.DMA((len(sources),))],
        compiler_params=pltpu.CompilerParams(vmem_limit_bytes=16 * 1024 * 1024),
        name="prepare",
    )(*[pltpu.with_memory_space_constraint(x, pltpu.HBM) for x in sources])


def pack_rows_of(real, imag, each):
    group = real.shape[0]
    row = lax.broadcasted_iota(jnp.int32, real.shape, 0)
    return jnp.where(row < each, real, pltpu.roll(imag, each, 0)), group - each


def split_two(value):
    high = value.astype(BF16)
    return high, (value - high.astype(F32)).astype(BF16)


def operator_kernel(index_ref, own_ref, partner_ref, out_ref, weights, *, dims, sections, group, each):
    levels, sides, parts, taps, beams = dims
    width = sections * group
    refs = (own_ref, partner_ref)
    weight_row = levels * sides * parts * taps
    start_row = weight_row + parts * width

    def band(ref, level, side):
        first = ((level * sides + side) * parts) * taps
        tables = [ref[first + p * taps : first + (p + 1) * taps].astype(F32) for p in range(parts)]
        start = ref[start_row : start_row + ceil_to(levels * sides, 16)].astype(F32)
        start = start[level * sides + side : level * sides + side + 1].astype(jnp.int32)
        found = [[], []]
        for c in range(0, beams, SUBL):
            column = lax.broadcasted_iota(jnp.int32, (SUBL, beams), 0) + c
            offset = column - start
            spot = offset & (SUBL - 1)
            for p in range(parts):
                value = jnp.zeros((SUBL, beams), F32)
                for t in range(0, taps, SUBL):
                    got = jnp.take_along_axis(
                        tables[p][t : t + SUBL], spot, axis=0, mode="promise_in_bounds"
                    )
                    value = jnp.where((offset >= t) & (offset < t + SUBL), got, value)
                found[p].append(value)
        return [jnp.concatenate(f, axis=0) for f in found]

    def complex_operand(real, imag):
        top = jnp.concatenate([real, imag], axis=1)
        low = jnp.concatenate([-imag, real], axis=1)
        return jnp.concatenate([top, low], axis=0).astype(BF16)

    section = index_ref[0]
    images = []
    for a in range(2):
        for p in range(parts):
            weights[...] = refs[a][weight_row + p * width : weight_row + (p + 1) * width].astype(F32)
            rows = []
            for j in range(sections):
                at = pl.multiple_of((section ^ j) * group, group)
                rows.append(weights[pl.ds(at, group)])
            images.append(jnp.concatenate(rows, axis=0))
    zero = jnp.zeros((width, 2 * beams), F32)
    own = jnp.concatenate([jnp.concatenate(images[0:2], axis=1), zero], axis=0)
    partner = jnp.concatenate([zero, jnp.concatenate(images[2:4], axis=1)], axis=0)
    for level in range(levels):
        own_high, own_low = split_two(own)
        partner_high, partner_low = split_two(partner)
        own_rows = jnp.concatenate([own_high, own_low], axis=0)
        partner_rows = jnp.concatenate([partner_high, partner_low], axis=0)

        def merged(ref, mine, other):
            product = jnp.dot(
                mine, complex_operand(*band(ref, level, 0)), preferred_element_type=F32
            ) + jnp.dot(other, complex_operand(*band(ref, level, 1)), preferred_element_type=F32)
            return product[: 2 * width] + product[2 * width :]

        following = merged(own_ref, own_rows, partner_rows)
        if level < levels - 1:
            partner = merged(partner_ref, partner_rows, own_rows)
        own = following
    full, left, right = [], [], []
    for j in range(2 * sections):
        real = own[j * group : (j + 1) * group, :beams]
        imag = own[j * group : (j + 1) * group, beams:]
        straight = jnp.concatenate([real, imag], axis=1)
        turned = jnp.concatenate([-imag, real], axis=1)
        lead, moved = pack_rows_of(straight, turned, each)
        row = lax.broadcasted_iota(jnp.int32, lead.shape, 0)
        full.append(lead)
        left.append(jnp.where(row < group // 2, pltpu.roll(turned, group - moved, 0), 0.0))
        right.append(jnp.where(row >= group // 2, pltpu.roll(turned, group // 2 - moved, 0), 0.0))
    pairs = sections // 2
    first_core = section % 2 == 0
    for half, rest in enumerate((left, right)):
        sources = [jnp.concatenate([full[j], rest[j]], axis=0) for j in range(2 * sections)]
        quarters = [jnp.concatenate(sources[q * pairs : (q + 1) * pairs], axis=0) for q in range(4)]
        quarters = [
            quarters[0],
            quarters[3],
            jnp.where(first_core, quarters[1], quarters[2]),
            jnp.where(first_core, quarters[2], quarters[1]),
        ]
        high, low = split_two(jnp.concatenate(quarters, axis=0).T)
        out_ref[half] = jnp.concatenate([high, low], axis=1)


def fold_operator(section, own, partner, dims, sections, group, each):
    beams = dims[-1]
    width = sections * group
    return pl.pallas_call(
        functools.partial(operator_kernel, dims=dims, sections=sections, group=group, each=each),
        out_shape=jax.ShapeDtypeStruct((2, 2 * beams, 8 * width), BF16),
        in_specs=[
            pl.BlockSpec(memory_space=pltpu.SMEM),
            pl.BlockSpec(memory_space=pltpu.VMEM),
            pl.BlockSpec(memory_space=pltpu.VMEM),
        ],
        scratch_shapes=[pltpu.VMEM((width, beams), F32)],
        compiler_params=pltpu.CompilerParams(vmem_limit_bytes=16 * 1024 * 1024),
        name="fold_operator",
    )(section, own, partner)


def lay_out(rows, refs, held, first, blocks, group, keep):
    span = blocks * LANE
    rows[...] = jnp.zeros_like(rows)
    for m, ref in enumerate(refs):
        for p in range(ref.shape[0]):
            samples = ref[p, :, :span].astype(F32)
            samples = samples if keep is None else jnp.where(keep, samples, 0.0)
            for c in range(2):
                rows[c, m * group + p : m * group + p + 1, :] = samples[c : c + 1]
    stack = rows.shape[1]
    for b in range(blocks):
        for c in range(2):
            held[(first + b) * stack : (first + b + 1) * stack, c * LANE : (c + 1) * LANE] = rows[
                c, :, b * LANE : (b + 1) * LANE
            ].astype(BF16)


def correlate(held, table, first, blocks, stack):
    lags = table.shape[0] // (2 * LANE)
    pieces = []
    for lag in range(lags):
        at = pl.multiple_of((first + lag) * stack, stack)
        pieces.append(held[pl.ds(at, blocks * stack)])
    return jnp.dot(jnp.concatenate(pieces, axis=1), table[...], preferred_element_type=F32)


def as_chunk(done, source, chunk, stack, group, each):
    real, imag = [
        jnp.concatenate(
            [
                done[b * stack + source * group : b * stack + (source + 1) * group, c * LANE : (c + 1) * LANE]
                for b in range(chunk)
            ],
            axis=1,
        )
        for c in range(2)
    ]
    middle = chunk * LANE // 2
    lead, moved = pack_rows_of(real, imag, each)
    row = lax.broadcasted_iota(jnp.int32, (group, middle), 0)
    rest = jnp.where(
        row < group // 2,
        pltpu.roll(imag[:, :middle], group - moved, 0),
        pltpu.roll(imag[:, middle:], group // 2 - moved, 0),
    )
    return jnp.concatenate([lead[:, :middle], lead[:, middle:], rest], axis=0).astype(BF16)


def table_kernel(chirp_ref, table):
    extra = chirp_ref.shape[1] // LANE
    reverse = LANE - 1 - lax.broadcasted_iota(jnp.int32, (2, LANE), 1)
    below = lax.broadcasted_iota(jnp.int32, (LANE, LANE), 1) <= lax.broadcasted_iota(
        jnp.int32, (LANE, LANE), 0
    )
    before = [jnp.zeros((LANE, LANE), F32)] * 2
    for lag in range(extra + 1):
        if lag < extra:
            piece = chirp_ref[:, lag * LANE : (lag + 1) * LANE].astype(F32)
            piece = jnp.take_along_axis(piece, reverse, axis=1, mode="promise_in_bounds")
            turned = [
                pltpu.roll(
                    jnp.broadcast_to(piece[c : c + 1], (LANE, LANE)), 1, 1, stride=1, stride_axis=0
                )
                for c in range(2)
            ]
        else:
            turned = [jnp.zeros((LANE, LANE), F32)] * 2
        real, imag = [jnp.where(below, turned[c], before[c]) for c in range(2)]
        before = turned
        at = lag * 2 * LANE
        table[at : at + LANE, :LANE] = real.astype(BF16)
        table[at : at + LANE, LANE:] = (-imag).astype(BF16)
        table[at + LANE : at + 2 * LANE, :LANE] = imag.astype(BF16)
        table[at + LANE : at + 2 * LANE, LANE:] = real.astype(BF16)


def begin_kernel(index_ref, echo_ref, other_ref, table, early_ref, late_ref, rows, held, *, group):
    pulses, _, length = echo_ref.shape
    blocks, stack = length // LANE, rows.shape[1]
    lay_out(rows, (echo_ref, other_ref), held, 0, blocks, group, None)
    kept = late_ref.shape[0]
    late_ref[...] = held[blocks * stack - kept :]
    chunk = 2 * early_ref.shape[1] // LANE
    done = correlate(held, table, index_ref[0] % 2 * chunk, chunk, stack)
    early_ref[...] = jnp.concatenate(
        [as_chunk(done, m, chunk, stack, group, pulses) for m in range(2)], axis=0
    )


def finish_kernel(
    index_ref, early_ref, late_ref, halo_ref, other_ref, table,
    near_ref, far_ref, first_ref, second_ref, rows, held, *, group, sections
):
    pulses = halo_ref.shape[0]
    section = lax.rem(index_ref[0], sections)
    side, core = section // 2, section % 2
    stack = rows.shape[1]
    kept, taps = late_ref.shape[0], rows.shape[2]
    held[:kept] = late_ref[...]
    lay_out(rows, (halo_ref, other_ref), held, kept // stack, taps // LANE, group, index_ref[0] >= sections)
    chunk = 2 * early_ref.shape[1] // LANE
    done = correlate(held, table, core * chunk, chunk, stack)
    early = early_ref[...]
    late = jnp.concatenate([as_chunk(done, m, chunk, stack, group, pulses) for m in range(2)], axis=0)

    def put(ref, is_late):
        @pl.when(is_late)
        def _():
            ref[...] = late

        @pl.when(jnp.logical_not(is_late))
        def _():
            ref[...] = early

    put(near_ref, side == 1)
    put(far_ref, side == 0)
    put(first_ref, side == core)
    put(second_ref, side != core)


def lag_tables(chirp):
    lags = chirp.shape[1] // LANE + 1
    return pl.pallas_call(
        table_kernel,
        out_shape=jax.ShapeDtypeStruct((lags * 2 * LANE, 2 * LANE), BF16),
        compiler_params=pltpu.CompilerParams(vmem_limit_bytes=16 * 1024 * 1024),
        name="lag_tables",
    )(chirp)


def begin_compression(section, echo, other, table, sections, group):
    _, _, length = echo.shape
    chunk, stack = length // sections, 2 * group
    return pl.pallas_call(
        functools.partial(begin_kernel, group=group),
        out_shape=(
            jax.ShapeDtypeStruct((6 * group, chunk // 2), BF16),
            jax.ShapeDtypeStruct((length // 2 // LANE * stack, 2 * LANE), BF16),
        ),
        in_specs=[pl.BlockSpec(memory_space=pltpu.SMEM)] + [pl.BlockSpec(memory_space=pltpu.VMEM)] * 3,
        scratch_shapes=[
            pltpu.VMEM((2, stack, length), F32),
            pltpu.VMEM((length // LANE * stack, 2 * LANE), BF16),
        ],
        compiler_params=pltpu.CompilerParams(vmem_limit_bytes=24 * 1024 * 1024),
        name="begin_compression",
    )(section, echo, other, table)


def finish_compression(place, early, late, halo, other, table, sections, group):
    stack, taps = 2 * group, table.shape[0] // 2 - LANE
    return pl.pallas_call(
        functools.partial(finish_kernel, group=group, sections=sections),
        out_shape=[jax.ShapeDtypeStruct(early.shape, BF16)] * 4,
        in_specs=[pl.BlockSpec(memory_space=pltpu.SMEM)] + [pl.BlockSpec(memory_space=pltpu.VMEM)] * 5,
        scratch_shapes=[
            pltpu.VMEM((2, stack, taps), F32),
            pltpu.VMEM((late.shape[0] + taps // LANE * stack, 2 * LANE), BF16),
        ],
        compiler_params=pltpu.CompilerParams(vmem_limit_bytes=24 * 1024 * 1024),
        name="finish_compression",
    )(place, early, late, halo, other, table)


def image_kernel(operator_ref, *refs, group):
    chunks, (out_ref, parts, sems) = refs[:-3], refs[-3:]
    count, _, tile = parts.shape
    width = chunks[0].shape[1]
    held = [chunk[...].astype(F32) for chunk in chunks]
    copies = []
    for i in range(count):
        half, at = divmod(i * tile, width)
        rows = []
        for value in held:
            for first in range(0, value.shape[0], 3 * group):
                rows.append(value[first + half * group : first + (half + 1) * group, at : at + tile])
                rows.append(value[first + 2 * group : first + 3 * group, at : at + tile])
        pulses = jnp.concatenate(rows, axis=0).astype(BF16)
        result = jnp.dot(
            operator_ref[half], jnp.concatenate([pulses, pulses], axis=0), preferred_element_type=F32
        )
        parts[i] = result.astype(BF16)
        copy = pltpu.make_async_copy(parts.at[i], out_ref.at[:, i * tile : (i + 1) * tile], sems.at[i])
        copy.start()
        copies.append(copy)
    for copy in copies:
        copy.wait()


def form_image(operator, chunks, group):
    height, half = operator.shape[1], chunks[0].shape[1]
    tile = 256 if half % 256 == 0 else half
    count = 2 * half // tile
    return pl.pallas_call(
        functools.partial(image_kernel, group=group),
        out_shape=jax.ShapeDtypeStruct((height, 2 * half), BF16),
        in_specs=[pl.BlockSpec(memory_space=pltpu.VMEM)] * (1 + len(chunks)),
        out_specs=pl.BlockSpec(memory_space=pl.ANY),
        scratch_shapes=[
            pltpu.VMEM((count, height, tile), BF16),
            pltpu.SemaphoreType.DMA((count,)),
        ],
        compiler_params=pltpu.CompilerParams(vmem_limit_bytes=16 * 1024 * 1024),
        name="form_image",
    )(operator, *chunks)


def swap(value, axis, by):
    count = lax.axis_size(axis)
    return lax.ppermute(value, axis, [(i, i ^ by) for i in range(count)])


def swap_by(value, move):
    sections, subs = lax.axis_size("section"), lax.axis_size("sub")
    pairs = []
    for s in range(sections):
        for a in range(subs):
            to_s, to_a = move(s, a)
            pairs.append((s * subs + a, to_s * subs + to_a))
    return lax.ppermute(value, ("section", "sub"), pairs)


def from_next(value, axis):
    count = lax.axis_size(axis)
    return lax.ppermute(value, axis, [(i, (i - 1) % count) for i in range(count)])


def on_device(echoes, chirp, steer, pulse_order, band_coef, band_start, band_width):
    sections, subs = lax.axis_size("section"), lax.axis_size("sub")
    pulses_each = echoes.shape[2]
    group = ceil_to(pulses_each, SUBL)
    section = lax.axis_index("section").astype(jnp.int32).reshape(1)
    coef = jnp.swapaxes(band_coef, 4, 5)
    weights = jnp.swapaxes(steer, 2, 3)
    levels, _, sides, parts, taps, beams = coef.shape
    dims = (levels, sides, parts, taps, beams)

    echo = jnp.transpose(echoes[:, 0], (1, 0, 2))
    halo = from_next(echo, "rng")
    other = swap(echo, "section", 1)
    has_next = (lax.axis_index("rng") < lax.axis_size("rng") - 1).astype(jnp.int32)
    echo, chirp, packed = prepare(
        echo, chirp, coef, band_start, band_width, weights, pulse_order, sections, group
    )
    packed_partner = swap(packed, "sub", 1) if subs == 2 else packed
    halo, table = lax.optimization_barrier((halo, lag_tables(chirp)))
    early, late = begin_compression(section, echo, other, table, sections, group)
    place = section + sections * has_next
    near, far, first, second = finish_compression(
        place, early, late, halo, swap(halo, "section", 1), table, sections, group
    )
    if subs != 2:
        chunks = [near, swap(far, "section", 2)]
        return merge_images(section, chunks, packed, dims, sections, group, pulses_each)
    chunks = [
        near,
        swap_by(far, lambda s, a: (s ^ 2, a ^ 1)),
        swap_by(first, lambda s, a: (s, a ^ 1) if s % 2 else (s ^ 2, a)),
        swap_by(second, lambda s, a: (s ^ 2, a) if s % 2 else (s, a ^ 1)),
    ]
    operator = fold_operator(section, packed, packed_partner, dims, sections, group, pulses_each)
    image = form_image(operator, chunks, group)
    return image.reshape(2, beams, 1, image.shape[1])


def unpack(chunk, group, each):
    lead = jnp.concatenate([chunk[:group], chunk[group : 2 * group]], axis=1)
    moved, rest = group - each, chunk[2 * group :]
    tail = jnp.concatenate([rest[: each - moved], rest[group // 2 : group // 2 + each - moved]], axis=1)
    return jnp.concatenate([lead, tail], axis=0)


def merge_images(section, chunks, packed, dims, sections, group, each):
    levels, sides, parts, taps, beams = dims
    width = sections * group
    first = levels * sides * parts * taps
    table = packed[first : first + parts * width].reshape(parts, sections, group, beams)
    table = jnp.take(table, section[0] ^ jnp.arange(sections), axis=1)[:, :, :each]
    chunks = [
        unpack(chunk[first : first + 3 * group], group, each)
        for chunk in chunks
        for first in range(0, chunk.shape[0], 3 * group)
    ]
    real, imag = table[0], table[1]
    rows = jnp.concatenate(
        [jnp.concatenate([real, -imag], axis=1), jnp.concatenate([imag, real], axis=1)], axis=2
    )
    image = lax.dot_general(
        rows.reshape(-1, 2 * beams), jnp.concatenate(chunks, axis=0), (((0,), (0,)), ((), ())), preferred_element_type=F32
    ).astype(BF16)
    starts = packed[first + parts * width :].astype(jnp.int32)
    column = jnp.arange(beams, dtype=jnp.int32)
    bits = lax.axis_size("sub").bit_length() - 1
    for level in range(levels):
        partner = swap(image, "sub", 1 << (level % bits))
        operands = []
        for side in range(sides):
            at = (level * sides + side) * parts * taps
            coef = packed[at : at + parts * taps].reshape(parts, taps, beams)
            offset = column[:, None] - starts[level * sides + side][None, :]
            hits = (offset[None] == jnp.arange(taps, dtype=jnp.int32)[:, None, None]).astype(BF16)
            operands.append(jnp.einsum("ptq,tcq->pqc", coef, hits, preferred_element_type=F32).astype(BF16))
        top = jnp.concatenate([operands[0][0], -operands[0][1], operands[1][0], -operands[1][1]], axis=1)
        low = jnp.concatenate([operands[0][1], operands[0][0], operands[1][1], operands[1][0]], axis=1)
        image = jnp.dot(
            jnp.concatenate([top, low], axis=0),
            jnp.concatenate([image, partner], axis=0),
            preferred_element_type=F32,
        ).astype(BF16)
    return image.reshape(2, beams, 1, image.shape[1])


def solution(mesh):
    return jax.shard_map(
        on_device,
        mesh=mesh,
        in_specs=(
            P(None, "sub", "section", "rng"),
            P(),
            P(None, "sub", None, None),
            P("sub", None),
            P(None, "sub", None, None, None, None),
            P(None, "sub", None, None),
            P(None, "sub", None, None),
        ),
        out_specs=P(None, "sub", "rng", "section"),
        check_vma=False,
    )
```

```python
import functools

import jax
import jax.numpy as jnp
from jax import lax
from jax.experimental import pallas as pl
from jax.experimental.pallas import tpu as pltpu
from jax.sharding import PartitionSpec as P

LANE = 128
SUBL = 8
F32 = jnp.float32
BF16 = jnp.bfloat16


def ceil_to(value, unit):
    return -(-value // unit) * unit


def prepare_kernel(*refs, sections, group):
    sources, (echo_out, chirp_out, pack_ref), scratch = refs[:7], refs[7:10], refs[10:]
    coef_ref, start_ref, width_ref, steer_ref, order_ref, starts, sems = scratch
    targets = (echo_out, coef_ref, start_ref, width_ref, steer_ref, order_ref, chirp_out)
    loads = [
        pltpu.make_async_copy(source, target, sems.at[i])
        for i, (source, target) in enumerate(zip(sources, targets))
    ]
    for load in loads:
        load.start()
    for load in loads:
        load.wait()
    levels, _, sides, parts, taps, beams = coef_ref.shape
    tap = lax.broadcasted_iota(jnp.int32, (taps, beams), 0)
    row = 0
    for level in range(levels):
        for side in range(sides):
            used = tap < width_ref[level, 0, side : side + 1, :]
            for part in range(parts):
                entries = coef_ref[level, 0, side, part].astype(F32)
                pack_ref[row : row + taps] = jnp.where(used, entries, 0.0).astype(BF16)
                row += taps
    pulses = order_ref.shape[1]
    each = pulses // sections
    position = lax.broadcasted_iota(jnp.int32, (pulses, pulses), 0)
    hit = (position == order_ref[0:1, :]).astype(F32)
    slot = lax.broadcasted_iota(jnp.int32, (sections * group, pulses), 0)
    pulse = lax.broadcasted_iota(jnp.int32, (sections * group, pulses), 1)
    place = jnp.zeros((sections * group, pulses), F32)
    for s in range(sections):
        inside = (pulse >= s * each) & (pulse < (s + 1) * each)
        place = jnp.where(inside & (slot - s * group == pulse - s * each), 1.0, place)
    pick = lax.dot_general(
        place.astype(BF16), hit.astype(BF16), (((1,), (1,)), ((), ())), preferred_element_type=F32
    )
    for part in range(parts):
        chosen = jnp.dot(pick.astype(BF16), steer_ref[part, 0], preferred_element_type=F32)
        pack_ref[row : row + sections * group] = chosen.astype(BF16)
        row += sections * group
    starts[...] = jnp.zeros_like(starts)
    for level in range(levels):
        starts[sides * level : sides * level + sides] = start_ref[level, 0].astype(F32)
    pack_ref[row : row + starts.shape[0]] = starts[...].astype(BF16)


def pack_rows(levels, sides, parts, taps, sections, group):
    return levels * sides * parts * taps + parts * sections * group + ceil_to(levels * sides, 16)


def prepare(echo, chirp, coef, start, width, steer, order, sections, group):
    levels, _, sides, parts, taps, beams = coef.shape
    sources = (echo, coef, start, width, steer, order, chirp)
    return pl.pallas_call(
        functools.partial(prepare_kernel, sections=sections, group=group),
        out_shape=(
            jax.ShapeDtypeStruct(echo.shape, BF16),
            jax.ShapeDtypeStruct(chirp.shape, BF16),
            jax.ShapeDtypeStruct((pack_rows(levels, sides, parts, taps, sections, group), beams), BF16),
        ),
        in_specs=[pl.BlockSpec(memory_space=pl.ANY)] * len(sources),
        scratch_shapes=[pltpu.VMEM(x.shape, x.dtype) for x in sources[1:6]]
        + [pltpu.VMEM((ceil_to(levels * sides, 16), beams), F32), pltpu.SemaphoreType.DMA((len(sources),))],
        compiler_params=pltpu.CompilerParams(vmem_limit_bytes=16 * 1024 * 1024),
        name="prepare",
    )(*[pltpu.with_memory_space_constraint(x, pltpu.HBM) for x in sources])


def pack_rows_of(real, imag, each):
    group = real.shape[0]
    row = lax.broadcasted_iota(jnp.int32, real.shape, 0)
    return jnp.where(row < each, real, pltpu.roll(imag, each, 0)), group - each


def split_two(value):
    high = value.astype(BF16)
    return high, (value - high.astype(F32)).astype(BF16)


def operator_kernel(index_ref, own_ref, partner_ref, out_ref, weights, *, dims, sections, group, each):
    levels, sides, parts, taps, beams = dims
    width = sections * group
    refs = (own_ref, partner_ref)
    weight_row = levels * sides * parts * taps
    start_row = weight_row + parts * width

    def band(ref, level, side):
        first = ((level * sides + side) * parts) * taps
        tables = [ref[first + p * taps : first + (p + 1) * taps].astype(F32) for p in range(parts)]
        start = ref[start_row : start_row + ceil_to(levels * sides, 16)].astype(F32)
        start = start[level * sides + side : level * sides + side + 1].astype(jnp.int32)
        found = [[], []]
        for c in range(0, beams, SUBL):
            column = lax.broadcasted_iota(jnp.int32, (SUBL, beams), 0) + c
            offset = column - start
            spot = offset & (SUBL - 1)
            for p in range(parts):
                value = jnp.zeros((SUBL, beams), F32)
                for t in range(0, taps, SUBL):
                    got = jnp.take_along_axis(
                        tables[p][t : t + SUBL], spot, axis=0, mode="promise_in_bounds"
                    )
                    value = jnp.where((offset >= t) & (offset < t + SUBL), got, value)
                found[p].append(value)
        return [jnp.concatenate(f, axis=0) for f in found]

    def complex_operand(real, imag):
        top = jnp.concatenate([real, imag], axis=1)
        low = jnp.concatenate([-imag, real], axis=1)
        return jnp.concatenate([top, low], axis=0).astype(BF16)

    section = index_ref[0]
    images = []
    for a in range(2):
        for p in range(parts):
            weights[...] = refs[a][weight_row + p * width : weight_row + (p + 1) * width].astype(F32)
            rows = []
            for j in range(sections):
                at = pl.multiple_of((section ^ j) * group, group)
                rows.append(weights[pl.ds(at, group)])
            images.append(jnp.concatenate(rows, axis=0))
    zero = jnp.zeros((width, 2 * beams), F32)
    own = jnp.concatenate([jnp.concatenate(images[0:2], axis=1), zero], axis=0)
    partner = jnp.concatenate([zero, jnp.concatenate(images[2:4], axis=1)], axis=0)
    for level in range(levels):
        own_high, own_low = split_two(own)
        partner_high, partner_low = split_two(partner)
        own_rows = jnp.concatenate([own_high, own_low], axis=0)
        partner_rows = jnp.concatenate([partner_high, partner_low], axis=0)

        def merged(ref, mine, other):
            product = jnp.dot(
                mine, complex_operand(*band(ref, level, 0)), preferred_element_type=F32
            ) + jnp.dot(other, complex_operand(*band(ref, level, 1)), preferred_element_type=F32)
            return product[: 2 * width] + product[2 * width :]

        following = merged(own_ref, own_rows, partner_rows)
        if level < levels - 1:
            partner = merged(partner_ref, partner_rows, own_rows)
        own = following
    full, left, right = [], [], []
    for j in range(2 * sections):
        real = own[j * group : (j + 1) * group, :beams]
        imag = own[j * group : (j + 1) * group, beams:]
        straight = jnp.concatenate([real, imag], axis=1)
        turned = jnp.concatenate([-imag, real], axis=1)
        lead, moved = pack_rows_of(straight, turned, each)
        row = lax.broadcasted_iota(jnp.int32, lead.shape, 0)
        full.append(lead)
        left.append(jnp.where(row < group // 2, pltpu.roll(turned, group - moved, 0), 0.0))
        right.append(jnp.where(row >= group // 2, pltpu.roll(turned, group // 2 - moved, 0), 0.0))
    pairs = sections // 2
    first_core = section % 2 == 0
    for half, rest in enumerate((left, right)):
        sources = [jnp.concatenate([full[j], rest[j]], axis=0) for j in range(2 * sections)]
        quarters = [jnp.concatenate(sources[q * pairs : (q + 1) * pairs], axis=0) for q in range(4)]
        quarters = [
            quarters[0],
            quarters[3],
            jnp.where(first_core, quarters[1], quarters[2]),
            jnp.where(first_core, quarters[2], quarters[1]),
        ]
        high, low = split_two(jnp.concatenate(quarters, axis=0).T)
        out_ref[half] = jnp.concatenate([high, low], axis=1)


def fold_operator(section, own, partner, dims, sections, group, each):
    beams = dims[-1]
    width = sections * group
    return pl.pallas_call(
        functools.partial(operator_kernel, dims=dims, sections=sections, group=group, each=each),
        out_shape=jax.ShapeDtypeStruct((2, 2 * beams, 8 * width), BF16),
        in_specs=[
            pl.BlockSpec(memory_space=pltpu.SMEM),
            pl.BlockSpec(memory_space=pltpu.VMEM),
            pl.BlockSpec(memory_space=pltpu.VMEM),
        ],
        scratch_shapes=[pltpu.VMEM((width, beams), F32)],
        compiler_params=pltpu.CompilerParams(vmem_limit_bytes=16 * 1024 * 1024),
        name="fold_operator",
    )(section, own, partner)


def correlate(rows, even, odd, table, blocks, group):
    extra = table.shape[0] // (2 * LANE) - 1
    total = blocks + extra
    held = [
        jnp.concatenate(
            [rows[:group, b * LANE : (b + 1) * LANE], rows[group:, b * LANE : (b + 1) * LANE]], axis=1
        )
        for b in range(total)
    ]
    for b in range(0, total, 2):
        even[b * group : (b + 2) * group] = jnp.concatenate(held[b : b + 2], axis=0).astype(BF16)
    for b in range(1, total - 1, 2):
        odd[(b - 1) * group : (b + 1) * group] = jnp.concatenate(held[b : b + 2], axis=0).astype(BF16)
    window = blocks * group
    pieces = []
    for lag in range(extra + 1):
        source, at = (even, lag) if lag % 2 == 0 else (odd, lag - 1)
        pieces.append(source[at * group : at * group + window])
    return jnp.dot(jnp.concatenate(pieces, axis=1), table[...], preferred_element_type=F32)


def as_chunk(done, s, chunk, group, each):
    real, imag = [
        jnp.concatenate(
            [
                done[(s * chunk + b) * group : (s * chunk + b + 1) * group, c * LANE : (c + 1) * LANE]
                for b in range(chunk)
            ],
            axis=1,
        )
        for c in range(2)
    ]
    middle = chunk * LANE // 2
    lead, moved = pack_rows_of(real, imag, each)
    row = lax.broadcasted_iota(jnp.int32, (group, middle), 0)
    rest = jnp.where(
        row < group // 2,
        pltpu.roll(imag[:, :middle], group - moved, 0),
        pltpu.roll(imag[:, middle:], group // 2 - moved, 0),
    )
    return jnp.concatenate([lead[:, :middle], lead[:, middle:], rest], axis=0).astype(BF16)


def begin_kernel(echo_ref, chirp_ref, early_ref, late_ref, table, rows, even, odd, *, group):
    pulses, _, length = echo_ref.shape
    extra = chirp_ref.shape[1] // LANE
    reverse = LANE - 1 - lax.broadcasted_iota(jnp.int32, (2, LANE), 1)
    below = lax.broadcasted_iota(jnp.int32, (LANE, LANE), 1) <= lax.broadcasted_iota(
        jnp.int32, (LANE, LANE), 0
    )
    before = [jnp.zeros((LANE, LANE), F32)] * 2
    for lag in range(extra + 1):
        if lag < extra:
            piece = chirp_ref[:, lag * LANE : (lag + 1) * LANE].astype(F32)
            piece = jnp.take_along_axis(piece, reverse, axis=1, mode="promise_in_bounds")
            turned = []
            for c in range(2):
                few = jnp.broadcast_to(piece[c : c + 1], (SUBL, LANE))
                few = pltpu.roll(few, 1, 1, stride=1, stride_axis=0)
                groups = [few] + [pltpu.roll(few, first, 1) for first in range(SUBL, LANE, SUBL)]
                turned.append(jnp.concatenate(groups, axis=0))
        else:
            turned = [jnp.zeros((LANE, LANE), F32)] * 2
        real, imag = [jnp.where(below, turned[c], before[c]) for c in range(2)]
        before = turned
        at = lag * 2 * LANE
        table[at : at + LANE, :LANE] = real.astype(BF16)
        table[at : at + LANE, LANE:] = (-imag).astype(BF16)
        table[at + LANE : at + 2 * LANE, :LANE] = imag.astype(BF16)
        table[at + LANE : at + 2 * LANE, LANE:] = real.astype(BF16)
    rows[...] = jnp.zeros_like(rows)
    for p in range(pulses):
        near = echo_ref[p].astype(F32)
        for c in range(2):
            rows[c * group + p : c * group + p + 1, :] = near[c : c + 1]
    late_ref[...] = rows[:, length - late_ref.shape[1] :]
    done = correlate(rows, even, odd, table, length // LANE - extra, group)
    for s in range(early_ref.shape[0]):
        early_ref[s] = as_chunk(done, s, 2 * early_ref.shape[2] // LANE, group, pulses)


def finish_kernel(index_ref, early_ref, late_ref, halo_ref, table, keep_ref, give_ref, rows, even, odd, *, group):
    pulses = halo_ref.shape[0]
    span = late_ref.shape[1]
    taps = rows.shape[1] - span
    ready = early_ref.shape[0]
    chunk = 2 * early_ref.shape[2]
    sections = ready + span // chunk
    section = lax.rem(index_ref[0], sections)
    has_next = index_ref[0] >= sections
    rows[:, :span] = late_ref[...]
    rows[:, span:] = jnp.zeros((2 * group, taps), F32)
    for p in range(pulses):
        far = jnp.where(has_next, halo_ref[p, :, :taps].astype(F32), 0.0)
        for c in range(2):
            rows[c * group + p : c * group + p + 1, span:] = far[c : c + 1]
    done = correlate(rows, even, odd, table, span // LANE, group)
    for s in range(sections):
        stacked = early_ref[s] if s < ready else as_chunk(done, s - ready, chunk // LANE, group, pulses)
        slot = section ^ s
        far_chunk, other_core = slot // 2, slot % 2
        place = far_chunk ^ 1 ^ (section % 2) ^ other_core

        @pl.when(other_core == 0)
        def _():
            keep_ref[place] = stacked

        @pl.when(other_core == 1)
        def _():
            give_ref[place] = stacked


def row_scratch(blocks, group):
    return [
        pltpu.VMEM((2 * group, blocks * LANE), F32),
        pltpu.VMEM((blocks * group, 2 * LANE), BF16),
        pltpu.VMEM((blocks * group, 2 * LANE), BF16),
    ]


def begin_compression(echo, chirp, sections, group):
    _, _, length = echo.shape
    taps = chirp.shape[1]
    chunk = length // sections
    early = (length - taps) // chunk
    return pl.pallas_call(
        functools.partial(begin_kernel, group=group),
        out_shape=(
            jax.ShapeDtypeStruct((early, 3 * group, chunk // 2), BF16),
            jax.ShapeDtypeStruct((2 * group, length - early * chunk), F32),
            jax.ShapeDtypeStruct(((taps // LANE + 1) * 2 * LANE, 2 * LANE), BF16),
        ),
        scratch_shapes=row_scratch(length // LANE, group),
        compiler_params=pltpu.CompilerParams(vmem_limit_bytes=24 * 1024 * 1024),
        name="begin_compression",
    )(echo, chirp)


def finish_compression(place, early, late, halo, table, group):
    blocks = late.shape[1] // LANE + table.shape[0] // (2 * LANE) - 1
    return pl.pallas_call(
        functools.partial(finish_kernel, group=group),
        out_shape=[jax.ShapeDtypeStruct((2, *early.shape[1:]), BF16)] * 2,
        in_specs=[pl.BlockSpec(memory_space=pltpu.SMEM)] + [pl.BlockSpec(memory_space=pltpu.VMEM)] * 4,
        scratch_shapes=row_scratch(blocks, group),
        compiler_params=pltpu.CompilerParams(vmem_limit_bytes=24 * 1024 * 1024),
        name="finish_compression",
    )(place, early, late, halo, table)


def image_kernel(index_ref, operator_ref, both_ref, *refs, group):
    chunks, (out_ref, parts, sems) = refs[:-3], refs[-3:]
    count, _, tile = parts.shape
    width = both_ref.shape[2]
    near = 1 - index_ref[0] % 2
    held = [both_ref[near]] + [chunk[...] for chunk in chunks]
    held = [value.astype(F32) for value in held]
    copies = []
    for i in range(count):
        half, at = divmod(i * tile, width)
        rows = []
        for value in held:
            for first in range(0, value.shape[0], 3 * group):
                rows.append(value[first + half * group : first + (half + 1) * group, at : at + tile])
                rows.append(value[first + 2 * group : first + 3 * group, at : at + tile])
        pulses = jnp.concatenate(rows, axis=0).astype(BF16)
        result = jnp.dot(
            operator_ref[half], jnp.concatenate([pulses, pulses], axis=0), preferred_element_type=F32
        )
        parts[i] = result.astype(BF16)
        copy = pltpu.make_async_copy(parts.at[i], out_ref.at[:, i * tile : (i + 1) * tile], sems.at[i])
        copy.start()
        copies.append(copy)
    for copy in copies:
        copy.wait()


def form_image(section, operator, both, chunks, group):
    height, half = operator.shape[1], both.shape[2]
    tile = 256 if half % 256 == 0 else half
    count = 2 * half // tile
    return pl.pallas_call(
        functools.partial(image_kernel, group=group),
        out_shape=jax.ShapeDtypeStruct((height, 2 * half), BF16),
        in_specs=[pl.BlockSpec(memory_space=pltpu.SMEM)]
        + [pl.BlockSpec(memory_space=pltpu.VMEM)] * (2 + len(chunks)),
        out_specs=pl.BlockSpec(memory_space=pl.ANY),
        scratch_shapes=[
            pltpu.VMEM((count, height, tile), BF16),
            pltpu.SemaphoreType.DMA((count,)),
        ],
        compiler_params=pltpu.CompilerParams(vmem_limit_bytes=16 * 1024 * 1024),
        name="form_image",
    )(section, operator, both, *chunks)


def swap(value, axis, by):
    count = lax.axis_size(axis)
    return lax.ppermute(value, axis, [(i, i ^ by) for i in range(count)])


def swap_by(value, move):
    sections, subs = lax.axis_size("section"), lax.axis_size("sub")
    pairs = []
    for s in range(sections):
        for a in range(subs):
            to_s, to_a = move(s, a)
            pairs.append((s * subs + a, to_s * subs + to_a))
    return lax.ppermute(value, ("section", "sub"), pairs)


def from_next(value, axis):
    count = lax.axis_size(axis)
    return lax.ppermute(value, axis, [(i, (i - 1) % count) for i in range(count)])


def on_device(echoes, chirp, steer, pulse_order, band_coef, band_start, band_width):
    sections, subs = lax.axis_size("section"), lax.axis_size("sub")
    pulses_each = echoes.shape[2]
    group = ceil_to(pulses_each, SUBL)
    section = lax.axis_index("section").astype(jnp.int32).reshape(1)
    coef = jnp.swapaxes(band_coef, 4, 5)
    weights = jnp.swapaxes(steer, 2, 3)
    levels, _, sides, parts, taps, beams = coef.shape
    dims = (levels, sides, parts, taps, beams)

    echo = jnp.transpose(echoes[:, 0], (1, 0, 2))
    halo = from_next(echo, "rng")
    echo, chirp, packed = prepare(
        echo, chirp, coef, band_start, band_width, weights, pulse_order, sections, group
    )
    has_next = (lax.axis_index("rng") < lax.axis_size("rng") - 1).astype(jnp.int32)
    if subs == 2:
        packed_partner = swap(packed, "sub", 1)
    early, late, table = begin_compression(echo, chirp, sections, group)
    place = section + sections * has_next
    keep, give = finish_compression(place, early, late, halo, table, group)
    both = jnp.concatenate([keep, swap(give, "section", 1)], axis=1)
    far = lax.dynamic_index_in_dim(both, section[0] % 2, 0, keepdims=False)
    if subs != 2:
        near = lax.dynamic_index_in_dim(both, 1 - section[0] % 2, 0, keepdims=False)
        chunks = [near, swap(far, "section", 2)]
        return merge_images(section, chunks, packed, dims, sections, group, pulses_each)
    chunks = [
        swap_by(far, lambda s, a: (s ^ 2, a ^ 1)),
        swap_by(both[0], lambda s, a: (s, a ^ 1) if s % 2 else (s ^ 2, a)),
        swap_by(both[1], lambda s, a: (s ^ 2, a) if s % 2 else (s, a ^ 1)),
    ]
    operator = fold_operator(section, packed, packed_partner, dims, sections, group, pulses_each)
    image = form_image(section, operator, both, chunks, group)
    return image.reshape(2, beams, 1, image.shape[1])


def unpack(chunk, group, each):
    lead = jnp.concatenate([chunk[:group], chunk[group : 2 * group]], axis=1)
    moved, rest = group - each, chunk[2 * group :]
    tail = jnp.concatenate([rest[: each - moved], rest[group // 2 : group // 2 + each - moved]], axis=1)
    return jnp.concatenate([lead, tail], axis=0)


def merge_images(section, chunks, packed, dims, sections, group, each):
    levels, sides, parts, taps, beams = dims
    width = sections * group
    first = levels * sides * parts * taps
    table = packed[first : first + parts * width].reshape(parts, sections, group, beams)
    table = jnp.take(table, section[0] ^ jnp.arange(sections), axis=1)[:, :, :each]
    chunks = [
        unpack(chunk[first : first + 3 * group], group, each)
        for chunk in chunks
        for first in range(0, chunk.shape[0], 3 * group)
    ]
    real, imag = table[0], table[1]
    rows = jnp.concatenate(
        [jnp.concatenate([real, -imag], axis=1), jnp.concatenate([imag, real], axis=1)], axis=2
    )
    image = lax.dot_general(
        rows.reshape(-1, 2 * beams), jnp.concatenate(chunks, axis=0), (((0,), (0,)), ((), ())), preferred_element_type=F32
    ).astype(BF16)
    starts = packed[first + parts * width :].astype(jnp.int32)
    column = jnp.arange(beams, dtype=jnp.int32)
    bits = lax.axis_size("sub").bit_length() - 1
    for level in range(levels):
        partner = swap(image, "sub", 1 << (level % bits))
        operands = []
        for side in range(sides):
            at = (level * sides + side) * parts * taps
            coef = packed[at : at + parts * taps].reshape(parts, taps, beams)
            offset = column[:, None] - starts[level * sides + side][None, :]
            hits = (offset[None] == jnp.arange(taps, dtype=jnp.int32)[:, None, None]).astype(BF16)
            operands.append(jnp.einsum("ptq,tcq->pqc", coef, hits, preferred_element_type=F32).astype(BF16))
        top = jnp.concatenate([operands[0][0], -operands[0][1], operands[1][0], -operands[1][1]], axis=1)
        low = jnp.concatenate([operands[0][1], operands[0][0], operands[1][1], operands[1][0]], axis=1)
        image = jnp.dot(
            jnp.concatenate([top, low], axis=0),
            jnp.concatenate([image, partner], axis=0),
            preferred_element_type=F32,
        ).astype(BF16)
    return image.reshape(2, beams, 1, image.shape[1])


def solution(mesh):
    return jax.shard_map(
        on_device,
        mesh=mesh,
        in_specs=(
            P(None, "sub", "section", "rng"),
            P(),
            P(None, "sub", None, None),
            P("sub", None),
            P(None, "sub", None, None, None, None),
            P(None, "sub", None, None),
            P(None, "sub", None, None),
        ),
        out_specs=P(None, "sub", "rng", "section"),
        check_vma=False,
    )
```

```python
import functools

import jax
import jax.numpy as jnp
from jax import lax
from jax.experimental import pallas as pl
from jax.experimental.pallas import tpu as pltpu
from jax.sharding import PartitionSpec as P

LANE = 128
SUBL = 8
F32 = jnp.float32
BF16 = jnp.bfloat16


def ceil_to(value, unit):
    return -(-value // unit) * unit


def prepare_kernel(*refs, sections, group):
    sources, (echo_out, chirp_out, pack_ref), scratch = refs[:7], refs[7:10], refs[10:]
    coef_ref, start_ref, width_ref, steer_ref, order_ref, starts, sems = scratch
    targets = (echo_out, coef_ref, start_ref, width_ref, steer_ref, order_ref, chirp_out)
    loads = [
        pltpu.make_async_copy(source, target, sems.at[i])
        for i, (source, target) in enumerate(zip(sources, targets))
    ]
    for load in loads:
        load.start()
    for load in loads:
        load.wait()
    levels, _, sides, parts, taps, beams = coef_ref.shape
    tap = lax.broadcasted_iota(jnp.int32, (taps, beams), 0)
    row = 0
    for level in range(levels):
        for side in range(sides):
            used = tap < width_ref[level, 0, side : side + 1, :]
            for part in range(parts):
                entries = coef_ref[level, 0, side, part].astype(F32)
                pack_ref[row : row + taps] = jnp.where(used, entries, 0.0).astype(BF16)
                row += taps
    pulses = order_ref.shape[1]
    each = pulses // sections
    position = lax.broadcasted_iota(jnp.int32, (pulses, pulses), 0)
    hit = (position == order_ref[0:1, :]).astype(F32)
    slot = lax.broadcasted_iota(jnp.int32, (sections * group, pulses), 0)
    pulse = lax.broadcasted_iota(jnp.int32, (sections * group, pulses), 1)
    place = jnp.zeros((sections * group, pulses), F32)
    for s in range(sections):
        inside = (pulse >= s * each) & (pulse < (s + 1) * each)
        place = jnp.where(inside & (slot - s * group == pulse - s * each), 1.0, place)
    pick = lax.dot_general(
        place.astype(BF16), hit.astype(BF16), (((1,), (1,)), ((), ())), preferred_element_type=F32
    )
    for part in range(parts):
        chosen = jnp.dot(pick.astype(BF16), steer_ref[part, 0], preferred_element_type=F32)
        pack_ref[row : row + sections * group] = chosen.astype(BF16)
        row += sections * group
    starts[...] = jnp.zeros_like(starts)
    for level in range(levels):
        starts[sides * level : sides * level + sides] = start_ref[level, 0].astype(F32)
    pack_ref[row : row + starts.shape[0]] = starts[...].astype(BF16)


def pack_rows(levels, sides, parts, taps, sections, group):
    return levels * sides * parts * taps + parts * sections * group + ceil_to(levels * sides, 16)


def prepare(echo, chirp, coef, start, width, steer, order, sections, group):
    levels, _, sides, parts, taps, beams = coef.shape
    sources = (echo, coef, start, width, steer, order, chirp)
    return pl.pallas_call(
        functools.partial(prepare_kernel, sections=sections, group=group),
        out_shape=(
            jax.ShapeDtypeStruct(echo.shape, BF16),
            jax.ShapeDtypeStruct(chirp.shape, BF16),
            jax.ShapeDtypeStruct((pack_rows(levels, sides, parts, taps, sections, group), beams), BF16),
        ),
        in_specs=[pl.BlockSpec(memory_space=pl.ANY)] * len(sources),
        scratch_shapes=[pltpu.VMEM(x.shape, x.dtype) for x in sources[1:6]]
        + [pltpu.VMEM((ceil_to(levels * sides, 16), beams), F32), pltpu.SemaphoreType.DMA((len(sources),))],
        compiler_params=pltpu.CompilerParams(vmem_limit_bytes=16 * 1024 * 1024),
        name="prepare",
    )(*[pltpu.with_memory_space_constraint(x, pltpu.HBM) for x in sources])


def pack_rows_of(real, imag, each):
    group = real.shape[0]
    row = lax.broadcasted_iota(jnp.int32, real.shape, 0)
    return jnp.where(row < each, real, pltpu.roll(imag, each, 0)), group - each


def split_two(value):
    high = value.astype(BF16)
    return high, (value - high.astype(F32)).astype(BF16)


def operator_kernel(index_ref, own_ref, partner_ref, out_ref, weights, *, dims, sections, group, each):
    levels, sides, parts, taps, beams = dims
    width = sections * group
    refs = (own_ref, partner_ref)
    weight_row = levels * sides * parts * taps
    start_row = weight_row + parts * width

    def band(ref, level, side):
        first = ((level * sides + side) * parts) * taps
        tables = [ref[first + p * taps : first + (p + 1) * taps].astype(F32) for p in range(parts)]
        start = ref[start_row : start_row + ceil_to(levels * sides, 16)].astype(F32)
        start = start[level * sides + side : level * sides + side + 1].astype(jnp.int32)
        found = [[], []]
        for c in range(0, beams, SUBL):
            column = lax.broadcasted_iota(jnp.int32, (SUBL, beams), 0) + c
            offset = column - start
            spot = offset & (SUBL - 1)
            for p in range(parts):
                value = jnp.zeros((SUBL, beams), F32)
                for t in range(0, taps, SUBL):
                    got = jnp.take_along_axis(
                        tables[p][t : t + SUBL], spot, axis=0, mode="promise_in_bounds"
                    )
                    value = jnp.where((offset >= t) & (offset < t + SUBL), got, value)
                found[p].append(value)
        return [jnp.concatenate(f, axis=0) for f in found]

    def complex_operand(real, imag):
        top = jnp.concatenate([real, imag], axis=1)
        low = jnp.concatenate([-imag, real], axis=1)
        return jnp.concatenate([top, low], axis=0).astype(BF16)

    section = index_ref[0]
    images = []
    for a in range(2):
        for p in range(parts):
            weights[...] = refs[a][weight_row + p * width : weight_row + (p + 1) * width].astype(F32)
            rows = []
            for j in range(sections):
                at = pl.multiple_of((section ^ j) * group, group)
                rows.append(weights[pl.ds(at, group)])
            images.append(jnp.concatenate(rows, axis=0))
    zero = jnp.zeros((width, 2 * beams), F32)
    own = jnp.concatenate([jnp.concatenate(images[0:2], axis=1), zero], axis=0)
    partner = jnp.concatenate([zero, jnp.concatenate(images[2:4], axis=1)], axis=0)
    for level in range(levels):
        own_high, own_low = split_two(own)
        partner_high, partner_low = split_two(partner)
        own_rows = jnp.concatenate([own_high, own_low], axis=0)
        partner_rows = jnp.concatenate([partner_high, partner_low], axis=0)

        def merged(ref, mine, other):
            product = jnp.dot(
                mine, complex_operand(*band(ref, level, 0)), preferred_element_type=F32
            ) + jnp.dot(other, complex_operand(*band(ref, level, 1)), preferred_element_type=F32)
            return product[: 2 * width] + product[2 * width :]

        following = merged(own_ref, own_rows, partner_rows)
        if level < levels - 1:
            partner = merged(partner_ref, partner_rows, own_rows)
        own = following
    full, left, right = [], [], []
    for j in range(2 * sections):
        real = own[j * group : (j + 1) * group, :beams]
        imag = own[j * group : (j + 1) * group, beams:]
        straight = jnp.concatenate([real, imag], axis=1)
        turned = jnp.concatenate([-imag, real], axis=1)
        lead, moved = pack_rows_of(straight, turned, each)
        row = lax.broadcasted_iota(jnp.int32, lead.shape, 0)
        full.append(lead)
        left.append(jnp.where(row < group // 2, pltpu.roll(turned, group - moved, 0), 0.0))
        right.append(jnp.where(row >= group // 2, pltpu.roll(turned, group // 2 - moved, 0), 0.0))
    pairs = sections // 2
    first_core = section % 2 == 0
    for half, rest in enumerate((left, right)):
        sources = [jnp.concatenate([full[j], rest[j]], axis=0) for j in range(2 * sections)]
        quarters = [jnp.concatenate(sources[q * pairs : (q + 1) * pairs], axis=0) for q in range(4)]
        quarters = [
            quarters[0],
            quarters[3],
            jnp.where(first_core, quarters[1], quarters[2]),
            jnp.where(first_core, quarters[2], quarters[1]),
        ]
        high, low = split_two(jnp.concatenate(quarters, axis=0).T)
        out_ref[half] = jnp.concatenate([high, low], axis=1)


def fold_operator(section, own, partner, dims, sections, group, each):
    beams = dims[-1]
    width = sections * group
    return pl.pallas_call(
        functools.partial(operator_kernel, dims=dims, sections=sections, group=group, each=each),
        out_shape=jax.ShapeDtypeStruct((2, 2 * beams, 8 * width), BF16),
        in_specs=[
            pl.BlockSpec(memory_space=pltpu.SMEM),
            pl.BlockSpec(memory_space=pltpu.VMEM),
            pl.BlockSpec(memory_space=pltpu.VMEM),
        ],
        scratch_shapes=[pltpu.VMEM((width, beams), F32)],
        compiler_params=pltpu.CompilerParams(vmem_limit_bytes=16 * 1024 * 1024),
        name="fold_operator",
    )(section, own, partner)


def correlate(rows, even, odd, table, blocks, group):
    extra = table.shape[0] // (2 * LANE) - 1
    total = blocks + extra
    held = [
        jnp.concatenate(
            [rows[:group, b * LANE : (b + 1) * LANE], rows[group:, b * LANE : (b + 1) * LANE]], axis=1
        )
        for b in range(total)
    ]
    for b in range(0, total, 2):
        even[b * group : (b + 2) * group] = jnp.concatenate(held[b : b + 2], axis=0).astype(BF16)
    for b in range(1, total - 1, 2):
        odd[(b - 1) * group : (b + 1) * group] = jnp.concatenate(held[b : b + 2], axis=0).astype(BF16)
    window = blocks * group
    pieces = []
    for lag in range(extra + 1):
        source, at = (even, lag) if lag % 2 == 0 else (odd, lag - 1)
        pieces.append(source[at * group : at * group + window])
    return jnp.dot(jnp.concatenate(pieces, axis=1), table[...], preferred_element_type=F32)


def as_chunk(done, s, chunk, group, each):
    real, imag = [
        jnp.concatenate(
            [
                done[(s * chunk + b) * group : (s * chunk + b + 1) * group, c * LANE : (c + 1) * LANE]
                for b in range(chunk)
            ],
            axis=1,
        )
        for c in range(2)
    ]
    middle = chunk * LANE // 2
    lead, moved = pack_rows_of(real, imag, each)
    row = lax.broadcasted_iota(jnp.int32, (group, middle), 0)
    rest = jnp.where(
        row < group // 2,
        pltpu.roll(imag[:, :middle], group - moved, 0),
        pltpu.roll(imag[:, middle:], group // 2 - moved, 0),
    )
    return jnp.concatenate([lead[:, :middle], lead[:, middle:], rest], axis=0).astype(BF16)


def begin_kernel(echo_ref, chirp_ref, early_ref, late_ref, table, rows, even, odd, *, group):
    pulses, _, length = echo_ref.shape
    extra = chirp_ref.shape[1] // LANE
    reverse = LANE - 1 - lax.broadcasted_iota(jnp.int32, (2, LANE), 1)
    below = lax.broadcasted_iota(jnp.int32, (LANE, LANE), 1) <= lax.broadcasted_iota(
        jnp.int32, (LANE, LANE), 0
    )
    before = [jnp.zeros((LANE, LANE), BF16)] * 2
    for lag in range(extra + 1):
        if lag < extra:
            piece = chirp_ref[:, lag * LANE : (lag + 1) * LANE].astype(F32)
            piece = jnp.take_along_axis(piece, reverse, axis=1, mode="promise_in_bounds")
            turned = []
            for c in range(2):
                few = jnp.broadcast_to(piece[c : c + 1], (2 * SUBL, LANE))
                few = pltpu.roll(few, 1, 1, stride=1, stride_axis=0).astype(BF16)
                groups = [few] + [pltpu.roll(few, at, 1) for at in range(2 * SUBL, LANE, 2 * SUBL)]
                turned.append(jnp.concatenate(groups, axis=0))
        else:
            turned = [jnp.zeros((LANE, LANE), BF16)] * 2
        real, imag = [jnp.where(below, turned[c], before[c]) for c in range(2)]
        before = turned
        at = lag * 2 * LANE
        table[at : at + LANE, :LANE] = real
        table[at : at + LANE, LANE:] = -imag
        table[at + LANE : at + 2 * LANE, :LANE] = imag
        table[at + LANE : at + 2 * LANE, LANE:] = real
    rows[...] = jnp.zeros_like(rows)
    for p in range(pulses):
        near = echo_ref[p].astype(F32)
        for c in range(2):
            rows[c * group + p : c * group + p + 1, :] = near[c : c + 1]
    late_ref[...] = rows[:, length - late_ref.shape[1] :]
    done = correlate(rows, even, odd, table, length // LANE - extra, group)
    for s in range(early_ref.shape[0]):
        early_ref[s] = as_chunk(done, s, 2 * early_ref.shape[2] // LANE, group, pulses)


def finish_kernel(index_ref, early_ref, late_ref, halo_ref, table, keep_ref, give_ref, rows, even, odd, *, group):
    pulses = halo_ref.shape[0]
    span = late_ref.shape[1]
    taps = rows.shape[1] - span
    ready = early_ref.shape[0]
    chunk = 2 * early_ref.shape[2]
    sections = ready + span // chunk
    section = lax.rem(index_ref[0], sections)
    has_next = index_ref[0] >= sections
    rows[:, :span] = late_ref[...]
    rows[:, span:] = jnp.zeros((2 * group, taps), F32)
    for p in range(pulses):
        far = jnp.where(has_next, halo_ref[p, :, :taps].astype(F32), 0.0)
        for c in range(2):
            rows[c * group + p : c * group + p + 1, span:] = far[c : c + 1]
    done = correlate(rows, even, odd, table, span // LANE, group)
    for s in range(sections):
        stacked = early_ref[s] if s < ready else as_chunk(done, s - ready, chunk // LANE, group, pulses)
        slot = section ^ s
        far_chunk, other_core = slot // 2, slot % 2
        place = far_chunk ^ 1 ^ (section % 2) ^ other_core

        @pl.when(other_core == 0)
        def _():
            keep_ref[place] = stacked

        @pl.when(other_core == 1)
        def _():
            give_ref[place] = stacked


def row_scratch(blocks, group):
    return [
        pltpu.VMEM((2 * group, blocks * LANE), F32),
        pltpu.VMEM((blocks * group, 2 * LANE), BF16),
        pltpu.VMEM((blocks * group, 2 * LANE), BF16),
    ]


def begin_compression(echo, chirp, sections, group):
    _, _, length = echo.shape
    taps = chirp.shape[1]
    chunk = length // sections
    early = (length - taps) // chunk
    return pl.pallas_call(
        functools.partial(begin_kernel, group=group),
        out_shape=(
            jax.ShapeDtypeStruct((early, 3 * group, chunk // 2), BF16),
            jax.ShapeDtypeStruct((2 * group, length - early * chunk), F32),
            jax.ShapeDtypeStruct(((taps // LANE + 1) * 2 * LANE, 2 * LANE), BF16),
        ),
        scratch_shapes=row_scratch(length // LANE, group),
        compiler_params=pltpu.CompilerParams(vmem_limit_bytes=24 * 1024 * 1024),
        name="begin_compression",
    )(echo, chirp)


def finish_compression(place, early, late, halo, table, group):
    blocks = late.shape[1] // LANE + table.shape[0] // (2 * LANE) - 1
    return pl.pallas_call(
        functools.partial(finish_kernel, group=group),
        out_shape=[jax.ShapeDtypeStruct((2, *early.shape[1:]), BF16)] * 2,
        in_specs=[pl.BlockSpec(memory_space=pltpu.SMEM)] + [pl.BlockSpec(memory_space=pltpu.VMEM)] * 4,
        scratch_shapes=row_scratch(blocks, group),
        compiler_params=pltpu.CompilerParams(vmem_limit_bytes=24 * 1024 * 1024),
        name="finish_compression",
    )(place, early, late, halo, table)


def image_kernel(index_ref, operator_ref, both_ref, *refs, group):
    chunks, (out_ref, parts, sems) = refs[:-3], refs[-3:]
    count, _, tile = parts.shape
    width = both_ref.shape[2]
    near = 1 - index_ref[0] % 2
    held = [both_ref[near]] + [chunk[...] for chunk in chunks]
    held = [value.astype(F32) for value in held]
    copies = []
    for i in range(count):
        half, at = divmod(i * tile, width)
        rows = []
        for value in held:
            for first in range(0, value.shape[0], 3 * group):
                rows.append(value[first + half * group : first + (half + 1) * group, at : at + tile])
                rows.append(value[first + 2 * group : first + 3 * group, at : at + tile])
        pulses = jnp.concatenate(rows, axis=0).astype(BF16)
        result = jnp.dot(
            operator_ref[half], jnp.concatenate([pulses, pulses], axis=0), preferred_element_type=F32
        )
        parts[i] = result.astype(BF16)
        copy = pltpu.make_async_copy(parts.at[i], out_ref.at[:, i * tile : (i + 1) * tile], sems.at[i])
        copy.start()
        copies.append(copy)
    for copy in copies:
        copy.wait()


def form_image(section, operator, both, chunks, group):
    height, half = operator.shape[1], both.shape[2]
    tile = 256 if half % 256 == 0 else half
    count = 2 * half // tile
    return pl.pallas_call(
        functools.partial(image_kernel, group=group),
        out_shape=jax.ShapeDtypeStruct((height, 2 * half), BF16),
        in_specs=[pl.BlockSpec(memory_space=pltpu.SMEM)]
        + [pl.BlockSpec(memory_space=pltpu.VMEM)] * (2 + len(chunks)),
        out_specs=pl.BlockSpec(memory_space=pl.ANY),
        scratch_shapes=[
            pltpu.VMEM((count, height, tile), BF16),
            pltpu.SemaphoreType.DMA((count,)),
        ],
        compiler_params=pltpu.CompilerParams(vmem_limit_bytes=16 * 1024 * 1024),
        name="form_image",
    )(section, operator, both, *chunks)


def swap(value, axis, by):
    count = lax.axis_size(axis)
    return lax.ppermute(value, axis, [(i, i ^ by) for i in range(count)])


def swap_by(value, move):
    sections, subs = lax.axis_size("section"), lax.axis_size("sub")
    pairs = []
    for s in range(sections):
        for a in range(subs):
            to_s, to_a = move(s, a)
            pairs.append((s * subs + a, to_s * subs + to_a))
    return lax.ppermute(value, ("section", "sub"), pairs)


def from_next(value, axis):
    count = lax.axis_size(axis)
    return lax.ppermute(value, axis, [(i, (i - 1) % count) for i in range(count)])


def on_device(echoes, chirp, steer, pulse_order, band_coef, band_start, band_width):
    sections, subs = lax.axis_size("section"), lax.axis_size("sub")
    pulses_each = echoes.shape[2]
    group = ceil_to(pulses_each, SUBL)
    section = lax.axis_index("section").astype(jnp.int32).reshape(1)
    coef = jnp.swapaxes(band_coef, 4, 5)
    weights = jnp.swapaxes(steer, 2, 3)
    levels, _, sides, parts, taps, beams = coef.shape
    dims = (levels, sides, parts, taps, beams)

    echo = jnp.transpose(echoes[:, 0], (1, 0, 2))
    halo = from_next(echo, "rng")
    echo, chirp, packed = prepare(
        echo, chirp, coef, band_start, band_width, weights, pulse_order, sections, group
    )
    has_next = (lax.axis_index("rng") < lax.axis_size("rng") - 1).astype(jnp.int32)
    if subs == 2:
        packed_partner = swap(packed, "sub", 1)
    early, late, table = begin_compression(echo, chirp, sections, group)
    place = section + sections * has_next
    keep, give = finish_compression(place, early, late, halo, table, group)
    both = jnp.concatenate([keep, swap(give, "section", 1)], axis=1)
    far = lax.dynamic_index_in_dim(both, section[0] % 2, 0, keepdims=False)
    if subs != 2:
        near = lax.dynamic_index_in_dim(both, 1 - section[0] % 2, 0, keepdims=False)
        chunks = [near, swap(far, "section", 2)]
        return merge_images(section, chunks, packed, dims, sections, group, pulses_each)
    chunks = [
        swap_by(far, lambda s, a: (s ^ 2, a ^ 1)),
        swap_by(both[0], lambda s, a: (s, a ^ 1) if s % 2 else (s ^ 2, a)),
        swap_by(both[1], lambda s, a: (s ^ 2, a) if s % 2 else (s, a ^ 1)),
    ]
    operator = fold_operator(section, packed, packed_partner, dims, sections, group, pulses_each)
    image = form_image(section, operator, both, chunks, group)
    return image.reshape(2, beams, 1, image.shape[1])


def unpack(chunk, group, each):
    lead = jnp.concatenate([chunk[:group], chunk[group : 2 * group]], axis=1)
    moved, rest = group - each, chunk[2 * group :]
    tail = jnp.concatenate([rest[: each - moved], rest[group // 2 : group // 2 + each - moved]], axis=1)
    return jnp.concatenate([lead, tail], axis=0)


def merge_images(section, chunks, packed, dims, sections, group, each):
    levels, sides, parts, taps, beams = dims
    width = sections * group
    first = levels * sides * parts * taps
    table = packed[first : first + parts * width].reshape(parts, sections, group, beams)
    table = jnp.take(table, section[0] ^ jnp.arange(sections), axis=1)[:, :, :each]
    chunks = [
        unpack(chunk[first : first + 3 * group], group, each)
        for chunk in chunks
        for first in range(0, chunk.shape[0], 3 * group)
    ]
    real, imag = table[0], table[1]
    rows = jnp.concatenate(
        [jnp.concatenate([real, -imag], axis=1), jnp.concatenate([imag, real], axis=1)], axis=2
    )
    image = lax.dot_general(
        rows.reshape(-1, 2 * beams), jnp.concatenate(chunks, axis=0), (((0,), (0,)), ((), ())), preferred_element_type=F32
    ).astype(BF16)
    starts = packed[first + parts * width :].astype(jnp.int32)
    column = jnp.arange(beams, dtype=jnp.int32)
    bits = lax.axis_size("sub").bit_length() - 1
    for level in range(levels):
        partner = swap(image, "sub", 1 << (level % bits))
        operands = []
        for side in range(sides):
            at = (level * sides + side) * parts * taps
            coef = packed[at : at + parts * taps].reshape(parts, taps, beams)
            offset = column[:, None] - starts[level * sides + side][None, :]
            hits = (offset[None] == jnp.arange(taps, dtype=jnp.int32)[:, None, None]).astype(BF16)
            operands.append(jnp.einsum("ptq,tcq->pqc", coef, hits, preferred_element_type=F32).astype(BF16))
        top = jnp.concatenate([operands[0][0], -operands[0][1], operands[1][0], -operands[1][1]], axis=1)
        low = jnp.concatenate([operands[0][1], operands[0][0], operands[1][1], operands[1][0]], axis=1)
        image = jnp.dot(
            jnp.concatenate([top, low], axis=0),
            jnp.concatenate([image, partner], axis=0),
            preferred_element_type=F32,
        ).astype(BF16)
    return image.reshape(2, beams, 1, image.shape[1])


def solution(mesh):
    return jax.shard_map(
        on_device,
        mesh=mesh,
        in_specs=(
            P(None, "sub", "section", "rng"),
            P(),
            P(None, "sub", None, None),
            P("sub", None),
            P(None, "sub", None, None, None, None),
            P(None, "sub", None, None),
            P(None, "sub", None, None),
        ),
        out_specs=P(None, "sub", "rng", "section"),
        check_vma=False,
    )
```

```python
import functools

import jax
import jax.numpy as jnp
from jax import lax
from jax.experimental import pallas as pl
from jax.experimental.pallas import tpu as pltpu
from jax.sharding import PartitionSpec as P

LANE = 128
SUBL = 8
F32 = jnp.float32
BF16 = jnp.bfloat16


def ceil_to(value, unit):
    return -(-value // unit) * unit


def prepare_kernel(*refs, sections, group):
    sources, (echo_out, chirp_out, pack_ref), scratch = refs[:7], refs[7:10], refs[10:]
    coef_ref, start_ref, width_ref, steer_ref, order_ref, starts, sems = scratch
    targets = (echo_out, coef_ref, start_ref, width_ref, steer_ref, order_ref, chirp_out)
    loads = [
        pltpu.make_async_copy(source, target, sems.at[i])
        for i, (source, target) in enumerate(zip(sources, targets))
    ]
    for load in loads:
        load.start()
    for load in loads:
        load.wait()
    levels, _, sides, parts, taps, beams = coef_ref.shape
    tap = lax.broadcasted_iota(jnp.int32, (taps, beams), 0)
    row = 0
    for level in range(levels):
        for side in range(sides):
            used = tap < width_ref[level, 0, side : side + 1, :]
            for part in range(parts):
                entries = coef_ref[level, 0, side, part].astype(F32)
                pack_ref[row : row + taps] = jnp.where(used, entries, 0.0).astype(BF16)
                row += taps
    pulses = order_ref.shape[1]
    each = pulses // sections
    position = lax.broadcasted_iota(jnp.int32, (pulses, pulses), 0)
    hit = (position == order_ref[0:1, :]).astype(F32)
    slot = lax.broadcasted_iota(jnp.int32, (sections * group, pulses), 0)
    pulse = lax.broadcasted_iota(jnp.int32, (sections * group, pulses), 1)
    place = jnp.zeros((sections * group, pulses), F32)
    for s in range(sections):
        inside = (pulse >= s * each) & (pulse < (s + 1) * each)
        place = jnp.where(inside & (slot - s * group == pulse - s * each), 1.0, place)
    pick = lax.dot_general(
        place.astype(BF16), hit.astype(BF16), (((1,), (1,)), ((), ())), preferred_element_type=F32
    )
    for part in range(parts):
        chosen = jnp.dot(pick.astype(BF16), steer_ref[part, 0], preferred_element_type=F32)
        pack_ref[row : row + sections * group] = chosen.astype(BF16)
        row += sections * group
    starts[...] = jnp.zeros_like(starts)
    for level in range(levels):
        starts[sides * level : sides * level + sides] = start_ref[level, 0].astype(F32)
    pack_ref[row : row + starts.shape[0]] = starts[...].astype(BF16)


def pack_rows(levels, sides, parts, taps, sections, group):
    return levels * sides * parts * taps + parts * sections * group + ceil_to(levels * sides, 16)


def prepare(echo, chirp, coef, start, width, steer, order, sections, group):
    levels, _, sides, parts, taps, beams = coef.shape
    sources = (echo, coef, start, width, steer, order, chirp)
    return pl.pallas_call(
        functools.partial(prepare_kernel, sections=sections, group=group),
        out_shape=(
            jax.ShapeDtypeStruct(echo.shape, BF16),
            jax.ShapeDtypeStruct(chirp.shape, BF16),
            jax.ShapeDtypeStruct((pack_rows(levels, sides, parts, taps, sections, group), beams), BF16),
        ),
        in_specs=[pl.BlockSpec(memory_space=pl.ANY)] * len(sources),
        scratch_shapes=[pltpu.VMEM(x.shape, x.dtype) for x in sources[1:6]]
        + [pltpu.VMEM((ceil_to(levels * sides, 16), beams), F32), pltpu.SemaphoreType.DMA((len(sources),))],
        compiler_params=pltpu.CompilerParams(vmem_limit_bytes=16 * 1024 * 1024),
        name="prepare",
    )(*[pltpu.with_memory_space_constraint(x, pltpu.HBM) for x in sources])


def pack_rows_of(real, imag, each):
    group = real.shape[0]
    row = lax.broadcasted_iota(jnp.int32, real.shape, 0)
    return jnp.where(row < each, real, pltpu.roll(imag, each, 0)), group - each


def split_two(value):
    high = value.astype(BF16)
    return high, (value - high.astype(F32)).astype(BF16)


def operator_kernel(index_ref, own_ref, partner_ref, out_ref, weights, *, dims, sections, group, each):
    levels, sides, parts, taps, beams = dims
    width = sections * group
    refs = (own_ref, partner_ref)
    weight_row = levels * sides * parts * taps
    start_row = weight_row + parts * width

    def band(ref, level, side):
        first = ((level * sides + side) * parts) * taps
        tables = [ref[first + p * taps : first + (p + 1) * taps].astype(F32) for p in range(parts)]
        start = ref[start_row : start_row + ceil_to(levels * sides, 16)].astype(F32)
        start = start[level * sides + side : level * sides + side + 1].astype(jnp.int32)
        found = [[], []]
        for c in range(0, beams, SUBL):
            column = lax.broadcasted_iota(jnp.int32, (SUBL, beams), 0) + c
            offset = column - start
            spot = offset & (SUBL - 1)
            for p in range(parts):
                value = jnp.zeros((SUBL, beams), F32)
                for t in range(0, taps, SUBL):
                    got = jnp.take_along_axis(
                        tables[p][t : t + SUBL], spot, axis=0, mode="promise_in_bounds"
                    )
                    value = jnp.where((offset >= t) & (offset < t + SUBL), got, value)
                found[p].append(value)
        return [jnp.concatenate(f, axis=0) for f in found]

    def complex_operand(real, imag):
        top = jnp.concatenate([real, imag], axis=1)
        low = jnp.concatenate([-imag, real], axis=1)
        return jnp.concatenate([top, low], axis=0).astype(BF16)

    section = index_ref[0]
    images = []
    for a in range(2):
        for p in range(parts):
            weights[...] = refs[a][weight_row + p * width : weight_row + (p + 1) * width].astype(F32)
            rows = []
            for j in range(sections):
                at = pl.multiple_of((section ^ j) * group, group)
                rows.append(weights[pl.ds(at, group)])
            images.append(jnp.concatenate(rows, axis=0))
    zero = jnp.zeros((width, 2 * beams), F32)
    own = jnp.concatenate([jnp.concatenate(images[0:2], axis=1), zero], axis=0)
    partner = jnp.concatenate([zero, jnp.concatenate(images[2:4], axis=1)], axis=0)
    for level in range(levels):
        own_high, own_low = split_two(own)
        partner_high, partner_low = split_two(partner)
        own_rows = jnp.concatenate([own_high, own_low], axis=0)
        partner_rows = jnp.concatenate([partner_high, partner_low], axis=0)

        def merged(ref, mine, other):
            product = jnp.dot(
                mine, complex_operand(*band(ref, level, 0)), preferred_element_type=F32
            ) + jnp.dot(other, complex_operand(*band(ref, level, 1)), preferred_element_type=F32)
            return product[: 2 * width] + product[2 * width :]

        following = merged(own_ref, own_rows, partner_rows)
        if level < levels - 1:
            partner = merged(partner_ref, partner_rows, own_rows)
        own = following
    full, left, right = [], [], []
    for j in range(2 * sections):
        real = own[j * group : (j + 1) * group, :beams]
        imag = own[j * group : (j + 1) * group, beams:]
        straight = jnp.concatenate([real, imag], axis=1)
        turned = jnp.concatenate([-imag, real], axis=1)
        lead, moved = pack_rows_of(straight, turned, each)
        row = lax.broadcasted_iota(jnp.int32, lead.shape, 0)
        full.append(lead)
        left.append(jnp.where(row < group // 2, pltpu.roll(turned, group - moved, 0), 0.0))
        right.append(jnp.where(row >= group // 2, pltpu.roll(turned, group // 2 - moved, 0), 0.0))
    pairs = sections // 2
    first_core = section % 2 == 0
    for half, rest in enumerate((left, right)):
        sources = [jnp.concatenate([full[j], rest[j]], axis=0) for j in range(2 * sections)]
        quarters = [jnp.concatenate(sources[q * pairs : (q + 1) * pairs], axis=0) for q in range(4)]
        quarters = [
            quarters[0],
            quarters[3],
            jnp.where(first_core, quarters[1], quarters[2]),
            jnp.where(first_core, quarters[2], quarters[1]),
        ]
        high, low = split_two(jnp.concatenate(quarters, axis=0).T)
        out_ref[half] = jnp.concatenate([high, low], axis=1)


def fold_operator(section, own, partner, dims, sections, group, each):
    beams = dims[-1]
    width = sections * group
    return pl.pallas_call(
        functools.partial(operator_kernel, dims=dims, sections=sections, group=group, each=each),
        out_shape=jax.ShapeDtypeStruct((2, 2 * beams, 8 * width), BF16),
        in_specs=[
            pl.BlockSpec(memory_space=pltpu.SMEM),
            pl.BlockSpec(memory_space=pltpu.VMEM),
            pl.BlockSpec(memory_space=pltpu.VMEM),
        ],
        scratch_shapes=[pltpu.VMEM((width, beams), F32)],
        compiler_params=pltpu.CompilerParams(vmem_limit_bytes=16 * 1024 * 1024),
        name="fold_operator",
    )(section, own, partner)


def correlate(rows, held, table, blocks, group):
    lags, stack = table.shape[0] // LANE, 2 * group
    for b in range(blocks + lags - 1):
        held[b * stack : (b + 1) * stack] = rows[:, b * LANE : (b + 1) * LANE].astype(BF16)
    pieces = [held[lag * stack : (lag + blocks) * stack] for lag in range(lags)]
    return jnp.dot(jnp.concatenate(pieces, axis=1), table[...], preferred_element_type=F32)


def as_chunk(done, s, chunk, group, each):
    real, imag = [], []
    for b in range(s * chunk, (s + 1) * chunk):
        at = 2 * b * group
        first, second = done[at : at + group], done[at + group : at + 2 * group]
        real.append(first[:, :LANE] + second[:, LANE:])
        imag.append(second[:, :LANE] - first[:, LANE:])
    real, imag = jnp.concatenate(real, axis=1), jnp.concatenate(imag, axis=1)
    middle = chunk * LANE // 2
    lead, moved = pack_rows_of(real, imag, each)
    row = lax.broadcasted_iota(jnp.int32, (group, middle), 0)
    rest = jnp.where(
        row < group // 2,
        pltpu.roll(imag[:, :middle], group - moved, 0),
        pltpu.roll(imag[:, middle:], group // 2 - moved, 0),
    )
    return jnp.concatenate([lead[:, :middle], lead[:, middle:], rest], axis=0).astype(BF16)


def begin_kernel(echo_ref, chirp_ref, early_ref, late_ref, table, rows, held, *, group):
    pulses, _, length = echo_ref.shape
    extra = chirp_ref.shape[1] // LANE
    reverse = LANE - 1 - lax.broadcasted_iota(jnp.int32, (2, LANE), 1)
    below = lax.broadcasted_iota(jnp.int32, (LANE, LANE), 1) <= lax.broadcasted_iota(
        jnp.int32, (LANE, LANE), 0
    )
    before = [jnp.zeros((LANE, LANE), BF16)] * 2
    for lag in range(extra + 1):
        if lag < extra:
            piece = chirp_ref[:, lag * LANE : (lag + 1) * LANE].astype(F32)
            piece = jnp.take_along_axis(piece, reverse, axis=1, mode="promise_in_bounds")
            turned = []
            for c in range(2):
                few = jnp.broadcast_to(piece[c : c + 1], (2 * SUBL, LANE))
                few = pltpu.roll(few, 1, 1, stride=1, stride_axis=0).astype(BF16)
                groups = [few] + [pltpu.roll(few, at, 1) for at in range(2 * SUBL, LANE, 2 * SUBL)]
                turned.append(jnp.concatenate(groups, axis=0))
        else:
            turned = [jnp.zeros((LANE, LANE), BF16)] * 2
        real, imag = [jnp.where(below, turned[c], before[c]) for c in range(2)]
        before = turned
        table[lag * LANE : (lag + 1) * LANE, :LANE] = real
        table[lag * LANE : (lag + 1) * LANE, LANE:] = imag
    rows[...] = jnp.zeros_like(rows)
    for p in range(pulses):
        near = echo_ref[p].astype(F32)
        for c in range(2):
            rows[c * group + p : c * group + p + 1, :] = near[c : c + 1]
    late_ref[...] = rows[:, length - late_ref.shape[1] :]
    done = correlate(rows, held, table, length // LANE - extra, group)
    for s in range(early_ref.shape[0]):
        early_ref[s] = as_chunk(done, s, 2 * early_ref.shape[2] // LANE, group, pulses)


def finish_kernel(index_ref, early_ref, late_ref, halo_ref, table, keep_ref, give_ref, rows, held, *, group):
    pulses = halo_ref.shape[0]
    span = late_ref.shape[1]
    taps = rows.shape[1] - span
    ready = early_ref.shape[0]
    chunk = 2 * early_ref.shape[2]
    sections = ready + span // chunk
    section = lax.rem(index_ref[0], sections)
    has_next = index_ref[0] >= sections
    rows[:, :span] = late_ref[...]
    rows[:, span:] = jnp.zeros((2 * group, taps), F32)
    for p in range(pulses):
        far = jnp.where(has_next, halo_ref[p, :, :taps].astype(F32), 0.0)
        for c in range(2):
            rows[c * group + p : c * group + p + 1, span:] = far[c : c + 1]
    done = correlate(rows, held, table, span // LANE, group)
    for s in range(sections):
        stacked = early_ref[s] if s < ready else as_chunk(done, s - ready, chunk // LANE, group, pulses)
        slot = section ^ s
        far_chunk, other_core = slot // 2, slot % 2
        place = far_chunk ^ 1 ^ (section % 2) ^ other_core

        @pl.when(other_core == 0)
        def _():
            keep_ref[place] = stacked

        @pl.when(other_core == 1)
        def _():
            give_ref[place] = stacked


def row_scratch(blocks, group):
    return [
        pltpu.VMEM((2 * group, blocks * LANE), F32),
        pltpu.VMEM((2 * blocks * group, LANE), BF16),
    ]


def begin_compression(echo, chirp, sections, group):
    _, _, length = echo.shape
    taps = chirp.shape[1]
    chunk = length // sections
    early = (length - taps) // chunk
    return pl.pallas_call(
        functools.partial(begin_kernel, group=group),
        out_shape=(
            jax.ShapeDtypeStruct((early, 3 * group, chunk // 2), BF16),
            jax.ShapeDtypeStruct((2 * group, length - early * chunk), F32),
            jax.ShapeDtypeStruct((taps + LANE, 2 * LANE), BF16),
        ),
        scratch_shapes=row_scratch(length // LANE, group),
        compiler_params=pltpu.CompilerParams(vmem_limit_bytes=24 * 1024 * 1024),
        name="begin_compression",
    )(echo, chirp)


def finish_compression(place, early, late, halo, table, group):
    blocks = late.shape[1] // LANE + table.shape[0] // LANE - 1
    return pl.pallas_call(
        functools.partial(finish_kernel, group=group),
        out_shape=[jax.ShapeDtypeStruct((2, *early.shape[1:]), BF16)] * 2,
        in_specs=[pl.BlockSpec(memory_space=pltpu.SMEM)] + [pl.BlockSpec(memory_space=pltpu.VMEM)] * 4,
        scratch_shapes=row_scratch(blocks, group),
        compiler_params=pltpu.CompilerParams(vmem_limit_bytes=24 * 1024 * 1024),
        name="finish_compression",
    )(place, early, late, halo, table)


def image_kernel(index_ref, operator_ref, both_ref, *refs, group):
    chunks, (out_ref, parts, sems) = refs[:-3], refs[-3:]
    count, _, tile = parts.shape
    width = both_ref.shape[2]
    near = 1 - index_ref[0] % 2
    held = [both_ref[near]] + [chunk[...] for chunk in chunks]
    held = [value.astype(F32) for value in held]
    copies = []
    for i in range(count):
        half, at = divmod(i * tile, width)
        rows = []
        for value in held:
            for first in range(0, value.shape[0], 3 * group):
                rows.append(value[first + half * group : first + (half + 1) * group, at : at + tile])
                rows.append(value[first + 2 * group : first + 3 * group, at : at + tile])
        pulses = jnp.concatenate(rows, axis=0).astype(BF16)
        result = jnp.dot(
            operator_ref[half], jnp.concatenate([pulses, pulses], axis=0), preferred_element_type=F32
        )
        parts[i] = result.astype(BF16)
        copy = pltpu.make_async_copy(parts.at[i], out_ref.at[:, i * tile : (i + 1) * tile], sems.at[i])
        copy.start()
        copies.append(copy)
    for copy in copies:
        copy.wait()


def form_image(section, operator, both, chunks, group):
    height, half = operator.shape[1], both.shape[2]
    tile = 256 if half % 256 == 0 else half
    count = 2 * half // tile
    return pl.pallas_call(
        functools.partial(image_kernel, group=group),
        out_shape=jax.ShapeDtypeStruct((height, 2 * half), BF16),
        in_specs=[pl.BlockSpec(memory_space=pltpu.SMEM)]
        + [pl.BlockSpec(memory_space=pltpu.VMEM)] * (2 + len(chunks)),
        out_specs=pl.BlockSpec(memory_space=pl.ANY),
        scratch_shapes=[
            pltpu.VMEM((count, height, tile), BF16),
            pltpu.SemaphoreType.DMA((count,)),
        ],
        compiler_params=pltpu.CompilerParams(vmem_limit_bytes=16 * 1024 * 1024),
        name="form_image",
    )(section, operator, both, *chunks)


def swap(value, axis, by):
    count = lax.axis_size(axis)
    return lax.ppermute(value, axis, [(i, i ^ by) for i in range(count)])


def swap_by(value, move):
    sections, subs = lax.axis_size("section"), lax.axis_size("sub")
    pairs = []
    for s in range(sections):
        for a in range(subs):
            to_s, to_a = move(s, a)
            pairs.append((s * subs + a, to_s * subs + to_a))
    return lax.ppermute(value, ("section", "sub"), pairs)


def from_next(value, axis):
    count = lax.axis_size(axis)
    return lax.ppermute(value, axis, [(i, (i - 1) % count) for i in range(count)])


def on_device(echoes, chirp, steer, pulse_order, band_coef, band_start, band_width):
    sections, subs = lax.axis_size("section"), lax.axis_size("sub")
    pulses_each = echoes.shape[2]
    group = ceil_to(pulses_each, SUBL)
    section = lax.axis_index("section").astype(jnp.int32).reshape(1)
    coef = jnp.swapaxes(band_coef, 4, 5)
    weights = jnp.swapaxes(steer, 2, 3)
    levels, _, sides, parts, taps, beams = coef.shape
    dims = (levels, sides, parts, taps, beams)

    echo = jnp.transpose(echoes[:, 0], (1, 0, 2))
    halo = from_next(echo, "rng")
    echo, chirp, packed = prepare(
        echo, chirp, coef, band_start, band_width, weights, pulse_order, sections, group
    )
    has_next = (lax.axis_index("rng") < lax.axis_size("rng") - 1).astype(jnp.int32)
    if subs == 2:
        packed_partner = swap(packed, "sub", 1)
    early, late, table = begin_compression(echo, chirp, sections, group)
    place = section + sections * has_next
    keep, give = finish_compression(place, early, late, halo, table, group)
    both = jnp.concatenate([keep, swap(give, "section", 1)], axis=1)
    far = lax.dynamic_index_in_dim(both, section[0] % 2, 0, keepdims=False)
    if subs != 2:
        near = lax.dynamic_index_in_dim(both, 1 - section[0] % 2, 0, keepdims=False)
        chunks = [near, swap(far, "section", 2)]
        return merge_images(section, chunks, packed, dims, sections, group, pulses_each)
    chunks = [
        swap_by(far, lambda s, a: (s ^ 2, a ^ 1)),
        swap_by(both[0], lambda s, a: (s, a ^ 1) if s % 2 else (s ^ 2, a)),
        swap_by(both[1], lambda s, a: (s ^ 2, a) if s % 2 else (s, a ^ 1)),
    ]
    operator = fold_operator(section, packed, packed_partner, dims, sections, group, pulses_each)
    image = form_image(section, operator, both, chunks, group)
    return image.reshape(2, beams, 1, image.shape[1])


def unpack(chunk, group, each):
    lead = jnp.concatenate([chunk[:group], chunk[group : 2 * group]], axis=1)
    moved, rest = group - each, chunk[2 * group :]
    tail = jnp.concatenate([rest[: each - moved], rest[group // 2 : group // 2 + each - moved]], axis=1)
    return jnp.concatenate([lead, tail], axis=0)


def merge_images(section, chunks, packed, dims, sections, group, each):
    levels, sides, parts, taps, beams = dims
    width = sections * group
    first = levels * sides * parts * taps
    table = packed[first : first + parts * width].reshape(parts, sections, group, beams)
    table = jnp.take(table, section[0] ^ jnp.arange(sections), axis=1)[:, :, :each]
    chunks = [
        unpack(chunk[first : first + 3 * group], group, each)
        for chunk in chunks
        for first in range(0, chunk.shape[0], 3 * group)
    ]
    real, imag = table[0], table[1]
    rows = jnp.concatenate(
        [jnp.concatenate([real, -imag], axis=1), jnp.concatenate([imag, real], axis=1)], axis=2
    )
    image = lax.dot_general(
        rows.reshape(-1, 2 * beams), jnp.concatenate(chunks, axis=0), (((0,), (0,)), ((), ())), preferred_element_type=F32
    ).astype(BF16)
    starts = packed[first + parts * width :].astype(jnp.int32)
    column = jnp.arange(beams, dtype=jnp.int32)
    bits = lax.axis_size("sub").bit_length() - 1
    for level in range(levels):
        partner = swap(image, "sub", 1 << (level % bits))
        operands = []
        for side in range(sides):
            at = (level * sides + side) * parts * taps
            coef = packed[at : at + parts * taps].reshape(parts, taps, beams)
            offset = column[:, None] - starts[level * sides + side][None, :]
            hits = (offset[None] == jnp.arange(taps, dtype=jnp.int32)[:, None, None]).astype(BF16)
            operands.append(jnp.einsum("ptq,tcq->pqc", coef, hits, preferred_element_type=F32).astype(BF16))
        top = jnp.concatenate([operands[0][0], -operands[0][1], operands[1][0], -operands[1][1]], axis=1)
        low = jnp.concatenate([operands[0][1], operands[0][0], operands[1][1], operands[1][0]], axis=1)
        image = jnp.dot(
            jnp.concatenate([top, low], axis=0),
            jnp.concatenate([image, partner], axis=0),
            preferred_element_type=F32,
        ).astype(BF16)
    return image.reshape(2, beams, 1, image.shape[1])


def solution(mesh):
    return jax.shard_map(
        on_device,
        mesh=mesh,
        in_specs=(
            P(None, "sub", "section", "rng"),
            P(),
            P(None, "sub", None, None),
            P("sub", None),
            P(None, "sub", None, None, None, None),
            P(None, "sub", None, None),
            P(None, "sub", None, None),
        ),
        out_specs=P(None, "sub", "rng", "section"),
        check_vma=False,
    )
```

```python
import functools

import jax
import jax.numpy as jnp
from jax import lax
from jax.experimental import pallas as pl
from jax.experimental.pallas import tpu as pltpu
from jax.sharding import PartitionSpec as P

LANE = 128
SUBL = 8
F32 = jnp.float32
BF16 = jnp.bfloat16


def ceil_to(value, unit):
    return -(-value // unit) * unit


def prepare_kernel(*refs, sections, group):
    sources, (echo_out, chirp_out, pack_ref), scratch = refs[:7], refs[7:10], refs[10:]
    coef_ref, start_ref, width_ref, steer_ref, order_ref, starts, sems = scratch
    targets = (echo_out, coef_ref, start_ref, width_ref, steer_ref, order_ref, chirp_out)
    loads = [
        pltpu.make_async_copy(source, target, sems.at[i])
        for i, (source, target) in enumerate(zip(sources, targets))
    ]
    for load in loads:
        load.start()
    for load in loads:
        load.wait()
    levels, _, sides, parts, taps, beams = coef_ref.shape
    tap = lax.broadcasted_iota(jnp.int32, (taps, beams), 0)
    row = 0
    for level in range(levels):
        for side in range(sides):
            used = tap < width_ref[level, 0, side : side + 1, :]
            for part in range(parts):
                entries = coef_ref[level, 0, side, part].astype(F32)
                pack_ref[row : row + taps] = jnp.where(used, entries, 0.0).astype(BF16)
                row += taps
    pulses = order_ref.shape[1]
    each = pulses // sections
    position = lax.broadcasted_iota(jnp.int32, (pulses, pulses), 0)
    hit = (position == order_ref[0:1, :]).astype(F32)
    slot = lax.broadcasted_iota(jnp.int32, (sections * group, pulses), 0)
    pulse = lax.broadcasted_iota(jnp.int32, (sections * group, pulses), 1)
    place = jnp.zeros((sections * group, pulses), F32)
    for s in range(sections):
        inside = (pulse >= s * each) & (pulse < (s + 1) * each)
        place = jnp.where(inside & (slot - s * group == pulse - s * each), 1.0, place)
    pick = lax.dot_general(
        place.astype(BF16), hit.astype(BF16), (((1,), (1,)), ((), ())), preferred_element_type=F32
    )
    for part in range(parts):
        chosen = jnp.dot(pick.astype(BF16), steer_ref[part, 0], preferred_element_type=F32)
        pack_ref[row : row + sections * group] = chosen.astype(BF16)
        row += sections * group
    starts[...] = jnp.zeros_like(starts)
    for level in range(levels):
        starts[sides * level : sides * level + sides] = start_ref[level, 0].astype(F32)
    pack_ref[row : row + starts.shape[0]] = starts[...].astype(BF16)


def pack_rows(levels, sides, parts, taps, sections, group):
    return levels * sides * parts * taps + parts * sections * group + ceil_to(levels * sides, 16)


def prepare(echo, chirp, coef, start, width, steer, order, sections, group):
    levels, _, sides, parts, taps, beams = coef.shape
    sources = (echo, coef, start, width, steer, order, chirp)
    return pl.pallas_call(
        functools.partial(prepare_kernel, sections=sections, group=group),
        out_shape=(
            jax.ShapeDtypeStruct(echo.shape, BF16),
            jax.ShapeDtypeStruct(chirp.shape, BF16),
            jax.ShapeDtypeStruct((pack_rows(levels, sides, parts, taps, sections, group), beams), BF16),
        ),
        in_specs=[pl.BlockSpec(memory_space=pl.ANY)] * len(sources),
        scratch_shapes=[pltpu.VMEM(x.shape, x.dtype) for x in sources[1:6]]
        + [pltpu.VMEM((ceil_to(levels * sides, 16), beams), F32), pltpu.SemaphoreType.DMA((len(sources),))],
        compiler_params=pltpu.CompilerParams(vmem_limit_bytes=16 * 1024 * 1024),
        name="prepare",
    )(*[pltpu.with_memory_space_constraint(x, pltpu.HBM) for x in sources])


def pack_rows_of(real, imag, each):
    group = real.shape[0]
    row = lax.broadcasted_iota(jnp.int32, real.shape, 0)
    return jnp.where(row < each, real, pltpu.roll(imag, each, 0)), group - each


def split_two(value):
    high = value.astype(BF16)
    return high, (value - high.astype(F32)).astype(BF16)


def operator_kernel(index_ref, own_ref, partner_ref, out_ref, weights, *, dims, sections, group, each):
    levels, sides, parts, taps, beams = dims
    width = sections * group
    refs = (own_ref, partner_ref)
    weight_row = levels * sides * parts * taps
    start_row = weight_row + parts * width

    def band(ref, level, side):
        first = ((level * sides + side) * parts) * taps
        tables = [ref[first + p * taps : first + (p + 1) * taps].astype(F32) for p in range(parts)]
        start = ref[start_row : start_row + ceil_to(levels * sides, 16)].astype(F32)
        start = start[level * sides + side : level * sides + side + 1].astype(jnp.int32)
        found = [[], []]
        for c in range(0, beams, SUBL):
            column = lax.broadcasted_iota(jnp.int32, (SUBL, beams), 0) + c
            offset = column - start
            spot = offset & (SUBL - 1)
            for p in range(parts):
                value = jnp.zeros((SUBL, beams), F32)
                for t in range(0, taps, SUBL):
                    got = jnp.take_along_axis(
                        tables[p][t : t + SUBL], spot, axis=0, mode="promise_in_bounds"
                    )
                    value = jnp.where((offset >= t) & (offset < t + SUBL), got, value)
                found[p].append(value)
        return [jnp.concatenate(f, axis=0) for f in found]

    def complex_operand(real, imag):
        top = jnp.concatenate([real, imag], axis=1)
        low = jnp.concatenate([-imag, real], axis=1)
        return jnp.concatenate([top, low], axis=0).astype(BF16)

    section = index_ref[0]
    images = []
    for a in range(2):
        for p in range(parts):
            weights[...] = refs[a][weight_row + p * width : weight_row + (p + 1) * width].astype(F32)
            rows = []
            for j in range(sections):
                at = pl.multiple_of((section ^ j) * group, group)
                rows.append(weights[pl.ds(at, group)])
            images.append(jnp.concatenate(rows, axis=0))
    zero = jnp.zeros((width, 2 * beams), F32)
    own = jnp.concatenate([jnp.concatenate(images[0:2], axis=1), zero], axis=0)
    partner = jnp.concatenate([zero, jnp.concatenate(images[2:4], axis=1)], axis=0)
    for level in range(levels):
        own_high, own_low = split_two(own)
        partner_high, partner_low = split_two(partner)
        own_rows = jnp.concatenate([own_high, own_low], axis=0)
        partner_rows = jnp.concatenate([partner_high, partner_low], axis=0)

        def merged(ref, mine, other):
            product = jnp.dot(
                mine, complex_operand(*band(ref, level, 0)), preferred_element_type=F32
            ) + jnp.dot(other, complex_operand(*band(ref, level, 1)), preferred_element_type=F32)
            return product[: 2 * width] + product[2 * width :]

        following = merged(own_ref, own_rows, partner_rows)
        if level < levels - 1:
            partner = merged(partner_ref, partner_rows, own_rows)
        own = following
    full, left, right = [], [], []
    for j in range(2 * sections):
        real = own[j * group : (j + 1) * group, :beams]
        imag = own[j * group : (j + 1) * group, beams:]
        straight = jnp.concatenate([real, imag], axis=1)
        turned = jnp.concatenate([-imag, real], axis=1)
        lead, moved = pack_rows_of(straight, turned, each)
        row = lax.broadcasted_iota(jnp.int32, lead.shape, 0)
        full.append(lead)
        left.append(jnp.where(row < group // 2, pltpu.roll(turned, group - moved, 0), 0.0))
        right.append(jnp.where(row >= group // 2, pltpu.roll(turned, group // 2 - moved, 0), 0.0))
    pairs = sections // 2
    first_core = section % 2 == 0
    for half, rest in enumerate((left, right)):
        sources = [jnp.concatenate([full[j], rest[j]], axis=0) for j in range(2 * sections)]
        quarters = [jnp.concatenate(sources[q * pairs : (q + 1) * pairs], axis=0) for q in range(4)]
        quarters = [
            quarters[0],
            quarters[3],
            jnp.where(first_core, quarters[1], quarters[2]),
            jnp.where(first_core, quarters[2], quarters[1]),
        ]
        high, low = split_two(jnp.concatenate(quarters, axis=0).T)
        out_ref[half] = jnp.concatenate([high, low], axis=1)


def fold_operator(section, own, partner, dims, sections, group, each):
    beams = dims[-1]
    width = sections * group
    return pl.pallas_call(
        functools.partial(operator_kernel, dims=dims, sections=sections, group=group, each=each),
        out_shape=jax.ShapeDtypeStruct((2, 2 * beams, 8 * width), BF16),
        in_specs=[
            pl.BlockSpec(memory_space=pltpu.SMEM),
            pl.BlockSpec(memory_space=pltpu.VMEM),
            pl.BlockSpec(memory_space=pltpu.VMEM),
        ],
        scratch_shapes=[pltpu.VMEM((width, beams), F32)],
        compiler_params=pltpu.CompilerParams(vmem_limit_bytes=16 * 1024 * 1024),
        name="fold_operator",
    )(section, own, partner)


def correlate(rows, even, odd, table, blocks, group):
    extra = table.shape[0] // (2 * LANE) - 1
    total = blocks + extra
    held = [
        jnp.concatenate(
            [rows[:group, b * LANE : (b + 1) * LANE], rows[group:, b * LANE : (b + 1) * LANE]], axis=1
        )
        for b in range(total)
    ]
    for b in range(0, total, 2):
        even[b * group : (b + 2) * group] = jnp.concatenate(held[b : b + 2], axis=0).astype(BF16)
    for b in range(1, total - 1, 2):
        odd[(b - 1) * group : (b + 1) * group] = jnp.concatenate(held[b : b + 2], axis=0).astype(BF16)
    window = blocks * group
    pieces = []
    for lag in range(extra + 1):
        source, at = (even, lag) if lag % 2 == 0 else (odd, lag - 1)
        pieces.append(source[at * group : at * group + window])
    return jnp.dot(jnp.concatenate(pieces, axis=1), table[...], preferred_element_type=F32)


def as_chunk(done, s, chunk, group, each):
    real, imag = [
        jnp.concatenate(
            [
                done[(s * chunk + b) * group : (s * chunk + b + 1) * group, c * LANE : (c + 1) * LANE]
                for b in range(chunk)
            ],
            axis=1,
        )
        for c in range(2)
    ]
    middle = chunk * LANE // 2
    lead, moved = pack_rows_of(real, imag, each)
    row = lax.broadcasted_iota(jnp.int32, (group, middle), 0)
    rest = jnp.where(
        row < group // 2,
        pltpu.roll(imag[:, :middle], group - moved, 0),
        pltpu.roll(imag[:, middle:], group // 2 - moved, 0),
    )
    return jnp.concatenate([lead[:, :middle], lead[:, middle:], rest], axis=0).astype(BF16)


def begin_kernel(echo_ref, chirp_ref, early_ref, late_ref, table, rows, even, odd, *, group):
    pulses, _, length = echo_ref.shape
    extra = chirp_ref.shape[1] // LANE
    reverse = LANE - 1 - lax.broadcasted_iota(jnp.int32, (2, LANE), 1)
    below = lax.broadcasted_iota(jnp.int32, (LANE, LANE), 1) <= lax.broadcasted_iota(
        jnp.int32, (LANE, LANE), 0
    )
    before = [jnp.zeros((LANE, LANE), BF16)] * 2
    for lag in range(extra + 1):
        if lag < extra:
            piece = chirp_ref[:, lag * LANE : (lag + 1) * LANE].astype(F32)
            piece = jnp.take_along_axis(piece, reverse, axis=1, mode="promise_in_bounds")
            turned = []
            for c in range(2):
                few = jnp.broadcast_to(piece[c : c + 1], (2 * SUBL, LANE))
                few = pltpu.roll(few, 1, 1, stride=1, stride_axis=0).astype(BF16)
                groups = [few] + [pltpu.roll(few, at, 1) for at in range(2 * SUBL, LANE, 2 * SUBL)]
                turned.append(jnp.concatenate(groups, axis=0))
        else:
            turned = [jnp.zeros((LANE, LANE), BF16)] * 2
        real, imag = [jnp.where(below, turned[c], before[c]) for c in range(2)]
        before = turned
        at = lag * 2 * LANE
        table[at : at + LANE, :LANE] = real
        table[at : at + LANE, LANE:] = -imag
        table[at + LANE : at + 2 * LANE, :LANE] = imag
        table[at + LANE : at + 2 * LANE, LANE:] = real
    rows[...] = jnp.zeros_like(rows)
    for p in range(pulses):
        near = echo_ref[p].astype(F32)
        for c in range(2):
            rows[c * group + p : c * group + p + 1, :] = near[c : c + 1]
    late_ref[...] = rows[:, length - late_ref.shape[1] :]
    done = correlate(rows, even, odd, table, length // LANE - extra, group)
    for s in range(early_ref.shape[0]):
        early_ref[s] = as_chunk(done, s, 2 * early_ref.shape[2] // LANE, group, pulses)


def finish_kernel(index_ref, early_ref, late_ref, halo_ref, table, keep_ref, give_ref, rows, even, odd, *, group):
    pulses = halo_ref.shape[0]
    span = late_ref.shape[1]
    taps = rows.shape[1] - span
    ready = early_ref.shape[0]
    chunk = 2 * early_ref.shape[2]
    sections = ready + span // chunk
    section = lax.rem(index_ref[0], sections)
    has_next = index_ref[0] >= sections
    rows[:, :span] = late_ref[...]
    rows[:, span:] = jnp.zeros((2 * group, taps), F32)
    for p in range(pulses):
        far = jnp.where(has_next, halo_ref[p, :, :taps].astype(F32), 0.0)
        for c in range(2):
            rows[c * group + p : c * group + p + 1, span:] = far[c : c + 1]
    done = correlate(rows, even, odd, table, span // LANE, group)
    for s in range(sections):
        stacked = early_ref[s] if s < ready else as_chunk(done, s - ready, chunk // LANE, group, pulses)
        slot = section ^ s
        far_chunk, other_core = slot // 2, slot % 2
        place = far_chunk ^ 1 ^ (section % 2) ^ other_core

        @pl.when(other_core == 0)
        def _():
            keep_ref[place] = stacked

        @pl.when(other_core == 1)
        def _():
            give_ref[place] = stacked


def row_scratch(blocks, group):
    return [
        pltpu.VMEM((2 * group, blocks * LANE), F32),
        pltpu.VMEM((blocks * group, 2 * LANE), BF16),
        pltpu.VMEM((blocks * group, 2 * LANE), BF16),
    ]


def begin_compression(echo, chirp, sections, group):
    _, _, length = echo.shape
    taps = chirp.shape[1]
    chunk = length // sections
    early = (length - taps) // chunk
    return pl.pallas_call(
        functools.partial(begin_kernel, group=group),
        out_shape=(
            jax.ShapeDtypeStruct((early, 3 * group, chunk // 2), BF16),
            jax.ShapeDtypeStruct((2 * group, length - early * chunk), F32),
            jax.ShapeDtypeStruct(((taps // LANE + 1) * 2 * LANE, 2 * LANE), BF16),
        ),
        scratch_shapes=row_scratch(length // LANE, group),
        compiler_params=pltpu.CompilerParams(vmem_limit_bytes=24 * 1024 * 1024),
        name="begin_compression",
    )(echo, chirp)


def finish_compression(place, early, late, halo, table, group):
    blocks = late.shape[1] // LANE + table.shape[0] // (2 * LANE) - 1
    return pl.pallas_call(
        functools.partial(finish_kernel, group=group),
        out_shape=[jax.ShapeDtypeStruct((2, *early.shape[1:]), BF16)] * 2,
        in_specs=[pl.BlockSpec(memory_space=pltpu.SMEM)] + [pl.BlockSpec(memory_space=pltpu.VMEM)] * 4,
        scratch_shapes=row_scratch(blocks, group),
        compiler_params=pltpu.CompilerParams(vmem_limit_bytes=24 * 1024 * 1024),
        name="finish_compression",
    )(place, early, late, halo, table)


def image_kernel(index_ref, operator_ref, both_ref, *refs, group):
    chunks, (out_ref, parts, sems) = refs[:-3], refs[-3:]
    count, _, tile = parts.shape
    width = both_ref.shape[2]
    near = 1 - index_ref[0] % 2
    held = [both_ref[near]] + [chunk[...] for chunk in chunks]
    held = [value.astype(F32) for value in held]
    copies = []
    for i in range(count):
        half, at = divmod(i * tile, width)
        rows = []
        for value in held:
            for first in range(0, value.shape[0], 3 * group):
                rows.append(value[first + half * group : first + (half + 1) * group, at : at + tile])
                rows.append(value[first + 2 * group : first + 3 * group, at : at + tile])
        pulses = jnp.concatenate(rows, axis=0).astype(BF16)
        result = jnp.dot(
            operator_ref[half], jnp.concatenate([pulses, pulses], axis=0), preferred_element_type=F32
        )
        parts[i] = result.astype(BF16)
        copy = pltpu.make_async_copy(parts.at[i], out_ref.at[:, i * tile : (i + 1) * tile], sems.at[i])
        copy.start()
        copies.append(copy)
    for copy in copies:
        copy.wait()


def form_image(section, operator, both, chunks, group):
    height, half = operator.shape[1], both.shape[2]
    tile = 256 if half % 256 == 0 else half
    count = 2 * half // tile
    return pl.pallas_call(
        functools.partial(image_kernel, group=group),
        out_shape=jax.ShapeDtypeStruct((height, 2 * half), BF16),
        in_specs=[pl.BlockSpec(memory_space=pltpu.SMEM)]
        + [pl.BlockSpec(memory_space=pltpu.VMEM)] * (2 + len(chunks)),
        out_specs=pl.BlockSpec(memory_space=pl.ANY),
        scratch_shapes=[
            pltpu.VMEM((count, height, tile), BF16),
            pltpu.SemaphoreType.DMA((count,)),
        ],
        compiler_params=pltpu.CompilerParams(vmem_limit_bytes=16 * 1024 * 1024),
        name="form_image",
    )(section, operator, both, *chunks)


def swap(value, axis, by):
    count = lax.axis_size(axis)
    return lax.ppermute(value, axis, [(i, i ^ by) for i in range(count)])


def swap_by(value, move):
    sections, subs = lax.axis_size("section"), lax.axis_size("sub")
    pairs = []
    for s in range(sections):
        for a in range(subs):
            to_s, to_a = move(s, a)
            pairs.append((s * subs + a, to_s * subs + to_a))
    return lax.ppermute(value, ("section", "sub"), pairs)


def from_next(value, axis):
    count = lax.axis_size(axis)
    return lax.ppermute(value, axis, [(i, (i - 1) % count) for i in range(count)])


def on_device(echoes, chirp, steer, pulse_order, band_coef, band_start, band_width):
    sections, subs = lax.axis_size("section"), lax.axis_size("sub")
    pulses_each = echoes.shape[2]
    group = ceil_to(pulses_each, SUBL)
    section = lax.axis_index("section").astype(jnp.int32).reshape(1)
    coef = jnp.swapaxes(band_coef, 4, 5)
    weights = jnp.swapaxes(steer, 2, 3)
    levels, _, sides, parts, taps, beams = coef.shape
    dims = (levels, sides, parts, taps, beams)

    echo = jnp.transpose(echoes[:, 0], (1, 0, 2))
    halo = from_next(echo, "rng")
    echo, chirp, packed = prepare(
        echo, chirp, coef, band_start, band_width, weights, pulse_order, sections, group
    )
    has_next = (lax.axis_index("rng") < lax.axis_size("rng") - 1).astype(jnp.int32)
    early, late, table = begin_compression(echo, chirp, sections, group)
    place = section + sections * has_next
    keep, give = finish_compression(place, early, late, halo, table, group)
    height = keep.shape[1]
    both = jnp.zeros((2, 2 * height, keep.shape[2]), BF16)
    both = lax.dynamic_update_slice(both, keep, (0, 0, 0))
    given = swap(give, "section", 1)
    both, packed = lax.optimization_barrier((both, packed))
    packed_partner = swap(packed, "sub", 1) if subs == 2 else packed
    both = lax.dynamic_update_slice(both, given, (0, height, 0))
    far = lax.dynamic_index_in_dim(both, section[0] % 2, 0, keepdims=False)
    if subs != 2:
        near = lax.dynamic_index_in_dim(both, 1 - section[0] % 2, 0, keepdims=False)
        chunks = [near, swap(far, "section", 2)]
        return merge_images(section, chunks, packed, dims, sections, group, pulses_each)
    chunks = [
        swap_by(far, lambda s, a: (s ^ 2, a ^ 1)),
        swap_by(both[0], lambda s, a: (s, a ^ 1) if s % 2 else (s ^ 2, a)),
        swap_by(both[1], lambda s, a: (s ^ 2, a) if s % 2 else (s, a ^ 1)),
    ]
    operator = fold_operator(section, packed, packed_partner, dims, sections, group, pulses_each)
    image = form_image(section, operator, both, chunks, group)
    return image.reshape(2, beams, 1, image.shape[1])


def unpack(chunk, group, each):
    lead = jnp.concatenate([chunk[:group], chunk[group : 2 * group]], axis=1)
    moved, rest = group - each, chunk[2 * group :]
    tail = jnp.concatenate([rest[: each - moved], rest[group // 2 : group // 2 + each - moved]], axis=1)
    return jnp.concatenate([lead, tail], axis=0)


def merge_images(section, chunks, packed, dims, sections, group, each):
    levels, sides, parts, taps, beams = dims
    width = sections * group
    first = levels * sides * parts * taps
    table = packed[first : first + parts * width].reshape(parts, sections, group, beams)
    table = jnp.take(table, section[0] ^ jnp.arange(sections), axis=1)[:, :, :each]
    chunks = [
        unpack(chunk[first : first + 3 * group], group, each)
        for chunk in chunks
        for first in range(0, chunk.shape[0], 3 * group)
    ]
    real, imag = table[0], table[1]
    rows = jnp.concatenate(
        [jnp.concatenate([real, -imag], axis=1), jnp.concatenate([imag, real], axis=1)], axis=2
    )
    image = lax.dot_general(
        rows.reshape(-1, 2 * beams), jnp.concatenate(chunks, axis=0), (((0,), (0,)), ((), ())), preferred_element_type=F32
    ).astype(BF16)
    starts = packed[first + parts * width :].astype(jnp.int32)
    column = jnp.arange(beams, dtype=jnp.int32)
    bits = lax.axis_size("sub").bit_length() - 1
    for level in range(levels):
        partner = swap(image, "sub", 1 << (level % bits))
        operands = []
        for side in range(sides):
            at = (level * sides + side) * parts * taps
            coef = packed[at : at + parts * taps].reshape(parts, taps, beams)
            offset = column[:, None] - starts[level * sides + side][None, :]
            hits = (offset[None] == jnp.arange(taps, dtype=jnp.int32)[:, None, None]).astype(BF16)
            operands.append(jnp.einsum("ptq,tcq->pqc", coef, hits, preferred_element_type=F32).astype(BF16))
        top = jnp.concatenate([operands[0][0], -operands[0][1], operands[1][0], -operands[1][1]], axis=1)
        low = jnp.concatenate([operands[0][1], operands[0][0], operands[1][1], operands[1][0]], axis=1)
        image = jnp.dot(
            jnp.concatenate([top, low], axis=0),
            jnp.concatenate([image, partner], axis=0),
            preferred_element_type=F32,
        ).astype(BF16)
    return image.reshape(2, beams, 1, image.shape[1])


def solution(mesh):
    return jax.shard_map(
        on_device,
        mesh=mesh,
        in_specs=(
            P(None, "sub", "section", "rng"),
            P(),
            P(None, "sub", None, None),
            P("sub", None),
            P(None, "sub", None, None, None, None),
            P(None, "sub", None, None),
            P(None, "sub", None, None),
        ),
        out_specs=P(None, "sub", "rng", "section"),
        check_vma=False,
    )
```

```python
import functools

import jax
import jax.numpy as jnp
from jax import lax
from jax.experimental import pallas as pl
from jax.experimental.pallas import tpu as pltpu
from jax.sharding import PartitionSpec as P

LANE = 128
SUBL = 8
F32 = jnp.float32
BF16 = jnp.bfloat16


def ceil_to(value, unit):
    return -(-value // unit) * unit


def prepare_kernel(*refs, sections, group):
    sources, (echo_out, chirp_out, pack_ref), scratch = refs[:7], refs[7:10], refs[10:]
    coef_ref, start_ref, width_ref, steer_ref, order_ref, starts, sems = scratch
    targets = (echo_out, coef_ref, start_ref, width_ref, steer_ref, order_ref, chirp_out)
    loads = [
        pltpu.make_async_copy(source, target, sems.at[i])
        for i, (source, target) in enumerate(zip(sources, targets))
    ]
    for load in loads:
        load.start()
    for load in loads:
        load.wait()
    levels, _, sides, parts, taps, beams = coef_ref.shape
    tap = lax.broadcasted_iota(jnp.int32, (taps, beams), 0)
    row = 0
    for level in range(levels):
        for side in range(sides):
            used = tap < width_ref[level, 0, side : side + 1, :]
            for part in range(parts):
                entries = coef_ref[level, 0, side, part].astype(F32)
                pack_ref[row : row + taps] = jnp.where(used, entries, 0.0).astype(BF16)
                row += taps
    pulses = order_ref.shape[1]
    each = pulses // sections
    position = lax.broadcasted_iota(jnp.int32, (pulses, pulses), 0)
    hit = (position == order_ref[0:1, :]).astype(F32)
    slot = lax.broadcasted_iota(jnp.int32, (sections * group, pulses), 0)
    pulse = lax.broadcasted_iota(jnp.int32, (sections * group, pulses), 1)
    place = jnp.zeros((sections * group, pulses), F32)
    for s in range(sections):
        inside = (pulse >= s * each) & (pulse < (s + 1) * each)
        place = jnp.where(inside & (slot - s * group == pulse - s * each), 1.0, place)
    pick = lax.dot_general(
        place.astype(BF16), hit.astype(BF16), (((1,), (1,)), ((), ())), preferred_element_type=F32
    )
    for part in range(parts):
        chosen = jnp.dot(pick.astype(BF16), steer_ref[part, 0], preferred_element_type=F32)
        pack_ref[row : row + sections * group] = chosen.astype(BF16)
        row += sections * group
    starts[...] = jnp.zeros_like(starts)
    for level in range(levels):
        starts[sides * level : sides * level + sides] = start_ref[level, 0].astype(F32)
    pack_ref[row : row + starts.shape[0]] = starts[...].astype(BF16)


def pack_rows(levels, sides, parts, taps, sections, group):
    return levels * sides * parts * taps + parts * sections * group + ceil_to(levels * sides, 16)


def prepare(echo, chirp, coef, start, width, steer, order, sections, group):
    levels, _, sides, parts, taps, beams = coef.shape
    sources = (echo, coef, start, width, steer, order, chirp)
    return pl.pallas_call(
        functools.partial(prepare_kernel, sections=sections, group=group),
        out_shape=(
            jax.ShapeDtypeStruct(echo.shape, BF16),
            jax.ShapeDtypeStruct(chirp.shape, BF16),
            jax.ShapeDtypeStruct((pack_rows(levels, sides, parts, taps, sections, group), beams), BF16),
        ),
        in_specs=[pl.BlockSpec(memory_space=pl.ANY)] * len(sources),
        scratch_shapes=[pltpu.VMEM(x.shape, x.dtype) for x in sources[1:6]]
        + [pltpu.VMEM((ceil_to(levels * sides, 16), beams), F32), pltpu.SemaphoreType.DMA((len(sources),))],
        compiler_params=pltpu.CompilerParams(vmem_limit_bytes=16 * 1024 * 1024),
        name="prepare",
    )(*[pltpu.with_memory_space_constraint(x, pltpu.HBM) for x in sources])


def pack_rows_of(real, imag, each):
    group = real.shape[0]
    row = lax.broadcasted_iota(jnp.int32, real.shape, 0)
    return jnp.where(row < each, real, pltpu.roll(imag, each, 0)), group - each


def split_two(value):
    high = value.astype(BF16)
    return high, (value - high.astype(F32)).astype(BF16)


def operator_kernel(index_ref, own_ref, partner_ref, out_ref, weights, *, dims, sections, group, each):
    levels, sides, parts, taps, beams = dims
    width = sections * group
    refs = (own_ref, partner_ref)
    weight_row = levels * sides * parts * taps
    start_row = weight_row + parts * width

    def band(ref, level, side):
        first = ((level * sides + side) * parts) * taps
        tables = [ref[first + p * taps : first + (p + 1) * taps].astype(F32) for p in range(parts)]
        start = ref[start_row : start_row + ceil_to(levels * sides, 16)].astype(F32)
        start = start[level * sides + side : level * sides + side + 1].astype(jnp.int32)
        found = [[], []]
        for c in range(0, beams, SUBL):
            column = lax.broadcasted_iota(jnp.int32, (SUBL, beams), 0) + c
            offset = column - start
            spot = offset & (SUBL - 1)
            for p in range(parts):
                value = jnp.zeros((SUBL, beams), F32)
                for t in range(0, taps, SUBL):
                    got = jnp.take_along_axis(
                        tables[p][t : t + SUBL], spot, axis=0, mode="promise_in_bounds"
                    )
                    value = jnp.where((offset >= t) & (offset < t + SUBL), got, value)
                found[p].append(value)
        return [jnp.concatenate(f, axis=0) for f in found]

    def complex_operand(real, imag):
        top = jnp.concatenate([real, imag], axis=1)
        low = jnp.concatenate([-imag, real], axis=1)
        return jnp.concatenate([top, low], axis=0).astype(BF16)

    section = index_ref[0]
    images = []
    for a in range(2):
        for p in range(parts):
            weights[...] = refs[a][weight_row + p * width : weight_row + (p + 1) * width].astype(F32)
            rows = []
            for j in range(sections):
                at = pl.multiple_of((section ^ j) * group, group)
                rows.append(weights[pl.ds(at, group)])
            images.append(jnp.concatenate(rows, axis=0))
    zero = jnp.zeros((width, 2 * beams), F32)
    own = jnp.concatenate([jnp.concatenate(images[0:2], axis=1), zero], axis=0)
    partner = jnp.concatenate([zero, jnp.concatenate(images[2:4], axis=1)], axis=0)
    for level in range(levels):
        own_high, own_low = split_two(own)
        partner_high, partner_low = split_two(partner)
        own_rows = jnp.concatenate([own_high, own_low], axis=0)
        partner_rows = jnp.concatenate([partner_high, partner_low], axis=0)

        def merged(ref, mine, other):
            product = jnp.dot(
                mine, complex_operand(*band(ref, level, 0)), preferred_element_type=F32
            ) + jnp.dot(other, complex_operand(*band(ref, level, 1)), preferred_element_type=F32)
            return product[: 2 * width] + product[2 * width :]

        following = merged(own_ref, own_rows, partner_rows)
        if level < levels - 1:
            partner = merged(partner_ref, partner_rows, own_rows)
        own = following
    full, left, right = [], [], []
    for j in range(2 * sections):
        real = own[j * group : (j + 1) * group, :beams]
        imag = own[j * group : (j + 1) * group, beams:]
        straight = jnp.concatenate([real, imag], axis=1)
        turned = jnp.concatenate([-imag, real], axis=1)
        lead, moved = pack_rows_of(straight, turned, each)
        row = lax.broadcasted_iota(jnp.int32, lead.shape, 0)
        full.append(lead)
        left.append(jnp.where(row < group // 2, pltpu.roll(turned, group - moved, 0), 0.0))
        right.append(jnp.where(row >= group // 2, pltpu.roll(turned, group // 2 - moved, 0), 0.0))
    pairs = sections // 2
    for half, rest in enumerate((left, right)):
        sources = [jnp.concatenate([full[j], rest[j]], axis=0) for j in range(2 * sections)]
        quarters = [jnp.concatenate(sources[q * pairs : (q + 1) * pairs], axis=0) for q in range(4)]
        quarters = [
            quarters[0],
            quarters[1],
            quarters[3],
            quarters[2],
        ]
        high, low = split_two(jnp.concatenate(quarters, axis=0).T)
        out_ref[half] = jnp.concatenate([high, low], axis=1)


def fold_operator(section, own, partner, dims, sections, group, each):
    beams = dims[-1]
    width = sections * group
    return pl.pallas_call(
        functools.partial(operator_kernel, dims=dims, sections=sections, group=group, each=each),
        out_shape=jax.ShapeDtypeStruct((2, 2 * beams, 8 * width), BF16),
        in_specs=[
            pl.BlockSpec(memory_space=pltpu.SMEM),
            pl.BlockSpec(memory_space=pltpu.VMEM),
            pl.BlockSpec(memory_space=pltpu.VMEM),
        ],
        scratch_shapes=[pltpu.VMEM((width, beams), F32)],
        compiler_params=pltpu.CompilerParams(vmem_limit_bytes=16 * 1024 * 1024),
        name="fold_operator",
    )(section, own, partner)


def correlate(rows, even, odd, table, blocks, group):
    extra = table.shape[0] // (2 * LANE) - 1
    total = blocks + extra
    held = [
        jnp.concatenate(
            [rows[:group, b * LANE : (b + 1) * LANE], rows[group:, b * LANE : (b + 1) * LANE]], axis=1
        )
        for b in range(total)
    ]
    for b in range(0, total, 2):
        even[b * group : (b + 2) * group] = jnp.concatenate(held[b : b + 2], axis=0).astype(BF16)
    for b in range(1, total - 1, 2):
        odd[(b - 1) * group : (b + 1) * group] = jnp.concatenate(held[b : b + 2], axis=0).astype(BF16)
    window = blocks * group
    pieces = []
    for lag in range(extra + 1):
        source, at = (even, lag) if lag % 2 == 0 else (odd, lag - 1)
        pieces.append(source[at * group : at * group + window])
    return jnp.dot(jnp.concatenate(pieces, axis=1), table[...], preferred_element_type=F32)


def as_chunk(done, s, chunk, group, each):
    real, imag = [
        jnp.concatenate(
            [
                done[(s * chunk + b) * group : (s * chunk + b + 1) * group, c * LANE : (c + 1) * LANE]
                for b in range(chunk)
            ],
            axis=1,
        )
        for c in range(2)
    ]
    middle = chunk * LANE // 2
    lead, moved = pack_rows_of(real, imag, each)
    row = lax.broadcasted_iota(jnp.int32, (group, middle), 0)
    rest = jnp.where(
        row < group // 2,
        pltpu.roll(imag[:, :middle], group - moved, 0),
        pltpu.roll(imag[:, middle:], group // 2 - moved, 0),
    )
    return jnp.concatenate([lead[:, :middle], lead[:, middle:], rest], axis=0).astype(BF16)


def begin_kernel(echo_ref, chirp_ref, early_ref, late_ref, table, rows, even, odd, *, group):
    pulses, _, length = echo_ref.shape
    extra = chirp_ref.shape[1] // LANE
    reverse = LANE - 1 - lax.broadcasted_iota(jnp.int32, (2, LANE), 1)
    below = lax.broadcasted_iota(jnp.int32, (LANE, LANE), 1) <= lax.broadcasted_iota(
        jnp.int32, (LANE, LANE), 0
    )
    before = [jnp.zeros((LANE, LANE), BF16)] * 2
    for lag in range(extra + 1):
        if lag < extra:
            piece = chirp_ref[:, lag * LANE : (lag + 1) * LANE].astype(F32)
            piece = jnp.take_along_axis(piece, reverse, axis=1, mode="promise_in_bounds")
            turned = []
            for c in range(2):
                few = jnp.broadcast_to(piece[c : c + 1], (2 * SUBL, LANE))
                few = pltpu.roll(few, 1, 1, stride=1, stride_axis=0).astype(BF16)
                groups = [few] + [pltpu.roll(few, at, 1) for at in range(2 * SUBL, LANE, 2 * SUBL)]
                turned.append(jnp.concatenate(groups, axis=0))
        else:
            turned = [jnp.zeros((LANE, LANE), BF16)] * 2
        real, imag = [jnp.where(below, turned[c], before[c]) for c in range(2)]
        before = turned
        at = lag * 2 * LANE
        table[at : at + LANE, :LANE] = real
        table[at : at + LANE, LANE:] = -imag
        table[at + LANE : at + 2 * LANE, :LANE] = imag
        table[at + LANE : at + 2 * LANE, LANE:] = real
    rows[...] = jnp.zeros_like(rows)
    for p in range(pulses):
        near = echo_ref[p].astype(F32)
        for c in range(2):
            rows[c * group + p : c * group + p + 1, :] = near[c : c + 1]
    late_ref[...] = rows[:, length - late_ref.shape[1] :]
    done = correlate(rows, even, odd, table, length // LANE - extra, group)
    for s in range(early_ref.shape[0]):
        early_ref[s] = as_chunk(done, s, 2 * early_ref.shape[2] // LANE, group, pulses)


def finish_kernel(index_ref, early_ref, late_ref, halo_ref, table, keep_ref, give_ref, rows, even, odd, *, group):
    pulses = halo_ref.shape[0]
    span = late_ref.shape[1]
    taps = rows.shape[1] - span
    ready = early_ref.shape[0]
    chunk = 2 * early_ref.shape[2]
    sections = ready + span // chunk
    section = lax.rem(index_ref[0], sections)
    has_next = index_ref[0] >= sections
    rows[:, :span] = late_ref[...]
    rows[:, span:] = jnp.zeros((2 * group, taps), F32)
    for p in range(pulses):
        far = jnp.where(has_next, halo_ref[p, :, :taps].astype(F32), 0.0)
        for c in range(2):
            rows[c * group + p : c * group + p + 1, span:] = far[c : c + 1]
    done = correlate(rows, even, odd, table, span // LANE, group)
    for s in range(sections):
        stacked = early_ref[s] if s < ready else as_chunk(done, s - ready, chunk // LANE, group, pulses)
        slot = section ^ s
        other_core = slot % 2
        place = 1 - slot // 2

        @pl.when(other_core == 0)
        def _():
            keep_ref[place] = stacked

        @pl.when(other_core == 1)
        def _():
            give_ref[place] = stacked


def row_scratch(blocks, group):
    return [
        pltpu.VMEM((2 * group, blocks * LANE), F32),
        pltpu.VMEM((blocks * group, 2 * LANE), BF16),
        pltpu.VMEM((blocks * group, 2 * LANE), BF16),
    ]


def begin_compression(echo, chirp, sections, group):
    _, _, length = echo.shape
    taps = chirp.shape[1]
    chunk = length // sections
    early = (length - taps) // chunk
    return pl.pallas_call(
        functools.partial(begin_kernel, group=group),
        out_shape=(
            jax.ShapeDtypeStruct((early, 3 * group, chunk // 2), BF16),
            jax.ShapeDtypeStruct((2 * group, length - early * chunk), F32),
            jax.ShapeDtypeStruct(((taps // LANE + 1) * 2 * LANE, 2 * LANE), BF16),
        ),
        scratch_shapes=row_scratch(length // LANE, group),
        compiler_params=pltpu.CompilerParams(vmem_limit_bytes=24 * 1024 * 1024),
        name="begin_compression",
    )(echo, chirp)


def finish_compression(place, early, late, halo, table, group):
    blocks = late.shape[1] // LANE + table.shape[0] // (2 * LANE) - 1
    return pl.pallas_call(
        functools.partial(finish_kernel, group=group),
        out_shape=[jax.ShapeDtypeStruct((2, *early.shape[1:]), BF16)] * 2,
        in_specs=[pl.BlockSpec(memory_space=pltpu.SMEM)] + [pl.BlockSpec(memory_space=pltpu.VMEM)] * 4,
        scratch_shapes=row_scratch(blocks, group),
        compiler_params=pltpu.CompilerParams(vmem_limit_bytes=24 * 1024 * 1024),
        name="finish_compression",
    )(place, early, late, halo, table)


def image_kernel(operator_ref, both_ref, *refs, group):
    chunks, (out_ref, parts, sems) = refs[:-3], refs[-3:]
    count, _, tile = parts.shape
    width = both_ref.shape[2]
    held = [both_ref[1]] + [chunk[...] for chunk in chunks]
    held = [value.astype(F32) for value in held]
    copies = []
    for i in range(count):
        half, at = divmod(i * tile, width)
        rows = []
        for value in held:
            for first in range(0, value.shape[0], 3 * group):
                rows.append(value[first + half * group : first + (half + 1) * group, at : at + tile])
                rows.append(value[first + 2 * group : first + 3 * group, at : at + tile])
        pulses = jnp.concatenate(rows, axis=0).astype(BF16)
        result = jnp.dot(
            operator_ref[half], jnp.concatenate([pulses, pulses], axis=0), preferred_element_type=F32
        )
        parts[i] = result.astype(BF16)
        copy = pltpu.make_async_copy(parts.at[i], out_ref.at[:, i * tile : (i + 1) * tile], sems.at[i])
        copy.start()
        copies.append(copy)
    for copy in copies:
        copy.wait()


def form_image(operator, both, chunks, group):
    height, half = operator.shape[1], both.shape[2]
    tile = 256 if half % 256 == 0 else half
    count = 2 * half // tile
    return pl.pallas_call(
        functools.partial(image_kernel, group=group),
        out_shape=jax.ShapeDtypeStruct((height, 2 * half), BF16),
        in_specs=[pl.BlockSpec(memory_space=pltpu.VMEM)] * (2 + len(chunks)),
        out_specs=pl.BlockSpec(memory_space=pl.ANY),
        scratch_shapes=[
            pltpu.VMEM((count, height, tile), BF16),
            pltpu.SemaphoreType.DMA((count,)),
        ],
        compiler_params=pltpu.CompilerParams(vmem_limit_bytes=16 * 1024 * 1024),
        name="form_image",
    )(operator, both, *chunks)


def swap(value, axis, by):
    count = lax.axis_size(axis)
    return lax.ppermute(value, axis, [(i, i ^ by) for i in range(count)])


def swap_by(value, move):
    sections, subs = lax.axis_size("section"), lax.axis_size("sub")
    pairs = []
    for s in range(sections):
        for a in range(subs):
            to_s, to_a = move(s, a)
            pairs.append((s * subs + a, to_s * subs + to_a))
    return lax.ppermute(value, ("section", "sub"), pairs)


def from_next(value, axis):
    count = lax.axis_size(axis)
    return lax.ppermute(value, axis, [(i, (i - 1) % count) for i in range(count)])


def on_device(echoes, chirp, steer, pulse_order, band_coef, band_start, band_width):
    sections, subs = lax.axis_size("section"), lax.axis_size("sub")
    pulses_each = echoes.shape[2]
    group = ceil_to(pulses_each, SUBL)
    section = lax.axis_index("section").astype(jnp.int32).reshape(1)
    coef = jnp.swapaxes(band_coef, 4, 5)
    weights = jnp.swapaxes(steer, 2, 3)
    levels, _, sides, parts, taps, beams = coef.shape
    dims = (levels, sides, parts, taps, beams)

    echo = jnp.transpose(echoes[:, 0], (1, 0, 2))
    halo = from_next(echo, "rng")
    echo, chirp, packed = prepare(
        echo, chirp, coef, band_start, band_width, weights, pulse_order, sections, group
    )
    has_next = (lax.axis_index("rng") < lax.axis_size("rng") - 1).astype(jnp.int32)
    early, late, table = begin_compression(echo, chirp, sections, group)
    place = section + sections * has_next
    keep, give = finish_compression(place, early, late, halo, table, group)
    height = keep.shape[1]
    both = jnp.zeros((2, 2 * height, keep.shape[2]), BF16)
    both = lax.dynamic_update_slice(both, keep, (0, 0, 0))
    given = swap(give, "section", 1)
    both, packed = lax.optimization_barrier((both, packed))
    packed_partner = swap(packed, "sub", 1) if subs == 2 else packed
    both = lax.dynamic_update_slice(both, given, (0, height, 0))
    if subs != 2:
        chunks = [both[1], swap(both[0], "section", 2)]
        return merge_images(section, chunks, packed, dims, sections, group, pulses_each)
    chunks = [
        swap_by(both[0], lambda s, a: (s ^ 2, a)),
        swap_by(both[0], lambda s, a: (s ^ 2, a ^ 1)),
        swap_by(both[1], lambda s, a: (s, a ^ 1)),
    ]
    operator = fold_operator(section, packed, packed_partner, dims, sections, group, pulses_each)
    image = form_image(operator, both, chunks, group)
    return image.reshape(2, beams, 1, image.shape[1])


def unpack(chunk, group, each):
    lead = jnp.concatenate([chunk[:group], chunk[group : 2 * group]], axis=1)
    moved, rest = group - each, chunk[2 * group :]
    tail = jnp.concatenate([rest[: each - moved], rest[group // 2 : group // 2 + each - moved]], axis=1)
    return jnp.concatenate([lead, tail], axis=0)


def merge_images(section, chunks, packed, dims, sections, group, each):
    levels, sides, parts, taps, beams = dims
    width = sections * group
    first = levels * sides * parts * taps
    table = packed[first : first + parts * width].reshape(parts, sections, group, beams)
    table = jnp.take(table, section[0] ^ jnp.arange(sections), axis=1)[:, :, :each]
    chunks = [
        unpack(chunk[first : first + 3 * group], group, each)
        for chunk in chunks
        for first in range(0, chunk.shape[0], 3 * group)
    ]
    real, imag = table[0], table[1]
    rows = jnp.concatenate(
        [jnp.concatenate([real, -imag], axis=1), jnp.concatenate([imag, real], axis=1)], axis=2
    )
    image = lax.dot_general(
        rows.reshape(-1, 2 * beams), jnp.concatenate(chunks, axis=0), (((0,), (0,)), ((), ())), preferred_element_type=F32
    ).astype(BF16)
    starts = packed[first + parts * width :].astype(jnp.int32)
    column = jnp.arange(beams, dtype=jnp.int32)
    bits = lax.axis_size("sub").bit_length() - 1
    for level in range(levels):
        partner = swap(image, "sub", 1 << (level % bits))
        operands = []
        for side in range(sides):
            at = (level * sides + side) * parts * taps
            coef = packed[at : at + parts * taps].reshape(parts, taps, beams)
            offset = column[:, None] - starts[level * sides + side][None, :]
            hits = (offset[None] == jnp.arange(taps, dtype=jnp.int32)[:, None, None]).astype(BF16)
            operands.append(jnp.einsum("ptq,tcq->pqc", coef, hits, preferred_element_type=F32).astype(BF16))
        top = jnp.concatenate([operands[0][0], -operands[0][1], operands[1][0], -operands[1][1]], axis=1)
        low = jnp.concatenate([operands[0][1], operands[0][0], operands[1][1], operands[1][0]], axis=1)
        image = jnp.dot(
            jnp.concatenate([top, low], axis=0),
            jnp.concatenate([image, partner], axis=0),
            preferred_element_type=F32,
        ).astype(BF16)
    return image.reshape(2, beams, 1, image.shape[1])


def solution(mesh):
    return jax.shard_map(
        on_device,
        mesh=mesh,
        in_specs=(
            P(None, "sub", "section", "rng"),
            P(),
            P(None, "sub", None, None),
            P("sub", None),
            P(None, "sub", None, None, None, None),
            P(None, "sub", None, None),
            P(None, "sub", None, None),
        ),
        out_specs=P(None, "sub", "rng", "section"),
        check_vma=False,
    )
```

```python
import functools

import jax
import jax.numpy as jnp
from jax import lax
from jax.experimental import pallas as pl
from jax.experimental.pallas import tpu as pltpu
from jax.sharding import PartitionSpec as P

LANE = 128
SUBL = 8
F32 = jnp.float32
BF16 = jnp.bfloat16


def ceil_to(value, unit):
    return -(-value // unit) * unit


def prepare_kernel(*refs, sections, group):
    sources, (echo_out, chirp_out, pack_ref), scratch = refs[:7], refs[7:10], refs[10:]
    coef_ref, start_ref, width_ref, steer_ref, order_ref, starts, sems = scratch
    targets = (echo_out, coef_ref, start_ref, width_ref, steer_ref, order_ref, chirp_out)
    loads = [
        pltpu.make_async_copy(source, target, sems.at[i])
        for i, (source, target) in enumerate(zip(sources, targets))
    ]
    for load in loads:
        load.start()
    for load in loads:
        load.wait()
    levels, _, sides, parts, taps, beams = coef_ref.shape
    tap = lax.broadcasted_iota(jnp.int32, (taps, beams), 0)
    row = 0
    for level in range(levels):
        for side in range(sides):
            used = tap < width_ref[level, 0, side : side + 1, :]
            for part in range(parts):
                entries = coef_ref[level, 0, side, part].astype(F32)
                pack_ref[row : row + taps] = jnp.where(used, entries, 0.0).astype(BF16)
                row += taps
    pulses = order_ref.shape[1]
    each = pulses // sections
    position = lax.broadcasted_iota(jnp.int32, (pulses, pulses), 0)
    hit = (position == order_ref[0:1, :]).astype(F32)
    slot = lax.broadcasted_iota(jnp.int32, (sections * group, pulses), 0)
    pulse = lax.broadcasted_iota(jnp.int32, (sections * group, pulses), 1)
    place = jnp.zeros((sections * group, pulses), F32)
    for s in range(sections):
        inside = (pulse >= s * each) & (pulse < (s + 1) * each)
        place = jnp.where(inside & (slot - s * group == pulse - s * each), 1.0, place)
    pick = lax.dot_general(
        place.astype(BF16), hit.astype(BF16), (((1,), (1,)), ((), ())), preferred_element_type=F32
    )
    for part in range(parts):
        chosen = jnp.dot(pick.astype(BF16), steer_ref[part, 0], preferred_element_type=F32)
        pack_ref[row : row + sections * group] = chosen.astype(BF16)
        row += sections * group
    starts[...] = jnp.zeros_like(starts)
    for level in range(levels):
        starts[sides * level : sides * level + sides] = start_ref[level, 0].astype(F32)
    pack_ref[row : row + starts.shape[0]] = starts[...].astype(BF16)
    row += starts.shape[0]
    pack_ref[row:] = jnp.zeros((pack_ref.shape[0] - row, pack_ref.shape[1]), BF16)


def pack_rows(levels, sides, parts, taps, sections, group):
    rows = levels * sides * parts * taps + parts * sections * group + ceil_to(levels * sides, 16)
    return ceil_to(rows, 32)


def prepare(echo, chirp, coef, start, width, steer, order, sections, group):
    levels, _, sides, parts, taps, beams = coef.shape
    sources = (echo, coef, start, width, steer, order, chirp)
    return pl.pallas_call(
        functools.partial(prepare_kernel, sections=sections, group=group),
        out_shape=(
            jax.ShapeDtypeStruct(echo.shape, BF16),
            jax.ShapeDtypeStruct(chirp.shape, BF16),
            jax.ShapeDtypeStruct((pack_rows(levels, sides, parts, taps, sections, group), beams), BF16),
        ),
        in_specs=[pl.BlockSpec(memory_space=pl.ANY)] * len(sources),
        scratch_shapes=[pltpu.VMEM(x.shape, x.dtype) for x in sources[1:6]]
        + [pltpu.VMEM((ceil_to(levels * sides, 16), beams), F32), pltpu.SemaphoreType.DMA((len(sources),))],
        compiler_params=pltpu.CompilerParams(vmem_limit_bytes=16 * 1024 * 1024),
        name="prepare",
    )(*[pltpu.with_memory_space_constraint(x, pltpu.HBM) for x in sources])


def pack_rows_of(real, imag, each):
    group = real.shape[0]
    row = lax.broadcasted_iota(jnp.int32, real.shape, 0)
    return jnp.where(row < each, real, pltpu.roll(imag, each, 0)), group - each


def split_two(value):
    high = value.astype(BF16)
    return high, (value - high.astype(F32)).astype(BF16)


def operator_kernel(index_ref, own_ref, partner_ref, out_ref, weights, *, dims, sections, group, each):
    levels, sides, parts, taps, beams = dims
    width = sections * group
    refs = (own_ref, partner_ref)
    weight_row = levels * sides * parts * taps
    start_row = weight_row + parts * width

    def band(ref, level, side):
        first = ((level * sides + side) * parts) * taps
        tables = [ref[first + p * taps : first + (p + 1) * taps].astype(F32) for p in range(parts)]
        start = ref[start_row : start_row + ceil_to(levels * sides, 16)].astype(F32)
        start = start[level * sides + side : level * sides + side + 1].astype(jnp.int32)
        found = [[], []]
        for c in range(0, beams, SUBL):
            column = lax.broadcasted_iota(jnp.int32, (SUBL, beams), 0) + c
            offset = column - start
            spot = offset & (SUBL - 1)
            for p in range(parts):
                value = jnp.zeros((SUBL, beams), F32)
                for t in range(0, taps, SUBL):
                    got = jnp.take_along_axis(
                        tables[p][t : t + SUBL], spot, axis=0, mode="promise_in_bounds"
                    )
                    value = jnp.where((offset >= t) & (offset < t + SUBL), got, value)
                found[p].append(value)
        return [jnp.concatenate(f, axis=0) for f in found]

    def complex_operand(real, imag):
        top = jnp.concatenate([real, imag], axis=1)
        low = jnp.concatenate([-imag, real], axis=1)
        return jnp.concatenate([top, low], axis=0).astype(BF16)

    section = index_ref[0]
    images = []
    for a in range(2):
        for p in range(parts):
            weights[...] = refs[a][weight_row + p * width : weight_row + (p + 1) * width].astype(F32)
            rows = []
            for j in range(sections):
                at = pl.multiple_of((section ^ j) * group, group)
                rows.append(weights[pl.ds(at, group)])
            images.append(jnp.concatenate(rows, axis=0))
    zero = jnp.zeros((width, 2 * beams), F32)
    own = jnp.concatenate([jnp.concatenate(images[0:2], axis=1), zero], axis=0)
    partner = jnp.concatenate([zero, jnp.concatenate(images[2:4], axis=1)], axis=0)
    for level in range(levels):
        own_high, own_low = split_two(own)
        partner_high, partner_low = split_two(partner)
        own_rows = jnp.concatenate([own_high, own_low], axis=0)
        partner_rows = jnp.concatenate([partner_high, partner_low], axis=0)

        def merged(ref, mine, other):
            product = jnp.dot(
                mine, complex_operand(*band(ref, level, 0)), preferred_element_type=F32
            ) + jnp.dot(other, complex_operand(*band(ref, level, 1)), preferred_element_type=F32)
            return product[: 2 * width] + product[2 * width :]

        following = merged(own_ref, own_rows, partner_rows)
        if level < levels - 1:
            partner = merged(partner_ref, partner_rows, own_rows)
        own = following
    full, left, right = [], [], []
    for j in range(2 * sections):
        real = own[j * group : (j + 1) * group, :beams]
        imag = own[j * group : (j + 1) * group, beams:]
        straight = jnp.concatenate([real, imag], axis=1)
        turned = jnp.concatenate([-imag, real], axis=1)
        lead, moved = pack_rows_of(straight, turned, each)
        row = lax.broadcasted_iota(jnp.int32, lead.shape, 0)
        full.append(lead)
        left.append(jnp.where(row < group // 2, pltpu.roll(turned, group - moved, 0), 0.0))
        right.append(jnp.where(row >= group // 2, pltpu.roll(turned, group // 2 - moved, 0), 0.0))
    pairs = sections // 2
    first_core = section % 2 == 0
    for half, rest in enumerate((left, right)):
        sources = [jnp.concatenate([full[j], rest[j]], axis=0) for j in range(2 * sections)]
        quarters = [jnp.concatenate(sources[q * pairs : (q + 1) * pairs], axis=0) for q in range(4)]
        quarters = [
            quarters[0],
            quarters[3],
            jnp.where(first_core, quarters[1], quarters[2]),
            jnp.where(first_core, quarters[2], quarters[1]),
        ]
        high, low = split_two(jnp.concatenate(quarters, axis=0).T)
        out_ref[half] = jnp.concatenate([high, low], axis=1)


def fold_operator(section, own, partner, dims, sections, group, each):
    beams = dims[-1]
    width = sections * group
    return pl.pallas_call(
        functools.partial(operator_kernel, dims=dims, sections=sections, group=group, each=each),
        out_shape=jax.ShapeDtypeStruct((2, 2 * beams, 8 * width), BF16),
        in_specs=[
            pl.BlockSpec(memory_space=pltpu.SMEM),
            pl.BlockSpec(memory_space=pltpu.VMEM),
            pl.BlockSpec(memory_space=pltpu.VMEM),
        ],
        scratch_shapes=[pltpu.VMEM((width, beams), F32)],
        compiler_params=pltpu.CompilerParams(vmem_limit_bytes=16 * 1024 * 1024),
        name="fold_operator",
    )(section, own, partner)


def correlate(rows, even, odd, table, blocks, group):
    extra = table.shape[0] // (2 * LANE) - 1
    total = blocks + extra
    held = [
        jnp.concatenate(
            [rows[:group, b * LANE : (b + 1) * LANE], rows[group:, b * LANE : (b + 1) * LANE]], axis=1
        )
        for b in range(total)
    ]
    for b in range(0, total, 2):
        even[b * group : (b + 2) * group] = jnp.concatenate(held[b : b + 2], axis=0).astype(BF16)
    for b in range(1, total - 1, 2):
        odd[(b - 1) * group : (b + 1) * group] = jnp.concatenate(held[b : b + 2], axis=0).astype(BF16)
    window = blocks * group
    pieces = []
    for lag in range(extra + 1):
        source, at = (even, lag) if lag % 2 == 0 else (odd, lag - 1)
        pieces.append(source[at * group : at * group + window])
    return jnp.dot(jnp.concatenate(pieces, axis=1), table[...], preferred_element_type=F32)


def as_chunk(done, s, chunk, group, each):
    real, imag = [
        jnp.concatenate(
            [
                done[(s * chunk + b) * group : (s * chunk + b + 1) * group, c * LANE : (c + 1) * LANE]
                for b in range(chunk)
            ],
            axis=1,
        )
        for c in range(2)
    ]
    middle = chunk * LANE // 2
    lead, moved = pack_rows_of(real, imag, each)
    row = lax.broadcasted_iota(jnp.int32, (group, middle), 0)
    rest = jnp.where(
        row < group // 2,
        pltpu.roll(imag[:, :middle], group - moved, 0),
        pltpu.roll(imag[:, middle:], group // 2 - moved, 0),
    )
    return jnp.concatenate([lead[:, :middle], lead[:, middle:], rest], axis=0).astype(BF16)


def begin_kernel(echo_ref, chirp_ref, early_ref, late_ref, table, rows, even, odd, *, group):
    pulses, _, length = echo_ref.shape
    extra = chirp_ref.shape[1] // LANE
    reverse = LANE - 1 - lax.broadcasted_iota(jnp.int32, (2, LANE), 1)
    below = lax.broadcasted_iota(jnp.int32, (LANE, LANE), 1) <= lax.broadcasted_iota(
        jnp.int32, (LANE, LANE), 0
    )
    before = [jnp.zeros((LANE, LANE), BF16)] * 2
    for lag in range(extra + 1):
        if lag < extra:
            piece = chirp_ref[:, lag * LANE : (lag + 1) * LANE].astype(F32)
            piece = jnp.take_along_axis(piece, reverse, axis=1, mode="promise_in_bounds")
            turned = []
            for c in range(2):
                few = jnp.broadcast_to(piece[c : c + 1], (2 * SUBL, LANE))
                few = pltpu.roll(few, 1, 1, stride=1, stride_axis=0).astype(BF16)
                groups = [few] + [pltpu.roll(few, at, 1) for at in range(2 * SUBL, LANE, 2 * SUBL)]
                turned.append(jnp.concatenate(groups, axis=0))
        else:
            turned = [jnp.zeros((LANE, LANE), BF16)] * 2
        real, imag = [jnp.where(below, turned[c], before[c]) for c in range(2)]
        before = turned
        at = lag * 2 * LANE
        table[at : at + LANE, :LANE] = real
        table[at : at + LANE, LANE:] = -imag
        table[at + LANE : at + 2 * LANE, :LANE] = imag
        table[at + LANE : at + 2 * LANE, LANE:] = real
    rows[...] = jnp.zeros_like(rows)
    for p in range(pulses):
        near = echo_ref[p].astype(F32)
        for c in range(2):
            rows[c * group + p : c * group + p + 1, :] = near[c : c + 1]
    late_ref[...] = rows[:, length - late_ref.shape[1] :]
    done = correlate(rows, even, odd, table, length // LANE - extra, group)
    for s in range(early_ref.shape[0]):
        early_ref[s] = as_chunk(done, s, 2 * early_ref.shape[2] // LANE, group, pulses)


def finish_kernel(index_ref, early_ref, late_ref, halo_ref, table, keep_ref, give_ref, rows, even, odd, *, group):
    pulses = halo_ref.shape[0]
    span = late_ref.shape[1]
    taps = rows.shape[1] - span
    ready = early_ref.shape[0]
    chunk = 2 * early_ref.shape[2]
    sections = ready + span // chunk
    section = lax.rem(index_ref[0], sections)
    has_next = index_ref[0] >= sections
    rows[:, :span] = late_ref[...]
    rows[:, span:] = jnp.zeros((2 * group, taps), F32)
    for p in range(pulses):
        far = jnp.where(has_next, halo_ref[p, :, :taps].astype(F32), 0.0)
        for c in range(2):
            rows[c * group + p : c * group + p + 1, span:] = far[c : c + 1]
    done = correlate(rows, even, odd, table, span // LANE, group)
    for s in range(sections):
        stacked = early_ref[s] if s < ready else as_chunk(done, s - ready, chunk // LANE, group, pulses)
        slot = section ^ s
        far_chunk, other_core = slot // 2, slot % 2
        place = far_chunk ^ 1 ^ (section % 2) ^ other_core

        @pl.when(other_core == 0)
        def _():
            keep_ref[place] = stacked

        @pl.when(other_core == 1)
        def _():
            give_ref[place] = stacked


def row_scratch(blocks, group):
    return [
        pltpu.VMEM((2 * group, blocks * LANE), F32),
        pltpu.VMEM((blocks * group, 2 * LANE), BF16),
        pltpu.VMEM((blocks * group, 2 * LANE), BF16),
    ]


def begin_compression(echo, chirp, sections, group):
    _, _, length = echo.shape
    taps = chirp.shape[1]
    chunk = length // sections
    early = (length - taps) // chunk
    return pl.pallas_call(
        functools.partial(begin_kernel, group=group),
        out_shape=(
            jax.ShapeDtypeStruct((early, 3 * group, chunk // 2), BF16),
            jax.ShapeDtypeStruct((2 * group, length - early * chunk), F32),
            jax.ShapeDtypeStruct(((taps // LANE + 1) * 2 * LANE, 2 * LANE), BF16),
        ),
        scratch_shapes=row_scratch(length // LANE, group),
        compiler_params=pltpu.CompilerParams(vmem_limit_bytes=24 * 1024 * 1024),
        name="begin_compression",
    )(echo, chirp)


def finish_compression(place, early, late, halo, table, group):
    blocks = late.shape[1] // LANE + table.shape[0] // (2 * LANE) - 1
    return pl.pallas_call(
        functools.partial(finish_kernel, group=group),
        out_shape=[jax.ShapeDtypeStruct((2, *early.shape[1:]), BF16)] * 2,
        in_specs=[pl.BlockSpec(memory_space=pltpu.SMEM)] + [pl.BlockSpec(memory_space=pltpu.VMEM)] * 4,
        scratch_shapes=row_scratch(blocks, group),
        compiler_params=pltpu.CompilerParams(vmem_limit_bytes=24 * 1024 * 1024),
        name="finish_compression",
    )(place, early, late, halo, table)


def image_kernel(index_ref, operator_ref, both_ref, *refs, group):
    chunks, (out_ref, parts, sems) = refs[:-3], refs[-3:]
    count, _, tile = parts.shape
    width = both_ref.shape[2]
    near = 1 - index_ref[0] % 2
    held = [both_ref[near]] + [chunk[...] for chunk in chunks]
    held = [value.astype(F32) for value in held]
    copies = []
    for i in range(count):
        half, at = divmod(i * tile, width)
        rows = []
        for value in held:
            for first in range(0, value.shape[0], 3 * group):
                rows.append(value[first + half * group : first + (half + 1) * group, at : at + tile])
                rows.append(value[first + 2 * group : first + 3 * group, at : at + tile])
        pulses = jnp.concatenate(rows, axis=0).astype(BF16)
        result = jnp.dot(
            operator_ref[half], jnp.concatenate([pulses, pulses], axis=0), preferred_element_type=F32
        )
        parts[i] = result.astype(BF16)
        copy = pltpu.make_async_copy(parts.at[i], out_ref.at[:, i * tile : (i + 1) * tile], sems.at[i])
        copy.start()
        copies.append(copy)
    for copy in copies:
        copy.wait()


def form_image(section, operator, both, chunks, group):
    height, half = operator.shape[1], both.shape[2]
    tile = 256 if half % 256 == 0 else half
    count = 2 * half // tile
    return pl.pallas_call(
        functools.partial(image_kernel, group=group),
        out_shape=jax.ShapeDtypeStruct((height, 2 * half), BF16),
        in_specs=[pl.BlockSpec(memory_space=pltpu.SMEM)]
        + [pl.BlockSpec(memory_space=pltpu.VMEM)] * (2 + len(chunks)),
        out_specs=pl.BlockSpec(memory_space=pl.ANY),
        scratch_shapes=[
            pltpu.VMEM((count, height, tile), BF16),
            pltpu.SemaphoreType.DMA((count,)),
        ],
        compiler_params=pltpu.CompilerParams(vmem_limit_bytes=16 * 1024 * 1024),
        name="form_image",
    )(section, operator, both, *chunks)


def swap(value, axis, by):
    count = lax.axis_size(axis)
    return lax.ppermute(value, axis, [(i, i ^ by) for i in range(count)])


def partner_parameters(packed, core):
    half = packed.shape[0] // 2
    mine = swap(lax.dynamic_slice_in_dim(packed, core * half, half, 0), "sub", 1)
    other = swap(mine, "section", 1)
    first, second = jnp.where(core == 0, mine, other), jnp.where(core == 0, other, mine)
    return jnp.concatenate([first, second], axis=0)


def swap_by(value, move):
    sections, subs = lax.axis_size("section"), lax.axis_size("sub")
    pairs = []
    for s in range(sections):
        for a in range(subs):
            to_s, to_a = move(s, a)
            pairs.append((s * subs + a, to_s * subs + to_a))
    return lax.ppermute(value, ("section", "sub"), pairs)


def from_next(value, axis):
    count = lax.axis_size(axis)
    return lax.ppermute(value, axis, [(i, (i - 1) % count) for i in range(count)])


def on_device(echoes, chirp, steer, pulse_order, band_coef, band_start, band_width):
    sections, subs = lax.axis_size("section"), lax.axis_size("sub")
    pulses_each = echoes.shape[2]
    group = ceil_to(pulses_each, SUBL)
    section = lax.axis_index("section").astype(jnp.int32).reshape(1)
    coef = jnp.swapaxes(band_coef, 4, 5)
    weights = jnp.swapaxes(steer, 2, 3)
    levels, _, sides, parts, taps, beams = coef.shape
    dims = (levels, sides, parts, taps, beams)

    echo = jnp.transpose(echoes[:, 0], (1, 0, 2))
    halo = from_next(echo, "rng")
    echo, chirp, packed = prepare(
        echo, chirp, coef, band_start, band_width, weights, pulse_order, sections, group
    )
    has_next = (lax.axis_index("rng") < lax.axis_size("rng") - 1).astype(jnp.int32)
    early, late, table = begin_compression(echo, chirp, sections, group)
    place = section + sections * has_next
    keep, give = finish_compression(place, early, late, halo, table, group)
    height = keep.shape[1]
    both = jnp.zeros((2, 2 * height, keep.shape[2]), BF16)
    both = lax.dynamic_update_slice(both, keep, (0, 0, 0))
    given = swap(give, "section", 1)
    both, packed = lax.optimization_barrier((both, packed))
    packed_partner = partner_parameters(packed, section[0] % 2) if subs == 2 else packed
    both = lax.dynamic_update_slice(both, given, (0, height, 0))
    far = lax.dynamic_index_in_dim(both, section[0] % 2, 0, keepdims=False)
    if subs != 2:
        near = lax.dynamic_index_in_dim(both, 1 - section[0] % 2, 0, keepdims=False)
        chunks = [near, swap(far, "section", 2)]
        return merge_images(section, chunks, packed, dims, sections, group, pulses_each)
    chunks = [
        swap_by(far, lambda s, a: (s ^ 2, a ^ 1)),
        swap_by(both[0], lambda s, a: (s, a ^ 1) if s % 2 else (s ^ 2, a)),
        swap_by(both[1], lambda s, a: (s ^ 2, a) if s % 2 else (s, a ^ 1)),
    ]
    operator = fold_operator(section, packed, packed_partner, dims, sections, group, pulses_each)
    image = form_image(section, operator, both, chunks, group)
    return image.reshape(2, beams, 1, image.shape[1])


def unpack(chunk, group, each):
    lead = jnp.concatenate([chunk[:group], chunk[group : 2 * group]], axis=1)
    moved, rest = group - each, chunk[2 * group :]
    tail = jnp.concatenate([rest[: each - moved], rest[group // 2 : group // 2 + each - moved]], axis=1)
    return jnp.concatenate([lead, tail], axis=0)


def merge_images(section, chunks, packed, dims, sections, group, each):
    levels, sides, parts, taps, beams = dims
    width = sections * group
    first = levels * sides * parts * taps
    table = packed[first : first + parts * width].reshape(parts, sections, group, beams)
    table = jnp.take(table, section[0] ^ jnp.arange(sections), axis=1)[:, :, :each]
    chunks = [
        unpack(chunk[first : first + 3 * group], group, each)
        for chunk in chunks
        for first in range(0, chunk.shape[0], 3 * group)
    ]
    real, imag = table[0], table[1]
    rows = jnp.concatenate(
        [jnp.concatenate([real, -imag], axis=1), jnp.concatenate([imag, real], axis=1)], axis=2
    )
    image = lax.dot_general(
        rows.reshape(-1, 2 * beams), jnp.concatenate(chunks, axis=0), (((0,), (0,)), ((), ())), preferred_element_type=F32
    ).astype(BF16)
    starts = packed[first + parts * width :].astype(jnp.int32)
    column = jnp.arange(beams, dtype=jnp.int32)
    bits = lax.axis_size("sub").bit_length() - 1
    for level in range(levels):
        partner = swap(image, "sub", 1 << (level % bits))
        operands = []
        for side in range(sides):
            at = (level * sides + side) * parts * taps
            coef = packed[at : at + parts * taps].reshape(parts, taps, beams)
            offset = column[:, None] - starts[level * sides + side][None, :]
            hits = (offset[None] == jnp.arange(taps, dtype=jnp.int32)[:, None, None]).astype(BF16)
            operands.append(jnp.einsum("ptq,tcq->pqc", coef, hits, preferred_element_type=F32).astype(BF16))
        top = jnp.concatenate([operands[0][0], -operands[0][1], operands[1][0], -operands[1][1]], axis=1)
        low = jnp.concatenate([operands[0][1], operands[0][0], operands[1][1], operands[1][0]], axis=1)
        image = jnp.dot(
            jnp.concatenate([top, low], axis=0),
            jnp.concatenate([image, partner], axis=0),
            preferred_element_type=F32,
        ).astype(BF16)
    return image.reshape(2, beams, 1, image.shape[1])


def solution(mesh):
    return jax.shard_map(
        on_device,
        mesh=mesh,
        in_specs=(
            P(None, "sub", "section", "rng"),
            P(),
            P(None, "sub", None, None),
            P("sub", None),
            P(None, "sub", None, None, None, None),
            P(None, "sub", None, None),
            P(None, "sub", None, None),
        ),
        out_specs=P(None, "sub", "rng", "section"),
        check_vma=False,
    )
```

```python
import functools

import jax
import jax.numpy as jnp
from jax import lax
from jax.experimental import pallas as pl
from jax.experimental.pallas import tpu as pltpu
from jax.sharding import PartitionSpec as P

LANE = 128
SUBL = 8
F32 = jnp.float32
BF16 = jnp.bfloat16


def ceil_to(value, unit):
    return -(-value // unit) * unit


def prepare_kernel(*refs, sections, group):
    sources, (echo_out, chirp_out, pack_ref), scratch = refs[:7], refs[7:10], refs[10:]
    coef_ref, start_ref, width_ref, steer_ref, order_ref, starts, sems = scratch
    targets = (echo_out, coef_ref, start_ref, width_ref, steer_ref, order_ref, chirp_out)
    loads = [
        pltpu.make_async_copy(source, target, sems.at[i])
        for i, (source, target) in enumerate(zip(sources, targets))
    ]
    for load in loads:
        load.start()
    for load in loads:
        load.wait()
    levels, _, sides, parts, taps, beams = coef_ref.shape
    tap = lax.broadcasted_iota(jnp.int32, (taps, beams), 0)
    row = 0
    for level in range(levels):
        for side in range(sides):
            used = tap < width_ref[level, 0, side : side + 1, :]
            for part in range(parts):
                entries = coef_ref[level, 0, side, part].astype(F32)
                pack_ref[row : row + taps] = jnp.where(used, entries, 0.0).astype(BF16)
                row += taps
    pulses = order_ref.shape[1]
    each = pulses // sections
    position = lax.broadcasted_iota(jnp.int32, (pulses, pulses), 0)
    hit = (position == order_ref[0:1, :]).astype(F32)
    slot = lax.broadcasted_iota(jnp.int32, (sections * group, pulses), 0)
    pulse = lax.broadcasted_iota(jnp.int32, (sections * group, pulses), 1)
    place = jnp.zeros((sections * group, pulses), F32)
    for s in range(sections):
        inside = (pulse >= s * each) & (pulse < (s + 1) * each)
        place = jnp.where(inside & (slot - s * group == pulse - s * each), 1.0, place)
    pick = lax.dot_general(
        place.astype(BF16), hit.astype(BF16), (((1,), (1,)), ((), ())), preferred_element_type=F32
    )
    for part in range(parts):
        chosen = jnp.dot(pick.astype(BF16), steer_ref[part, 0], preferred_element_type=F32)
        pack_ref[row : row + sections * group] = chosen.astype(BF16)
        row += sections * group
    starts[...] = jnp.zeros_like(starts)
    for level in range(levels):
        starts[sides * level : sides * level + sides] = start_ref[level, 0].astype(F32)
    pack_ref[row : row + starts.shape[0]] = starts[...].astype(BF16)


def pack_rows(levels, sides, parts, taps, sections, group):
    return levels * sides * parts * taps + parts * sections * group + ceil_to(levels * sides, 16)


def prepare(echo, chirp, coef, start, width, steer, order, sections, group):
    levels, _, sides, parts, taps, beams = coef.shape
    sources = (echo, coef, start, width, steer, order, chirp)
    return pl.pallas_call(
        functools.partial(prepare_kernel, sections=sections, group=group),
        out_shape=(
            jax.ShapeDtypeStruct(echo.shape, BF16),
            jax.ShapeDtypeStruct(chirp.shape, BF16),
            jax.ShapeDtypeStruct((pack_rows(levels, sides, parts, taps, sections, group), beams), BF16),
        ),
        in_specs=[pl.BlockSpec(memory_space=pl.ANY)] * len(sources),
        scratch_shapes=[pltpu.VMEM(x.shape, x.dtype) for x in sources[1:6]]
        + [pltpu.VMEM((ceil_to(levels * sides, 16), beams), F32), pltpu.SemaphoreType.DMA((len(sources),))],
        compiler_params=pltpu.CompilerParams(vmem_limit_bytes=16 * 1024 * 1024),
        name="prepare",
    )(*[pltpu.with_memory_space_constraint(x, pltpu.HBM) for x in sources])


def pack_rows_of(real, imag, each):
    group = real.shape[0]
    row = lax.broadcasted_iota(jnp.int32, real.shape, 0)
    return jnp.where(row < each, real, pltpu.roll(imag, each, 0)), group - each


def split_two(value):
    high = value.astype(BF16)
    return high, (value - high.astype(F32)).astype(BF16)


def operator_kernel(index_ref, own_ref, partner_ref, out_ref, weights, *, dims, sections, group, each):
    levels, sides, parts, taps, beams = dims
    width = sections * group
    refs = (own_ref, partner_ref)
    weight_row = levels * sides * parts * taps
    start_row = weight_row + parts * width

    def band(ref, level, side):
        first = ((level * sides + side) * parts) * taps
        tables = [ref[first + p * taps : first + (p + 1) * taps].astype(F32) for p in range(parts)]
        start = ref[start_row : start_row + ceil_to(levels * sides, 16)].astype(F32)
        start = start[level * sides + side : level * sides + side + 1].astype(jnp.int32)
        found = [[], []]
        for c in range(0, beams, SUBL):
            column = lax.broadcasted_iota(jnp.int32, (SUBL, beams), 0) + c
            offset = column - start
            spot = offset & (SUBL - 1)
            for p in range(parts):
                value = jnp.zeros((SUBL, beams), F32)
                for t in range(0, taps, SUBL):
                    got = jnp.take_along_axis(
                        tables[p][t : t + SUBL], spot, axis=0, mode="promise_in_bounds"
                    )
                    value = jnp.where((offset >= t) & (offset < t + SUBL), got, value)
                found[p].append(value)
        return [jnp.concatenate(f, axis=0) for f in found]

    def complex_operand(real, imag):
        top = jnp.concatenate([real, imag], axis=1)
        low = jnp.concatenate([-imag, real], axis=1)
        return jnp.concatenate([top, low], axis=0).astype(BF16)

    section = index_ref[0]
    images = []
    for a in range(2):
        for p in range(parts):
            weights[...] = refs[a][weight_row + p * width : weight_row + (p + 1) * width].astype(F32)
            rows = []
            for j in range(sections):
                at = pl.multiple_of((section ^ j) * group, group)
                rows.append(weights[pl.ds(at, group)])
            images.append(jnp.concatenate(rows, axis=0))
    zero = jnp.zeros((width, 2 * beams), F32)
    own = jnp.concatenate([jnp.concatenate(images[0:2], axis=1), zero], axis=0)
    partner = jnp.concatenate([zero, jnp.concatenate(images[2:4], axis=1)], axis=0)
    for level in range(levels):
        own_high, own_low = split_two(own)
        partner_high, partner_low = split_two(partner)
        own_rows = jnp.concatenate([own_high, own_low], axis=0)
        partner_rows = jnp.concatenate([partner_high, partner_low], axis=0)

        def merged(ref, mine, other):
            product = jnp.dot(
                mine, complex_operand(*band(ref, level, 0)), preferred_element_type=F32
            ) + jnp.dot(other, complex_operand(*band(ref, level, 1)), preferred_element_type=F32)
            return product[: 2 * width] + product[2 * width :]

        following = merged(own_ref, own_rows, partner_rows)
        if level < levels - 1:
            partner = merged(partner_ref, partner_rows, own_rows)
        own = following
    full, left, right = [], [], []
    for j in range(2 * sections):
        real = own[j * group : (j + 1) * group, :beams]
        imag = own[j * group : (j + 1) * group, beams:]
        straight = jnp.concatenate([real, imag], axis=1)
        turned = jnp.concatenate([-imag, real], axis=1)
        lead, moved = pack_rows_of(straight, turned, each)
        row = lax.broadcasted_iota(jnp.int32, lead.shape, 0)
        full.append(lead)
        left.append(jnp.where(row < group // 2, pltpu.roll(turned, group - moved, 0), 0.0))
        right.append(jnp.where(row >= group // 2, pltpu.roll(turned, group // 2 - moved, 0), 0.0))
    pairs = sections // 2
    for half, rest in enumerate((left, right)):
        sources = [jnp.concatenate([full[j], rest[j]], axis=0) for j in range(2 * sections)]
        quarters = [jnp.concatenate(sources[q * pairs : (q + 1) * pairs], axis=0) for q in range(4)]
        quarters = [
            quarters[0],
            quarters[3],
            quarters[1],
            quarters[2],
        ]
        high, low = split_two(jnp.concatenate(quarters, axis=0).T)
        out_ref[half] = jnp.concatenate([high, low], axis=1)


def fold_operator(section, own, partner, dims, sections, group, each):
    beams = dims[-1]
    width = sections * group
    return pl.pallas_call(
        functools.partial(operator_kernel, dims=dims, sections=sections, group=group, each=each),
        out_shape=jax.ShapeDtypeStruct((2, 2 * beams, 8 * width), BF16),
        in_specs=[
            pl.BlockSpec(memory_space=pltpu.SMEM),
            pl.BlockSpec(memory_space=pltpu.VMEM),
            pl.BlockSpec(memory_space=pltpu.VMEM),
        ],
        scratch_shapes=[pltpu.VMEM((width, beams), F32)],
        compiler_params=pltpu.CompilerParams(vmem_limit_bytes=16 * 1024 * 1024),
        name="fold_operator",
    )(section, own, partner)


def correlate(rows, even, odd, table, blocks, group):
    extra = table.shape[0] // (2 * LANE) - 1
    total = blocks + extra
    held = [
        jnp.concatenate(
            [rows[:group, b * LANE : (b + 1) * LANE], rows[group:, b * LANE : (b + 1) * LANE]], axis=1
        )
        for b in range(total)
    ]
    for b in range(0, total, 2):
        even[b * group : (b + 2) * group] = jnp.concatenate(held[b : b + 2], axis=0).astype(BF16)
    for b in range(1, total - 1, 2):
        odd[(b - 1) * group : (b + 1) * group] = jnp.concatenate(held[b : b + 2], axis=0).astype(BF16)
    window = blocks * group
    pieces = []
    for lag in range(extra + 1):
        source, at = (even, lag) if lag % 2 == 0 else (odd, lag - 1)
        pieces.append(source[at * group : at * group + window])
    return jnp.dot(jnp.concatenate(pieces, axis=1), table[...], preferred_element_type=F32)


def as_chunk(done, s, chunk, group, each):
    real, imag = [
        jnp.concatenate(
            [
                done[(s * chunk + b) * group : (s * chunk + b + 1) * group, c * LANE : (c + 1) * LANE]
                for b in range(chunk)
            ],
            axis=1,
        )
        for c in range(2)
    ]
    middle = chunk * LANE // 2
    lead, moved = pack_rows_of(real, imag, each)
    row = lax.broadcasted_iota(jnp.int32, (group, middle), 0)
    rest = jnp.where(
        row < group // 2,
        pltpu.roll(imag[:, :middle], group - moved, 0),
        pltpu.roll(imag[:, middle:], group // 2 - moved, 0),
    )
    return jnp.concatenate([lead[:, :middle], lead[:, middle:], rest], axis=0).astype(BF16)


def begin_kernel(echo_ref, chirp_ref, early_ref, late_ref, table, rows, even, odd, *, group):
    pulses, _, length = echo_ref.shape
    extra = chirp_ref.shape[1] // LANE
    reverse = LANE - 1 - lax.broadcasted_iota(jnp.int32, (2, LANE), 1)
    below = lax.broadcasted_iota(jnp.int32, (LANE, LANE), 1) <= lax.broadcasted_iota(
        jnp.int32, (LANE, LANE), 0
    )
    before = [jnp.zeros((LANE, LANE), BF16)] * 2
    for lag in range(extra + 1):
        if lag < extra:
            piece = chirp_ref[:, lag * LANE : (lag + 1) * LANE].astype(F32)
            piece = jnp.take_along_axis(piece, reverse, axis=1, mode="promise_in_bounds")
            turned = []
            for c in range(2):
                few = jnp.broadcast_to(piece[c : c + 1], (2 * SUBL, LANE))
                few = pltpu.roll(few, 1, 1, stride=1, stride_axis=0).astype(BF16)
                groups = [few] + [pltpu.roll(few, at, 1) for at in range(2 * SUBL, LANE, 2 * SUBL)]
                turned.append(jnp.concatenate(groups, axis=0))
        else:
            turned = [jnp.zeros((LANE, LANE), BF16)] * 2
        real, imag = [jnp.where(below, turned[c], before[c]) for c in range(2)]
        before = turned
        at = lag * 2 * LANE
        table[at : at + LANE, :LANE] = real
        table[at : at + LANE, LANE:] = -imag
        table[at + LANE : at + 2 * LANE, :LANE] = imag
        table[at + LANE : at + 2 * LANE, LANE:] = real
    rows[...] = jnp.zeros_like(rows)
    for p in range(pulses):
        near = echo_ref[p].astype(F32)
        for c in range(2):
            rows[c * group + p : c * group + p + 1, :] = near[c : c + 1]
    late_ref[...] = rows[:, length - late_ref.shape[1] :]
    done = correlate(rows, even, odd, table, length // LANE - extra, group)
    for s in range(early_ref.shape[0]):
        early_ref[s] = as_chunk(done, s, 2 * early_ref.shape[2] // LANE, group, pulses)


def finish_kernel(index_ref, early_ref, late_ref, halo_ref, table, keep_ref, give_ref, rows, even, odd, *, group):
    pulses = halo_ref.shape[0]
    span = late_ref.shape[1]
    taps = rows.shape[1] - span
    ready = early_ref.shape[0]
    chunk = 2 * early_ref.shape[2]
    sections = ready + span // chunk
    section = lax.rem(index_ref[0], sections)
    has_next = index_ref[0] >= sections
    rows[:, :span] = late_ref[...]
    rows[:, span:] = jnp.zeros((2 * group, taps), F32)
    for p in range(pulses):
        far = jnp.where(has_next, halo_ref[p, :, :taps].astype(F32), 0.0)
        for c in range(2):
            rows[c * group + p : c * group + p + 1, span:] = far[c : c + 1]
    done = correlate(rows, even, odd, table, span // LANE, group)
    for s in range(sections):
        stacked = early_ref[s] if s < ready else as_chunk(done, s - ready, chunk // LANE, group, pulses)
        slot = section ^ s
        other_core = slot % 2
        place = 1 - slot // 2

        @pl.when(other_core == 0)
        def _():
            keep_ref[place] = stacked

        @pl.when(other_core == 1)
        def _():
            give_ref[place] = stacked


def row_scratch(blocks, group):
    return [
        pltpu.VMEM((2 * group, blocks * LANE), F32),
        pltpu.VMEM((blocks * group, 2 * LANE), BF16),
        pltpu.VMEM((blocks * group, 2 * LANE), BF16),
    ]


def begin_compression(echo, chirp, sections, group):
    _, _, length = echo.shape
    taps = chirp.shape[1]
    chunk = length // sections
    early = (length - taps) // chunk
    return pl.pallas_call(
        functools.partial(begin_kernel, group=group),
        out_shape=(
            jax.ShapeDtypeStruct((early, 3 * group, chunk // 2), BF16),
            jax.ShapeDtypeStruct((2 * group, length - early * chunk), F32),
            jax.ShapeDtypeStruct(((taps // LANE + 1) * 2 * LANE, 2 * LANE), BF16),
        ),
        scratch_shapes=row_scratch(length // LANE, group),
        compiler_params=pltpu.CompilerParams(vmem_limit_bytes=24 * 1024 * 1024),
        name="begin_compression",
    )(echo, chirp)


def finish_compression(place, early, late, halo, table, group):
    blocks = late.shape[1] // LANE + table.shape[0] // (2 * LANE) - 1
    return pl.pallas_call(
        functools.partial(finish_kernel, group=group),
        out_shape=[jax.ShapeDtypeStruct((2, *early.shape[1:]), BF16)] * 2,
        in_specs=[pl.BlockSpec(memory_space=pltpu.SMEM)] + [pl.BlockSpec(memory_space=pltpu.VMEM)] * 4,
        scratch_shapes=row_scratch(blocks, group),
        compiler_params=pltpu.CompilerParams(vmem_limit_bytes=24 * 1024 * 1024),
        name="finish_compression",
    )(place, early, late, halo, table)


def image_kernel(operator_ref, both_ref, *refs, group):
    chunks, (out_ref, parts, sems) = refs[:-3], refs[-3:]
    count, _, tile = parts.shape
    width = both_ref.shape[2]
    held = [both_ref[1]] + [chunk[...] for chunk in chunks]
    held = [value.astype(F32) for value in held]
    copies = []
    for i in range(count):
        half, at = divmod(i * tile, width)
        rows = []
        for value in held:
            for first in range(0, value.shape[0], 3 * group):
                rows.append(value[first + half * group : first + (half + 1) * group, at : at + tile])
                rows.append(value[first + 2 * group : first + 3 * group, at : at + tile])
        pulses = jnp.concatenate(rows, axis=0).astype(BF16)
        result = jnp.dot(
            operator_ref[half], jnp.concatenate([pulses, pulses], axis=0), preferred_element_type=F32
        )
        parts[i] = result.astype(BF16)
        copy = pltpu.make_async_copy(parts.at[i], out_ref.at[:, i * tile : (i + 1) * tile], sems.at[i])
        copy.start()
        copies.append(copy)
    for copy in copies:
        copy.wait()


def form_image(operator, both, chunks, group):
    height, half = operator.shape[1], both.shape[2]
    tile = 256 if half % 256 == 0 else half
    count = 2 * half // tile
    return pl.pallas_call(
        functools.partial(image_kernel, group=group),
        out_shape=jax.ShapeDtypeStruct((height, 2 * half), BF16),
        in_specs=[pl.BlockSpec(memory_space=pltpu.VMEM)] * (2 + len(chunks)),
        out_specs=pl.BlockSpec(memory_space=pl.ANY),
        scratch_shapes=[
            pltpu.VMEM((count, height, tile), BF16),
            pltpu.SemaphoreType.DMA((count,)),
        ],
        compiler_params=pltpu.CompilerParams(vmem_limit_bytes=16 * 1024 * 1024),
        name="form_image",
    )(operator, both, *chunks)


def swap(value, axis, by):
    count = lax.axis_size(axis)
    return lax.ppermute(value, axis, [(i, i ^ by) for i in range(count)])


def swap_by(value, move):
    sections, subs = lax.axis_size("section"), lax.axis_size("sub")
    pairs = []
    for s in range(sections):
        for a in range(subs):
            to_s, to_a = move(s, a)
            pairs.append((s * subs + a, to_s * subs + to_a))
    return lax.ppermute(value, ("section", "sub"), pairs)


def from_next(value, axis):
    count = lax.axis_size(axis)
    return lax.ppermute(value, axis, [(i, (i - 1) % count) for i in range(count)])


def on_device(echoes, chirp, steer, pulse_order, band_coef, band_start, band_width):
    sections, subs = lax.axis_size("section"), lax.axis_size("sub")
    pulses_each = echoes.shape[2]
    group = ceil_to(pulses_each, SUBL)
    section = lax.axis_index("section").astype(jnp.int32).reshape(1)
    coef = jnp.swapaxes(band_coef, 4, 5)
    weights = jnp.swapaxes(steer, 2, 3)
    levels, _, sides, parts, taps, beams = coef.shape
    dims = (levels, sides, parts, taps, beams)

    echo = jnp.transpose(echoes[:, 0], (1, 0, 2))
    halo = from_next(echo, "rng")
    echo, chirp, packed = prepare(
        echo, chirp, coef, band_start, band_width, weights, pulse_order, sections, group
    )
    has_next = (lax.axis_index("rng") < lax.axis_size("rng") - 1).astype(jnp.int32)
    early, late, table = begin_compression(echo, chirp, sections, group)
    place = section + sections * has_next
    keep, give = finish_compression(place, early, late, halo, table, group)
    height = keep.shape[1]
    both = jnp.zeros((2, 2 * height, keep.shape[2]), BF16)
    both = lax.dynamic_update_slice(both, keep, (0, 0, 0))
    given = swap(give, "section", 1)
    both, packed = lax.optimization_barrier((both, packed))
    packed_partner = swap(packed, "sub", 1) if subs == 2 else packed
    both = lax.dynamic_update_slice(both, given, (0, height, 0))
    if subs != 2:
        chunks = [both[1], swap(both[0], "section", 2)]
        return merge_images(section, chunks, packed, dims, sections, group, pulses_each)
    chunks = [
        swap_by(both[0], lambda s, a: (s ^ 2, a ^ 1)),
        swap_by(both[0], lambda s, a: (s ^ 2, a)),
        swap_by(both[1], lambda s, a: (s, a ^ 1)),
    ]
    operator = fold_operator(section, packed, packed_partner, dims, sections, group, pulses_each)
    image = form_image(operator, both, chunks, group)
    return image.reshape(2, beams, 1, image.shape[1])


def unpack(chunk, group, each):
    lead = jnp.concatenate([chunk[:group], chunk[group : 2 * group]], axis=1)
    moved, rest = group - each, chunk[2 * group :]
    tail = jnp.concatenate([rest[: each - moved], rest[group // 2 : group // 2 + each - moved]], axis=1)
    return jnp.concatenate([lead, tail], axis=0)


def merge_images(section, chunks, packed, dims, sections, group, each):
    levels, sides, parts, taps, beams = dims
    width = sections * group
    first = levels * sides * parts * taps
    table = packed[first : first + parts * width].reshape(parts, sections, group, beams)
    table = jnp.take(table, section[0] ^ jnp.arange(sections), axis=1)[:, :, :each]
    chunks = [
        unpack(chunk[first : first + 3 * group], group, each)
        for chunk in chunks
        for first in range(0, chunk.shape[0], 3 * group)
    ]
    real, imag = table[0], table[1]
    rows = jnp.concatenate(
        [jnp.concatenate([real, -imag], axis=1), jnp.concatenate([imag, real], axis=1)], axis=2
    )
    image = lax.dot_general(
        rows.reshape(-1, 2 * beams), jnp.concatenate(chunks, axis=0), (((0,), (0,)), ((), ())), preferred_element_type=F32
    ).astype(BF16)
    starts = packed[first + parts * width :].astype(jnp.int32)
    column = jnp.arange(beams, dtype=jnp.int32)
    bits = lax.axis_size("sub").bit_length() - 1
    for level in range(levels):
        partner = swap(image, "sub", 1 << (level % bits))
        operands = []
        for side in range(sides):
            at = (level * sides + side) * parts * taps
            coef = packed[at : at + parts * taps].reshape(parts, taps, beams)
            offset = column[:, None] - starts[level * sides + side][None, :]
            hits = (offset[None] == jnp.arange(taps, dtype=jnp.int32)[:, None, None]).astype(BF16)
            operands.append(jnp.einsum("ptq,tcq->pqc", coef, hits, preferred_element_type=F32).astype(BF16))
        top = jnp.concatenate([operands[0][0], -operands[0][1], operands[1][0], -operands[1][1]], axis=1)
        low = jnp.concatenate([operands[0][1], operands[0][0], operands[1][1], operands[1][0]], axis=1)
        image = jnp.dot(
            jnp.concatenate([top, low], axis=0),
            jnp.concatenate([image, partner], axis=0),
            preferred_element_type=F32,
        ).astype(BF16)
    return image.reshape(2, beams, 1, image.shape[1])


def solution(mesh):
    return jax.shard_map(
        on_device,
        mesh=mesh,
        in_specs=(
            P(None, "sub", "section", "rng"),
            P(),
            P(None, "sub", None, None),
            P("sub", None),
            P(None, "sub", None, None, None, None),
            P(None, "sub", None, None),
            P(None, "sub", None, None),
        ),
        out_specs=P(None, "sub", "rng", "section"),
        check_vma=False,
    )
```
